32 devices in a mesh: expert: 8 (over y, x, core), shard: 4 (over z).
Axes of the slice: x: 2, y: 2, z: 4, core: 2. Of those that a mesh axis runs over, the one named last changes fastest.
Arguments:
- tokens: bfloat16 [4096, 2048], P(('expert', 'shard')), may hold values from -6 to 6
- segments: int32 [32, 128], P(('expert', 'shard')), may hold values from 0 to 15, never falling along the last dimension, each value on 1 to 64 neighbouring positions
- routes: int32 [4096, 8], P(('expert', 'shard')), may hold values from 0 to 63, all different within a row; in each aligned block of 128 rows (0 to 127, 128 to 255, ...) at most 24 rows name the same one
- attn_gain: bfloat16 [2048], P('shard'), may hold values from 0.25 to 1.75
- query_key_value_weight: bfloat16 [2048, 5120], P('shard'), may hold values from -0.125 to 0.125
- query_norm_gain: bfloat16 [128], P('shard'), may hold values from 0.25 to 1.75
- k_gain: bfloat16 [128], P('shard'), may hold values from 0.25 to 1.75
- w_out: bfloat16 [4096, 2048], P('shard'), may hold values from -0.5 to 0.5
- ffn_gain: bfloat16 [2048], P('shard'), may hold values from 0.25 to 1.75
- router: bfloat16 [2048, 64], P('shard'), may hold values from -0.0625 to 0.0625
- w_gate: bfloat16 [64, 768, 2048], P('expert', 'shard'), may hold values from -0.125 to 0.125
- w_up: bfloat16 [64, 768, 2048], P('expert', 'shard'), may hold values from -0.125 to 0.125
- w_down: bfloat16 [64, 2048, 768], P('expert', None, 'shard'), may hold values from -0.625 to 0.625
- d_out: bfloat16 [4096, 2048], P(('expert', 'shard')), may hold values from -6 to 6
Outputs:
- result: bfloat16 [4096, 2048], P(('expert', 'shard'))
- d_tokens: bfloat16 [4096, 2048], P(('expert', 'shard'))
- d_attn_gain: float32 [2048], P('shard')
- d_w_qkv: float32 [2048, 5120], P('shard')
- d_q_gain: float32 [128], P('shard')
- d_k_gain: float32 [128], P('shard')
- d_w_out: float32 [4096, 2048], P('shard')
- d_ffn_gain: float32 [2048], P('shard')
- d_router: float32 [2048, 64], P('shard')
- d_w_gate: float32 [64, 768, 2048], P('expert', 'shard')
- d_w_up: float32 [64, 768, 2048], P('expert', 'shard')
- d_w_down: float32 [64, 2048, 768], P('expert', None, 'shard')
The draws below stay inside these ranges and needn't reach their ends.
Inputs may be any that keep to these rules, and one draw needn't show every extreme that they name: `segments`: in each device's row the numbers never fall, each document has 1 to 64 tokens and one has exactly 64. `routes`: each token names 8 different experts; among the tokens of one device no expert is named more than 24 times, a bound that some block reaches.
All inputs are finite; a program needn't handle non-finite values.
Results may differ from the reference program's by a relative error of at most 0.023.
Values may be sent and summed in bfloat16 or wider, within the bound.
A program may use at most 448 MiB of HBM per device.

```python
import math
import jax
import jax.numpy as jnp
import numpy as np
from jax import lax

MODEL_WIDTH = 2048
QUERY_HEADS = 32
KEY_VALUE_HEADS = 4
HEAD_SIZE = 128
FF = 768
TOPK = 8
TOK_DEV = 128
EXPERTS = 64
TOKENS = 4096
CAP = 24
DOC_MOST = 64
SEG_COUNT = 16
N_EXPERT = 8
N_SHARD = 4


def levels(own_key, dims, cuts, least, largest):
    def one(axis_at, blocks):
        heights = jax.random.uniform(jax.random.fold_in(jax.random.fold_in(own_key, 6), axis_at), (blocks,), jnp.float32, least / len(cuts), largest / len(cuts))
        return jnp.repeat(jnp.exp(heights), dims[axis_at] // blocks).reshape((-1,) + (1,) * (len(dims) - axis_at - 1))

    loudness = one(*cuts[0])
    for cut in cuts[1:]:
        loudness = loudness * one(*cut)
    return loudness


def split_up(count, total, bound, skew):
    loads = [(1 << 20) // math.isqrt(rank ** skew) + 1 for rank in range(2, count + 1)]
    spare, given = total - bound - (count - 1), [1] * (count - 1)
    while spare > 0:
        movable = [i for i in range(count - 1) if given[i] < bound]
        whole, remaining = sum([loads[i] for i in movable]), spare
        for i in movable:
            extra = min(bound - given[i], max(1, remaining * loads[i] // whole), spare)
            given[i] = given[i] + extra
            spare = spare - extra
    return np.array([bound] + given)


def ragged(key, number_of, total, most, lean):
    if number_of == 2:
        one = jax.random.randint(key, (), max(1, total - most), min(most, total - 1) + 1)
        return jnp.stack([one, total - one])
    lengths = jnp.asarray(split_up(number_of, total, most, lean), jnp.int32)
    couples = (number_of - 1) // 2
    source_of, receiver = lengths[1:1 + 2 * couples:2], lengths[2:2 + 2 * couples:2]
    room = jnp.minimum(source_of - 1, most - receiver)
    shifted = jax.random.randint(jax.random.fold_in(key, 1), (couples,), 0, 1 << 20) % (room + 1)
    lengths = lengths.at[1:1 + 2 * couples:2].set(source_of - shifted).at[2:2 + 2 * couples:2].set(receiver + shifted)
    return lengths[jax.random.permutation(jax.random.fold_in(key, 2), number_of)]


def routed_block(key, own, number, rows, amount, top, limit, lean):
    order = jax.random.permutation(key, amount)
    crowded, common = shares(amount, rows * top, limit, lean, True), shares(amount, rows * top, limit, lean, False)
    places = jnp.arange(amount)

    def named(tallies, turn):
        used = int((tallies > 0).sum())
        fixed = max(1, used // 4)
        shifted = fixed + (places - fixed + turn * (used - fixed)) % max(1, amount - fixed)
        return jnp.zeros((amount,), jnp.int32).at[order[jnp.where(places < fixed, places, shifted)]].set(jnp.asarray(tallies, jnp.int32))

    tallies = jnp.where(number % 4 == 0, named(crowded, number // 4), named(common, number - number // 4 - 1))
    mixed = jax.random.permutation(jax.random.fold_in(own, 3), amount)
    donor, taker = mixed[0:amount // 2 * 2:2], mixed[1:amount // 2 * 2:2]
    slack = jnp.minimum(tallies[donor] - 1, limit - tallies[taker]) // 2
    slack = jnp.where((donor == order[0]) | (taker == order[0]) | (tallies[taker] == 0), 0, jnp.maximum(slack, 0))
    shifted = jax.random.randint(jax.random.fold_in(own, 4), (amount // 2,), 0, 1 << 20) % (slack + 1)
    tallies = tallies.at[donor].add(-shifted).at[taker].add(shifted)
    items = jnp.searchsorted(jnp.cumsum(tallies), jnp.arange(rows * top), side="right").astype(jnp.int32)
    grid = items.reshape(top, rows).T
    grid = grid[jax.random.permutation(jax.random.fold_in(own, 1), rows)]
    turn = jax.random.randint(jax.random.fold_in(own, 2), (rows, 1), 0, top)
    return jnp.take_along_axis(grid, (jnp.arange(top)[None, :] + turn) % top, axis=1)


def shares(number_of, total, most, slope, full):
    portions = [(1 << 20) // math.isqrt(standing ** slope) + 1 for standing in range(1, number_of + 1)]
    largest = most if full else min(most, max(-(-total // number_of), total * portions[0] // sum(portions)))
    least = 1 if total - largest >= number_of - 1 else 0
    holding, surplus = [largest] + [least] * (number_of - 1), total - largest - least * (number_of - 1)
    while surplus > 0:
        free = [i for i in range(1, number_of) if holding[i] < largest] or [i for i in range(1, number_of) if holding[i] < most]
        whole, budget = sum([portions[i] for i in free]), surplus
        for i in free:
            extra = min(most - holding[i], max(1, budget * portions[i] // whole), surplus)
            holding[i] = holding[i] + extra
            surplus = surplus - extra
    return np.array(holding)


def noise(rng, extent, scale, bound, cuts=(), kind=jnp.bfloat16):
    array = scale * jax.random.normal(rng, extent, jnp.float32)
    if cuts:
        array = array * levels(rng, extent, cuts, -0.22, 0.18)
    return jnp.clip(array, -bound, bound).astype(kind)


def setup_inputs(seed: int = 0) -> dict:
    key_list = jax.random.split(jax.random.key(seed), 15)
    tokens = noise(key_list[0], (TOKENS, MODEL_WIDTH), 1.0, 6.0, ((0, 32),))
    segments = jax.vmap(lambda own: jnp.searchsorted(jnp.cumsum(ragged(own, SEG_COUNT, TOK_DEV, DOC_MOST, 2)), jnp.arange(TOK_DEV), side="right"))(jax.random.split(key_list[1], (N_EXPERT * N_SHARD))).reshape((N_EXPERT * N_SHARD, TOK_DEV)).astype(jnp.int32)
    routes_keys = jax.random.split(jax.random.fold_in(key_list[2], 1), TOKENS // TOK_DEV)
    routes_turns = jax.random.permutation(jax.random.fold_in(key_list[2], 3), TOKENS // TOK_DEV)
    routes = jax.vmap(lambda own, number: routed_block(jax.random.fold_in(key_list[2], 2), own, number, TOK_DEV, EXPERTS, TOPK, CAP, 1))(routes_keys, routes_turns).reshape((TOKENS, TOPK))
    attn_gain = jnp.clip(1.0 + 0.15 * jax.random.normal(key_list[3], (MODEL_WIDTH,), jnp.float32), 0.25, 1.75).astype(jnp.bfloat16)
    query_key_value_weight = noise(key_list[4], (MODEL_WIDTH, (QUERY_HEADS + 2 * KEY_VALUE_HEADS) * HEAD_SIZE), MODEL_WIDTH ** -0.5, 0.125, ((0, 4),))
    query_norm_gain = jnp.clip(1.0 + 0.15 * jax.random.normal(key_list[5], (HEAD_SIZE,), jnp.float32), 0.25, 1.75).astype(jnp.bfloat16)
    k_gain = jnp.clip(1.0 + 0.15 * jax.random.normal(key_list[6], (HEAD_SIZE,), jnp.float32), 0.25, 1.75).astype(jnp.bfloat16)
    w_out = noise(key_list[7], (QUERY_HEADS * HEAD_SIZE, MODEL_WIDTH), (QUERY_HEADS * HEAD_SIZE // 32) ** -0.5, 0.5, ((0, 4),))
    ffn_gain = jnp.clip(1.0 + 0.15 * jax.random.normal(key_list[8], (MODEL_WIDTH,), jnp.float32), 0.25, 1.75).astype(jnp.bfloat16)
    router = noise(key_list[9], (MODEL_WIDTH, EXPERTS), (4 * MODEL_WIDTH) ** -0.5, 0.0625, ((0, 4),))
    w_gate = noise(key_list[10], (EXPERTS, FF, MODEL_WIDTH), MODEL_WIDTH ** -0.5, 0.125, ((0, 8), (1, 4)))
    w_up = noise(key_list[11], (EXPERTS, FF, MODEL_WIDTH), MODEL_WIDTH ** -0.5, 0.125, ((0, 8), (1, 4)))
    w_down = noise(key_list[12], (EXPERTS, MODEL_WIDTH, FF), (FF // 8) ** -0.5, 0.625, ((0, 8), (2, 4)))
    d_out = noise(key_list[13], (TOKENS, MODEL_WIDTH), 1.0, 6.0, ((0, 32),))
    return dict(tokens=tokens, segments=segments, routes=routes, attn_gain=attn_gain, query_key_value_weight=query_key_value_weight, query_norm_gain=query_norm_gain, k_gain=k_gain, w_out=w_out, ffn_gain=ffn_gain, router=router, w_gate=w_gate, w_up=w_up, w_down=w_down, d_out=d_out)


@jax.custom_vjp
def reduced_precision(v):
    return lax.optimization_barrier(v.astype(jnp.bfloat16)).astype(jnp.float32)

@jax.custom_vjp
def low_back(v):
    return v

def low_keep(v):
    return (reduced_precision(v), None)

def low_pass(kept, grad):
    return (grad,)

def back_keep(v):
    return (v, None)

def back_low(kept, grad):
    return (reduced_precision(grad),)
reduced_precision.defvjp(low_keep, low_pass)
low_back.defvjp(back_keep, back_low)
EPS = 1e-06
THETA = 1000000.0
HIGHEST = lax.Precision.HIGHEST

def product(left, right):
    return jnp.dot(left, right, precision=HIGHEST)

def row_norm_values(values, gain):
    return values * lax.rsqrt(lax.optimization_barrier(jnp.mean(values * values, axis=-1, keepdims=True)) + EPS) * gain

def doc_positions(segment_row):
    places = jnp.arange(segment_row.shape[0], dtype=jnp.int32)
    change = jnp.concatenate([jnp.ones((1,), jnp.int32), (segment_row[1:] != segment_row[:-1]).astype(jnp.int32)])
    return places - lax.cummax(places * change, axis=0)

def apply_rotary(values, token_positions):
    half_width = HEAD_SIZE // 2
    frequency = THETA ** (-2.0 * jnp.arange(half_width, dtype=jnp.float32) / HEAD_SIZE)
    angles = token_positions.astype(jnp.float32)[:, None] * frequency[None, :]
    cosine = jnp.cos(angles)[:, None, :]
    sine_part = jnp.sin(angles)[:, None, :]
    first_half = values[..., :half_width]
    second_half = values[..., half_width:]
    return jnp.concatenate([first_half * cosine - second_half * sine_part, second_half * cosine + first_half * sine_part], axis=-1)

def attend_device(packed, query_norm_gain, k_gain):
    query_key_value_rows, segment_row = packed
    sequence_length = query_key_value_rows.shape[0]
    token_positions = doc_positions(segment_row)
    query_matrix = query_key_value_rows[:, :QUERY_HEADS * HEAD_SIZE].reshape(sequence_length, QUERY_HEADS, HEAD_SIZE)
    key_row_block = query_key_value_rows[:, QUERY_HEADS * HEAD_SIZE:(QUERY_HEADS + KEY_VALUE_HEADS) * HEAD_SIZE].reshape(sequence_length, KEY_VALUE_HEADS, HEAD_SIZE)
    value_row_block = query_key_value_rows[:, (QUERY_HEADS + KEY_VALUE_HEADS) * HEAD_SIZE:].reshape(sequence_length, KEY_VALUE_HEADS, HEAD_SIZE)
    query_matrix = reduced_precision(apply_rotary(row_norm_values(query_matrix, query_norm_gain), token_positions)).reshape(sequence_length, KEY_VALUE_HEADS, QUERY_HEADS // KEY_VALUE_HEADS, HEAD_SIZE)
    key_row_block = reduced_precision(apply_rotary(row_norm_values(key_row_block, k_gain), token_positions))
    value_row_block = reduced_precision(value_row_block)
    scores = jnp.einsum('qhgd,khd->hgqk', query_matrix, key_row_block, precision=HIGHEST) * HEAD_SIZE ** (-0.5)
    scores = low_back(scores)
    places = jnp.arange(sequence_length, dtype=jnp.int32)
    allowed = (segment_row[:, None] == segment_row[None, :]) & (places[None, :] <= places[:, None])
    scores = jnp.where(allowed, scores, -1e+30)
    weights = reduced_precision(jax.nn.softmax(scores, axis=-1))
    mixed_heads = jnp.einsum('hgqk,khd->qhgd', weights, value_row_block, precision=HIGHEST).reshape(sequence_length, QUERY_HEADS * HEAD_SIZE)
    return low_back(reduced_precision(mixed_heads))

def layer(tokens, attn_gain, query_key_value_weight, query_norm_gain, k_gain, w_out, ffn_gain, router, w_gate, w_up, w_down, segments, routes, token_table, pair_table):
    devices = segments.shape[0]
    normed_one = reduced_precision(row_norm_values(tokens, attn_gain))
    projected_rows = low_back(product(normed_one, query_key_value_weight))

    def one_device(packed):
        return attend_device(packed, query_norm_gain, k_gain)
    mixed_heads = lax.map(jax.checkpoint(one_device), (projected_rows.reshape(devices, TOK_DEV, -1), segments))
    mixed_heads = mixed_heads.reshape(tokens.shape[0], QUERY_HEADS * HEAD_SIZE)
    branch = low_back(product(mixed_heads, w_out))
    middle = tokens + branch
    normed_two = reduced_precision(row_norm_values(middle, ffn_gain))
    logits = low_back(product(normed_two, router))
    chance = jax.nn.softmax(logits, axis=-1)
    chosen = jnp.take_along_axis(chance, routes, axis=1)
    gates = chosen / lax.optimization_barrier(jnp.sum(chosen, axis=1, keepdims=True))
    padded_rows = jnp.concatenate([normed_two, jnp.zeros((1, MODEL_WIDTH), normed_two.dtype)], axis=0)
    padded_gates = jnp.concatenate([gates.reshape(-1), jnp.zeros((1,), gates.dtype)])

    def one_expert(packed):
        token_ids, pair_ids, gate_mat, up_mat, down_mat = packed
        rows_in = low_back(padded_rows[token_ids])
        gate_proj = low_back(product(rows_in, gate_mat.T))
        up_proj = low_back(product(rows_in, up_mat.T))
        activation = reduced_precision(jax.nn.silu(gate_proj) * up_proj)
        expert_out = low_back(reduced_precision(product(activation, down_mat.T)))
        return expert_out * padded_gates[pair_ids][:, None]
    weighted = lax.map(jax.checkpoint(one_expert), (token_table, pair_table, w_gate, w_up, w_down))
    mixture = jnp.zeros((tokens.shape[0] + 1, MODEL_WIDTH), tokens.dtype).at[token_table.reshape(-1)].add(weighted.reshape(-1, MODEL_WIDTH))
    return middle + mixture[:-1]

def reference(tokens, segments, routes, attn_gain, query_key_value_weight, query_norm_gain, k_gain, w_out, ffn_gain, router, w_gate, w_up, w_down, d_out):
    devices = segments.shape[0]
    per_device = TOK_DEV * TOPK
    flat_routes = routes.reshape(devices, per_device)
    onehot = (flat_routes[:, :, None] == jnp.arange(EXPERTS, dtype=jnp.int32)[None, None, :]).astype(jnp.int32)
    ranks = lax.optimization_barrier(jnp.sum((jnp.cumsum(onehot, axis=1) - 1) * onehot, axis=2))
    pair_ids = jnp.arange(devices * per_device, dtype=jnp.int32).reshape(devices, per_device)
    device_ids = jnp.broadcast_to(jnp.arange(devices, dtype=jnp.int32)[:, None], flat_routes.shape)
    pair_table = jnp.full((EXPERTS, devices, CAP), devices * per_device, jnp.int32)
    pair_table = pair_table.at[flat_routes, device_ids, ranks].set(pair_ids).reshape(EXPERTS, devices * CAP)
    token_table = pair_table // TOPK

    def forward(tokens_f, attn_f, qkv_f, qgain_f, kgain_f, out_f, ffn_f, router_f, gate_f, up_f, down_f):
        return layer(tokens_f, attn_f, qkv_f, qgain_f, kgain_f, out_f, ffn_f, router_f, gate_f, up_f, down_f, segments, routes, token_table, pair_table)
    result, pullback = jax.vjp(forward, tokens.astype(jnp.float32), attn_gain.astype(jnp.float32), query_key_value_weight.astype(jnp.float32), query_norm_gain.astype(jnp.float32), k_gain.astype(jnp.float32), w_out.astype(jnp.float32), ffn_gain.astype(jnp.float32), router.astype(jnp.float32), w_gate.astype(jnp.float32), w_up.astype(jnp.float32), w_down.astype(jnp.float32))
    grads_all = pullback(d_out.astype(jnp.float32))
    return (result.astype(jnp.bfloat16), grads_all[0].astype(jnp.bfloat16), grads_all[1], grads_all[2], grads_all[3], grads_all[4], grads_all[5], grads_all[6], grads_all[7], grads_all[8], grads_all[9], grads_all[10])
```

```python
import jax
import jax.numpy as jnp
from jax import lax
from jax.sharding import PartitionSpec as P

MODEL_WIDTH = 2048
QUERY_HEADS = 32
KEY_VALUE_HEADS = 4
HEAD_SIZE = 128
TOPK = 8
EXP_DEV = 8
TAIL = 128
GROUP_BLOCKS = 32

EPS = 1e-06
THETA = 1000000.0
LOW = jnp.bfloat16
FULL = jnp.float32


def unit_norm(values):
    inverse = lax.rsqrt(jnp.mean(values * values, axis=-1, keepdims=True) + EPS)
    return values * inverse, inverse


def norm_back(incoming, unit_rows, inverse, gain):
    inner = incoming * gain
    return inverse * (inner - unit_rows * jnp.mean(inner * unit_rows, axis=-1, keepdims=True))


def rotate(values, cosine, sine):
    half = values.shape[-1] // 2
    a, b = values[..., :half], values[..., half:]
    return jnp.concatenate([a * cosine - b * sine, b * cosine + a * sine], axis=-1)


def rotate_back(values, cosine, sine):
    half = values.shape[-1] // 2
    a, b = values[..., :half], values[..., half:]
    return jnp.concatenate([a * cosine + b * sine, b * cosine - a * sine], axis=-1)


def dot(spec, left, right):
    return jnp.einsum(spec, left, right, preferred_element_type=FULL)


def positions_of(segment_row):
    places = jnp.arange(segment_row.shape[0], dtype=jnp.int32)
    before = (segment_row[None, :] == segment_row[:, None]) & (places[None, :] < places[:, None])
    return jnp.sum(before.astype(jnp.int32), axis=1)


def columns(parts, rows):
    wide = jnp.concatenate([part.astype(LOW) for part in parts], axis=1)
    return jnp.pad(wide, ((0, rows - wide.shape[0]), (0, TAIL - wide.shape[1])))


def per_device(
    tokens,
    segments,
    routes,
    attn_gain,
    qkv_weight,
    query_gain,
    k_gain,
    w_out,
    ffn_gain,
    router,
    w_gate,
    w_up,
    w_down,
    d_out,
):
    owners = lax.axis_size("expert")
    planes = lax.axis_size("shard")
    me = lax.axis_index("expert")
    plane = lax.axis_index("shard")
    length = tokens.shape[0]
    blocks = owners * planes
    experts_all = router.shape[1]
    capacity = 3 * length * TOPK // (2 * experts_all)
    heads = QUERY_HEADS // owners
    query_cols = heads * HEAD_SIZE
    scaling = HEAD_SIZE ** (-0.5)
    both = ("expert", "shard")
    rows_in = qkv_weight.shape[0]

    kv_head = me * KEY_VALUE_HEADS // owners
    k_at = QUERY_HEADS * HEAD_SIZE + kv_head * HEAD_SIZE
    v_at = k_at + KEY_VALUE_HEADS * HEAD_SIZE
    gains = columns(
        [
            router,
            attn_gain[:, None],
            ffn_gain[:, None],
            jnp.pad(query_gain, (0, rows_in - query_gain.shape[0]))[:, None],
            jnp.pad(k_gain, (0, rows_in - k_gain.shape[0]))[:, None],
        ],
        rows_in,
    )
    mine = jnp.concatenate(
        [
            lax.dynamic_slice_in_dim(qkv_weight, me * query_cols, query_cols, 1),
            lax.dynamic_slice_in_dim(qkv_weight, k_at, HEAD_SIZE, 1),
            lax.dynamic_slice_in_dim(qkv_weight, v_at, HEAD_SIZE, 1),
            gains,
        ],
        axis=1,
    )
    gathered = lax.all_gather(mine, "shard", axis=0, tiled=True)
    qkv_cols = query_cols + 2 * HEAD_SIZE
    wqkv = gathered[:, :qkv_cols]
    router_full = gathered[:, qkv_cols : qkv_cols + experts_all]
    gain_cols = gathered[:, qkv_cols + experts_all :].astype(FULL)
    gain_one, gain_two = gain_cols[:, 0], gain_cols[:, 1]
    per = query_gain.shape[0]
    by_plane = gain_cols.reshape(planes, rows_in, -1)[:, :per]
    gain_query = by_plane[:, :, 2].reshape(-1)
    gain_key = by_plane[:, :, 3].reshape(-1)

    segment_row = segments[0]
    token_tail = columns(
        [segment_row[:, None], positions_of(segment_row)[:, None]], length
    )
    plane_rows = lax.all_gather(
        jnp.concatenate([tokens, token_tail], axis=1), "expert", axis=0, tiled=False
    )
    plane_tokens = plane_rows[:, :, :MODEL_WIDTH].astype(FULL)
    plane_segments = plane_rows[:, :, MODEL_WIDTH]
    plane_places = plane_rows[:, :, MODEL_WIDTH + 1].astype(FULL)

    out_rows = w_out.shape[0]
    first = me * query_cols
    offset = first - plane * out_rows
    if out_rows >= query_cols:
        held = (offset >= 0) & (offset < out_rows)
        piece = lax.dynamic_slice_in_dim(w_out, jnp.where(held, offset, 0), query_cols, 0)
        w_mine = lax.psum(jnp.where(held, piece, 0).astype(LOW), "shard")
    else:
        parts = query_cols // out_rows
        at = plane - me * parts
        held = (at >= 0) & (at < parts)
        spread = jnp.where(held & (jnp.arange(parts) == at)[:, None, None], w_out[None], 0)
        w_mine = lax.psum(spread.astype(LOW), "shard").reshape(query_cols, MODEL_WIDTH)

    d_tail = columns([routes], length)
    d_all = lax.all_gather(
        jnp.concatenate([d_out, d_tail], axis=1), both, axis=0, tiled=False
    )

    unit_plane, inverse_plane = unit_norm(plane_tokens)
    h1 = (unit_plane * gain_one).astype(LOW)
    projected = dot("bqd,df->bqf", h1, wqkv)
    half = HEAD_SIZE // 2
    frequency = THETA ** (-2.0 * jnp.arange(half, dtype=FULL) / HEAD_SIZE)
    angles = plane_places[:, :, None] * frequency
    cosine, sine = jnp.cos(angles), jnp.sin(angles)
    cosine_q, sine_q = cosine[:, :, None, :], sine[:, :, None, :]
    query_raw = projected[:, :, :query_cols].reshape(owners, length, heads, HEAD_SIZE)
    key_raw = projected[:, :, query_cols : query_cols + HEAD_SIZE]
    value = projected[:, :, query_cols + HEAD_SIZE :].astype(LOW)
    query_unit, query_inverse = unit_norm(query_raw)
    key_unit, key_inverse = unit_norm(key_raw)
    query = rotate(query_unit * gain_query, cosine_q, sine_q).astype(LOW)
    key = rotate(key_unit * gain_key, cosine, sine).astype(LOW)
    places = jnp.arange(length, dtype=jnp.int32)
    allowed = (plane_segments[:, :, None] == plane_segments[:, None, :]) & (
        places[None, :] <= places[:, None]
    )
    scores = dot("bqhd,bkd->bhqk", query, key) * scaling
    scores = jnp.where(allowed[:, None], scores, -1e30)
    highest = jnp.max(scores, axis=-1, keepdims=True)
    exponent = jnp.exp(scores - highest)
    probs = exponent / jnp.sum(exponent, axis=-1, keepdims=True)
    probs_low = probs.astype(LOW)
    mixed = dot("bhqk,bkd->bqhd", probs_low, value).astype(LOW)
    mixed = mixed.reshape(owners, length, query_cols)
    partial = dot("bqf,fd->bqd", mixed, w_mine).astype(LOW)
    branch = lax.psum_scatter(partial, "expert", scatter_dimension=0, tiled=False)

    middle = tokens.astype(FULL) + branch.astype(FULL)
    unit_two, inverse_two = unit_norm(middle)
    h2 = (unit_two * gain_two).astype(LOW)
    logits = dot("nd,de->ne", h2, router_full)
    chance = jax.nn.softmax(logits, axis=-1)
    named = jnp.sum(
        (routes[:, :, None] == jnp.arange(experts_all, dtype=jnp.int32)).astype(FULL), axis=1
    )
    chosen_sum = jnp.sum(named * chance, axis=1, keepdims=True)
    gates = named * chance / chosen_sum
    gates_high = gates.astype(LOW)
    gates_rest = (gates - gates_high.astype(FULL)).astype(LOW)
    h_all = lax.all_gather(
        jnp.concatenate([h2, gates_high, gates_rest], axis=1), both, axis=0, tiled=False
    )

    route_all = d_all[:, :, MODEL_WIDTH : MODEL_WIDTH + TOPK].astype(FULL)
    own_experts = (me * EXP_DEV + jnp.arange(EXP_DEV, dtype=jnp.int32)).astype(FULL)
    match = jnp.sum((route_all[:, :, :, None] == own_experts).astype(FULL), axis=2)
    earlier = (places[None, :] < places[:, None]).astype(LOW)
    rank = dot("ts,bsj->btj", earlier, match.astype(LOW))
    slot_ids = jnp.arange(capacity, dtype=jnp.int32).astype(FULL)
    place = jnp.where(match > 0, rank, -1.0).transpose(0, 2, 1)
    dispatch = (place[:, :, None, :] == slot_ids[:, None]).astype(LOW)

    def experts(h_rows, d_rows, gate_high, gate_rest, put):
        count = h_rows.shape[0]
        flat = put.reshape(count, EXP_DEV * capacity, length)
        x = dot("bst,btd->bsd", flat, h_rows).astype(LOW)
        dy = dot("bst,btd->bsd", flat, d_rows).astype(LOW)

        def by_expert(v):
            v = v.reshape(count, EXP_DEV, capacity, v.shape[-1])
            return v.transpose(1, 0, 2, 3).reshape(EXP_DEV, count * capacity, v.shape[-1])

        def by_block(v):
            v = v.reshape(EXP_DEV, count, capacity, v.shape[-1])
            return v.transpose(1, 0, 2, 3).reshape(count, EXP_DEV * capacity, v.shape[-1])

        x, dy = by_expert(x), by_expert(dy)
        gate_slot = dot("bjct,btj->jbc", put, gate_high) + dot("bjct,btj->jbc", put, gate_rest)
        gate_slot = gate_slot.reshape(EXP_DEV, count * capacity, 1)
        g = dot("erd,efd->erf", x, w_gate)
        u = dot("erd,efd->erf", x, w_up)
        da = dot("erd,edf->erf", dy, w_down)
        sigma = jax.nn.sigmoid(g)
        silu = g * sigma
        act = (silu * u).astype(LOW).astype(FULL)
        d_gate_slot = jnp.sum(act * da, axis=-1)
        act_gated = (act * gate_slot).astype(LOW)
        d_act = da * gate_slot
        dg = (d_act * u * sigma * (1.0 + g * (1.0 - sigma))).astype(LOW)
        du = (d_act * silu).astype(LOW)
        y = dot("erf,edf->erd", act_gated, w_down).astype(LOW)
        d_down = dot("erd,erf->edf", dy, act_gated)
        d_gate = dot("erf,erd->efd", dg, x)
        d_up = dot("erf,erd->efd", du, x)
        dx = (dot("erf,efd->erd", dg, w_gate) + dot("erf,efd->erd", du, w_up)).astype(LOW)
        mix = dot("bst,bsd->btd", flat, by_block(y)).astype(LOW)
        d_h = dot("bst,bsd->btd", flat, by_block(dx)).astype(LOW)
        d_g = dot(
            "bjct,jbc->btj", put.astype(FULL), d_gate_slot.reshape(EXP_DEV, count, capacity)
        )
        return mix, d_h, d_g, d_gate, d_up, d_down

    gate_cols = lax.dynamic_slice_in_dim(h_all, MODEL_WIDTH + me * EXP_DEV, EXP_DEV, 2)
    rest_cols = lax.dynamic_slice_in_dim(
        h_all, MODEL_WIDTH + experts_all + me * EXP_DEV, EXP_DEV, 2
    )
    step = min(blocks, GROUP_BLOCKS)
    mixes, d_hs, d_gs, totals = [], [], [], None
    for at in range(0, blocks, step):
        cut = slice(at, at + step)
        mix, d_h, d_g, *grads = experts(
            h_all[cut, :, :MODEL_WIDTH],
            d_all[cut, :, :MODEL_WIDTH],
            gate_cols[cut],
            rest_cols[cut],
            dispatch[cut],
        )
        mixes.append(mix)
        d_hs.append(d_h)
        d_gs.append(d_g)
        totals = grads if totals is None else [a + b for a, b in zip(totals, grads)]
    d_gate, d_up, d_down = totals
    d_g = jnp.concatenate(d_gs, axis=0)
    spread = jnp.zeros((blocks, length, TAIL), LOW)
    spread = lax.dynamic_update_slice_in_dim(spread, d_g.astype(LOW), me * EXP_DEV, 2)
    d_h_wide = jnp.concatenate([jnp.concatenate(d_hs, axis=0), spread], axis=2)

    def home(v):
        v = v.reshape(owners, planes, length, v.shape[-1])
        v = lax.psum_scatter(v, "expert", scatter_dimension=0, tiled=False)
        return lax.psum_scatter(v, "shard", scatter_dimension=0, tiled=False)

    d_home = home(d_h_wide)
    mixture = home(jnp.concatenate(mixes, axis=0))
    result = (middle + mixture.astype(FULL)).astype(LOW)

    upstream = d_out.astype(FULL)
    d_gates = d_home[:, MODEL_WIDTH : MODEL_WIDTH + experts_all].astype(FULL)
    d_chance = named * (d_gates - jnp.sum(d_gates * gates, axis=1, keepdims=True)) / chosen_sum
    d_logits = chance * (d_chance - jnp.sum(d_chance * chance, axis=1, keepdims=True))
    d_logits = d_logits.astype(LOW)
    d_h2 = d_home[:, :MODEL_WIDTH].astype(FULL) + dot("ne,de->nd", d_logits, router_full)
    d_gain_two = jnp.sum(d_h2 * unit_two, axis=0)
    d_middle = upstream + norm_back(d_h2, unit_two, inverse_two, gain_two)
    d_router = dot("nd,ne->de", h2, d_logits)

    d_branch = lax.all_gather(d_middle.astype(LOW), "expert", axis=0, tiled=False)
    d_w_out = dot("bqf,bqd->fd", mixed, d_branch).astype(LOW)
    d_mixed = dot("bqd,fd->bqf", d_branch, w_mine).astype(LOW)
    d_mixed = d_mixed.reshape(owners, length, heads, HEAD_SIZE)
    d_probs = dot("bqhd,bkd->bhqk", d_mixed, value)
    d_scores = probs * (d_probs - jnp.sum(d_probs * probs, axis=-1, keepdims=True))
    d_scores = d_scores.astype(LOW)
    d_query = dot("bhqk,bkd->bqhd", d_scores, key) * scaling
    d_key = dot("bhqk,bqhd->bkd", d_scores, query) * scaling
    d_value = dot("bhqk,bqhd->bkd", probs_low, d_mixed)
    d_query = rotate_back(d_query, cosine_q, sine_q)
    d_key = rotate_back(d_key, cosine, sine)
    d_gain_query = jnp.sum(d_query * query_unit, axis=(0, 1, 2))
    d_gain_key = jnp.sum(d_key * key_unit, axis=(0, 1))
    d_query = norm_back(d_query, query_unit, query_inverse, gain_query)
    d_key = norm_back(d_key, key_unit, key_inverse, gain_key)
    d_projected = jnp.concatenate(
        [d_query.reshape(owners, length, query_cols), d_key, d_value], axis=2
    ).astype(LOW)
    d_h1_part = dot("bqf,df->bqd", d_projected, wqkv).astype(LOW)
    d_h1 = lax.psum_scatter(d_h1_part, "expert", scatter_dimension=0, tiled=False).astype(FULL)
    resident = tokens.astype(FULL)
    unit_one, inverse_one = unit_norm(resident)
    d_gain_one = jnp.sum(d_h1 * unit_one, axis=0)
    d_tokens = (d_middle + norm_back(d_h1, unit_one, inverse_one, gain_one)).astype(LOW)

    d_wqkv = dot("bqd,bqf->df", h1, d_projected).astype(LOW)

    def by_rows(v):
        v = v.reshape(planes, per)
        return jnp.pad(v, ((0, 0), (0, rows_in - per))).reshape(-1)[:, None]

    d_tail = columns(
        [
            d_router,
            d_gain_one[:, None],
            d_gain_two[:, None],
            by_rows(d_gain_query),
            by_rows(d_gain_key),
        ],
        MODEL_WIDTH,
    )
    d_pack = lax.psum_scatter(
        jnp.concatenate([d_wqkv, d_tail], axis=1), "shard", scatter_dimension=0, tiled=True
    )
    d_pack = lax.all_gather(d_pack, "expert", axis=0, tiled=False).astype(FULL)
    d_q_cols = d_pack[:, :, :query_cols].transpose(1, 0, 2).reshape(rows_in, -1)
    d_kv = d_pack[:, :, query_cols:qkv_cols]
    d_kv = jnp.sum(d_kv.reshape(KEY_VALUE_HEADS, -1, rows_in, 2, HEAD_SIZE), axis=1)
    d_kv = d_kv.transpose(1, 2, 0, 3).reshape(rows_in, -1)
    d_qkv_weight = jnp.concatenate([d_q_cols, d_kv], axis=1)
    d_rest = jnp.sum(d_pack[:, :, qkv_cols:], axis=0)
    d_router_out = d_rest[:, :experts_all]
    d_gain_out = d_rest[:, experts_all:]

    d_w_out = d_w_out.reshape(query_cols, owners, -1)
    d_w_out = lax.all_to_all(d_w_out, "expert", split_axis=1, concat_axis=0, tiled=False)
    d_w_out = d_w_out.reshape(QUERY_HEADS * HEAD_SIZE, -1)
    d_w_out = lax.psum_scatter(d_w_out, "shard", scatter_dimension=0, tiled=True)
    d_w_out = lax.all_gather(d_w_out, "expert", axis=1, tiled=True).astype(FULL)

    return (
        result,
        d_tokens,
        d_gain_out[:, 0],
        d_qkv_weight,
        d_gain_out[:per, 2],
        d_gain_out[:per, 3],
        d_w_out,
        d_gain_out[:, 1],
        d_router_out,
        d_gate,
        d_up,
        d_down,
    )


def solution(mesh):
    placed = (
        P(("expert", "shard"), None),
        P(("expert", "shard"), None),
        P(("expert", "shard"), None),
        P("shard"),
        P("shard", None),
        P("shard"),
        P("shard"),
        P("shard", None),
        P("shard"),
        P("shard", None),
        P("expert", "shard", None),
        P("expert", "shard", None),
        P("expert", None, "shard"),
        P(("expert", "shard"), None),
    )
    return jax.shard_map(
        per_device,
        mesh=mesh,
        in_specs=placed,
        out_specs=(
            P(("expert", "shard"), None),
            P(("expert", "shard"), None),
            P("shard"),
            P("shard", None),
            P("shard"),
            P("shard"),
            P("shard", None),
            P("shard"),
            P("shard", None),
            P("expert", "shard", None),
            P("expert", "shard", None),
            P("expert", None, "shard"),
        ),
        check_vma=False,
    )
```

```python
import functools

import jax
import jax.numpy as jnp
from jax import lax
from jax.experimental import pallas as pl
from jax.experimental.pallas import tpu as pltpu
from jax.sharding import PartitionSpec as P

MODEL_WIDTH = 2048
QUERY_HEADS = 32
KEY_VALUE_HEADS = 4
HEAD_SIZE = 128
TOPK = 8
EXP_DEV = 8
TAIL = 128
GROUP_BLOCKS = 32
RESIDENT = 20 << 20

EPS = 1e-06
THETA = 1000000.0
LOW = jnp.bfloat16
FULL = jnp.float32


def unit_norm(values):
    inverse = lax.rsqrt(jnp.mean(values * values, axis=-1, keepdims=True) + EPS)
    return values * inverse, inverse


def norm_back(incoming, unit_rows, inverse, gain):
    inner = incoming * gain
    return inverse * (inner - unit_rows * jnp.mean(inner * unit_rows, axis=-1, keepdims=True))


def rotate(values, cosine, sine):
    half = values.shape[-1] // 2
    a, b = values[..., :half], values[..., half:]
    return jnp.concatenate([a * cosine - b * sine, b * cosine + a * sine], axis=-1)


def rotate_back(values, cosine, sine):
    half = values.shape[-1] // 2
    a, b = values[..., :half], values[..., half:]
    return jnp.concatenate([a * cosine + b * sine, b * cosine - a * sine], axis=-1)


def dot(spec, left, right):
    return jnp.einsum(spec, left, right, preferred_element_type=FULL)


def positions_of(segment_row):
    places = jnp.arange(segment_row.shape[0], dtype=jnp.int32)
    before = (segment_row[None, :] == segment_row[:, None]) & (places[None, :] < places[:, None])
    return jnp.sum(before.astype(jnp.int32), axis=1)


def columns(parts, rows):
    wide = jnp.concatenate([part.astype(LOW) for part in parts], axis=1)
    return jnp.pad(wide, ((0, rows - wide.shape[0]), (0, TAIL - wide.shape[1])))


MESH = pl.DeviceIdType.MESH
ANY = pl.BlockSpec(memory_space=pl.ANY)
VM = pl.BlockSpec(memory_space=pltpu.VMEM)
DMA = pltpu.SemaphoreType.DMA
VMEM_LIMIT = 58 << 20
TILE = 512


def neighbours():
    e = lax.axis_index("expert")
    core = e + 1 - 2 * (e % 2)
    flip_x = e + 2 - 4 * ((e // 2) % 2)
    flip_y = e + 4 - 8 * ((e // 4) % 2)
    diagonal = flip_x + flip_y - e
    return e, core, flip_x, flip_y, diagonal


def greet(planes):
    e, core, flip_x, flip_y, _ = neighbours()
    s = lax.axis_index("shard")
    barrier = pltpu.get_barrier_semaphore()
    for other in (core, flip_x, flip_y):
        pl.semaphore_signal(barrier, 1, device_id=(other, s), device_id_type=MESH)

    @pl.when(s > 0)
    def _():
        pl.semaphore_signal(barrier, 1, device_id=(e, s - 1), device_id_type=MESH)

    @pl.when(s < planes - 1)
    def _():
        pl.semaphore_signal(barrier, 1, device_id=(e, s + 1), device_id_type=MESH)

    inner = (s > 0) & (s < planes - 1)

    @pl.when(inner)
    def _():
        pl.semaphore_wait(barrier, 5)

    @pl.when(jnp.logical_not(inner))
    def _():
        pl.semaphore_wait(barrier, 4)


def send(source, target, send_sem, recv_sem, device):
    return pltpu.make_async_remote_copy(
        src_ref=source,
        dst_ref=target,
        send_sem=send_sem,
        recv_sem=recv_sem,
        device_id=device,
        device_id_type=MESH,
    )


def one_hot_pair(place_ref, pair, hot_ref, slots):
    rows = place_ref[pair]
    at = lax.broadcasted_iota(jnp.int32, (slots, rows.shape[1]), 0).astype(FULL)
    for j in range(EXP_DEV):
        hot_ref[pl.ds(j * slots, slots), :] = (at == rows[j : j + 1, :]).astype(LOW)


def gather_dispatch_kernel(
    planes, slots, x_ref, d_ref, place_ref, outx_ref, outd_ref,
    buf, hot, stage_x, stage_d, load_d,
    z_send, z_recv, x_send, x_recv, y_send, y_recv, c_send, c_recv, out_x, out_d, in_d,
):
    e, core, flip_x, flip_y, diagonal = neighbours()
    s = lax.axis_index("shard")
    length = x_ref.shape[0]
    half = length // 2
    width = x_ref.shape[1]
    low_half, high_half = pl.ds(0, half), pl.ds(half, half)
    greet(planes)
    buf[e, s] = x_ref[...]

    def up(sp):
        return send(buf.at[e, sp], buf.at[e, sp], z_send.at[0, sp], z_recv.at[sp], (e, s + 1))

    def down(sp):
        return send(buf.at[e, sp], buf.at[e, sp], z_send.at[1, sp], z_recv.at[sp], (e, s - 1))

    def first(sp):
        block = buf.at[e, sp]
        return [
            send(block, block, x_send.at[0, sp], x_recv.at[0, sp], (flip_x, s)),
            send(block, block, y_send.at[0, sp], y_recv.at[0, sp], (flip_y, s)),
            send(block, block, c_send.at[0, sp], c_recv.at[0, sp], (core, s)),
        ]

    def from_x(sp):
        block = buf.at[flip_x, sp]
        part = buf.at[flip_x, sp, low_half]
        return [
            send(part, part, y_send.at[1, sp], y_recv.at[1, sp], (flip_y, s)),
            send(block, block, c_send.at[1, sp], c_recv.at[1, sp], (core, s)),
        ]

    def from_y(sp):
        block = buf.at[flip_y, sp]
        part = buf.at[flip_y, sp, high_half]
        return [
            send(part, part, x_send.at[1, sp], x_recv.at[1, sp], (flip_x, s)),
            send(block, block, c_send.at[2, sp], c_recv.at[2, sp], (core, s)),
        ]

    def from_diagonal(sp):
        block = buf.at[diagonal, sp]
        return send(block, block, c_send.at[3, sp], c_recv.at[3, sp], (core, s))

    def arrived(block, sem):
        send(block, block, sem, sem, (core, s)).wait_recv()

    def plane_at(i):
        distance = (i + 1) // 2
        sign = 2 * (i % 2) - 1
        sp = s + sign * distance
        return sp, (sp >= 0) & (sp < planes) & (i >= 0) & (i <= 2 * planes - 2)

    def step_first(sp, i):
        @pl.when(i > 0)
        def _():
            arrived(buf.at[e, sp], z_recv.at[sp])

        @pl.when((sp <= s) & (s < planes - 1))
        def _():
            up(sp).start()

        @pl.when((sp >= s) & (s > 0))
        def _():
            down(sp).start()

        for copy in first(sp):
            copy.start()

    def step_second(sp):
        arrived(buf.at[flip_x, sp], x_recv.at[0, sp])
        for copy in from_x(sp):
            copy.start()
        arrived(buf.at[flip_y, sp], y_recv.at[0, sp])
        for copy in from_y(sp):
            copy.start()

    def step_third(sp):
        arrived(buf.at[diagonal, sp, low_half], y_recv.at[1, sp])
        arrived(buf.at[diagonal, sp, high_half], x_recv.at[1, sp])
        from_diagonal(sp).start()

    def copy_out(stage, out, sem, q, sp):
        rows = pl.ds(pl.multiple_of((q * planes + sp) * slots, 16), slots)
        return pltpu.make_async_copy(stage.at[q], out.at[:, rows, :], sem.at[q])

    def load(q, sp, k):
        return pltpu.make_async_copy(
            d_ref.at[2 * q + k, sp, :, pl.ds(0, MODEL_WIDTH)],
            load_d.at[q, pl.ds(k * length, length), :],
            in_d.at[q, k],
        )

    def start_loads(sp):
        for q in range(4):
            for k in range(2):
                load(q, sp, k).start()

    def dispatch(sp, i):
        for k, other in enumerate((core, core + flip_x - e, core + flip_y - e, core + diagonal - e)):
            arrived(buf.at[other, sp], c_recv.at[k, sp])

        def one(q, carry):
            one_hot_pair(place_ref, q * planes + sp, hot, slots)
            d_wide = load_d.shape[2]

            @pl.when(i > 0)
            def _():
                copy_out(stage_x, outx_ref, out_x, q, sp).wait()
                copy_out(stage_d, outd_ref, out_d, q, sp).wait()

            for k in range(2):
                load(q, sp, k).wait()

            def columns_of(at, wide, with_d):
                rows = jnp.concatenate(
                    [buf[2 * q, sp, :, at], buf[2 * q + 1, sp, :, at]], axis=0
                )
                got = jnp.dot(hot[...], rows, preferred_element_type=FULL).astype(LOW)
                stage_x[q, :, :, at] = got.reshape(EXP_DEV, slots, wide)
                if with_d:
                    got = jnp.dot(
                        hot[...], load_d[q, :, at], preferred_element_type=FULL
                    ).astype(LOW)
                    stage_d[q, :, :, at] = got.reshape(EXP_DEV, slots, wide)

            def tile(t, inner):
                columns_of(pl.ds(pl.multiple_of(t * TILE, TILE), TILE), TILE, True)
                return inner

            lax.fori_loop(0, MODEL_WIDTH // TILE, tile, 0)
            if width > MODEL_WIDTH:
                columns_of(pl.ds(MODEL_WIDTH, width - MODEL_WIDTH), width - MODEL_WIDTH, False)
            copy_out(stage_x, outx_ref, out_x, q, sp).start()
            copy_out(stage_d, outd_ref, out_d, q, sp).start()
            return carry

        lax.fori_loop(0, 4, one, 0)

    def step(i, carry):
        for lag, work in ((0, step_first), (1, step_second), (2, step_third), (3, dispatch)):
            sp, there = plane_at(i - lag)

            @pl.when(there)
            def _(sp=sp, lag=lag, work=work):
                if lag in (0, 3):
                    work(sp, i - lag)
                else:
                    work(sp)

        sp, there = plane_at(i - 2)

        @pl.when(there)
        def _():
            start_loads(sp)

        return carry

    lax.fori_loop(0, 2 * planes + 2, step, 0)

    def drain(sp, carry):
        for copy in first(sp) + from_x(sp) + from_y(sp) + [from_diagonal(sp)]:
            copy.wait_send()

        @pl.when((sp <= s) & (s < planes - 1))
        def _():
            up(sp).wait_send()

        @pl.when((sp >= s) & (s > 0))
        def _():
            down(sp).wait_send()

        return carry

    lax.fori_loop(0, planes, drain, 0)
    for q in range(4):
        copy_out(stage_x, outx_ref, out_x, q, 0).wait()
        copy_out(stage_d, outd_ref, out_d, q, 0).wait()


def gather_dispatch(rows, d_all, place, planes, slots, identity):
    owners = lax.axis_size("expert")
    length, width = rows.shape
    total = place.shape[0] * slots
    kernel = functools.partial(gather_dispatch_kernel, planes, slots)
    return pl.pallas_call(
        kernel,
        out_shape=[
            jax.ShapeDtypeStruct((EXP_DEV, total, width), LOW),
            jax.ShapeDtypeStruct((EXP_DEV, total, MODEL_WIDTH), LOW),
        ],
        in_specs=[VM, ANY, VM],
        out_specs=[ANY, ANY],
        scratch_shapes=[
            pltpu.VMEM((owners, planes, length, width), LOW),
            pltpu.VMEM((EXP_DEV * slots, 2 * length), LOW),
            pltpu.VMEM((4, EXP_DEV, slots, width), LOW),
            pltpu.VMEM((4, EXP_DEV, slots, MODEL_WIDTH), LOW),
            pltpu.VMEM((4, 2 * length, MODEL_WIDTH), LOW),
            DMA((2, planes)),
            DMA((planes,)),
            DMA((2, planes)),
            DMA((2, planes)),
            DMA((2, planes)),
            DMA((2, planes)),
            DMA((4, planes)),
            DMA((4, planes)),
            DMA((4,)),
            DMA((4,)),
            DMA((4, 2)),
        ],
        compiler_params=pltpu.CompilerParams(
            collective_id=identity, has_side_effects=True, vmem_limit_bytes=VMEM_LIMIT
        ),
    )(rows, d_all, place)


def expert_kernel(
    sel_ref, x_ref, dy_ref, wg_ref, wu_ref, wd_ref,
    y_ref, dx_ref, dwg_ref, dwu_ref, dwd_ref, a_all, dg_all, du_all,
):
    rows = x_ref.shape[1]
    step = 256
    experts = sel_ref.shape[2] // 2
    sel = sel_ref[0, 0:1, :]
    lane = lax.broadcasted_iota(jnp.int32, sel.shape, 1)
    high_sel = jnp.where(lane < experts, sel, 0.0)
    rest_sel = sel - high_sel
    nt = (((1,), (1,)), ((), ()))
    tn = (((0,), (0,)), ((), ()))

    def chunk(r, carry):
        at = pl.ds(pl.multiple_of(r * step, step), step)
        x = x_ref[0, at, :MODEL_WIDTH]
        tail = x_ref[0, at, MODEL_WIDTH:].astype(FULL)
        dy = dy_ref[0, at, :]
        gate = jnp.sum(tail * sel, axis=1, keepdims=True)
        g = lax.dot_general(x, wg_ref[0], nt, preferred_element_type=FULL)
        u = lax.dot_general(x, wu_ref[0], nt, preferred_element_type=FULL)
        da = jnp.dot(dy, wd_ref[0], preferred_element_type=FULL)
        sigma = 1.0 / (1.0 + jnp.exp(-g))
        silu = g * sigma
        act = (silu * u).astype(LOW).astype(FULL)
        d_gate = jnp.sum(act * da, axis=1, keepdims=True)
        d_act = da * gate
        a_all[at, :] = (act * gate).astype(LOW)
        dg_all[at, :] = (d_act * u * sigma * (1.0 + g * (1.0 - sigma))).astype(LOW)
        du_all[at, :] = (d_act * silu).astype(LOW)
        high = d_gate.astype(LOW).astype(FULL)
        dx_ref[0, at, MODEL_WIDTH:] = (high * high_sel + (d_gate - high) * rest_sel).astype(LOW)
        y_ref[0, at, :] = lax.dot_general(
            a_all[at, :], wd_ref[0], nt, preferred_element_type=FULL
        ).astype(LOW)
        dx_ref[0, at, :MODEL_WIDTH] = (
            jnp.dot(dg_all[at, :], wg_ref[0], preferred_element_type=FULL)
            + jnp.dot(du_all[at, :], wu_ref[0], preferred_element_type=FULL)
        ).astype(LOW)
        return carry

    lax.fori_loop(0, rows // step, chunk, 0)

    def tile(t, carry):
        at = pl.ds(pl.multiple_of(t * TILE, TILE), TILE)
        dwg_ref[0, :, at] = lax.dot_general(
            dg_all[...], x_ref[0, :, at], tn, preferred_element_type=FULL
        )
        dwu_ref[0, :, at] = lax.dot_general(
            du_all[...], x_ref[0, :, at], tn, preferred_element_type=FULL
        )
        dwd_ref[0, at, :] = lax.dot_general(
            dy_ref[0, :, at], a_all[...], tn, preferred_element_type=FULL
        )
        return carry

    lax.fori_loop(0, MODEL_WIDTH // TILE, tile, 0)


def expert_pass(sel, x, dy, w_gate, w_up, w_down):
    rows, width = x.shape[1:]
    hidden = w_gate.shape[1]

    def spec(*shape):
        return pl.BlockSpec((1,) + shape, lambda j: (j, 0, 0))

    def out(*shape, dtype=LOW):
        return jax.ShapeDtypeStruct((EXP_DEV,) + shape, dtype)

    return pl.pallas_call(
        expert_kernel,
        grid=(EXP_DEV,),
        in_specs=[
            spec(*sel.shape[1:]),
            spec(rows, width),
            spec(rows, MODEL_WIDTH),
            spec(hidden, MODEL_WIDTH),
            spec(hidden, MODEL_WIDTH),
            spec(MODEL_WIDTH, hidden),
        ],
        out_specs=[
            spec(rows, MODEL_WIDTH),
            spec(rows, width),
            spec(hidden, MODEL_WIDTH),
            spec(hidden, MODEL_WIDTH),
            spec(MODEL_WIDTH, hidden),
        ],
        out_shape=[
            out(rows, MODEL_WIDTH),
            out(rows, width),
            out(hidden, MODEL_WIDTH, dtype=FULL),
            out(hidden, MODEL_WIDTH, dtype=FULL),
            out(MODEL_WIDTH, hidden, dtype=FULL),
        ],
        scratch_shapes=[pltpu.VMEM((rows, hidden), LOW)] * 3,
        compiler_params=pltpu.CompilerParams(vmem_limit_bytes=VMEM_LIMIT),
        cost_estimate=pl.CostEstimate(
            flops=EXP_DEV * rows * MODEL_WIDTH * hidden * 18,
            bytes_accessed=160 << 20,
            transcendentals=EXP_DEV * rows * hidden,
        ),
    )(sel, x, dy, w_gate, w_up, w_down)


def combine_home_kernel(
    planes, slots, place_ref, v_ref, out_ref,
    hot, load, mine, away, c_in, x_in, y_in, x_half, y_half, u_in, d_in,
    in_sem, c_send, c_recv, x_send, x_recv, y_send, y_recv, z_send, z_recv,
):
    e, core, flip_x, flip_y, diagonal = neighbours()
    s = lax.axis_index("shard")
    q_own, q_x, q_y, q_d = e // 2, flip_x // 2, flip_y // 2, diagonal // 2
    parity = e % 2
    length, width = out_ref.shape
    half = length // 2
    low_half, high_half = pl.ds(0, half), pl.ds(half, half)

    def fetch(q, sp):
        rows = pl.ds(pl.multiple_of((q * planes + sp) * slots, 16), slots)
        return pltpu.make_async_copy(v_ref.at[:, rows, :], load.at[q], in_sem.at[q])

    def to_core(q, sp):
        return send(away.at[q, sp], c_in.at[q, sp], c_send.at[q, sp], c_recv.at[q, sp], (core, s))

    def halves(sp):
        return [
            send(
                mine.at[q_d, sp, low_half], y_half.at[sp], y_send.at[0, sp], y_recv.at[0, sp],
                (flip_y, s),
            ),
            send(
                mine.at[q_d, sp, high_half], x_half.at[sp], x_send.at[0, sp], x_recv.at[0, sp],
                (flip_x, s),
            ),
        ]

    def to_x(sp):
        return send(mine.at[q_x, sp], x_in.at[sp], x_send.at[1, sp], x_recv.at[1, sp], (flip_x, s))

    def to_y(sp):
        return send(mine.at[q_y, sp], y_in.at[sp], y_send.at[1, sp], y_recv.at[1, sp], (flip_y, s))

    def up(sp):
        return send(mine.at[q_own, sp], u_in.at[sp], z_send.at[0, sp], z_recv.at[0, sp], (e, s + 1))

    def down(sp):
        return send(mine.at[q_own, sp], d_in.at[sp], z_send.at[1, sp], z_recv.at[1, sp], (e, s - 1))

    def arrived(block, sem):
        send(block, block, sem, sem, (core, s)).wait_recv()

    def plane_at(i):
        back = 2 * planes - 2 - i
        sp = s + (2 * (back % 2) - 1) * ((back + 1) // 2)
        return sp, (sp >= 0) & (sp < planes) & (i >= 0) & (back >= 0)

    def add(target, *others):
        total = target[...].astype(FULL)
        for other in others:
            total = total + other[...].astype(FULL)
        target[...] = total.astype(LOW)

    def work(sp):
        for q in range(4):
            fetch(q, sp).start()

        def one(q, carry):
            one_hot_pair(place_ref, q * planes + sp, hot, slots)
            fetch(q, sp).wait()

            def part(at, wide):
                rows = load[q, :, :, at].reshape(EXP_DEV * slots, wide)
                got = lax.dot_general(
                    hot[...], rows, (((0,), (0,)), ((), ())), preferred_element_type=FULL
                ).astype(LOW)
                got = got.reshape(2, length, wide)

                @pl.when(parity == 0)
                def _():
                    mine[q, sp, :, at] = got[0]
                    away[q, sp, :, at] = got[1]

                @pl.when(parity == 1)
                def _():
                    mine[q, sp, :, at] = got[1]
                    away[q, sp, :, at] = got[0]

            def tile(t, inner):
                part(pl.ds(pl.multiple_of(t * TILE, TILE), TILE), TILE)
                return inner

            lax.fori_loop(0, MODEL_WIDTH // TILE, tile, 0)
            if width > MODEL_WIDTH:
                part(pl.ds(MODEL_WIDTH, width - MODEL_WIDTH), width - MODEL_WIDTH)
            to_core(q, sp).start()
            return carry

        lax.fori_loop(0, 4, one, 0)

    def pairs(sp):
        def one(q, carry):
            arrived(c_in.at[q, sp], c_recv.at[q, sp])
            add(mine.at[q, sp], c_in.at[q, sp])
            return carry

        one(q_d, 0)
        for copy in halves(sp):
            copy.start()
        for q in (q_x, q_y, q_own):
            one(q, 0)

    def sides(sp):
        arrived(y_half.at[sp], y_recv.at[0, sp])
        add(mine.at[q_x, sp, low_half], y_half.at[sp])
        to_x(sp).start()
        arrived(x_half.at[sp], x_recv.at[0, sp])
        add(mine.at[q_y, sp, high_half], x_half.at[sp])
        to_y(sp).start()

    def line(sp):
        arrived(x_in.at[sp], x_recv.at[1, sp])
        arrived(y_in.at[sp], y_recv.at[1, sp])
        add(mine.at[q_own, sp], x_in.at[sp], y_in.at[sp])

        @pl.when((sp >= s) & (s > 0))
        def _():
            arrived(u_in.at[sp], z_recv.at[0, sp])
            add(mine.at[q_own, sp], u_in.at[sp])

        @pl.when((sp <= s) & (s < planes - 1))
        def _():
            arrived(d_in.at[sp], z_recv.at[1, sp])
            add(mine.at[q_own, sp], d_in.at[sp])

        @pl.when(sp > s)
        def _():
            up(sp).start()

        @pl.when(sp < s)
        def _():
            down(sp).start()

    greet(planes)

    def step(i, carry):
        for lag, job in ((0, work), (1, pairs), (2, sides), (3, line)):
            sp, there = plane_at(i - lag)

            @pl.when(there)
            def _(sp=sp, job=job):
                job(sp)

        return carry

    lax.fori_loop(0, 2 * planes + 2, step, 0)
    out_ref[...] = mine[q_own, s].astype(FULL)

    def drain(sp, carry):
        for q in range(4):
            to_core(q, sp).wait_send()
        for copy in halves(sp) + [to_x(sp), to_y(sp)]:
            copy.wait_send()

        @pl.when(sp > s)
        def _():
            up(sp).wait_send()

        @pl.when(sp < s)
        def _():
            down(sp).wait_send()

        return carry

    lax.fori_loop(0, planes, drain, 0)


def combine_home(place, v, length, planes, slots, identity):
    width = v.shape[2]
    block = (planes, length, width)
    return pl.pallas_call(
        functools.partial(combine_home_kernel, planes, slots),
        out_shape=jax.ShapeDtypeStruct((length, width), FULL),
        in_specs=[VM, ANY],
        out_specs=VM,
        scratch_shapes=[
            pltpu.VMEM((EXP_DEV * slots, 2 * length), LOW),
            pltpu.VMEM((4, EXP_DEV, slots, width), LOW),
            pltpu.VMEM((4,) + block, LOW),
            pltpu.VMEM((4,) + block, LOW),
            pltpu.VMEM((4,) + block, LOW),
            pltpu.VMEM(block, LOW),
            pltpu.VMEM(block, LOW),
            pltpu.VMEM((planes, length // 2, width), LOW),
            pltpu.VMEM((planes, length // 2, width), LOW),
            pltpu.VMEM(block, LOW),
            pltpu.VMEM(block, LOW),
            DMA((4,)),
            DMA((4, planes)),
            DMA((4, planes)),
            DMA((2, planes)),
            DMA((2, planes)),
            DMA((2, planes)),
            DMA((2, planes)),
            DMA((2, planes)),
            DMA((2, planes)),
        ],
        compiler_params=pltpu.CompilerParams(
            collective_id=identity, has_side_effects=True, vmem_limit_bytes=VMEM_LIMIT
        ),
    )(place, v)


def per_device(
    tokens,
    segments,
    routes,
    attn_gain,
    qkv_weight,
    query_gain,
    k_gain,
    w_out,
    ffn_gain,
    router,
    w_gate,
    w_up,
    w_down,
    d_out,
):
    owners = lax.axis_size("expert")
    planes = lax.axis_size("shard")
    me = lax.axis_index("expert")
    plane = lax.axis_index("shard")
    length = tokens.shape[0]
    blocks = owners * planes
    experts_all = router.shape[1]
    capacity = 3 * length * TOPK // (2 * experts_all)
    heads = QUERY_HEADS // owners
    query_cols = heads * HEAD_SIZE
    scaling = HEAD_SIZE ** (-0.5)
    both = ("expert", "shard")
    rows_in = qkv_weight.shape[0]

    kv_head = me * KEY_VALUE_HEADS // owners
    k_at = QUERY_HEADS * HEAD_SIZE + kv_head * HEAD_SIZE
    v_at = k_at + KEY_VALUE_HEADS * HEAD_SIZE
    gains = columns(
        [
            router,
            attn_gain[:, None],
            ffn_gain[:, None],
            jnp.pad(query_gain, (0, rows_in - query_gain.shape[0]))[:, None],
            jnp.pad(k_gain, (0, rows_in - k_gain.shape[0]))[:, None],
        ],
        rows_in,
    )
    mine = jnp.concatenate(
        [
            lax.dynamic_slice_in_dim(qkv_weight, me * query_cols, query_cols, 1),
            lax.dynamic_slice_in_dim(qkv_weight, k_at, HEAD_SIZE, 1),
            lax.dynamic_slice_in_dim(qkv_weight, v_at, HEAD_SIZE, 1),
            gains,
        ],
        axis=1,
    )
    gathered = lax.all_gather(mine, "shard", axis=0, tiled=True)
    qkv_cols = query_cols + 2 * HEAD_SIZE
    wqkv = gathered[:, :qkv_cols]
    router_full = gathered[:, qkv_cols : qkv_cols + experts_all]
    gain_cols = gathered[:, qkv_cols + experts_all :].astype(FULL)
    gain_one, gain_two = gain_cols[:, 0], gain_cols[:, 1]
    per = query_gain.shape[0]
    by_plane = gain_cols.reshape(planes, rows_in, -1)[:, :per]
    gain_query = by_plane[:, :, 2].reshape(-1)
    gain_key = by_plane[:, :, 3].reshape(-1)

    segment_row = segments[0]
    token_tail = columns(
        [segment_row[:, None], positions_of(segment_row)[:, None]], length
    )
    plane_rows = lax.all_gather(
        jnp.concatenate([tokens, token_tail], axis=1), "expert", axis=0, tiled=False
    )
    plane_tokens = plane_rows[:, :, :MODEL_WIDTH].astype(FULL)
    plane_segments = plane_rows[:, :, MODEL_WIDTH]
    plane_places = plane_rows[:, :, MODEL_WIDTH + 1].astype(FULL)

    out_rows = w_out.shape[0]
    first = me * query_cols
    offset = first - plane * out_rows
    if out_rows >= query_cols:
        held = (offset >= 0) & (offset < out_rows)
        piece = lax.dynamic_slice_in_dim(w_out, jnp.where(held, offset, 0), query_cols, 0)
        w_mine = lax.psum(jnp.where(held, piece, 0).astype(LOW), "shard")
    else:
        parts = query_cols // out_rows
        at = plane - me * parts
        held = (at >= 0) & (at < parts)
        spread = jnp.where(held & (jnp.arange(parts) == at)[:, None, None], w_out[None], 0)
        w_mine = lax.psum(spread.astype(LOW), "shard").reshape(query_cols, MODEL_WIDTH)

    d_tail = columns([routes], length)
    d_all = lax.all_gather(
        jnp.concatenate([d_out, d_tail], axis=1), both, axis=0, tiled=False
    )

    unit_plane, inverse_plane = unit_norm(plane_tokens)
    h1 = (unit_plane * gain_one).astype(LOW)
    projected = dot("bqd,df->bqf", h1, wqkv)
    half = HEAD_SIZE // 2
    frequency = THETA ** (-2.0 * jnp.arange(half, dtype=FULL) / HEAD_SIZE)
    angles = plane_places[:, :, None] * frequency
    cosine, sine = jnp.cos(angles), jnp.sin(angles)
    cosine_q, sine_q = cosine[:, :, None, :], sine[:, :, None, :]
    query_raw = projected[:, :, :query_cols].reshape(owners, length, heads, HEAD_SIZE)
    key_raw = projected[:, :, query_cols : query_cols + HEAD_SIZE]
    value = projected[:, :, query_cols + HEAD_SIZE :].astype(LOW)
    query_unit, query_inverse = unit_norm(query_raw)
    key_unit, key_inverse = unit_norm(key_raw)
    query = rotate(query_unit * gain_query, cosine_q, sine_q).astype(LOW)
    key = rotate(key_unit * gain_key, cosine, sine).astype(LOW)
    places = jnp.arange(length, dtype=jnp.int32)
    allowed = (plane_segments[:, :, None] == plane_segments[:, None, :]) & (
        places[None, :] <= places[:, None]
    )
    scores = dot("bqhd,bkd->bhqk", query, key) * scaling
    scores = jnp.where(allowed[:, None], scores, -1e30)
    highest = jnp.max(scores, axis=-1, keepdims=True)
    exponent = jnp.exp(scores - highest)
    probs = exponent / jnp.sum(exponent, axis=-1, keepdims=True)
    probs_low = probs.astype(LOW)
    mixed = dot("bhqk,bkd->bqhd", probs_low, value).astype(LOW)
    mixed = mixed.reshape(owners, length, query_cols)
    partial = dot("bqf,fd->bqd", mixed, w_mine).astype(LOW)
    branch = lax.psum_scatter(partial, "expert", scatter_dimension=0, tiled=False)

    middle = tokens.astype(FULL) + branch.astype(FULL)
    unit_two, inverse_two = unit_norm(middle)
    h2 = (unit_two * gain_two).astype(LOW)
    logits = dot("nd,de->ne", h2, router_full)
    chance = jax.nn.softmax(logits, axis=-1)
    named = jnp.sum(
        (routes[:, :, None] == jnp.arange(experts_all, dtype=jnp.int32)).astype(FULL), axis=1
    )
    chosen_sum = jnp.sum(named * chance, axis=1, keepdims=True)
    gates = named * chance / chosen_sum
    gates_high = gates.astype(LOW)
    gates_rest = (gates - gates_high.astype(FULL)).astype(LOW)
    h_rows = jnp.concatenate([h2, gates_high, gates_rest], axis=1)
    resident_pass = blocks * length * h_rows.shape[1] * 2 <= RESIDENT

    route_all = d_all[:, :, MODEL_WIDTH : MODEL_WIDTH + TOPK].astype(FULL)
    own_experts = (me * EXP_DEV + jnp.arange(EXP_DEV, dtype=jnp.int32)).astype(FULL)
    match = jnp.sum((route_all[:, :, :, None] == own_experts).astype(FULL), axis=2)
    earlier = (places[None, :] < places[:, None]).astype(LOW)
    rank = dot("ts,bsj->btj", earlier, match.astype(LOW))
    slot_ids = jnp.arange(capacity, dtype=jnp.int32).astype(FULL)
    place = jnp.where(match > 0, rank, -1.0).transpose(0, 2, 1)
    if resident_pass:
        place = place.reshape(owners // 2, 2, planes, EXP_DEV, length)
        offset = (capacity * jnp.arange(2, dtype=jnp.int32)).astype(FULL)
        place = jnp.where(place >= 0, place + offset[:, None, None, None], -1.0)
        place = place.transpose(0, 2, 3, 1, 4).reshape(blocks // 2, EXP_DEV, 2 * length)
        lanes = jnp.arange(2 * experts_all, dtype=jnp.int32) % experts_all
        own = (me * EXP_DEV + jnp.arange(EXP_DEV, dtype=jnp.int32))[:, None] == lanes
        sel = jnp.broadcast_to(own.astype(FULL)[:, None, :], (EXP_DEV, 8, 2 * experts_all))
        slots = 2 * capacity
        x, dy = gather_dispatch(
            h_rows, d_all.reshape(owners, planes, length, -1), place, planes, slots, 1
        )
        y, dx, d_gate, d_up, d_down = expert_pass(sel, x, dy, w_gate, w_up, w_down)
        d_home = combine_home(place, dx, length, planes, slots, 2)
        mixture = combine_home(place, y, length, planes, slots, 3)
    else:
        dispatch = (place[:, :, None, :] == slot_ids[:, None]).astype(LOW)

        def experts(h_rows, d_rows, gate_high, gate_rest, put):
            count = h_rows.shape[0]
            flat = put.reshape(count, EXP_DEV * capacity, length)
            x = dot("bst,btd->bsd", flat, h_rows).astype(LOW)
            dy = dot("bst,btd->bsd", flat, d_rows).astype(LOW)

            def by_expert(v):
                v = v.reshape(count, EXP_DEV, capacity, v.shape[-1])
                return v.transpose(1, 0, 2, 3).reshape(EXP_DEV, count * capacity, v.shape[-1])

            def by_block(v):
                v = v.reshape(EXP_DEV, count, capacity, v.shape[-1])
                return v.transpose(1, 0, 2, 3).reshape(count, EXP_DEV * capacity, v.shape[-1])

            x, dy = by_expert(x), by_expert(dy)
            gate_slot = dot("bjct,btj->jbc", put, gate_high) + dot("bjct,btj->jbc", put, gate_rest)
            gate_slot = gate_slot.reshape(EXP_DEV, count * capacity, 1)
            g = dot("erd,efd->erf", x, w_gate)
            u = dot("erd,efd->erf", x, w_up)
            da = dot("erd,edf->erf", dy, w_down)
            sigma = jax.nn.sigmoid(g)
            silu = g * sigma
            act = (silu * u).astype(LOW).astype(FULL)
            d_gate_slot = jnp.sum(act * da, axis=-1)
            act_gated = (act * gate_slot).astype(LOW)
            d_act = da * gate_slot
            dg = (d_act * u * sigma * (1.0 + g * (1.0 - sigma))).astype(LOW)
            du = (d_act * silu).astype(LOW)
            y = dot("erf,edf->erd", act_gated, w_down).astype(LOW)
            d_down = dot("erd,erf->edf", dy, act_gated)
            d_gate = dot("erf,erd->efd", dg, x)
            d_up = dot("erf,erd->efd", du, x)
            dx = (dot("erf,efd->erd", dg, w_gate) + dot("erf,efd->erd", du, w_up)).astype(LOW)
            mix = dot("bst,bsd->btd", flat, by_block(y)).astype(LOW)
            d_h = dot("bst,bsd->btd", flat, by_block(dx)).astype(LOW)
            d_g = dot(
                "bjct,jbc->btj", put.astype(FULL), d_gate_slot.reshape(EXP_DEV, count, capacity)
            )
            return mix, d_h, d_g, d_gate, d_up, d_down

        h_all = lax.all_gather(h_rows, both, axis=0, tiled=False)
        gate_cols = lax.dynamic_slice_in_dim(h_all, MODEL_WIDTH + me * EXP_DEV, EXP_DEV, 2)
        rest_cols = lax.dynamic_slice_in_dim(
            h_all, MODEL_WIDTH + experts_all + me * EXP_DEV, EXP_DEV, 2
        )
        step = min(blocks, GROUP_BLOCKS)
        mixes, d_hs, d_gs, totals = [], [], [], None
        for at in range(0, blocks, step):
            cut = slice(at, at + step)
            mix, d_h, d_g, *grads = experts(
                h_all[cut, :, :MODEL_WIDTH],
                d_all[cut, :, :MODEL_WIDTH],
                gate_cols[cut],
                rest_cols[cut],
                dispatch[cut],
            )
            mixes.append(mix)
            d_hs.append(d_h)
            d_gs.append(d_g)
            totals = grads if totals is None else [a + b for a, b in zip(totals, grads)]
        d_gate, d_up, d_down = totals
        d_g = jnp.concatenate(d_gs, axis=0)
        spread = jnp.zeros((blocks, length, 2 * experts_all), LOW)
        spread = lax.dynamic_update_slice_in_dim(spread, d_g.astype(LOW), me * EXP_DEV, 2)
        d_h_wide = jnp.concatenate([jnp.concatenate(d_hs, axis=0), spread], axis=2)

        def home(v):
            v = v.reshape(owners, planes, length, v.shape[-1])
            v = lax.psum_scatter(v, "expert", scatter_dimension=0, tiled=False)
            return lax.psum_scatter(v, "shard", scatter_dimension=0, tiled=False)

        d_home = home(d_h_wide)
        mixture = home(jnp.concatenate(mixes, axis=0))
    result = (middle + mixture.astype(FULL)).astype(LOW)

    upstream = d_out.astype(FULL)
    d_gates = d_home[:, MODEL_WIDTH:].astype(FULL)
    d_gates = d_gates[:, :experts_all] + d_gates[:, experts_all:]
    d_chance = named * (d_gates - jnp.sum(d_gates * gates, axis=1, keepdims=True)) / chosen_sum
    d_logits = chance * (d_chance - jnp.sum(d_chance * chance, axis=1, keepdims=True))
    d_logits = d_logits.astype(LOW)
    d_h2 = d_home[:, :MODEL_WIDTH].astype(FULL) + dot("ne,de->nd", d_logits, router_full)
    d_gain_two = jnp.sum(d_h2 * unit_two, axis=0)
    d_middle = upstream + norm_back(d_h2, unit_two, inverse_two, gain_two)
    d_router = dot("nd,ne->de", h2, d_logits)

    d_branch = lax.all_gather(d_middle.astype(LOW), "expert", axis=0, tiled=False)
    d_w_out = dot("bqf,bqd->fd", mixed, d_branch).astype(LOW)
    d_mixed = dot("bqd,fd->bqf", d_branch, w_mine).astype(LOW)
    d_mixed = d_mixed.reshape(owners, length, heads, HEAD_SIZE)
    d_probs = dot("bqhd,bkd->bhqk", d_mixed, value)
    d_scores = probs * (d_probs - jnp.sum(d_probs * probs, axis=-1, keepdims=True))
    d_scores = d_scores.astype(LOW)
    d_query = dot("bhqk,bkd->bqhd", d_scores, key) * scaling
    d_key = dot("bhqk,bqhd->bkd", d_scores, query) * scaling
    d_value = dot("bhqk,bqhd->bkd", probs_low, d_mixed)
    d_query = rotate_back(d_query, cosine_q, sine_q)
    d_key = rotate_back(d_key, cosine, sine)
    d_gain_query = jnp.sum(d_query * query_unit, axis=(0, 1, 2))
    d_gain_key = jnp.sum(d_key * key_unit, axis=(0, 1))
    d_query = norm_back(d_query, query_unit, query_inverse, gain_query)
    d_key = norm_back(d_key, key_unit, key_inverse, gain_key)
    d_projected = jnp.concatenate(
        [d_query.reshape(owners, length, query_cols), d_key, d_value], axis=2
    ).astype(LOW)
    d_h1_part = dot("bqf,df->bqd", d_projected, wqkv).astype(LOW)
    d_h1 = lax.psum_scatter(d_h1_part, "expert", scatter_dimension=0, tiled=False).astype(FULL)
    resident = tokens.astype(FULL)
    unit_one, inverse_one = unit_norm(resident)
    d_gain_one = jnp.sum(d_h1 * unit_one, axis=0)
    d_tokens = (d_middle + norm_back(d_h1, unit_one, inverse_one, gain_one)).astype(LOW)

    d_wqkv = dot("bqd,bqf->df", h1, d_projected).astype(LOW)

    def by_rows(v):
        v = v.reshape(planes, per)
        return jnp.pad(v, ((0, 0), (0, rows_in - per))).reshape(-1)[:, None]

    d_tail = columns(
        [
            d_router,
            d_gain_one[:, None],
            d_gain_two[:, None],
            by_rows(d_gain_query),
            by_rows(d_gain_key),
        ],
        MODEL_WIDTH,
    )
    d_pack = lax.psum_scatter(
        jnp.concatenate([d_wqkv, d_tail], axis=1), "shard", scatter_dimension=0, tiled=True
    )
    d_pack = lax.all_gather(d_pack, "expert", axis=0, tiled=False).astype(FULL)
    d_q_cols = d_pack[:, :, :query_cols].transpose(1, 0, 2).reshape(rows_in, -1)
    d_kv = d_pack[:, :, query_cols:qkv_cols]
    d_kv = jnp.sum(d_kv.reshape(KEY_VALUE_HEADS, -1, rows_in, 2, HEAD_SIZE), axis=1)
    d_kv = d_kv.transpose(1, 2, 0, 3).reshape(rows_in, -1)
    d_qkv_weight = jnp.concatenate([d_q_cols, d_kv], axis=1)
    d_rest = jnp.sum(d_pack[:, :, qkv_cols:], axis=0)
    d_router_out = d_rest[:, :experts_all]
    d_gain_out = d_rest[:, experts_all:]

    d_w_out = d_w_out.reshape(query_cols, owners, -1)
    d_w_out = lax.all_to_all(d_w_out, "expert", split_axis=1, concat_axis=0, tiled=False)
    d_w_out = d_w_out.reshape(QUERY_HEADS * HEAD_SIZE, -1)
    d_w_out = lax.psum_scatter(d_w_out, "shard", scatter_dimension=0, tiled=True)
    d_w_out = lax.all_gather(d_w_out, "expert", axis=1, tiled=True).astype(FULL)

    return (
        result,
        d_tokens,
        d_gain_out[:, 0],
        d_qkv_weight,
        d_gain_out[:per, 2],
        d_gain_out[:per, 3],
        d_w_out,
        d_gain_out[:, 1],
        d_router_out,
        d_gate,
        d_up,
        d_down,
    )


def solution(mesh):
    placed = (
        P(("expert", "shard"), None),
        P(("expert", "shard"), None),
        P(("expert", "shard"), None),
        P("shard"),
        P("shard", None),
        P("shard"),
        P("shard"),
        P("shard", None),
        P("shard"),
        P("shard", None),
        P("expert", "shard", None),
        P("expert", "shard", None),
        P("expert", None, "shard"),
        P(("expert", "shard"), None),
    )
    return jax.shard_map(
        per_device,
        mesh=mesh,
        in_specs=placed,
        out_specs=(
            P(("expert", "shard"), None),
            P(("expert", "shard"), None),
            P("shard"),
            P("shard", None),
            P("shard"),
            P("shard"),
            P("shard", None),
            P("shard"),
            P("shard", None),
            P("expert", "shard", None),
            P("expert", "shard", None),
            P("expert", None, "shard"),
        ),
        check_vma=False,
    )
```

```python
import functools

import jax
import jax.numpy as jnp
from jax import lax
from jax.experimental import pallas as pl
from jax.experimental.pallas import tpu as pltpu
from jax.sharding import PartitionSpec as P

MODEL_WIDTH = 2048
QUERY_HEADS = 32
KEY_VALUE_HEADS = 4
HEAD_SIZE = 128
TOPK = 8
EXP_DEV = 8
TAIL = 128
GROUP_BLOCKS = 32
RESIDENT = 20 << 20

EPS = 1e-06
THETA = 1000000.0
LOW = jnp.bfloat16
FULL = jnp.float32


def unit_norm(values):
    inverse = lax.rsqrt(jnp.mean(values * values, axis=-1, keepdims=True) + EPS)
    return values * inverse, inverse


def norm_back(incoming, unit_rows, inverse, gain):
    inner = incoming * gain
    return inverse * (inner - unit_rows * jnp.mean(inner * unit_rows, axis=-1, keepdims=True))


def rotate(values, cosine, sine):
    half = values.shape[-1] // 2
    a, b = values[..., :half], values[..., half:]
    return jnp.concatenate([a * cosine - b * sine, b * cosine + a * sine], axis=-1)


def rotate_back(values, cosine, sine):
    half = values.shape[-1] // 2
    a, b = values[..., :half], values[..., half:]
    return jnp.concatenate([a * cosine + b * sine, b * cosine - a * sine], axis=-1)


def dot(spec, left, right):
    return jnp.einsum(spec, left, right, preferred_element_type=FULL)


def positions_of(segment_row):
    places = jnp.arange(segment_row.shape[0], dtype=jnp.int32)
    before = (segment_row[None, :] == segment_row[:, None]) & (places[None, :] < places[:, None])
    return jnp.sum(before.astype(jnp.int32), axis=1)


def columns(parts, rows):
    wide = jnp.concatenate([part.astype(LOW) for part in parts], axis=1)
    return jnp.pad(wide, ((0, rows - wide.shape[0]), (0, TAIL - wide.shape[1])))


MESH = pl.DeviceIdType.MESH
ANY = pl.BlockSpec(memory_space=pl.ANY)
VM = pl.BlockSpec(memory_space=pltpu.VMEM)
DMA = pltpu.SemaphoreType.DMA
VMEM_LIMIT = 58 << 20
TILE = 512


def neighbours():
    e = lax.axis_index("expert")
    core = e + 1 - 2 * (e % 2)
    flip_x = e + 2 - 4 * ((e // 2) % 2)
    flip_y = e + 4 - 8 * ((e // 4) % 2)
    diagonal = flip_x + flip_y - e
    return e, core, flip_x, flip_y, diagonal


def greet(planes):
    e, core, flip_x, flip_y, _ = neighbours()
    s = lax.axis_index("shard")
    barrier = pltpu.get_barrier_semaphore()
    for other in (core, flip_x, flip_y):
        pl.semaphore_signal(barrier, 1, device_id=(other, s), device_id_type=MESH)

    @pl.when(s > 0)
    def _():
        pl.semaphore_signal(barrier, 1, device_id=(e, s - 1), device_id_type=MESH)

    @pl.when(s < planes - 1)
    def _():
        pl.semaphore_signal(barrier, 1, device_id=(e, s + 1), device_id_type=MESH)

    inner = (s > 0) & (s < planes - 1)

    @pl.when(inner)
    def _():
        pl.semaphore_wait(barrier, 5)

    @pl.when(jnp.logical_not(inner))
    def _():
        pl.semaphore_wait(barrier, 4)


def send(source, target, send_sem, recv_sem, device):
    return pltpu.make_async_remote_copy(
        src_ref=source,
        dst_ref=target,
        send_sem=send_sem,
        recv_sem=recv_sem,
        device_id=device,
        device_id_type=MESH,
    )


def one_hot_pair(place_ref, pair, hot_ref, slots):
    rows = place_ref[pair]
    at = lax.broadcasted_iota(jnp.int32, (slots, rows.shape[1]), 0).astype(FULL)
    for j in range(EXP_DEV):
        hot_ref[pl.ds(j * slots, slots), :] = (at == rows[j : j + 1, :]).astype(LOW)


def gather_dispatch_kernel(
    planes, slots, x_ref, d_ref, place_ref, outx_ref, outd_ref,
    buf, hot, stage_x, stage_d, load_d,
    z_send, z_recv, x_send, x_recv, y_send, y_recv, c_send, c_recv, out_x, out_d, in_d,
):
    e, core, flip_x, flip_y, diagonal = neighbours()
    s = lax.axis_index("shard")
    length = x_ref.shape[0]
    half = length // 2
    width = x_ref.shape[1]
    low_half, high_half = pl.ds(0, half), pl.ds(half, half)
    greet(planes)
    buf[e, s] = x_ref[...]

    def up(sp):
        return send(buf.at[e, sp], buf.at[e, sp], z_send.at[0, sp], z_recv.at[sp], (e, s + 1))

    def down(sp):
        return send(buf.at[e, sp], buf.at[e, sp], z_send.at[1, sp], z_recv.at[sp], (e, s - 1))

    def first(sp):
        block = buf.at[e, sp]
        return [
            send(block, block, x_send.at[0, sp], x_recv.at[0, sp], (flip_x, s)),
            send(block, block, y_send.at[0, sp], y_recv.at[0, sp], (flip_y, s)),
            send(block, block, c_send.at[0, sp], c_recv.at[0, sp], (core, s)),
        ]

    def from_x(sp):
        block = buf.at[flip_x, sp]
        part = buf.at[flip_x, sp, low_half]
        return [
            send(part, part, y_send.at[1, sp], y_recv.at[1, sp], (flip_y, s)),
            send(block, block, c_send.at[1, sp], c_recv.at[1, sp], (core, s)),
        ]

    def from_y(sp):
        block = buf.at[flip_y, sp]
        part = buf.at[flip_y, sp, high_half]
        return [
            send(part, part, x_send.at[1, sp], x_recv.at[1, sp], (flip_x, s)),
            send(block, block, c_send.at[2, sp], c_recv.at[2, sp], (core, s)),
        ]

    def from_diagonal(sp):
        block = buf.at[diagonal, sp]
        return send(block, block, c_send.at[3, sp], c_recv.at[3, sp], (core, s))

    def arrived(block, sem):
        send(block, block, sem, sem, (core, s)).wait_recv()

    def plane_at(i):
        distance = (i + 1) // 2
        sign = 2 * (i % 2) - 1
        sp = s + sign * distance
        return sp, (sp >= 0) & (sp < planes) & (i >= 0) & (i <= 2 * planes - 2)

    def step_first(sp, i):
        @pl.when(i > 0)
        def _():
            arrived(buf.at[e, sp], z_recv.at[sp])

        @pl.when((sp <= s) & (s < planes - 1))
        def _():
            up(sp).start()

        @pl.when((sp >= s) & (s > 0))
        def _():
            down(sp).start()

        for copy in first(sp):
            copy.start()

    def step_second(sp):
        arrived(buf.at[flip_x, sp], x_recv.at[0, sp])
        for copy in from_x(sp):
            copy.start()
        arrived(buf.at[flip_y, sp], y_recv.at[0, sp])
        for copy in from_y(sp):
            copy.start()

    def step_third(sp):
        arrived(buf.at[diagonal, sp, low_half], y_recv.at[1, sp])
        arrived(buf.at[diagonal, sp, high_half], x_recv.at[1, sp])
        from_diagonal(sp).start()

    def copy_out(stage, out, sem, q, sp):
        rows = pl.ds(pl.multiple_of((q * planes + sp) * slots, 16), slots)
        return pltpu.make_async_copy(stage.at[q], out.at[:, rows, :], sem.at[q])

    def load(q, sp, k):
        return pltpu.make_async_copy(
            d_ref.at[2 * q + k, sp, :, pl.ds(0, MODEL_WIDTH)],
            load_d.at[q, pl.ds(k * length, length), :],
            in_d.at[q, k],
        )

    def start_loads(sp):
        for q in range(4):
            for k in range(2):
                load(q, sp, k).start()

    def dispatch(sp, i):
        for k, other in enumerate((core, core + flip_x - e, core + flip_y - e, core + diagonal - e)):
            arrived(buf.at[other, sp], c_recv.at[k, sp])

        def one(q, carry):
            one_hot_pair(place_ref, q * planes + sp, hot, slots)
            d_wide = load_d.shape[2]

            @pl.when(i > 0)
            def _():
                copy_out(stage_x, outx_ref, out_x, q, sp).wait()
                copy_out(stage_d, outd_ref, out_d, q, sp).wait()

            for k in range(2):
                load(q, sp, k).wait()

            def columns_of(at, wide, with_d):
                rows = jnp.concatenate(
                    [buf[2 * q, sp, :, at], buf[2 * q + 1, sp, :, at]], axis=0
                )
                got = jnp.dot(hot[...], rows, preferred_element_type=FULL).astype(LOW)
                stage_x[q, :, :, at] = got.reshape(EXP_DEV, slots, wide)
                if with_d:
                    got = jnp.dot(
                        hot[...], load_d[q, :, at], preferred_element_type=FULL
                    ).astype(LOW)
                    stage_d[q, :, :, at] = got.reshape(EXP_DEV, slots, wide)

            def tile(t, inner):
                columns_of(pl.ds(pl.multiple_of(t * TILE, TILE), TILE), TILE, True)
                return inner

            lax.fori_loop(0, MODEL_WIDTH // TILE, tile, 0)
            if width > MODEL_WIDTH:
                columns_of(pl.ds(MODEL_WIDTH, width - MODEL_WIDTH), width - MODEL_WIDTH, False)
            copy_out(stage_x, outx_ref, out_x, q, sp).start()
            copy_out(stage_d, outd_ref, out_d, q, sp).start()
            return carry

        lax.fori_loop(0, 4, one, 0)

    def step(i, carry):
        for lag, work in ((0, step_first), (1, step_second), (2, step_third), (3, dispatch)):
            sp, there = plane_at(i - lag)

            @pl.when(there)
            def _(sp=sp, lag=lag, work=work):
                if lag in (0, 3):
                    work(sp, i - lag)
                else:
                    work(sp)

        sp, there = plane_at(i - 2)

        @pl.when(there)
        def _():
            start_loads(sp)

        return carry

    lax.fori_loop(0, 2 * planes + 2, step, 0)

    def drain(sp, carry):
        for copy in first(sp) + from_x(sp) + from_y(sp) + [from_diagonal(sp)]:
            copy.wait_send()

        @pl.when((sp <= s) & (s < planes - 1))
        def _():
            up(sp).wait_send()

        @pl.when((sp >= s) & (s > 0))
        def _():
            down(sp).wait_send()

        return carry

    lax.fori_loop(0, planes, drain, 0)
    for q in range(4):
        copy_out(stage_x, outx_ref, out_x, q, 0).wait()
        copy_out(stage_d, outd_ref, out_d, q, 0).wait()


def gather_dispatch(rows, d_all, place, planes, slots, identity):
    owners = lax.axis_size("expert")
    length, width = rows.shape
    total = place.shape[0] * slots
    kernel = functools.partial(gather_dispatch_kernel, planes, slots)
    return pl.pallas_call(
        kernel,
        out_shape=[
            jax.ShapeDtypeStruct((EXP_DEV, total, width), LOW),
            jax.ShapeDtypeStruct((EXP_DEV, total, MODEL_WIDTH), LOW),
        ],
        in_specs=[VM, ANY, VM],
        out_specs=[ANY, ANY],
        scratch_shapes=[
            pltpu.VMEM((owners, planes, length, width), LOW),
            pltpu.VMEM((EXP_DEV * slots, 2 * length), LOW),
            pltpu.VMEM((4, EXP_DEV, slots, width), LOW),
            pltpu.VMEM((4, EXP_DEV, slots, MODEL_WIDTH), LOW),
            pltpu.VMEM((4, 2 * length, MODEL_WIDTH), LOW),
            DMA((2, planes)),
            DMA((planes,)),
            DMA((2, planes)),
            DMA((2, planes)),
            DMA((2, planes)),
            DMA((2, planes)),
            DMA((4, planes)),
            DMA((4, planes)),
            DMA((4,)),
            DMA((4,)),
            DMA((4, 2)),
        ],
        compiler_params=pltpu.CompilerParams(
            collective_id=identity, has_side_effects=True, vmem_limit_bytes=VMEM_LIMIT
        ),
    )(rows, d_all, place)


def expert_kernel(
    sel_ref, x_ref, dy_ref, wg_ref, wu_ref, wd_ref,
    y_ref, dx_ref, dwg_ref, dwu_ref, dwd_ref, a_all, dg_all, du_all,
):
    rows = x_ref.shape[1]
    step = 256
    experts = sel_ref.shape[2] // 2
    sel = sel_ref[0, 0:1, :]
    lane = lax.broadcasted_iota(jnp.int32, sel.shape, 1)
    high_sel = jnp.where(lane < experts, sel, 0.0)
    rest_sel = sel - high_sel
    nt = (((1,), (1,)), ((), ()))
    tn = (((0,), (0,)), ((), ()))

    def chunk(r, carry):
        at = pl.ds(pl.multiple_of(r * step, step), step)
        x = x_ref[0, at, :MODEL_WIDTH]
        tail = x_ref[0, at, MODEL_WIDTH:].astype(FULL)
        dy = dy_ref[0, at, :]
        gate = jnp.sum(tail * sel, axis=1, keepdims=True)
        g = lax.dot_general(x, wg_ref[0], nt, preferred_element_type=FULL)
        u = lax.dot_general(x, wu_ref[0], nt, preferred_element_type=FULL)
        da = lax.dot_general(dy, wd_ref[0], nt, preferred_element_type=FULL)
        sigma = 1.0 / (1.0 + jnp.exp(-g))
        silu = g * sigma
        act = (silu * u).astype(LOW).astype(FULL)
        d_gate = jnp.sum(act * da, axis=1, keepdims=True)
        d_act = da * gate
        a_all[at, :] = (act * gate).astype(LOW)
        dg_all[at, :] = (d_act * u * sigma * (1.0 + g * (1.0 - sigma))).astype(LOW)
        du_all[at, :] = (d_act * silu).astype(LOW)
        high = d_gate.astype(LOW).astype(FULL)
        dx_ref[0, at, MODEL_WIDTH:] = (high * high_sel + (d_gate - high) * rest_sel).astype(LOW)
        y_ref[0, at, :] = jnp.dot(
            a_all[at, :], wd_ref[0], preferred_element_type=FULL
        ).astype(LOW)
        dx_ref[0, at, :MODEL_WIDTH] = (
            jnp.dot(dg_all[at, :], wg_ref[0], preferred_element_type=FULL)
            + jnp.dot(du_all[at, :], wu_ref[0], preferred_element_type=FULL)
        ).astype(LOW)
        return carry

    lax.fori_loop(0, rows // step, chunk, 0)

    def tile(t, carry):
        at = pl.ds(pl.multiple_of(t * TILE, TILE), TILE)
        dwg_ref[0, :, at] = lax.dot_general(
            dg_all[...], x_ref[0, :, at], tn, preferred_element_type=FULL
        )
        dwu_ref[0, :, at] = lax.dot_general(
            du_all[...], x_ref[0, :, at], tn, preferred_element_type=FULL
        )
        dwd_ref[0, :, at] = lax.dot_general(
            a_all[...], dy_ref[0, :, at], tn, preferred_element_type=FULL
        )
        return carry

    lax.fori_loop(0, MODEL_WIDTH // TILE, tile, 0)


def expert_pass(sel, x, dy, w_gate, w_up, w_down):
    rows, width = x.shape[1:]
    hidden = w_gate.shape[1]

    def spec(*shape):
        return pl.BlockSpec((1,) + shape, lambda j: (j, 0, 0))

    def out(*shape, dtype=LOW):
        return jax.ShapeDtypeStruct((EXP_DEV,) + shape, dtype)

    return pl.pallas_call(
        expert_kernel,
        grid=(EXP_DEV,),
        in_specs=[
            spec(*sel.shape[1:]),
            spec(rows, width),
            spec(rows, MODEL_WIDTH),
            spec(hidden, MODEL_WIDTH),
            spec(hidden, MODEL_WIDTH),
            spec(hidden, MODEL_WIDTH),
        ],
        out_specs=[
            spec(rows, MODEL_WIDTH),
            spec(rows, width),
            spec(hidden, MODEL_WIDTH),
            spec(hidden, MODEL_WIDTH),
            spec(hidden, MODEL_WIDTH),
        ],
        out_shape=[
            out(rows, MODEL_WIDTH),
            out(rows, width),
            out(hidden, MODEL_WIDTH, dtype=FULL),
            out(hidden, MODEL_WIDTH, dtype=FULL),
            out(hidden, MODEL_WIDTH, dtype=FULL),
        ],
        scratch_shapes=[pltpu.VMEM((rows, hidden), LOW)] * 3,
        compiler_params=pltpu.CompilerParams(vmem_limit_bytes=VMEM_LIMIT),
        cost_estimate=pl.CostEstimate(
            flops=EXP_DEV * rows * MODEL_WIDTH * hidden * 18,
            bytes_accessed=160 << 20,
            transcendentals=EXP_DEV * rows * hidden,
        ),
    )(sel, x, dy, w_gate, w_up, w_down)


def combine_home_kernel(
    planes, slots, place_ref, v_ref, m_ref, out_ref, mix_ref,
    hot, load, load_m, stage, mine, away, c_in, x_in, y_in, x_half, y_half, u_in, d_in,
    in_sem, m_sem, stage_sem, c_send, c_recv, x_send, x_recv, y_send, y_recv, z_send, z_recv,
):
    e, core, flip_x, flip_y, diagonal = neighbours()
    s = lax.axis_index("shard")
    q_own, q_x, q_y, q_d = e // 2, flip_x // 2, flip_y // 2, diagonal // 2
    parity = e % 2
    length, width = out_ref.shape
    half = length // 2
    low_half, high_half = pl.ds(0, half), pl.ds(half, half)

    def fetch(q, sp):
        rows = pl.ds(pl.multiple_of((q * planes + sp) * slots, 16), slots)
        return pltpu.make_async_copy(v_ref.at[:, rows, :], load.at[q], in_sem.at[q])

    def fetch_mix(q, sp):
        rows = pl.ds(pl.multiple_of((q * planes + sp) * slots, 16), slots)
        return pltpu.make_async_copy(m_ref.at[:, rows, :], load_m.at[q % 2], m_sem.at[q % 2])

    def store_mix(q, sp):
        return pltpu.make_async_copy(
            stage.at[q % 2], mix_ref.at[q, :, sp], stage_sem.at[q % 2]
        )

    def mix(sp):
        for q in range(2):
            fetch_mix(q, sp).start()
        for q in range(4):
            one_hot_pair(place_ref, q * planes + sp, hot, slots)
            fetch_mix(q, sp).wait()
            if q >= 2:
                store_mix(q - 2, sp).wait()

            def tile(t, inner, q=q):
                at = pl.ds(pl.multiple_of(t * TILE, TILE), TILE)
                rows = load_m[q % 2, :, :, at].reshape(EXP_DEV * slots, TILE)
                got = lax.dot_general(
                    hot[...], rows, (((0,), (0,)), ((), ())), preferred_element_type=FULL
                ).astype(LOW)
                stage[q % 2, :, :, at] = got.reshape(2, length, TILE)
                return inner

            lax.fori_loop(0, MODEL_WIDTH // TILE, tile, 0)
            store_mix(q, sp).start()
            if q < 2:
                fetch_mix(q + 2, sp).start()
        for q in (2, 3):
            store_mix(q, sp).wait()

    def to_core(q, sp):
        return send(away.at[q, sp], c_in.at[q, sp], c_send.at[q, sp], c_recv.at[q, sp], (core, s))

    def halves(sp):
        return [
            send(
                mine.at[q_d, sp, low_half], y_half.at[sp], y_send.at[0, sp], y_recv.at[0, sp],
                (flip_y, s),
            ),
            send(
                mine.at[q_d, sp, high_half], x_half.at[sp], x_send.at[0, sp], x_recv.at[0, sp],
                (flip_x, s),
            ),
        ]

    def to_x(sp):
        return send(mine.at[q_x, sp], x_in.at[sp], x_send.at[1, sp], x_recv.at[1, sp], (flip_x, s))

    def to_y(sp):
        return send(mine.at[q_y, sp], y_in.at[sp], y_send.at[1, sp], y_recv.at[1, sp], (flip_y, s))

    def up(sp):
        return send(mine.at[q_own, sp], u_in.at[sp], z_send.at[0, sp], z_recv.at[0, sp], (e, s + 1))

    def down(sp):
        return send(mine.at[q_own, sp], d_in.at[sp], z_send.at[1, sp], z_recv.at[1, sp], (e, s - 1))

    def arrived(block, sem):
        send(block, block, sem, sem, (core, s)).wait_recv()

    def plane_at(i):
        back = 2 * planes - 2 - i
        sp = s + (2 * (back % 2) - 1) * ((back + 1) // 2)
        return sp, (sp >= 0) & (sp < planes) & (i >= 0) & (back >= 0)

    def add(target, *others):
        total = target[...].astype(FULL)
        for other in others:
            total = total + other[...].astype(FULL)
        target[...] = total.astype(LOW)

    def work(sp):
        for q in range(4):
            fetch(q, sp).start()

        def one(q, carry):
            one_hot_pair(place_ref, q * planes + sp, hot, slots)
            fetch(q, sp).wait()

            def part(at, wide):
                rows = load[q, :, :, at].reshape(EXP_DEV * slots, wide)
                got = lax.dot_general(
                    hot[...], rows, (((0,), (0,)), ((), ())), preferred_element_type=FULL
                ).astype(LOW)
                got = got.reshape(2, length, wide)

                @pl.when(parity == 0)
                def _():
                    mine[q, sp, :, at] = got[0]
                    away[q, sp, :, at] = got[1]

                @pl.when(parity == 1)
                def _():
                    mine[q, sp, :, at] = got[1]
                    away[q, sp, :, at] = got[0]

            def tile(t, inner):
                part(pl.ds(pl.multiple_of(t * TILE, TILE), TILE), TILE)
                return inner

            lax.fori_loop(0, MODEL_WIDTH // TILE, tile, 0)
            if width > MODEL_WIDTH:
                part(pl.ds(MODEL_WIDTH, width - MODEL_WIDTH), width - MODEL_WIDTH)
            to_core(q, sp).start()
            return carry

        lax.fori_loop(0, 4, one, 0)

    def pairs(sp):
        def one(q, carry):
            arrived(c_in.at[q, sp], c_recv.at[q, sp])
            add(mine.at[q, sp], c_in.at[q, sp])
            return carry

        one(q_d, 0)
        for copy in halves(sp):
            copy.start()
        for q in (q_x, q_y, q_own):
            one(q, 0)

    def sides(sp):
        arrived(y_half.at[sp], y_recv.at[0, sp])
        add(mine.at[q_x, sp, low_half], y_half.at[sp])
        to_x(sp).start()
        arrived(x_half.at[sp], x_recv.at[0, sp])
        add(mine.at[q_y, sp, high_half], x_half.at[sp])
        to_y(sp).start()

    def line(sp):
        arrived(x_in.at[sp], x_recv.at[1, sp])
        arrived(y_in.at[sp], y_recv.at[1, sp])
        add(mine.at[q_own, sp], x_in.at[sp], y_in.at[sp])

        @pl.when((sp >= s) & (s > 0))
        def _():
            arrived(u_in.at[sp], z_recv.at[0, sp])
            add(mine.at[q_own, sp], u_in.at[sp])

        @pl.when((sp <= s) & (s < planes - 1))
        def _():
            arrived(d_in.at[sp], z_recv.at[1, sp])
            add(mine.at[q_own, sp], d_in.at[sp])

        @pl.when(sp > s)
        def _():
            up(sp).start()

        @pl.when(sp < s)
        def _():
            down(sp).start()

    greet(planes)

    def step(i, carry):
        for lag, job in ((0, work), (1, pairs), (2, sides), (3, line), (0, mix)):
            sp, there = plane_at(i - lag)

            @pl.when(there)
            def _(sp=sp, job=job):
                job(sp)

        return carry

    lax.fori_loop(0, 2 * planes + 2, step, 0)
    out_ref[...] = mine[q_own, s].astype(FULL)

    def drain(sp, carry):
        for q in range(4):
            to_core(q, sp).wait_send()
        for copy in halves(sp) + [to_x(sp), to_y(sp)]:
            copy.wait_send()

        @pl.when(sp > s)
        def _():
            up(sp).wait_send()

        @pl.when(sp < s)
        def _():
            down(sp).wait_send()

        return carry

    lax.fori_loop(0, planes, drain, 0)


def combine_home(place, v, m, length, planes, slots, identity):
    width = v.shape[2]
    block = (planes, length, width)
    pairs = place.shape[0] // planes
    return pl.pallas_call(
        functools.partial(combine_home_kernel, planes, slots),
        out_shape=[
            jax.ShapeDtypeStruct((length, width), FULL),
            jax.ShapeDtypeStruct((pairs, 2, planes, length, MODEL_WIDTH), LOW),
        ],
        in_specs=[VM, ANY, ANY],
        out_specs=[VM, ANY],
        scratch_shapes=[
            pltpu.VMEM((EXP_DEV * slots, 2 * length), LOW),
            pltpu.VMEM((4, EXP_DEV, slots, width), LOW),
            pltpu.VMEM((2, EXP_DEV, slots, MODEL_WIDTH), LOW),
            pltpu.VMEM((2, 2, length, MODEL_WIDTH), LOW),
            pltpu.VMEM((4,) + block, LOW),
            pltpu.VMEM((4,) + block, LOW),
            pltpu.VMEM((4,) + block, LOW),
            pltpu.VMEM(block, LOW),
            pltpu.VMEM(block, LOW),
            pltpu.VMEM((planes, length // 2, width), LOW),
            pltpu.VMEM((planes, length // 2, width), LOW),
            pltpu.VMEM(block, LOW),
            pltpu.VMEM(block, LOW),
            DMA((4,)),
            DMA((2,)),
            DMA((2,)),
            DMA((4, planes)),
            DMA((4, planes)),
            DMA((2, planes)),
            DMA((2, planes)),
            DMA((2, planes)),
            DMA((2, planes)),
            DMA((2, planes)),
            DMA((2, planes)),
        ],
        compiler_params=pltpu.CompilerParams(
            collective_id=identity, has_side_effects=True, vmem_limit_bytes=VMEM_LIMIT
        ),
    )(place, v, m)


def greet_plane(planes, owners):
    e, s = lax.axis_index("expert"), lax.axis_index("shard")
    barrier = pltpu.get_barrier_semaphore()
    for o in range(1, owners):
        pl.semaphore_signal(
            barrier, 1, device_id=(lax.rem(e + o, owners), s), device_id_type=MESH
        )

    @pl.when(s > 0)
    def _():
        pl.semaphore_signal(barrier, 1, device_id=(e, s - 1), device_id_type=MESH)

    @pl.when(s < planes - 1)
    def _():
        pl.semaphore_signal(barrier, 1, device_id=(e, s + 1), device_id_type=MESH)

    inner = (s > 0) & (s < planes - 1)

    @pl.when(inner)
    def _():
        pl.semaphore_wait(barrier, owners + 1)

    @pl.when(jnp.logical_not(inner))
    def _():
        pl.semaphore_wait(barrier, owners)


def share_kernel(
    planes, owners, head_ref, rest_ref, rows_ref, out_rows, out_head, out_rest,
    acc_rows, acc_head, acc_rest, u_rows, u_head, u_rest, d_rows, d_head, d_rest,
    load_sem, a_send, a_recv, z_send, z_recv, x_send, x_recv, y_send, y_recv, c_send, c_recv, own_sem,
):
    e, core, flip_x, flip_y, diagonal = neighbours()
    s = lax.axis_index("shard")
    lanes = owners // planes
    share = rows_ref.shape[1] // owners
    acc = (acc_rows, acc_head, acc_rest)
    up_in, down_in = (u_rows, u_head, u_rest), (d_rows, d_head, d_rest)
    outs = (out_rows, out_head, out_rest)
    sources = (None, head_ref, rest_ref)

    def load(k, sp):
        return pltpu.make_async_copy(sources[k].at[sp], acc[k].at[sp], load_sem.at[k - 1, sp])

    for k in (1, 2):
        for sp in range(planes):
            load(k, sp).start()

    def part(sp):
        return acc_rows.at[pl.ds(sp * lanes, lanes)]

    def chunk(k, sp):
        return part(sp) if k == 0 else acc[k].at[sp]

    def spread(o):
        other = lax.rem(e + o, owners)
        at = pl.ds(pl.multiple_of(other * share, share), share)
        return send(
            rows_ref.at[:, at], acc_rows.at[e], a_send.at[o], a_recv.at[e], (other, s)
        )

    def arrived(block, sem):
        send(block, block, sem, sem, (core, s)).wait_recv()

    greet_plane(planes, owners)
    for o in range(1, owners):
        spread(o).start()
    acc_rows[e] = rows_ref[:, pl.ds(pl.multiple_of(e * share, share), share)]

    def add(target, other):
        count = target.shape[1] // 128
        for lead in range(target.shape[0]):

            def one(r, carry, lead=lead):
                at = pl.ds(pl.multiple_of(r * 128, 128), 128)
                target[lead, at, :] = (
                    target[lead, at, :].astype(FULL) + other[lead, at, :].astype(FULL)
                ).astype(LOW)
                return carry

            lax.fori_loop(0, count, one, 0)

    def up(k, sp):
        return send(
            chunk(k, sp), up_in[k].at[sp], z_send.at[k, 0, sp], z_recv.at[k, 0, sp], (e, s + 1)
        )

    def down(k, sp):
        return send(
            chunk(k, sp), down_in[k].at[sp], z_send.at[k, 1, sp], z_recv.at[k, 1, sp], (e, s - 1)
        )

    def line(k, sp):
        if k == 0:
            for lane in range(lanes):
                source = sp * lanes + lane

                @pl.when(source != e)
                def _(source=source):
                    arrived(acc_rows.at[source], a_recv.at[source])

        else:
            load(k, sp).wait()

        @pl.when((sp >= s) & (s > 0))
        def _():
            arrived(up_in[k].at[sp], z_recv.at[k, 0, sp])
            add(chunk(k, sp), up_in[k].at[sp])

        @pl.when((sp <= s) & (s < planes - 1))
        def _():
            arrived(down_in[k].at[sp], z_recv.at[k, 1, sp])
            add(chunk(k, sp), down_in[k].at[sp])

        @pl.when(sp > s)
        def _():
            up(k, sp).start()

        @pl.when(sp < s)
        def _():
            down(k, sp).start()

    def others(k):
        def one(i, carry):
            back = 2 * planes - 2 - i
            sp = s + (2 * (back % 2) - 1) * ((back + 1) // 2)

            @pl.when((sp >= 0) & (sp < planes))
            def _():
                line(k, sp)

            return carry

        lax.fori_loop(0, 2 * planes - 2, one, 0)

    def first(k):
        block = chunk(k, s)
        target = outs[k].at[e]
        return [
            send(block, target, x_send.at[k, 0], x_recv.at[k, 0], (flip_x, s)),
            send(block, target, y_send.at[k, 0], y_recv.at[k, 0], (flip_y, s)),
            send(block, target, c_send.at[k, 0], c_recv.at[k, 0], (core, s)),
        ]

    def half(k, lane, at):
        count = outs[k].shape[1] // 2
        return outs[k].at[lane, pl.ds(at * count, count)]

    def from_x(k):
        block, piece = outs[k].at[flip_x], half(k, flip_x, 0)
        return [
            send(piece, piece, y_send.at[k, 1], y_recv.at[k, 1], (flip_y, s)),
            send(block, block, c_send.at[k, 1], c_recv.at[k, 1], (core, s)),
        ]

    def from_y(k):
        block, piece = outs[k].at[flip_y], half(k, flip_y, 1)
        return [
            send(piece, piece, x_send.at[k, 1], x_recv.at[k, 1], (flip_x, s)),
            send(block, block, c_send.at[k, 2], c_recv.at[k, 2], (core, s)),
        ]

    def from_diagonal(k):
        block = outs[k].at[diagonal]
        return send(block, block, c_send.at[k, 3], c_recv.at[k, 3], (core, s))

    def keep(k):
        return pltpu.make_async_copy(chunk(k, s), outs[k].at[e], own_sem.at[k])

    def own(k):
        line(k, s)
        for copy in first(k):
            copy.start()
        keep(k).start()

    def second(k):
        arrived(outs[k].at[flip_x], x_recv.at[k, 0])
        for copy in from_x(k):
            copy.start()
        arrived(outs[k].at[flip_y], y_recv.at[k, 0])
        for copy in from_y(k):
            copy.start()

    def third(k):
        arrived(half(k, diagonal, 0), y_recv.at[k, 1])
        arrived(half(k, diagonal, 1), x_recv.at[k, 1])
        from_diagonal(k).start()

    a, b, c = 1, 0, 2
    others(a)
    others(b)
    own(a)
    others(c)
    second(a)
    own(b)
    third(a)
    own(c)
    second(b)
    third(b)
    second(c)
    third(c)
    for k in range(3):
        keep(k).wait()
        for j, lane in enumerate(
            (core, core + flip_x - e, core + flip_y - e, core + diagonal - e)
        ):
            arrived(outs[k].at[lane], c_recv.at[k, j])
        for copy in first(k) + from_x(k) + from_y(k) + [from_diagonal(k)]:
            copy.wait_send()
    for o in range(1, owners):
        spread(o).wait_send()

    def drain(sp, carry):
        for k in range(3):

            @pl.when(sp > s)
            def _(k=k):
                up(k, sp).wait_send()

            @pl.when(sp < s)
            def _(k=k):
                down(k, sp).wait_send()

        return carry

    lax.fori_loop(0, planes, drain, 0)


def share_grads(head, rest, rows, planes, owners, identity):
    share = rows.shape[1] // owners
    shapes = (
        (owners // planes, rows.shape[0], share),
        head.shape[1:],
        rest.shape[1:],
    )
    acc = [pltpu.VMEM((owners,) + shapes[0][1:], LOW)]
    acc += [pltpu.VMEM((planes,) + shape, LOW) for shape in shapes[1:]]
    landing = [pltpu.VMEM((planes,) + shape, LOW) for shape in shapes]
    return pl.pallas_call(
        functools.partial(share_kernel, planes, owners),
        out_shape=[jax.ShapeDtypeStruct((owners,) + shape, LOW) for shape in shapes],
        in_specs=[ANY, ANY, VM],
        out_specs=[ANY, ANY, ANY],
        scratch_shapes=acc
        + landing
        + landing
        + [
            DMA((2, planes)),
            DMA((owners,)),
            DMA((owners,)),
            DMA((3, 2, planes)),
            DMA((3, 2, planes)),
            DMA((3, 2)),
            DMA((3, 2)),
            DMA((3, 2)),
            DMA((3, 2)),
            DMA((3, 4)),
            DMA((3, 4)),
            DMA((3,)),
        ],
        compiler_params=pltpu.CompilerParams(
            collective_id=identity, has_side_effects=True, vmem_limit_bytes=VMEM_LIMIT
        ),
    )(head, rest, rows)


def finish_kernel(owners, rows_ref, head_ref, kv_ref, tail_ref, out_rows, out_qkv, out_tail):
    i = pl.program_id(0)

    @pl.when(i < owners)
    def _():
        out_rows[...] = rows_ref[0].astype(FULL)
        out_qkv[...] = head_ref[0].astype(FULL)

    @pl.when(i >= owners)
    def _():
        each = owners // KEY_VALUE_HEADS
        for h in range(KEY_VALUE_HEADS):
            total = kv_ref[h * each].astype(FULL)
            for j in range(1, each):
                total = total + kv_ref[h * each + j].astype(FULL)
            out_qkv[:, h * HEAD_SIZE : (h + 1) * HEAD_SIZE] = total

    @pl.when(i == 0)
    def _():
        total = tail_ref[0].astype(FULL)
        for lane in range(1, owners):
            total = total + tail_ref[lane].astype(FULL)
        out_tail[...] = total


def finish_grads(rows, head, rest, owners):
    rows = rows.reshape(owners, -1, rows.shape[-1])
    head = head.reshape(owners, -1, head.shape[-1])
    rest = rest.reshape(owners, -1, rest.shape[-1])
    count, share = rows.shape[1:]
    height, wide = head.shape[1:]
    last = owners - 1
    return pl.pallas_call(
        functools.partial(finish_kernel, owners),
        grid=(owners + 2,),
        in_specs=[
            pl.BlockSpec((1, count, share), lambda i: (jnp.minimum(i, last), 0, 0)),
            pl.BlockSpec((1, height, wide), lambda i: (jnp.minimum(i, last), 0, 0)),
            pl.BlockSpec((owners, height, HEAD_SIZE), lambda i: (0, 0, i // (owners + 1))),
            pl.BlockSpec((owners, height, TAIL), lambda i: (0, 0, 2)),
        ],
        out_specs=[
            pl.BlockSpec((count, share), lambda i: (0, jnp.minimum(i, last))),
            pl.BlockSpec((height, wide), lambda i: (0, i)),
            pl.BlockSpec((height, TAIL), lambda i: (0, 0)),
        ],
        out_shape=[
            jax.ShapeDtypeStruct((count, owners * share), FULL),
            jax.ShapeDtypeStruct((height, (owners + 2) * wide), FULL),
            jax.ShapeDtypeStruct((height, TAIL), FULL),
        ],
        compiler_params=pltpu.CompilerParams(vmem_limit_bytes=VMEM_LIMIT),
    )(rows, head, rest, rest)


def gather_steps(at, cut, source, x_send, x_recv, y_send, y_recv, c_send, c_recv):
    e, core, flip_x, flip_y, diagonal = neighbours()
    s = lax.axis_index("shard")

    def arrived(block, sem):
        send(block, block, sem, sem, (core, s)).wait_recv()

    def first():
        return [
            send(source, at(e), x_send(0), x_recv(0), (flip_x, s)),
            send(source, at(e), y_send(0), y_recv(0), (flip_y, s)),
            send(source, at(e), c_send(0), c_recv(0), (core, s)),
        ]

    def from_x():
        return [
            send(cut(flip_x, 0), cut(flip_x, 0), y_send(1), y_recv(1), (flip_y, s)),
            send(at(flip_x), at(flip_x), c_send(1), c_recv(1), (core, s)),
        ]

    def from_y():
        return [
            send(cut(flip_y, 1), cut(flip_y, 1), x_send(1), x_recv(1), (flip_x, s)),
            send(at(flip_y), at(flip_y), c_send(2), c_recv(2), (core, s)),
        ]

    def from_diagonal():
        return [send(at(diagonal), at(diagonal), c_send(3), c_recv(3), (core, s))]

    def begin():
        for copy in first():
            copy.start()

    def second():
        arrived(at(flip_x), x_recv(0))
        for copy in from_x():
            copy.start()
        arrived(at(flip_y), y_recv(0))
        for copy in from_y():
            copy.start()

    def third():
        arrived(cut(diagonal, 0), y_recv(1))
        arrived(cut(diagonal, 1), x_recv(1))
        for copy in from_diagonal():
            copy.start()

    def last():
        for k, lane in enumerate((core, core + flip_x - e, core + flip_y - e, core + diagonal - e)):
            arrived(at(lane), c_recv(k))

    def sent():
        for copy in first() + from_x() + from_y() + from_diagonal():
            copy.wait_send()

    return begin, second, third, last, sent


def start_kernel(
    planes, owners, w_ref, tok_ref, out_ref, d_ref, w_all, tok_all, w_out_mine, d_all,
    o_rows, keep_sem, w_send, w_recv, o_send, o_recv, z_send, z_recv,
    tx_send, tx_recv, ty_send, ty_recv, tc_send, tc_recv,
    dx_send, dx_recv, dy_send, dy_recv, dc_send, dc_recv,
):
    e, core, _, _, _ = neighbours()
    s = lax.axis_index("shard")
    lanes = owners // planes
    home = e // lanes
    length = tok_ref.shape[0]
    half = length // 2
    count = w_out_mine.shape[0]
    pieces = 4
    out_part = count // pieces

    def arrived(block, sem):
        send(block, block, sem, sem, (core, s)).wait_recv()

    def w_copy(sp, way):
        block = w_all.at[sp]
        return send(block, block, w_send.at[way, sp], w_recv.at[sp], (e, s + 1 - 2 * way))

    def d_copy(sp, way):
        block = d_all.at[e, sp]
        return send(block, block, z_send.at[way, sp], z_recv.at[sp], (e, s + 1 - 2 * way))

    def o_copy(k, way):
        block = w_out_mine.at[pl.ds(k * out_part, out_part)]
        return send(block, block, o_send.at[way, k], o_recv.at[k], (e, s + 1 - 2 * way))

    def tokens():
        return gather_steps(
            lambda lane: tok_all.at[lane],
            lambda lane, k: tok_all.at[lane, pl.ds(k * half, half)],
            tok_ref,
            lambda k: tx_send.at[k],
            lambda k: tx_recv.at[k],
            lambda k: ty_send.at[k],
            lambda k: ty_recv.at[k],
            lambda k: tc_send.at[k],
            lambda k: tc_recv.at[k],
        )

    def d_rows(sp):
        return gather_steps(
            lambda lane: d_all.at[lane, sp],
            lambda lane, k: d_all.at[lane, sp, pl.ds(k * half, half)],
            d_all.at[e, sp],
            lambda k: dx_send.at[k, sp],
            lambda k: dx_recv.at[k, sp],
            lambda k: dy_send.at[k, sp],
            lambda k: dy_recv.at[k, sp],
            lambda k: dc_send.at[k, sp],
            lambda k: dc_recv.at[k, sp],
        )

    keep_w = pltpu.make_async_copy(w_ref, w_all.at[s], keep_sem.at[0])
    keep_t = pltpu.make_async_copy(tok_ref, tok_all.at[e], keep_sem.at[1])
    keep_d = pltpu.make_async_copy(d_ref, d_all.at[e, s], keep_sem.at[2])
    rows = pl.ds(pl.multiple_of((e - home * lanes) * count, 16), count)
    load_o = pltpu.make_async_copy(out_ref.at[rows], o_rows, keep_sem.at[3])
    keep_o = pltpu.make_async_copy(o_rows, w_out_mine, keep_sem.at[3])
    keep_w.start()
    keep_t.start()
    keep_d.start()

    @pl.when(s == home)
    def _():
        load_o.start()

    greet(planes)

    def both_ways(copy, sp):
        @pl.when((sp <= s) & (s < planes - 1))
        def _():
            copy(sp, 0).start()

        @pl.when((sp >= s) & (s > 0))
        def _():
            copy(sp, 1).start()

    tokens()[0]()
    keep_w.wait()
    both_ways(w_copy, s)
    keep_d.wait()
    both_ways(d_copy, s)
    d_rows(s)[0]()

    def out_step(k):
        @pl.when(s != home)
        def _():
            arrived(w_out_mine.at[pl.ds(k * out_part, out_part)], o_recv.at[k])

        @pl.when((s >= home) & (s < planes - 1))
        def _():
            o_copy(k, 0).start()

        @pl.when((s <= home) & (s > 0))
        def _():
            o_copy(k, 1).start()

    @pl.when(s == home)
    def _():
        load_o.wait()
        keep_o.start()
        keep_o.wait()
        for k in range(pieces):
            out_step(k)

    def plane_at(i):
        sp = s + (2 * (i % 2) - 1) * ((i + 1) // 2)
        return sp, (sp >= 0) & (sp < planes) & (i >= 0) & (i <= 2 * planes - 2)

    def step(i, carry):
        sp, there = plane_at(i)

        @pl.when(there & (i > 0))
        def _():
            arrived(w_all.at[sp], w_recv.at[sp])
            both_ways(w_copy, sp)
            arrived(d_all.at[e, sp], z_recv.at[sp])
            both_ways(d_copy, sp)
            d_rows(sp)[0]()

        @pl.when(i == 1)
        def _():
            tokens()[1]()

        @pl.when(i == 2)
        def _():
            tokens()[2]()

        @pl.when((i > 0) & ((2 * (s - home) == i) | (2 * (home - s) == i)))
        def _():
            for k in range(pieces):
                out_step(k)

        for lag in (1, 2):
            sp, there = plane_at(i - lag)

            @pl.when(there)
            def _(sp=sp, lag=lag):
                d_rows(sp)[lag]()

        return carry

    lax.fori_loop(0, 2 * planes + 1, step, 0)
    tokens()[3]()
    tokens()[4]()
    keep_t.wait()

    def finish(copy, sp):
        @pl.when((sp <= s) & (s < planes - 1))
        def _():
            copy(sp, 0).wait_send()

        @pl.when((sp >= s) & (s > 0))
        def _():
            copy(sp, 1).wait_send()

    def drain(sp, carry):
        d_rows(sp)[3]()
        d_rows(sp)[4]()
        finish(w_copy, sp)
        finish(d_copy, sp)
        return carry

    lax.fori_loop(0, planes, drain, 0)
    for k in range(pieces):

        @pl.when((s >= home) & (s < planes - 1))
        def _(k=k):
            o_copy(k, 0).wait_send()

        @pl.when((s <= home) & (s > 0))
        def _(k=k):
            o_copy(k, 1).wait_send()


def start_gather(w, tokens, w_out, d_rows, planes, owners, identity):
    def out(*shape):
        return jax.ShapeDtypeStruct(shape, LOW)

    count = w_out.shape[0] * planes // owners
    return pl.pallas_call(
        functools.partial(start_kernel, planes, owners),
        out_shape=[
            out(planes, *w.shape),
            out(owners, *tokens.shape),
            out(count, w_out.shape[1]),
            out(owners, planes, *d_rows.shape),
        ],
        in_specs=[VM, VM, ANY, VM],
        out_specs=[ANY] * 4,
        scratch_shapes=[
            pltpu.VMEM((count, w_out.shape[1]), LOW),
            DMA((4,)),
            DMA((2, planes)),
            DMA((planes,)),
            DMA((2, 4)),
            DMA((4,)),
            DMA((2, planes)),
            DMA((planes,)),
            DMA((2,)),
            DMA((2,)),
            DMA((2,)),
            DMA((2,)),
            DMA((4,)),
            DMA((4,)),
            DMA((2, planes)),
            DMA((2, planes)),
            DMA((2, planes)),
            DMA((2, planes)),
            DMA((4, planes)),
            DMA((4, planes)),
        ],
        compiler_params=pltpu.CompilerParams(collective_id=identity, has_side_effects=True),
    )(w, tokens, w_out, d_rows)


def greet_near():
    e, core, flip_x, flip_y, _ = neighbours()
    s = lax.axis_index("shard")
    barrier = pltpu.get_barrier_semaphore()
    for other in (core, flip_x, flip_y):
        pl.semaphore_signal(barrier, 1, device_id=(other, s), device_id_type=MESH)
    pl.semaphore_wait(barrier, 3)


def plane_gather_kernel(rows_ref, all_ref, keep_sem, xs, xr, ys, yr, cs, cr):
    e = lax.axis_index("expert")
    half = rows_ref.shape[0] // 2
    keep = pltpu.make_async_copy(rows_ref, all_ref.at[e], keep_sem)
    keep.start()
    greet_near()
    begin, second, third, last, sent = gather_steps(
        lambda lane: all_ref.at[lane],
        lambda lane, k: all_ref.at[lane, pl.ds(k * half, half)],
        rows_ref,
        lambda k: xs.at[k],
        lambda k: xr.at[k],
        lambda k: ys.at[k],
        lambda k: yr.at[k],
        lambda k: cs.at[k],
        lambda k: cr.at[k],
    )
    begin()
    second()
    third()
    last()
    sent()
    keep.wait()


def plane_gather(rows, owners, identity):
    return pl.pallas_call(
        plane_gather_kernel,
        out_shape=jax.ShapeDtypeStruct((owners,) + rows.shape, LOW),
        in_specs=[VM],
        out_specs=ANY,
        scratch_shapes=[DMA(()), DMA((2,)), DMA((2,)), DMA((2,)), DMA((2,)), DMA((4,)), DMA((4,))],
        compiler_params=pltpu.CompilerParams(collective_id=identity, has_side_effects=True),
    )(rows)


def project_home_kernel(
    turned, rows_ref, w_ref, out_ref, mine, away, c_in, x_in, y_in, x_half, y_half,
    cs, cr, xs, xr, ys, yr,
):
    e, core, flip_x, flip_y, diagonal = neighbours()
    s = lax.axis_index("shard")
    q_own, q_x, q_y, q_d = e // 2, flip_x // 2, flip_y // 2, diagonal // 2
    parity = e % 2
    half = out_ref.shape[0] // 2
    low_half, high_half = pl.ds(0, half), pl.ds(half, half)
    across = (((1,), (1 if turned else 0,)), ((), ()))

    def arrived(block, sem):
        send(block, block, sem, sem, (core, s)).wait_recv()

    def add(target, *others):
        total = target[...].astype(FULL)
        for other in others:
            total = total + other[...].astype(FULL)
        target[...] = total.astype(LOW)

    def to_core(q):
        return send(away.at[q], c_in.at[q], cs.at[q], cr.at[q], (core, s))

    def compute(q, lane, into):
        rows = rows_ref[2 * q + lane]

        def tile(t, carry):
            at = pl.ds(pl.multiple_of(t * TILE, TILE), TILE)
            w = w_ref[at, :] if turned else w_ref[:, at]
            into[q, :, at] = lax.dot_general(
                rows, w, across, preferred_element_type=FULL
            ).astype(LOW)
            return carry

        lax.fori_loop(0, MODEL_WIDTH // TILE, tile, 0)

    halves = [
        send(mine.at[q_d, low_half], y_half, ys.at[0], yr.at[0], (flip_y, s)),
        send(mine.at[q_d, high_half], x_half, xs.at[0], xr.at[0], (flip_x, s)),
    ]
    to_x = send(mine.at[q_x], x_in, xs.at[1], xr.at[1], (flip_x, s))
    to_y = send(mine.at[q_y], y_in, ys.at[1], yr.at[1], (flip_y, s))
    greet_near()
    order = (q_d, q_x, q_y, q_own)
    for q in order:
        compute(q, 1 - parity, away)
        to_core(q).start()
    for q in order:
        compute(q, parity, mine)

    def joined(q):
        arrived(c_in.at[q], cr.at[q])
        add(mine.at[q], c_in.at[q])

    joined(q_d)
    for copy in halves:
        copy.start()
    joined(q_x)
    joined(q_y)
    arrived(y_half, yr.at[0])
    add(mine.at[q_x, low_half], y_half)
    to_x.start()
    arrived(x_half, xr.at[0])
    add(mine.at[q_y, high_half], x_half)
    to_y.start()
    joined(q_own)
    arrived(x_in, xr.at[1])
    arrived(y_in, yr.at[1])
    out_ref[...] = mine[q_own].astype(FULL) + x_in[...].astype(FULL) + y_in[...].astype(FULL)
    for q in order:
        to_core(q).wait_send()
    for copy in halves + [to_x, to_y]:
        copy.wait_send()


def project_home(rows, w, turned, identity):
    length = rows.shape[1]
    block = (length, MODEL_WIDTH)
    part = (length // 2, MODEL_WIDTH)
    return pl.pallas_call(
        functools.partial(project_home_kernel, turned),
        out_shape=jax.ShapeDtypeStruct(block, FULL),
        in_specs=[VM, VM],
        out_specs=VM,
        scratch_shapes=[
            pltpu.VMEM((4,) + block, LOW),
            pltpu.VMEM((4,) + block, LOW),
            pltpu.VMEM((4,) + block, LOW),
            pltpu.VMEM(block, LOW),
            pltpu.VMEM(block, LOW),
            pltpu.VMEM(part, LOW),
            pltpu.VMEM(part, LOW),
            DMA((4,)),
            DMA((4,)),
            DMA((2,)),
            DMA((2,)),
            DMA((2,)),
            DMA((2,)),
        ],
        compiler_params=pltpu.CompilerParams(
            collective_id=identity, has_side_effects=True, vmem_limit_bytes=VMEM_LIMIT
        ),
    )(rows, w)


def per_device(
    tokens,
    segments,
    routes,
    attn_gain,
    qkv_weight,
    query_gain,
    k_gain,
    w_out,
    ffn_gain,
    router,
    w_gate,
    w_up,
    w_down,
    d_out,
):
    owners = lax.axis_size("expert")
    planes = lax.axis_size("shard")
    me = lax.axis_index("expert")
    plane = lax.axis_index("shard")
    length = tokens.shape[0]
    blocks = owners * planes
    experts_all = router.shape[1]
    capacity = 3 * length * TOPK // (2 * experts_all)
    heads = QUERY_HEADS // owners
    query_cols = heads * HEAD_SIZE
    scaling = HEAD_SIZE ** (-0.5)
    both = ("expert", "shard")
    rows_in = qkv_weight.shape[0]

    resident_pass = blocks * length * (MODEL_WIDTH + 2 * experts_all) * 2 <= RESIDENT

    kv_head = me * KEY_VALUE_HEADS // owners
    k_at = QUERY_HEADS * HEAD_SIZE + kv_head * HEAD_SIZE
    v_at = k_at + KEY_VALUE_HEADS * HEAD_SIZE
    gains = columns(
        [
            router,
            attn_gain[:, None],
            ffn_gain[:, None],
            jnp.pad(query_gain, (0, rows_in - query_gain.shape[0]))[:, None],
            jnp.pad(k_gain, (0, rows_in - k_gain.shape[0]))[:, None],
        ],
        rows_in,
    )
    mine = jnp.concatenate(
        [
            lax.dynamic_slice_in_dim(qkv_weight, me * query_cols, query_cols, 1),
            lax.dynamic_slice_in_dim(qkv_weight, k_at, HEAD_SIZE, 1),
            lax.dynamic_slice_in_dim(qkv_weight, v_at, HEAD_SIZE, 1),
            gains,
        ],
        axis=1,
    )
    segment_row = segments[0]
    token_tail = columns(
        [segment_row[:, None], positions_of(segment_row)[:, None]], length
    )
    token_rows = jnp.concatenate([tokens, token_tail], axis=1)
    d_rows = jnp.concatenate([d_out, columns([routes], length)], axis=1)
    if resident_pass:
        gathered, plane_rows, w_mine, d_all = start_gather(
            mine, token_rows, w_out, d_rows, planes, owners, 5
        )
        gathered = gathered.reshape(MODEL_WIDTH, -1)
        d_all = d_all.reshape(blocks, length, -1)
    else:
        gathered = lax.all_gather(mine, "shard", axis=0, tiled=True)
        plane_rows = lax.all_gather(token_rows, "expert", axis=0, tiled=False)
        d_all = lax.all_gather(d_rows, both, axis=0, tiled=False)
        out_rows = w_out.shape[0]
        first = me * query_cols
        offset = first - plane * out_rows
        if out_rows >= query_cols:
            held = (offset >= 0) & (offset < out_rows)
            piece = lax.dynamic_slice_in_dim(w_out, jnp.where(held, offset, 0), query_cols, 0)
            w_mine = lax.psum(jnp.where(held, piece, 0).astype(LOW), "shard")
        else:
            parts = query_cols // out_rows
            at = plane - me * parts
            held = (at >= 0) & (at < parts)
            spread = jnp.where(held & (jnp.arange(parts) == at)[:, None, None], w_out[None], 0)
            w_mine = lax.psum(spread.astype(LOW), "shard").reshape(query_cols, MODEL_WIDTH)
    qkv_cols = query_cols + 2 * HEAD_SIZE
    wqkv = gathered[:, :qkv_cols]
    router_full = gathered[:, qkv_cols : qkv_cols + experts_all]
    gain_cols = gathered[:, qkv_cols + experts_all :].astype(FULL)
    gain_one, gain_two = gain_cols[:, 0], gain_cols[:, 1]
    per = query_gain.shape[0]
    by_plane = gain_cols.reshape(planes, rows_in, -1)[:, :per]
    gain_query = by_plane[:, :, 2].reshape(-1)
    gain_key = by_plane[:, :, 3].reshape(-1)
    plane_tokens = plane_rows[:, :, :MODEL_WIDTH].astype(FULL)
    plane_segments = plane_rows[:, :, MODEL_WIDTH]
    plane_places = plane_rows[:, :, MODEL_WIDTH + 1].astype(FULL)

    unit_plane, inverse_plane = unit_norm(plane_tokens)
    h1 = (unit_plane * gain_one).astype(LOW)
    projected = dot("bqd,df->bqf", h1, wqkv)
    half = HEAD_SIZE // 2
    frequency = THETA ** (-2.0 * jnp.arange(half, dtype=FULL) / HEAD_SIZE)
    angles = plane_places[:, :, None] * frequency
    cosine, sine = jnp.cos(angles), jnp.sin(angles)
    cosine_q, sine_q = cosine[:, :, None, :], sine[:, :, None, :]
    query_raw = projected[:, :, :query_cols].reshape(owners, length, heads, HEAD_SIZE)
    key_raw = projected[:, :, query_cols : query_cols + HEAD_SIZE]
    value = projected[:, :, query_cols + HEAD_SIZE :].astype(LOW)
    query_unit, query_inverse = unit_norm(query_raw)
    key_unit, key_inverse = unit_norm(key_raw)
    query = rotate(query_unit * gain_query, cosine_q, sine_q).astype(LOW)
    key = rotate(key_unit * gain_key, cosine, sine).astype(LOW)
    places = jnp.arange(length, dtype=jnp.int32)
    allowed = (plane_segments[:, :, None] == plane_segments[:, None, :]) & (
        places[None, :] <= places[:, None]
    )
    scores = dot("bqhd,bkd->bhqk", query, key) * scaling
    scores = jnp.where(allowed[:, None], scores, -1e30)
    highest = jnp.max(scores, axis=-1, keepdims=True)
    exponent = jnp.exp(scores - highest)
    probs = exponent / jnp.sum(exponent, axis=-1, keepdims=True)
    probs_low = probs.astype(LOW)
    mixed = dot("bhqk,bkd->bqhd", probs_low, value).astype(LOW)
    mixed = mixed.reshape(owners, length, query_cols)
    if resident_pass:
        branch = project_home(mixed, w_mine, False, 6)
    else:
        partial = dot("bqf,fd->bqd", mixed, w_mine).astype(LOW)
        branch = lax.psum_scatter(partial, "expert", scatter_dimension=0, tiled=False)

    route_all = d_all[:, :, MODEL_WIDTH : MODEL_WIDTH + TOPK].astype(FULL)
    own_experts = (me * EXP_DEV + jnp.arange(EXP_DEV, dtype=jnp.int32)).astype(FULL)
    match = jnp.sum((route_all[:, :, :, None] == own_experts).astype(FULL), axis=2)
    earlier = (places[None, :] < places[:, None]).astype(LOW)
    rank = dot("ts,bsj->btj", earlier, match.astype(LOW))
    slot_ids = jnp.arange(capacity, dtype=jnp.int32).astype(FULL)
    place = jnp.where(match > 0, rank, -1.0).transpose(0, 2, 1)
    if resident_pass:
        place = place.reshape(owners // 2, 2, planes, EXP_DEV, length)
        offset = (capacity * jnp.arange(2, dtype=jnp.int32)).astype(FULL)
        place = jnp.where(place >= 0, place + offset[:, None, None, None], -1.0)
        place = place.transpose(0, 2, 3, 1, 4).reshape(blocks // 2, EXP_DEV, 2 * length)
        lanes = jnp.arange(2 * experts_all, dtype=jnp.int32) % experts_all
        own = (me * EXP_DEV + jnp.arange(EXP_DEV, dtype=jnp.int32))[:, None] == lanes
        sel = jnp.broadcast_to(own.astype(FULL)[:, None, :], (EXP_DEV, 8, 2 * experts_all))
        slots = 2 * capacity

    middle = tokens.astype(FULL) + branch.astype(FULL)
    unit_two, inverse_two = unit_norm(middle)
    h2 = (unit_two * gain_two).astype(LOW)
    logits = dot("nd,de->ne", h2, router_full)
    chance = jax.nn.softmax(logits, axis=-1)
    named = jnp.sum(
        (routes[:, :, None] == jnp.arange(experts_all, dtype=jnp.int32)).astype(FULL), axis=1
    )
    chosen_sum = jnp.sum(named * chance, axis=1, keepdims=True)
    gates = named * chance / chosen_sum
    gates_high = gates.astype(LOW)
    gates_rest = (gates - gates_high.astype(FULL)).astype(LOW)
    h_rows = jnp.concatenate([h2, gates_high, gates_rest], axis=1)

    if resident_pass:
        x, dy = gather_dispatch(
            h_rows, d_all.reshape(owners, planes, length, -1), place, planes, slots, 1
        )
        y, dx, d_gate, d_up, d_down = expert_pass(
            sel, x, dy, w_gate, w_up, w_down.swapaxes(1, 2)
        )
        d_down = d_down.swapaxes(1, 2)
        d_home, mixture = combine_home(place, dx, y, length, planes, slots, 2)
        mixture = mixture.reshape(owners, planes, length, MODEL_WIDTH)
        mixture = lax.psum_scatter(mixture, "expert", scatter_dimension=0, tiled=False)
    else:
        dispatch = (place[:, :, None, :] == slot_ids[:, None]).astype(LOW)

        def experts(h_rows, d_rows, gate_high, gate_rest, put):
            count = h_rows.shape[0]
            flat = put.reshape(count, EXP_DEV * capacity, length)
            x = dot("bst,btd->bsd", flat, h_rows).astype(LOW)
            dy = dot("bst,btd->bsd", flat, d_rows).astype(LOW)

            def by_expert(v):
                v = v.reshape(count, EXP_DEV, capacity, v.shape[-1])
                return v.transpose(1, 0, 2, 3).reshape(EXP_DEV, count * capacity, v.shape[-1])

            def by_block(v):
                v = v.reshape(EXP_DEV, count, capacity, v.shape[-1])
                return v.transpose(1, 0, 2, 3).reshape(count, EXP_DEV * capacity, v.shape[-1])

            x, dy = by_expert(x), by_expert(dy)
            gate_slot = dot("bjct,btj->jbc", put, gate_high) + dot("bjct,btj->jbc", put, gate_rest)
            gate_slot = gate_slot.reshape(EXP_DEV, count * capacity, 1)
            g = dot("erd,efd->erf", x, w_gate)
            u = dot("erd,efd->erf", x, w_up)
            da = dot("erd,edf->erf", dy, w_down)
            sigma = jax.nn.sigmoid(g)
            silu = g * sigma
            act = (silu * u).astype(LOW).astype(FULL)
            d_gate_slot = jnp.sum(act * da, axis=-1)
            act_gated = (act * gate_slot).astype(LOW)
            d_act = da * gate_slot
            dg = (d_act * u * sigma * (1.0 + g * (1.0 - sigma))).astype(LOW)
            du = (d_act * silu).astype(LOW)
            y = dot("erf,edf->erd", act_gated, w_down).astype(LOW)
            d_down = dot("erd,erf->edf", dy, act_gated)
            d_gate = dot("erf,erd->efd", dg, x)
            d_up = dot("erf,erd->efd", du, x)
            dx = (dot("erf,efd->erd", dg, w_gate) + dot("erf,efd->erd", du, w_up)).astype(LOW)
            mix = dot("bst,bsd->btd", flat, by_block(y)).astype(LOW)
            d_h = dot("bst,bsd->btd", flat, by_block(dx)).astype(LOW)
            d_g = dot(
                "bjct,jbc->btj", put.astype(FULL), d_gate_slot.reshape(EXP_DEV, count, capacity)
            )
            return mix, d_h, d_g, d_gate, d_up, d_down

        h_all = lax.all_gather(h_rows, both, axis=0, tiled=False)
        gate_cols = lax.dynamic_slice_in_dim(h_all, MODEL_WIDTH + me * EXP_DEV, EXP_DEV, 2)
        rest_cols = lax.dynamic_slice_in_dim(
            h_all, MODEL_WIDTH + experts_all + me * EXP_DEV, EXP_DEV, 2
        )
        step = min(blocks, GROUP_BLOCKS)
        mixes, d_hs, d_gs, totals = [], [], [], None
        for at in range(0, blocks, step):
            cut = slice(at, at + step)
            mix, d_h, d_g, *grads = experts(
                h_all[cut, :, :MODEL_WIDTH],
                d_all[cut, :, :MODEL_WIDTH],
                gate_cols[cut],
                rest_cols[cut],
                dispatch[cut],
            )
            mixes.append(mix)
            d_hs.append(d_h)
            d_gs.append(d_g)
            totals = grads if totals is None else [a + b for a, b in zip(totals, grads)]
        d_gate, d_up, d_down = totals
        d_g = jnp.concatenate(d_gs, axis=0)
        spread = jnp.zeros((blocks, length, 2 * experts_all), LOW)
        spread = lax.dynamic_update_slice_in_dim(spread, d_g.astype(LOW), me * EXP_DEV, 2)
        d_h_wide = jnp.concatenate([jnp.concatenate(d_hs, axis=0), spread], axis=2)

        def home(v):
            v = v.reshape(owners, planes, length, v.shape[-1])
            v = lax.psum_scatter(v, "expert", scatter_dimension=0, tiled=False)
            return lax.psum_scatter(v, "shard", scatter_dimension=0, tiled=False)

        d_home = home(d_h_wide)
        mixture = home(jnp.concatenate(mixes, axis=0))
    upstream = d_out.astype(FULL)
    d_gates = d_home[:, MODEL_WIDTH:].astype(FULL)
    d_gates = d_gates[:, :experts_all] + d_gates[:, experts_all:]
    d_chance = named * (d_gates - jnp.sum(d_gates * gates, axis=1, keepdims=True)) / chosen_sum
    d_logits = chance * (d_chance - jnp.sum(d_chance * chance, axis=1, keepdims=True))
    d_logits = d_logits.astype(LOW)
    d_h2 = d_home[:, :MODEL_WIDTH].astype(FULL) + dot("ne,de->nd", d_logits, router_full)
    d_gain_two = jnp.sum(d_h2 * unit_two, axis=0)
    d_middle = upstream + norm_back(d_h2, unit_two, inverse_two, gain_two)
    d_router = dot("nd,ne->de", h2, d_logits)

    if resident_pass:
        d_branch = plane_gather(d_middle.astype(LOW), owners, 7)
    else:
        d_branch = lax.all_gather(d_middle.astype(LOW), "expert", axis=0, tiled=False)
    d_w_out = dot("bqf,bqd->fd", mixed, d_branch).astype(LOW)
    d_mixed = dot("bqd,fd->bqf", d_branch, w_mine).astype(LOW)
    d_mixed = d_mixed.reshape(owners, length, heads, HEAD_SIZE)
    d_probs = dot("bqhd,bkd->bhqk", d_mixed, value)
    d_scores = probs * (d_probs - jnp.sum(d_probs * probs, axis=-1, keepdims=True))
    d_scores = d_scores.astype(LOW)
    d_query = dot("bhqk,bkd->bqhd", d_scores, key) * scaling
    d_key = dot("bhqk,bqhd->bkd", d_scores, query) * scaling
    d_value = dot("bhqk,bqhd->bkd", probs_low, d_mixed)
    d_query = rotate_back(d_query, cosine_q, sine_q)
    d_key = rotate_back(d_key, cosine, sine)
    d_gain_query = jnp.sum(d_query * query_unit, axis=(0, 1, 2))
    d_gain_key = jnp.sum(d_key * key_unit, axis=(0, 1))
    d_query = norm_back(d_query, query_unit, query_inverse, gain_query)
    d_key = norm_back(d_key, key_unit, key_inverse, gain_key)
    d_projected = jnp.concatenate(
        [d_query.reshape(owners, length, query_cols), d_key, d_value], axis=2
    ).astype(LOW)
    if resident_pass:
        d_h1 = project_home(d_projected, wqkv, True, 8)
        mixture, d_h1 = lax.optimization_barrier((mixture, d_h1))
        mixture = lax.psum_scatter(mixture, "shard", scatter_dimension=0, tiled=False)
    else:
        d_h1 = dot("bqf,df->bqd", d_projected, wqkv).astype(LOW)
        d_h1 = lax.psum_scatter(d_h1, "expert", scatter_dimension=0, tiled=False).astype(FULL)
    resident = tokens.astype(FULL)
    unit_one, inverse_one = unit_norm(resident)
    d_gain_one = jnp.sum(d_h1 * unit_one, axis=0)
    d_tokens = (d_middle + norm_back(d_h1, unit_one, inverse_one, gain_one)).astype(LOW)

    result = (middle + mixture.astype(FULL)).astype(LOW)

    d_wqkv = dot("bqd,bqf->df", h1, d_projected).astype(LOW)

    def by_rows(v):
        v = v.reshape(planes, per)
        return jnp.pad(v, ((0, 0), (0, rows_in - per))).reshape(-1)[:, None]

    d_tail = columns(
        [
            d_router,
            d_gain_one[:, None],
            d_gain_two[:, None],
            by_rows(d_gain_query),
            by_rows(d_gain_key),
        ],
        MODEL_WIDTH,
    )
    d_pack = jnp.concatenate([d_wqkv, d_tail], axis=1)
    if resident_pass:
        shape = (planes, 2, rows_in // 2)
        parts = share_grads(
            d_pack[:, :query_cols].reshape(shape + (query_cols,)),
            d_pack[:, query_cols:].reshape(shape + (-1,)),
            d_w_out,
            planes,
            owners,
            4,
        )
        d_w_out, d_qkv_weight, d_rest = finish_grads(*parts, owners)
    else:
        d_pack = lax.psum_scatter(d_pack, "shard", scatter_dimension=0, tiled=True)
        d_pack = lax.all_gather(d_pack, "expert", axis=0, tiled=False).astype(FULL)
        d_q_cols = d_pack[:, :, :query_cols].transpose(1, 0, 2).reshape(rows_in, -1)
        d_kv = d_pack[:, :, query_cols:qkv_cols]
        d_kv = jnp.sum(d_kv.reshape(KEY_VALUE_HEADS, -1, rows_in, 2, HEAD_SIZE), axis=1)
        d_kv = d_kv.transpose(1, 2, 0, 3).reshape(rows_in, -1)
        d_qkv_weight = jnp.concatenate([d_q_cols, d_kv], axis=1)
        d_rest = jnp.sum(d_pack[:, :, qkv_cols:], axis=0)

        d_w_out = d_w_out.reshape(query_cols, owners, -1)
        d_w_out = lax.all_to_all(d_w_out, "expert", split_axis=1, concat_axis=0, tiled=False)
        d_w_out = d_w_out.reshape(QUERY_HEADS * HEAD_SIZE, -1)
        d_w_out = lax.psum_scatter(d_w_out, "shard", scatter_dimension=0, tiled=True)
        d_w_out = lax.all_gather(d_w_out, "expert", axis=1, tiled=True).astype(FULL)
    d_router_out = d_rest[:, :experts_all]
    d_gain_out = d_rest[:, experts_all:]

    return (
        result,
        d_tokens,
        d_gain_out[:, 0],
        d_qkv_weight,
        d_gain_out[:per, 2],
        d_gain_out[:per, 3],
        d_w_out,
        d_gain_out[:, 1],
        d_router_out,
        d_gate,
        d_up,
        d_down,
    )


def solution(mesh):
    placed = (
        P(("expert", "shard"), None),
        P(("expert", "shard"), None),
        P(("expert", "shard"), None),
        P("shard"),
        P("shard", None),
        P("shard"),
        P("shard"),
        P("shard", None),
        P("shard"),
        P("shard", None),
        P("expert", "shard", None),
        P("expert", "shard", None),
        P("expert", None, "shard"),
        P(("expert", "shard"), None),
    )
    return jax.shard_map(
        per_device,
        mesh=mesh,
        in_specs=placed,
        out_specs=(
            P(("expert", "shard"), None),
            P(("expert", "shard"), None),
            P("shard"),
            P("shard", None),
            P("shard"),
            P("shard"),
            P("shard", None),
            P("shard"),
            P("shard", None),
            P("expert", "shard", None),
            P("expert", "shard", None),
            P("expert", None, "shard"),
        ),
        check_vma=False,
    )
```

```python
import functools

import jax
import jax.numpy as jnp
from jax import lax
from jax.experimental import pallas as pl
from jax.experimental.pallas import tpu as pltpu
from jax.sharding import PartitionSpec as P

MODEL_WIDTH = 2048
QUERY_HEADS = 32
KEY_VALUE_HEADS = 4
HEAD_SIZE = 128
TOPK = 8
EXP_DEV = 8
TAIL = 128
GAIN_ONE = 67
GROUP_BLOCKS = 32
RESIDENT = 20 << 20

EPS = 1e-06
THETA = 1000000.0
LOW = jnp.bfloat16
FULL = jnp.float32


def unit_norm(values):
    inverse = lax.rsqrt(jnp.mean(values * values, axis=-1, keepdims=True) + EPS)
    return values * inverse, inverse


def norm_back(incoming, unit_rows, inverse, gain):
    inner = incoming * gain
    return inverse * (inner - unit_rows * jnp.mean(inner * unit_rows, axis=-1, keepdims=True))


def rotate(values, cosine, sine):
    half = values.shape[-1] // 2
    a, b = values[..., :half], values[..., half:]
    return jnp.concatenate([a * cosine - b * sine, b * cosine + a * sine], axis=-1)


def rotate_back(values, cosine, sine):
    half = values.shape[-1] // 2
    a, b = values[..., :half], values[..., half:]
    return jnp.concatenate([a * cosine + b * sine, b * cosine - a * sine], axis=-1)


def dot(spec, left, right):
    return jnp.einsum(spec, left, right, preferred_element_type=FULL)


def positions_of(segment_row):
    places = jnp.arange(segment_row.shape[0], dtype=jnp.int32)
    before = (segment_row[None, :] == segment_row[:, None]) & (places[None, :] < places[:, None])
    return jnp.sum(before.astype(jnp.int32), axis=1)


def columns(parts, rows):
    wide = jnp.concatenate([part.astype(LOW) for part in parts], axis=1)
    return jnp.pad(wide, ((0, rows - wide.shape[0]), (0, TAIL - wide.shape[1])))


MESH = pl.DeviceIdType.MESH
ANY = pl.BlockSpec(memory_space=pl.ANY)
VM = pl.BlockSpec(memory_space=pltpu.VMEM)
DMA = pltpu.SemaphoreType.DMA
VMEM_LIMIT = 58 << 20
TILE = 512


def neighbours():
    e = lax.axis_index("expert")
    core = e + 1 - 2 * (e % 2)
    flip_x = e + 2 - 4 * ((e // 2) % 2)
    flip_y = e + 4 - 8 * ((e // 4) % 2)
    diagonal = flip_x + flip_y - e
    return e, core, flip_x, flip_y, diagonal


def greet(planes):
    e, core, flip_x, flip_y, _ = neighbours()
    s = lax.axis_index("shard")
    barrier = pltpu.get_barrier_semaphore()
    for other in (core, flip_x, flip_y):
        pl.semaphore_signal(barrier, 1, device_id=(other, s), device_id_type=MESH)

    @pl.when(s > 0)
    def _():
        pl.semaphore_signal(barrier, 1, device_id=(e, s - 1), device_id_type=MESH)

    @pl.when(s < planes - 1)
    def _():
        pl.semaphore_signal(barrier, 1, device_id=(e, s + 1), device_id_type=MESH)

    inner = (s > 0) & (s < planes - 1)

    @pl.when(inner)
    def _():
        pl.semaphore_wait(barrier, 5)

    @pl.when(jnp.logical_not(inner))
    def _():
        pl.semaphore_wait(barrier, 4)


def send(source, target, send_sem, recv_sem, device):
    return pltpu.make_async_remote_copy(
        src_ref=source,
        dst_ref=target,
        send_sem=send_sem,
        recv_sem=recv_sem,
        device_id=device,
        device_id_type=MESH,
    )


def one_hot_pair(place_ref, pair, hot_ref, slots):
    rows = place_ref[pair]
    at = lax.broadcasted_iota(jnp.int32, (slots, rows.shape[1]), 0).astype(FULL)
    for j in range(EXP_DEV):
        hot_ref[pl.ds(j * slots, slots), :] = (at == rows[j : j + 1, :]).astype(LOW)


def gather_dispatch_kernel(
    planes, slots, x_ref, d_ref, place_ref, outx_ref, outd_ref,
    buf, hot, stage_x, stage_d, load_d,
    z_send, z_recv, x_send, x_recv, y_send, y_recv, c_send, c_recv, out_x, out_d, in_d,
):
    e, core, flip_x, flip_y, diagonal = neighbours()
    s = lax.axis_index("shard")
    length = x_ref.shape[0]
    half = length // 2
    width = x_ref.shape[1]
    low_half, high_half = pl.ds(0, half), pl.ds(half, half)
    greet(planes)
    buf[e, s] = x_ref[...]

    def up(sp):
        return send(buf.at[e, sp], buf.at[e, sp], z_send.at[0, sp], z_recv.at[sp], (e, s + 1))

    def down(sp):
        return send(buf.at[e, sp], buf.at[e, sp], z_send.at[1, sp], z_recv.at[sp], (e, s - 1))

    def first(sp):
        block = buf.at[e, sp]
        return [
            send(block, block, x_send.at[0, sp], x_recv.at[0, sp], (flip_x, s)),
            send(block, block, y_send.at[0, sp], y_recv.at[0, sp], (flip_y, s)),
            send(block, block, c_send.at[0, sp], c_recv.at[0, sp], (core, s)),
        ]

    def from_x(sp):
        block = buf.at[flip_x, sp]
        part = buf.at[flip_x, sp, low_half]
        return [
            send(part, part, y_send.at[1, sp], y_recv.at[1, sp], (flip_y, s)),
            send(block, block, c_send.at[1, sp], c_recv.at[1, sp], (core, s)),
        ]

    def from_y(sp):
        block = buf.at[flip_y, sp]
        part = buf.at[flip_y, sp, high_half]
        return [
            send(part, part, x_send.at[1, sp], x_recv.at[1, sp], (flip_x, s)),
            send(block, block, c_send.at[2, sp], c_recv.at[2, sp], (core, s)),
        ]

    def from_diagonal(sp):
        block = buf.at[diagonal, sp]
        return send(block, block, c_send.at[3, sp], c_recv.at[3, sp], (core, s))

    def arrived(block, sem):
        send(block, block, sem, sem, (core, s)).wait_recv()

    def plane_at(i):
        distance = (i + 1) // 2
        sign = 2 * (i % 2) - 1
        sp = s + sign * distance
        return sp, (sp >= 0) & (sp < planes) & (i >= 0) & (i <= 2 * planes - 2)

    def step_first(sp, i):
        @pl.when(i > 0)
        def _():
            arrived(buf.at[e, sp], z_recv.at[sp])

        @pl.when((sp <= s) & (s < planes - 1))
        def _():
            up(sp).start()

        @pl.when((sp >= s) & (s > 0))
        def _():
            down(sp).start()

        for copy in first(sp):
            copy.start()

    def step_second(sp):
        arrived(buf.at[flip_x, sp], x_recv.at[0, sp])
        for copy in from_x(sp):
            copy.start()
        arrived(buf.at[flip_y, sp], y_recv.at[0, sp])
        for copy in from_y(sp):
            copy.start()

    def step_third(sp):
        arrived(buf.at[diagonal, sp, low_half], y_recv.at[1, sp])
        arrived(buf.at[diagonal, sp, high_half], x_recv.at[1, sp])
        from_diagonal(sp).start()

    def copy_out(stage, out, sem, q, sp):
        rows = pl.ds(pl.multiple_of((q * planes + sp) * slots, 16), slots)
        return pltpu.make_async_copy(stage.at[q], out.at[:, rows, :], sem.at[q])

    def load(q, sp, k):
        return pltpu.make_async_copy(
            d_ref.at[2 * q + k, sp, :, pl.ds(0, MODEL_WIDTH)],
            load_d.at[q, pl.ds(k * length, length), :],
            in_d.at[q, k],
        )

    def start_loads(sp):
        for q in range(4):
            for k in range(2):
                load(q, sp, k).start()

    def dispatch(sp, i):
        for k, other in enumerate((core, core + flip_x - e, core + flip_y - e, core + diagonal - e)):
            arrived(buf.at[other, sp], c_recv.at[k, sp])

        def one(q, carry):
            one_hot_pair(place_ref, q * planes + sp, hot, slots)
            d_wide = load_d.shape[2]

            @pl.when(i > 0)
            def _():
                copy_out(stage_x, outx_ref, out_x, q, sp).wait()
                copy_out(stage_d, outd_ref, out_d, q, sp).wait()

            for k in range(2):
                load(q, sp, k).wait()

            def columns_of(at, wide, with_d):
                rows = jnp.concatenate(
                    [buf[2 * q, sp, :, at], buf[2 * q + 1, sp, :, at]], axis=0
                )
                got = jnp.dot(hot[...], rows, preferred_element_type=FULL).astype(LOW)
                stage_x[q, :, :, at] = got.reshape(EXP_DEV, slots, wide)
                if with_d:
                    got = jnp.dot(
                        hot[...], load_d[q, :, at], preferred_element_type=FULL
                    ).astype(LOW)
                    stage_d[q, :, :, at] = got.reshape(EXP_DEV, slots, wide)

            def tile(t, inner):
                columns_of(pl.ds(pl.multiple_of(t * TILE, TILE), TILE), TILE, True)
                return inner

            lax.fori_loop(0, MODEL_WIDTH // TILE, tile, 0)
            if width > MODEL_WIDTH:
                columns_of(pl.ds(MODEL_WIDTH, width - MODEL_WIDTH), width - MODEL_WIDTH, False)
            copy_out(stage_x, outx_ref, out_x, q, sp).start()
            copy_out(stage_d, outd_ref, out_d, q, sp).start()
            return carry

        lax.fori_loop(0, 4, one, 0)

    def step(i, carry):
        for lag, work in ((0, step_first), (1, step_second), (2, step_third), (3, dispatch)):
            sp, there = plane_at(i - lag)

            @pl.when(there)
            def _(sp=sp, lag=lag, work=work):
                if lag in (0, 3):
                    work(sp, i - lag)
                else:
                    work(sp)

        sp, there = plane_at(i - 2)

        @pl.when(there)
        def _():
            start_loads(sp)

        return carry

    lax.fori_loop(0, 2 * planes + 2, step, 0)

    def drain(sp, carry):
        for copy in first(sp) + from_x(sp) + from_y(sp) + [from_diagonal(sp)]:
            copy.wait_send()

        @pl.when((sp <= s) & (s < planes - 1))
        def _():
            up(sp).wait_send()

        @pl.when((sp >= s) & (s > 0))
        def _():
            down(sp).wait_send()

        return carry

    lax.fori_loop(0, planes, drain, 0)
    for q in range(4):
        copy_out(stage_x, outx_ref, out_x, q, 0).wait()
        copy_out(stage_d, outd_ref, out_d, q, 0).wait()


def gather_dispatch(rows, d_all, place, planes, slots, identity):
    owners = lax.axis_size("expert")
    length, width = rows.shape
    total = place.shape[0] * slots
    kernel = functools.partial(gather_dispatch_kernel, planes, slots)
    return pl.pallas_call(
        kernel,
        out_shape=[
            jax.ShapeDtypeStruct((EXP_DEV, total, width), LOW),
            jax.ShapeDtypeStruct((EXP_DEV, total, MODEL_WIDTH), LOW),
        ],
        in_specs=[VM, ANY, VM],
        out_specs=[ANY, ANY],
        scratch_shapes=[
            pltpu.VMEM((owners, planes, length, width), LOW),
            pltpu.VMEM((EXP_DEV * slots, 2 * length), LOW),
            pltpu.VMEM((4, EXP_DEV, slots, width), LOW),
            pltpu.VMEM((4, EXP_DEV, slots, MODEL_WIDTH), LOW),
            pltpu.VMEM((4, 2 * length, MODEL_WIDTH), LOW),
            DMA((2, planes)),
            DMA((planes,)),
            DMA((2, planes)),
            DMA((2, planes)),
            DMA((2, planes)),
            DMA((2, planes)),
            DMA((4, planes)),
            DMA((4, planes)),
            DMA((4,)),
            DMA((4,)),
            DMA((4, 2)),
        ],
        compiler_params=pltpu.CompilerParams(
            collective_id=identity, has_side_effects=True, vmem_limit_bytes=VMEM_LIMIT
        ),
    )(rows, d_all, place)


def expert_kernel(
    sel_ref, x_ref, dy_ref, wg_ref, wu_ref, wd_ref,
    y_ref, dx_ref, dwg_ref, dwu_ref, dwd_ref, a_all, dg_all, du_all,
):
    rows = x_ref.shape[1]
    step = 256
    experts = sel_ref.shape[2] // 2
    sel = sel_ref[0, 0:1, :]
    lane = lax.broadcasted_iota(jnp.int32, sel.shape, 1)
    high_sel = jnp.where(lane < experts, sel, 0.0)
    rest_sel = sel - high_sel
    nt = (((1,), (1,)), ((), ()))
    tn = (((0,), (0,)), ((), ()))

    def chunk(r, carry):
        at = pl.ds(pl.multiple_of(r * step, step), step)
        x = x_ref[0, at, :MODEL_WIDTH]
        tail = x_ref[0, at, MODEL_WIDTH:].astype(FULL)
        dy = dy_ref[0, at, :]
        gate = jnp.sum(tail * sel, axis=1, keepdims=True)
        g = lax.dot_general(x, wg_ref[0], nt, preferred_element_type=FULL)
        u = lax.dot_general(x, wu_ref[0], nt, preferred_element_type=FULL)
        da = lax.dot_general(dy, wd_ref[0], nt, preferred_element_type=FULL)
        sigma = 1.0 / (1.0 + jnp.exp(-g))
        silu = g * sigma
        act = (silu * u).astype(LOW).astype(FULL)
        d_gate = jnp.sum(act * da, axis=1, keepdims=True)
        d_act = da * gate
        a_all[at, :] = (act * gate).astype(LOW)
        dg_all[at, :] = (d_act * u * sigma * (1.0 + g * (1.0 - sigma))).astype(LOW)
        du_all[at, :] = (d_act * silu).astype(LOW)
        high = d_gate.astype(LOW).astype(FULL)
        dx_ref[0, at, MODEL_WIDTH:] = (high * high_sel + (d_gate - high) * rest_sel).astype(LOW)
        y_ref[0, at, :] = jnp.dot(
            a_all[at, :], wd_ref[0], preferred_element_type=FULL
        ).astype(LOW)
        dx_ref[0, at, :MODEL_WIDTH] = (
            jnp.dot(dg_all[at, :], wg_ref[0], preferred_element_type=FULL)
            + jnp.dot(du_all[at, :], wu_ref[0], preferred_element_type=FULL)
        ).astype(LOW)
        return carry

    lax.fori_loop(0, rows // step, chunk, 0)

    def tile(t, carry):
        at = pl.ds(pl.multiple_of(t * TILE, TILE), TILE)
        dwg_ref[0, :, at] = lax.dot_general(
            dg_all[...], x_ref[0, :, at], tn, preferred_element_type=FULL
        )
        dwu_ref[0, :, at] = lax.dot_general(
            du_all[...], x_ref[0, :, at], tn, preferred_element_type=FULL
        )
        dwd_ref[0, :, at] = lax.dot_general(
            a_all[...], dy_ref[0, :, at], tn, preferred_element_type=FULL
        )
        return carry

    lax.fori_loop(0, MODEL_WIDTH // TILE, tile, 0)


def expert_pass(sel, x, dy, w_gate, w_up, w_down):
    rows, width = x.shape[1:]
    hidden = w_gate.shape[1]

    def spec(*shape):
        return pl.BlockSpec((1,) + shape, lambda j: (j, 0, 0))

    def out(*shape, dtype=LOW):
        return jax.ShapeDtypeStruct((EXP_DEV,) + shape, dtype)

    return pl.pallas_call(
        expert_kernel,
        grid=(EXP_DEV,),
        in_specs=[
            spec(*sel.shape[1:]),
            spec(rows, width),
            spec(rows, MODEL_WIDTH),
            spec(hidden, MODEL_WIDTH),
            spec(hidden, MODEL_WIDTH),
            spec(hidden, MODEL_WIDTH),
        ],
        out_specs=[
            spec(rows, MODEL_WIDTH),
            spec(rows, width),
            spec(hidden, MODEL_WIDTH),
            spec(hidden, MODEL_WIDTH),
            spec(hidden, MODEL_WIDTH),
        ],
        out_shape=[
            out(rows, MODEL_WIDTH),
            out(rows, width),
            out(hidden, MODEL_WIDTH, dtype=FULL),
            out(hidden, MODEL_WIDTH, dtype=FULL),
            out(hidden, MODEL_WIDTH, dtype=FULL),
        ],
        scratch_shapes=[pltpu.VMEM((rows, hidden), LOW)] * 3,
        compiler_params=pltpu.CompilerParams(vmem_limit_bytes=VMEM_LIMIT),
        cost_estimate=pl.CostEstimate(
            flops=EXP_DEV * rows * MODEL_WIDTH * hidden * 18,
            bytes_accessed=160 << 20,
            transcendentals=EXP_DEV * rows * hidden,
        ),
    )(sel, x, dy, w_gate, w_up, w_down)


def combine_home_kernel(
    planes, slots, place_ref, v_ref, m_ref, out_ref, mix_ref,
    hot, hot_t, load, mine, away, c_in, x_in, y_in, x_half, y_half, u_in, d_in,
    in_sem, free, c_send, c_recv, x_send, x_recv, y_send, y_recv, z_send, z_recv,
):
    e, core, flip_x, flip_y, diagonal = neighbours()
    s = lax.axis_index("shard")
    q_own, q_x, q_y, q_d = e // 2, flip_x // 2, flip_y // 2, diagonal // 2
    parity = e % 2
    length, width = out_ref.shape
    half = length // 2
    low_half, high_half = pl.ds(0, half), pl.ds(half, half)
    order = (q_d, q_x, q_y, q_own)

    def fetch(kind, k, sp):
        rows = pl.ds(pl.multiple_of((order[k] * planes + sp) * slots, 16), slots)
        if kind == 0:
            return pltpu.make_async_copy(v_ref.at[:, rows, :], load.at[k % 2], in_sem.at[k % 2])
        return pltpu.make_async_copy(
            m_ref.at[:, rows, :], load.at[k % 2, :, :, pl.ds(0, MODEL_WIDTH)], in_sem.at[k % 2]
        )

    def to_core(kind, q, sp):
        return send(
            away.at[q, sp], c_in.at[q, sp], c_send.at[kind, q, sp], c_recv.at[kind, q, sp],
            (core, s),
        )

    def halves(kind, sp):
        return [
            send(
                mine.at[q_d, sp, low_half], y_half.at[kind, sp],
                y_send.at[kind, 0, sp], y_recv.at[kind, 0, sp], (flip_y, s),
            ),
            send(
                mine.at[q_d, sp, high_half], x_half.at[kind, sp],
                x_send.at[kind, 0, sp], x_recv.at[kind, 0, sp], (flip_x, s),
            ),
        ]

    def to_x(kind, sp):
        return send(
            mine.at[q_x, sp], x_in.at[kind, sp], x_send.at[kind, 1, sp], x_recv.at[kind, 1, sp],
            (flip_x, s),
        )

    def to_y(kind, sp):
        return send(
            mine.at[q_y, sp], y_in.at[kind, sp], y_send.at[kind, 1, sp], y_recv.at[kind, 1, sp],
            (flip_y, s),
        )

    def up(kind, sp):
        return send(
            mine.at[q_own, sp], u_in.at[kind, sp], z_send.at[kind, 0, sp], z_recv.at[kind, 0, sp],
            (e, s + 1),
        )

    def down(kind, sp):
        return send(
            mine.at[q_own, sp], d_in.at[kind, sp], z_send.at[kind, 1, sp], z_recv.at[kind, 1, sp],
            (e, s - 1),
        )

    def settled(kind, sp):
        for q in range(4):
            to_core(kind, q, sp).wait_send()
        for copy in halves(kind, sp) + [to_x(kind, sp), to_y(kind, sp)]:
            copy.wait_send()

        @pl.when(sp > s)
        def _():
            up(kind, sp).wait_send()

        @pl.when(sp < s)
        def _():
            down(kind, sp).wait_send()

    def arrived(block, sem):
        send(block, block, sem, sem, (core, s)).wait_recv()

    def plane_at(i):
        back = 2 * planes - 2 - i
        sp = s + (2 * (back % 2) - 1) * ((back + 1) // 2)
        return sp, (sp >= 0) & (sp < planes) & (i >= 0) & (back >= 0)

    def add(target, *others):
        total = target[...].astype(FULL)
        for other in others:
            total = total + other[...].astype(FULL)
        target[...] = total.astype(LOW)

    def work(kind, sp):
        if kind == 1:
            settled(0, sp)
            pl.semaphore_wait(free.at[sp], 1)
        for k in range(2):
            fetch(kind, k, sp).start()
        for k, q in enumerate(order):
            one_hot_pair(place_ref, q * planes + sp, hot, slots)
            hot_t[...] = hot[...].T
            fetch(kind, k, sp).wait()

            def part(at, wide, q=q, k=k):
                rows = load[k % 2, :, :, at].reshape(EXP_DEV * slots, wide)
                got = jnp.dot(hot_t[...], rows, preferred_element_type=FULL).astype(LOW)
                got = got.reshape(2, length, wide)

                @pl.when(parity == 0)
                def _():
                    mine[q, sp, :, at] = got[0]
                    away[q, sp, :, at] = got[1]

                @pl.when(parity == 1)
                def _():
                    mine[q, sp, :, at] = got[1]
                    away[q, sp, :, at] = got[0]

            def tile(t, inner, part=part):
                part(pl.ds(pl.multiple_of(t * TILE, TILE), TILE), TILE)
                return inner

            lax.fori_loop(0, MODEL_WIDTH // TILE, tile, 0)
            if kind == 0 and width > MODEL_WIDTH:
                part(pl.ds(MODEL_WIDTH, width - MODEL_WIDTH), width - MODEL_WIDTH)
            to_core(kind, q, sp).start()
            if k < 2:
                fetch(kind, k + 2, sp).start()

    def pairs(kind, sp):
        for k, q in enumerate(order):
            arrived(c_in.at[q, sp], c_recv.at[kind, q, sp])
            add(mine.at[q, sp], c_in.at[q, sp])
            if k == 0:
                for copy in halves(kind, sp):
                    copy.start()
        if kind == 0:
            pl.semaphore_signal(free.at[sp], 1, device_id=(core, s), device_id_type=MESH)

    def sides(kind, sp):
        arrived(y_half.at[kind, sp], y_recv.at[kind, 0, sp])
        add(mine.at[q_x, sp, low_half], y_half.at[kind, sp])
        to_x(kind, sp).start()
        arrived(x_half.at[kind, sp], x_recv.at[kind, 0, sp])
        add(mine.at[q_y, sp, high_half], x_half.at[kind, sp])
        to_y(kind, sp).start()

    def line(kind, sp):
        arrived(x_in.at[kind, sp], x_recv.at[kind, 1, sp])
        arrived(y_in.at[kind, sp], y_recv.at[kind, 1, sp])
        add(mine.at[q_own, sp], x_in.at[kind, sp], y_in.at[kind, sp])

        @pl.when((sp >= s) & (s > 0))
        def _():
            arrived(u_in.at[kind, sp], z_recv.at[kind, 0, sp])
            add(mine.at[q_own, sp], u_in.at[kind, sp])

        @pl.when((sp <= s) & (s < planes - 1))
        def _():
            arrived(d_in.at[kind, sp], z_recv.at[kind, 1, sp])
            add(mine.at[q_own, sp], d_in.at[kind, sp])

        @pl.when(sp > s)
        def _():
            up(kind, sp).start()

        @pl.when(sp < s)
        def _():
            down(kind, sp).start()

        @pl.when(sp == s)
        def _():
            if kind == 0:
                out_ref[...] = mine[q_own, sp].astype(FULL)
            else:
                mix_ref[...] = mine[q_own, sp, :, :MODEL_WIDTH].astype(FULL)

    greet(planes)
    span = 2 * planes - 1

    def step(t, carry):
        for lag, job in ((0, work), (1, pairs), (2, sides), (3, line)):
            for kind in range(2):
                sp, there = plane_at(t - lag - kind * span)

                @pl.when(there)
                def _(sp=sp, job=job, kind=kind):
                    job(kind, sp)

        return carry

    lax.fori_loop(0, 2 * span + 3, step, 0)

    def drain(sp, carry):
        settled(1, sp)
        return carry

    lax.fori_loop(0, planes, drain, 0)


def combine_home(place, v, m, length, planes, slots, identity):
    width = v.shape[2]
    block = (planes, length, width)
    part = (planes, length // 2, width)
    return pl.pallas_call(
        functools.partial(combine_home_kernel, planes, slots),
        out_shape=[
            jax.ShapeDtypeStruct((length, width), FULL),
            jax.ShapeDtypeStruct((length, MODEL_WIDTH), FULL),
        ],
        in_specs=[VM, ANY, ANY],
        out_specs=[VM, VM],
        scratch_shapes=[
            pltpu.VMEM((EXP_DEV * slots, 2 * length), LOW),
            pltpu.VMEM((2 * length, EXP_DEV * slots), LOW),
            pltpu.VMEM((2, EXP_DEV, slots, width), LOW),
            pltpu.VMEM((4,) + block, LOW),
            pltpu.VMEM((4,) + block, LOW),
            pltpu.VMEM((4,) + block, LOW),
            pltpu.VMEM((2,) + block, LOW),
            pltpu.VMEM((2,) + block, LOW),
            pltpu.VMEM((2,) + part, LOW),
            pltpu.VMEM((2,) + part, LOW),
            pltpu.VMEM((2,) + block, LOW),
            pltpu.VMEM((2,) + block, LOW),
            DMA((2,)),
            pltpu.SemaphoreType.REGULAR((planes,)),
            DMA((2, 4, planes)),
            DMA((2, 4, planes)),
            DMA((2, 2, planes)),
            DMA((2, 2, planes)),
            DMA((2, 2, planes)),
            DMA((2, 2, planes)),
            DMA((2, 2, planes)),
            DMA((2, 2, planes)),
        ],
        compiler_params=pltpu.CompilerParams(
            collective_id=identity, has_side_effects=True, vmem_limit_bytes=VMEM_LIMIT
        ),
    )(place, v, m)


def greet_plane(planes, owners):
    e, s = lax.axis_index("expert"), lax.axis_index("shard")
    barrier = pltpu.get_barrier_semaphore()
    for o in range(1, owners):
        pl.semaphore_signal(
            barrier, 1, device_id=(lax.rem(e + o, owners), s), device_id_type=MESH
        )

    @pl.when(s > 0)
    def _():
        pl.semaphore_signal(barrier, 1, device_id=(e, s - 1), device_id_type=MESH)

    @pl.when(s < planes - 1)
    def _():
        pl.semaphore_signal(barrier, 1, device_id=(e, s + 1), device_id_type=MESH)

    inner = (s > 0) & (s < planes - 1)

    @pl.when(inner)
    def _():
        pl.semaphore_wait(barrier, owners + 1)

    @pl.when(jnp.logical_not(inner))
    def _():
        pl.semaphore_wait(barrier, owners)


def finish_kernel(owners, rows_ref, head_ref, kv_ref, tail_ref, out_rows, out_qkv, out_tail):
    i = pl.program_id(0)

    @pl.when(i < owners)
    def _():
        out_rows[...] = rows_ref[0].astype(FULL)
        out_qkv[...] = head_ref[0].astype(FULL)

    @pl.when(i >= owners)
    def _():
        each = owners // KEY_VALUE_HEADS
        for h in range(KEY_VALUE_HEADS):
            total = kv_ref[h * each].astype(FULL)
            for j in range(1, each):
                total = total + kv_ref[h * each + j].astype(FULL)
            out_qkv[:, h * HEAD_SIZE : (h + 1) * HEAD_SIZE] = total

    @pl.when(i == 0)
    def _():
        total = tail_ref[0].astype(FULL)
        for lane in range(1, owners):
            total = total + tail_ref[lane].astype(FULL)
        out_tail[...] = total


def finish_grads(rows, head, rest, owners):
    rows = rows.reshape(owners, -1, rows.shape[-1])
    head = head.reshape(owners, -1, head.shape[-1])
    rest = rest.reshape(owners, -1, rest.shape[-1])
    count, share = rows.shape[1:]
    height, wide = head.shape[1:]
    last = owners - 1
    return pl.pallas_call(
        functools.partial(finish_kernel, owners),
        grid=(owners + 2,),
        in_specs=[
            pl.BlockSpec((1, count, share), lambda i: (jnp.minimum(i, last), 0, 0)),
            pl.BlockSpec((1, height, wide), lambda i: (jnp.minimum(i, last), 0, 0)),
            pl.BlockSpec((owners, height, HEAD_SIZE), lambda i: (0, 0, i // (owners + 1))),
            pl.BlockSpec((owners, height, TAIL), lambda i: (0, 0, 2)),
        ],
        out_specs=[
            pl.BlockSpec((count, share), lambda i: (0, jnp.minimum(i, last))),
            pl.BlockSpec((height, wide), lambda i: (0, i)),
            pl.BlockSpec((height, TAIL), lambda i: (0, 0)),
        ],
        out_shape=[
            jax.ShapeDtypeStruct((count, owners * share), FULL),
            jax.ShapeDtypeStruct((height, (owners + 2) * wide), FULL),
            jax.ShapeDtypeStruct((height, TAIL), FULL),
        ],
        compiler_params=pltpu.CompilerParams(vmem_limit_bytes=VMEM_LIMIT),
    )(rows, head, rest, rest)


def gather_steps(at, cut, source, x_send, x_recv, y_send, y_recv, c_send, c_recv):
    e, core, flip_x, flip_y, diagonal = neighbours()
    s = lax.axis_index("shard")

    def arrived(block, sem):
        send(block, block, sem, sem, (core, s)).wait_recv()

    def first():
        return [
            send(source, at(e), x_send(0), x_recv(0), (flip_x, s)),
            send(source, at(e), y_send(0), y_recv(0), (flip_y, s)),
            send(source, at(e), c_send(0), c_recv(0), (core, s)),
        ]

    def from_x():
        return [
            send(cut(flip_x, 0), cut(flip_x, 0), y_send(1), y_recv(1), (flip_y, s)),
            send(at(flip_x), at(flip_x), c_send(1), c_recv(1), (core, s)),
        ]

    def from_y():
        return [
            send(cut(flip_y, 1), cut(flip_y, 1), x_send(1), x_recv(1), (flip_x, s)),
            send(at(flip_y), at(flip_y), c_send(2), c_recv(2), (core, s)),
        ]

    def from_diagonal():
        return [send(at(diagonal), at(diagonal), c_send(3), c_recv(3), (core, s))]

    def begin():
        for copy in first():
            copy.start()

    def second():
        arrived(at(flip_x), x_recv(0))
        for copy in from_x():
            copy.start()
        arrived(at(flip_y), y_recv(0))
        for copy in from_y():
            copy.start()

    def third():
        arrived(cut(diagonal, 0), y_recv(1))
        arrived(cut(diagonal, 1), x_recv(1))
        for copy in from_diagonal():
            copy.start()

    def last():
        for k, lane in enumerate((core, core + flip_x - e, core + flip_y - e, core + diagonal - e)):
            arrived(at(lane), c_recv(k))

    def sent():
        for copy in first() + from_x() + from_y() + from_diagonal():
            copy.wait_send()

    return begin, second, third, last, sent


def rope_tables(places, frequency):
    angles = places * frequency
    lane = lax.broadcasted_iota(jnp.int32, angles.shape, 1)
    sine = jnp.sin(angles)
    return jnp.cos(angles), jnp.where(lane < HEAD_SIZE // 2, -sine, sine)


def half_turn(v):
    return pltpu.roll(v, HEAD_SIZE // 2, 1)


def front_kernel(
    planes, owners, w_ref, gain_ref, tok_ref, d_ref, freq_ref, out_ref,
    d_all, w_out_all, w_all_out, gains, tail_ref, h1_ref, proj_ref, probs_ref, mixed_ref, branch_ref,
    w_all, tok_all, w_mine, q_rows, mine, away, c_in, x_in, y_in, x_half, y_half,
    keep_sem, w_send, w_recv, g_send, g_recv, o_send, o_recv, z_send, z_recv,
    tx_send, tx_recv, ty_send, ty_recv, tc_send, tc_recv,
    dx_send, dx_recv, dy_send, dy_recv, dc_send, dc_recv,
    px_send, px_recv, py_send, py_recv, pc_send, pc_recv,
):
    e, core, flip_x, flip_y, diagonal = neighbours()
    s = lax.axis_index("shard")
    lanes = owners // planes
    home = e // lanes
    length = tok_ref.shape[0]
    half = length // 2
    count = w_mine.shape[0]
    heads = count // HEAD_SIZE
    pieces = 4
    out_part = count // pieces
    deep = w_ref.shape[0]
    qkv_cols = proj_ref.shape[2]

    def arrived(block, sem):
        send(block, block, sem, sem, (core, s)).wait_recv()

    def w_copy(sp, way):
        block = w_all.at[sp]
        return send(block, block, w_send.at[way, sp], w_recv.at[sp], (e, s + 1 - 2 * way))

    def g_copy(sp, way):
        block = gains.at[sp]
        return send(block, block, g_send.at[way, sp], g_recv.at[sp], (e, s + 1 - 2 * way))

    def d_copy(sp, way):
        block = d_all.at[e, sp]
        return send(block, block, z_send.at[way, sp], z_recv.at[sp], (e, s + 1 - 2 * way))

    def o_copy(k, way):
        block = w_mine.at[pl.ds(k * out_part, out_part)]
        return send(block, block, o_send.at[way, k], o_recv.at[k], (e, s + 1 - 2 * way))

    t_begin, t_second, t_third, t_last, t_sent = gather_steps(
        lambda lane: tok_all.at[lane],
        lambda lane, k: tok_all.at[lane, pl.ds(k * half, half)],
        tok_ref,
        lambda k: tx_send.at[k],
        lambda k: tx_recv.at[k],
        lambda k: ty_send.at[k],
        lambda k: ty_recv.at[k],
        lambda k: tc_send.at[k],
        lambda k: tc_recv.at[k],
    )

    def d_rows(sp):
        return gather_steps(
            lambda lane: d_all.at[lane, sp],
            lambda lane, k: d_all.at[lane, sp, pl.ds(k * half, half)],
            d_all.at[e, sp],
            lambda k: dx_send.at[k, sp],
            lambda k: dx_recv.at[k, sp],
            lambda k: dy_send.at[k, sp],
            lambda k: dy_recv.at[k, sp],
            lambda k: dc_send.at[k, sp],
            lambda k: dc_recv.at[k, sp],
        )

    keep_d = pltpu.make_async_copy(d_ref, d_all.at[e, s], keep_sem.at[0])
    rows = pl.ds(pl.multiple_of((e - home * lanes) * count, 16), count)
    load_o = pltpu.make_async_copy(out_ref.at[rows], w_mine, keep_sem.at[1])
    keep_w = pltpu.make_async_copy(w_all, w_all_out, keep_sem.at[2])
    keep_o = pltpu.make_async_copy(w_mine, w_out_all, keep_sem.at[3])
    keep_d.start()

    @pl.when(s == home)
    def _():
        load_o.start()

    w_all[s] = w_ref[...]
    gains[s] = gain_ref[...]
    tok_all[e] = tok_ref[...]
    greet(planes)

    def both_ways(copy, sp):
        @pl.when((sp <= s) & (s < planes - 1))
        def _():
            copy(sp, 0).start()

        @pl.when((sp >= s) & (s > 0))
        def _():
            copy(sp, 1).start()

    def plane_at(i):
        sp = s + (2 * (i % 2) - 1) * ((i + 1) // 2)
        return sp, (sp >= 0) & (sp < planes) & (i >= 0) & (i <= 2 * planes - 2)

    def out_step(k):
        @pl.when(s != home)
        def _():
            arrived(w_mine.at[pl.ds(k * out_part, out_part)], o_recv.at[k])

        @pl.when((s >= home) & (s < planes - 1))
        def _():
            o_copy(k, 0).start()

        @pl.when((s <= home) & (s > 0))
        def _():
            o_copy(k, 1).start()

    t_begin()
    both_ways(g_copy, s)
    both_ways(w_copy, s)

    keep_d.wait()
    d_rows(s)[0]()

    def weights(i, carry):
        sp, there = plane_at(i)

        @pl.when(there & (i > 0))
        def _():
            arrived(gains.at[sp], g_recv.at[sp])
            both_ways(g_copy, sp)
            arrived(w_all.at[sp], w_recv.at[sp])
            both_ways(w_copy, sp)

        @pl.when(i == 1)
        def _():
            t_second()

        @pl.when(i == 2)
        def _():
            t_third()
            d_rows(s)[1]()

        @pl.when(i == 3)
        def _():
            d_rows(s)[2]()

        @pl.when((i == 2) & (s == home))
        def _():
            load_o.wait()
            for k in range(pieces):
                out_step(k)

        return carry

    lax.fori_loop(1, 2 * planes - 1, weights, 0)
    t_last()
    keep_w.start()

    def far(n):
        for i in (2 * n - 1, 2 * n):
            sp, there = plane_at(i)

            @pl.when(there)
            def _(sp=sp):
                arrived(d_all.at[e, sp], z_recv.at[sp])
                both_ways(d_copy, sp)
                d_rows(sp)[0]()

    def rows_onward(n):
        @pl.when((s - home == n) | (home - s == n))
        def _():
            for k in range(pieces):
                out_step(k)

    def near(n, stage):
        for i in (2 * n - 1, 2 * n):
            sp, there = plane_at(i)

            @pl.when(there)
            def _(sp=sp):
                d_rows(sp)[stage]()

    gain_query = gains[0, 2:3, :HEAD_SIZE].astype(FULL)
    gain_key = gains[0, 3:4, :HEAD_SIZE].astype(FULL)
    for sp in range(1, planes):
        gain_query = gain_query + gains[sp, 2:3, :HEAD_SIZE].astype(FULL)
        gain_key = gain_key + gains[sp, 3:4, :HEAD_SIZE].astype(FULL)
    row = lax.broadcasted_iota(jnp.int32, (length, length), 0).astype(FULL)
    column = lax.broadcasted_iota(jnp.int32, (length, length), 1).astype(FULL)

    def attend(b, carry):
        x = tok_all[b, :, :MODEL_WIDTH].astype(FULL)
        inverse = lax.rsqrt(jnp.mean(x * x, axis=1, keepdims=True) + EPS)
        total = jnp.zeros((length, qkv_cols), FULL)
        for sp in range(planes):
            at = slice(sp * deep, (sp + 1) * deep)
            part = x[:, at] * inverse * gains[sp, 0:1, :].astype(FULL)
            part = part.astype(LOW)
            h1_ref[b, :, at] = part
            total = total + jnp.dot(part, w_all[sp, :, :qkv_cols], preferred_element_type=FULL)
        proj_ref[b] = total
        tail_ref[b] = tok_all[b, :, MODEL_WIDTH:]
        places = tok_all[b, :, MODEL_WIDTH:].astype(FULL)[:, 1:2]
        cosine, sine = rope_tables(places, freq_ref[0:1, :])

        def normed(v, gain):
            v = v * lax.rsqrt(jnp.mean(v * v, axis=1, keepdims=True) + EPS) * gain
            return (v * cosine + half_turn(v) * sine).astype(LOW)

        for h in range(heads):
            at = slice(h * HEAD_SIZE, (h + 1) * HEAD_SIZE)
            q_rows[h * length : (h + 1) * length, :] = normed(total[:, at], gain_query)
        key = normed(total[:, count : count + HEAD_SIZE], gain_key)
        value = total[:, count + HEAD_SIZE :].astype(LOW)
        scores = lax.dot_general(
            q_rows[...], key, (((1,), (1,)), ((), ())), preferred_element_type=FULL
        ) * (HEAD_SIZE**-0.5)
        allowed = (column <= row) & (column >= row - places)
        scores = jnp.where(jnp.concatenate([allowed] * heads, axis=0), scores, -1e30)
        exponent = jnp.exp(scores - jnp.max(scores, axis=1, keepdims=True))
        probs = (exponent / jnp.sum(exponent, axis=1, keepdims=True)).astype(LOW)
        probs_ref[b] = probs
        mixed = jnp.dot(probs, value, preferred_element_type=FULL).astype(LOW)
        for h in range(heads):
            at = slice(h * HEAD_SIZE, (h + 1) * HEAD_SIZE)
            mixed_ref[b, :, at] = mixed[h * length : (h + 1) * length]

        for k in range(pieces):

            @pl.when((b == 2 * k) & ((s - home == 1) | (home - s == 1)))
            def _(k=k):
                out_step(k)

        return carry

    lax.fori_loop(0, owners, attend, 0)
    both_ways(d_copy, s)
    rows_onward(2)
    far(1)
    for n in range(3, planes):
        rows_onward(n)
    keep_o.start()
    begin, middle, finish, sent = project_steps(
        False, mixed_ref, w_mine, branch_ref, mine, away, c_in, x_in, y_in, x_half, y_half,
        pc_send, pc_recv, px_send, px_recv, py_send, py_recv,
    )
    begin()
    near(1, 1)
    far(2)
    middle()
    near(1, 2)
    near(2, 1)
    for n in range(3, planes):
        far(n)
    finish()
    near(2, 2)
    for n in range(3, planes):
        near(n, 1)
    for n in range(3, planes):
        near(n, 2)
    t_sent()
    sent()

    def settled(copy, sp):
        @pl.when((sp <= s) & (s < planes - 1))
        def _():
            copy(sp, 0).wait_send()

        @pl.when((sp >= s) & (s > 0))
        def _():
            copy(sp, 1).wait_send()

    def drain(sp, carry):
        d_rows(sp)[3]()
        d_rows(sp)[4]()
        settled(w_copy, sp)
        settled(g_copy, sp)
        settled(d_copy, sp)
        return carry

    lax.fori_loop(0, planes, drain, 0)
    for k in range(pieces):

        @pl.when((s >= home) & (s < planes - 1))
        def _(k=k):
            o_copy(k, 0).wait_send()

        @pl.when((s <= home) & (s > 0))
        def _(k=k):
            o_copy(k, 1).wait_send()

    keep_w.wait()
    keep_o.wait()


def front(w, gain_rows, tokens, w_out, d_rows, frequency, planes, owners, identity):
    def out(*shape, dtype=LOW):
        return jax.ShapeDtypeStruct(shape, dtype)

    length = tokens.shape[0]
    count = w_out.shape[0] * planes // owners
    qkv_cols = count + 2 * HEAD_SIZE
    block = (length, MODEL_WIDTH)
    part = (length // 2, MODEL_WIDTH)
    return pl.pallas_call(
        functools.partial(front_kernel, planes, owners),
        out_shape=[
            out(owners, planes, *d_rows.shape),
            out(count, MODEL_WIDTH),
            out(planes, *w.shape),
            out(planes, *gain_rows.shape),
            out(owners, length, TAIL),
            out(owners, length, MODEL_WIDTH),
            out(owners, length, qkv_cols, dtype=FULL),
            out(owners, length * count // HEAD_SIZE, length),
            out(owners, length, count),
            out(length, MODEL_WIDTH, dtype=FULL),
        ],
        in_specs=[VM, VM, VM, VM, VM, ANY],
        out_specs=[ANY, ANY, ANY, VM, VM, VM, VM, VM, VM, VM],
        scratch_shapes=[
            pltpu.VMEM((planes,) + w.shape, LOW),
            pltpu.VMEM((owners,) + tokens.shape, LOW),
            pltpu.VMEM((count, MODEL_WIDTH), LOW),
            pltpu.VMEM((length * count // HEAD_SIZE, HEAD_SIZE), LOW),
            pltpu.VMEM((4,) + block, LOW),
            pltpu.VMEM((4,) + block, LOW),
            pltpu.VMEM((4,) + block, LOW),
            pltpu.VMEM(block, LOW),
            pltpu.VMEM(block, LOW),
            pltpu.VMEM(part, LOW),
            pltpu.VMEM(part, LOW),
            DMA((4,)),
            DMA((2, planes)),
            DMA((planes,)),
            DMA((2, planes)),
            DMA((planes,)),
            DMA((2, 4)),
            DMA((4,)),
            DMA((2, planes)),
            DMA((planes,)),
            DMA((2,)),
            DMA((2,)),
            DMA((2,)),
            DMA((2,)),
            DMA((4,)),
            DMA((4,)),
            DMA((2, planes)),
            DMA((2, planes)),
            DMA((2, planes)),
            DMA((2, planes)),
            DMA((4, planes)),
            DMA((4, planes)),
            DMA((2,)),
            DMA((2,)),
            DMA((2,)),
            DMA((2,)),
            DMA((4,)),
            DMA((4,)),
        ],
        compiler_params=pltpu.CompilerParams(
            collective_id=identity, has_side_effects=True, vmem_limit_bytes=VMEM_LIMIT
        ),
    )(w, gain_rows, tokens, d_rows, frequency, w_out)


def project_steps(
    turned, rows_ref, w_ref, out_ref, mine, away, c_in, x_in, y_in, x_half, y_half,
    cs, cr, xs, xr, ys, yr,
):
    e, core, flip_x, flip_y, diagonal = neighbours()
    s = lax.axis_index("shard")
    q_own, q_x, q_y, q_d = e // 2, flip_x // 2, flip_y // 2, diagonal // 2
    parity = e % 2
    half = out_ref.shape[0] // 2
    low_half, high_half = pl.ds(0, half), pl.ds(half, half)
    across = (((1,), (1 if turned else 0,)), ((), ()))
    order = (q_d, q_x, q_y, q_own)

    def arrived(block, sem):
        send(block, block, sem, sem, (core, s)).wait_recv()

    def add(target, *others):
        total = target[...].astype(FULL)
        for other in others:
            total = total + other[...].astype(FULL)
        target[...] = total.astype(LOW)

    def to_core(q):
        return send(away.at[q], c_in.at[q], cs.at[q], cr.at[q], (core, s))

    def compute(q, lane, into):
        rows = rows_ref[2 * q + lane]

        def tile(t, carry):
            at = pl.ds(pl.multiple_of(t * TILE, TILE), TILE)
            if turned:
                deep = w_ref.shape[1]
                w = w_ref[t * TILE // deep, :, : rows.shape[1]]
            else:
                w = w_ref[:, at]
            into[q, :, at] = lax.dot_general(
                rows, w, across, preferred_element_type=FULL
            ).astype(LOW)
            return carry

        lax.fori_loop(0, MODEL_WIDTH // TILE, tile, 0)

    halves = [
        send(mine.at[q_d, low_half], y_half, ys.at[0], yr.at[0], (flip_y, s)),
        send(mine.at[q_d, high_half], x_half, xs.at[0], xr.at[0], (flip_x, s)),
    ]
    to_x = send(mine.at[q_x], x_in, xs.at[1], xr.at[1], (flip_x, s))
    to_y = send(mine.at[q_y], y_in, ys.at[1], yr.at[1], (flip_y, s))

    def joined(q):
        arrived(c_in.at[q], cr.at[q])
        add(mine.at[q], c_in.at[q])

    def begin():
        for q in order:
            compute(q, 1 - parity, away)
            to_core(q).start()
        for k, q in enumerate(order):
            compute(q, parity, mine)
            if k == 0:
                joined(q_d)
                for copy in halves:
                    copy.start()

    def middle():
        joined(q_x)
        arrived(y_half, yr.at[0])
        add(mine.at[q_x, low_half], y_half)
        to_x.start()
        joined(q_y)
        arrived(x_half, xr.at[0])
        add(mine.at[q_y, high_half], x_half)
        to_y.start()

    def finish():
        joined(q_own)
        arrived(x_in, xr.at[1])
        arrived(y_in, yr.at[1])
        out_ref[...] = (
            mine[q_own].astype(FULL) + x_in[...].astype(FULL) + y_in[...].astype(FULL)
        )

    def sent():
        for q in order:
            to_core(q).wait_send()
        for copy in halves + [to_x, to_y]:
            copy.wait_send()

    return begin, middle, finish, sent


def back_kernel(
    planes, owners, dm_ref, w_ref, mixed_ref, proj_ref, probs_ref, tail_ref, gain_ref, freq_ref,
    dproj_ref, sum_ref, dgain_ref,
    dm_all, mixed_t, rows, acc, up_in, down_in, q_rows, dm_rows,
    keep_sem, xs, xr, ys, yr, cs, cr, a_send, a_recv, z_send, z_recv,
):
    e, core, _, _, _ = neighbours()
    s = lax.axis_index("shard")
    lanes = owners // planes
    length = dm_ref.shape[0]
    half = length // 2
    count = w_ref.shape[0]
    heads = count // HEAD_SIZE
    share = acc.shape[2]
    scaling = HEAD_SIZE**-0.5
    nt = (((1,), (1,)), ((), ()))
    tn = (((0,), (0,)), ((), ()))

    def arrived(block, sem):
        send(block, block, sem, sem, (core, s)).wait_recv()

    greet_plane(planes, owners)
    begin, second, third, last, sent = gather_steps(
        lambda lane: dm_all.at[lane],
        lambda lane, k: dm_all.at[lane, pl.ds(k * half, half)],
        dm_ref,
        lambda k: xs.at[k],
        lambda k: xr.at[k],
        lambda k: ys.at[k],
        lambda k: yr.at[k],
        lambda k: cs.at[k],
        lambda k: cr.at[k],
    )
    begin()
    dm_all[e] = dm_ref[...]
    for b in range(owners):
        mixed_t[:, b * length : (b + 1) * length] = mixed_ref[b].T
    second()
    third()
    last()

    def spread(other):
        return send(
            rows.at[:, pl.ds(other * share, share)], acc.at[e], a_send.at[other], a_recv.at[e],
            (other, s),
        )

    for other in range(owners):
        at = pl.ds(other * share, share)
        got = jnp.dot(
            mixed_t[...],
            dm_all[:, :, at].reshape(owners * length, share),
            preferred_element_type=FULL,
        ).astype(LOW)
        rows[:, at] = got

        @pl.when(other != e)
        def _(other=other):
            spread(other).start()

        @pl.when(other == e)
        def _(got=got):
            acc[e] = got

    def chunk(sp):
        return acc.at[pl.ds(sp * lanes, lanes)]

    def up(sp):
        return send(chunk(sp), up_in.at[sp], z_send.at[0, sp], z_recv.at[0, sp], (e, s + 1))

    def down(sp):
        return send(chunk(sp), down_in.at[sp], z_send.at[1, sp], z_recv.at[1, sp], (e, s - 1))

    def line(sp):
        for lane in range(lanes):
            source = sp * lanes + lane

            @pl.when(source != e)
            def _(source=source):
                arrived(acc.at[source], a_recv.at[source])

        @pl.when((sp >= s) & (s > 0))
        def _():
            arrived(up_in.at[sp], z_recv.at[0, sp])
            add_blocks(chunk(sp), up_in.at[sp])

        @pl.when((sp <= s) & (s < planes - 1))
        def _():
            arrived(down_in.at[sp], z_recv.at[1, sp])
            add_blocks(chunk(sp), down_in.at[sp])

        @pl.when(sp > s)
        def _():
            up(sp).start()

        @pl.when(sp < s)
        def _():
            down(sp).start()

    dgain_ref[...] = jnp.zeros_like(dgain_ref)
    gain_query = gain_ref[0, 2:3, :HEAD_SIZE].astype(FULL)
    gain_key = gain_ref[0, 3:4, :HEAD_SIZE].astype(FULL)
    for sp in range(1, planes):
        gain_query = gain_query + gain_ref[sp, 2:3, :HEAD_SIZE].astype(FULL)
        gain_key = gain_key + gain_ref[sp, 3:4, :HEAD_SIZE].astype(FULL)

    def attend(b, carry):
        places = tail_ref[b].astype(FULL)[:, 1:2]
        cosine, sine = rope_tables(places, freq_ref[0:1, :])

        def unit(v):
            inverse = lax.rsqrt(jnp.mean(v * v, axis=1, keepdims=True) + EPS)
            return v * inverse, inverse

        def turned(v):
            return (v * cosine + half_turn(v) * sine).astype(LOW)

        def back(v, units, inverse, gain, row):
            v = v * cosine - half_turn(v) * sine
            dgain_ref[row : row + 1, :] += jnp.sum(v * units, axis=0, keepdims=True)
            v = v * gain
            return inverse * (v - units * jnp.mean(v * units, axis=1, keepdims=True))

        d_mixed = lax.dot_general(
            dm_all[b], w_ref[...], nt, preferred_element_type=FULL
        ).astype(LOW)
        for h in range(heads):
            at = slice(h * HEAD_SIZE, (h + 1) * HEAD_SIZE)
            here = slice(h * length, (h + 1) * length)
            dm_rows[here, :] = d_mixed[:, at]
            units, _ = unit(proj_ref[b, :, at])
            q_rows[here, :] = turned(units * gain_query)
        key_units, key_inverse = unit(proj_ref[b, :, count : count + HEAD_SIZE])
        key = turned(key_units * gain_key)
        value = proj_ref[b, :, count + HEAD_SIZE :].astype(LOW)
        probs = probs_ref[b]
        wide = probs.astype(FULL)
        d_probs = lax.dot_general(dm_rows[...], value, nt, preferred_element_type=FULL)
        d_scores = wide * (d_probs - jnp.sum(d_probs * wide, axis=1, keepdims=True))
        d_scores = d_scores.astype(LOW)
        d_query = jnp.dot(d_scores, key, preferred_element_type=FULL) * scaling
        d_key = lax.dot_general(d_scores, q_rows[...], tn, preferred_element_type=FULL) * scaling
        d_value = lax.dot_general(probs, dm_rows[...], tn, preferred_element_type=FULL)
        for h in range(heads):
            at = slice(h * HEAD_SIZE, (h + 1) * HEAD_SIZE)
            units, inverse = unit(proj_ref[b, :, at])
            got = back(d_query[h * length : (h + 1) * length], units, inverse, gain_query, 0)
            dproj_ref[b, :, at] = got.astype(LOW)
        got = back(d_key, key_units, key_inverse, gain_key, 1)
        dproj_ref[b, :, count : count + HEAD_SIZE] = got.astype(LOW)
        dproj_ref[b, :, count + HEAD_SIZE :] = d_value.astype(LOW)

        i = b - (owners - 2 * planes + 2)
        distance = (2 * planes - 2 - i + 1) // 2
        sp = s + (2 * (i % 2) - 1) * (0 - distance)

        @pl.when((i >= 0) & (sp >= 0) & (sp < planes))
        def _():
            line(sp)

        return carry

    lax.fori_loop(0, owners, attend, 0)
    line(s)
    sum_ref[...] = chunk(s)[...]
    sent()
    for other in range(owners):

        @pl.when(other != e)
        def _(other=other):
            spread(other).wait_send()

    def drain(sp, carry):
        @pl.when(sp > s)
        def _():
            up(sp).wait_send()

        @pl.when(sp < s)
        def _():
            down(sp).wait_send()

        return carry

    lax.fori_loop(0, planes, drain, 0)


def add_blocks(target, other):
    step = min(128, target.shape[1])
    for lead in range(target.shape[0]):

        def one(r, carry, lead=lead):
            at = pl.ds(pl.multiple_of(r * step, step), step)
            target[lead, at, :] = (
                target[lead, at, :].astype(FULL) + other[lead, at, :].astype(FULL)
            ).astype(LOW)
            return carry

        lax.fori_loop(0, target.shape[1] // step, one, 0)


def back(dm, w, mixed, proj, probs, tail, gains, frequency, planes, owners, identity):
    length = dm.shape[0]
    count = w.shape[0]
    share = MODEL_WIDTH // owners
    lanes = owners // planes
    return pl.pallas_call(
        functools.partial(back_kernel, planes, owners),
        out_shape=[
            jax.ShapeDtypeStruct(proj.shape, LOW),
            jax.ShapeDtypeStruct((lanes, count, share), LOW),
            jax.ShapeDtypeStruct((8, HEAD_SIZE), FULL),
        ],
        in_specs=[VM] * 8,
        out_specs=[VM] * 3,
        scratch_shapes=[
            pltpu.VMEM((owners, length, MODEL_WIDTH), LOW),
            pltpu.VMEM((count, owners * length), LOW),
            pltpu.VMEM((count, MODEL_WIDTH), LOW),
            pltpu.VMEM((owners, count, share), LOW),
            pltpu.VMEM((planes, lanes, count, share), LOW),
            pltpu.VMEM((planes, lanes, count, share), LOW),
            pltpu.VMEM((length * count // HEAD_SIZE, HEAD_SIZE), LOW),
            pltpu.VMEM((length * count // HEAD_SIZE, HEAD_SIZE), LOW),
            DMA(()),
            DMA((2,)),
            DMA((2,)),
            DMA((2,)),
            DMA((2,)),
            DMA((4,)),
            DMA((4,)),
            DMA((owners,)),
            DMA((owners,)),
            DMA((2, planes)),
            DMA((2, planes)),
        ],
        compiler_params=pltpu.CompilerParams(
            collective_id=identity, has_side_effects=True, vmem_limit_bytes=VMEM_LIMIT
        ),
    )(dm, w, mixed, proj, probs, tail, gains, frequency)


def share_kernel(
    planes, owners, h1_ref, dproj_ref, w_ref, unit_ref, tail_ref, sum_ref,
    out_rows, out_head, out_rest, dh1_ref,
    acc_head, acc_rest, u_head, u_rest, d_head, d_rest, column, mine, away, c_in, x_in, y_in, x_half, y_half,
    z_send, z_recv, x_send, x_recv, y_send, y_recv, c_send, c_recv, own_sem,
    pc_send, pc_recv, px_send, px_recv, py_send, py_recv,
):
    e, core, flip_x, flip_y, diagonal = neighbours()
    s = lax.axis_index("shard")
    deep = acc_head.shape[1] * acc_head.shape[2]
    half = deep // 2
    wide = acc_head.shape[3]
    acc = (None, acc_head, acc_rest)
    up_in = (None, u_head, u_rest)
    down_in = (None, d_head, d_rest)
    outs = (out_rows, out_head, out_rest)
    tn = (((0,), (0,)), ((), ()))

    def arrived(block, sem):
        send(block, block, sem, sem, (core, s)).wait_recv()

    greet(planes)

    def chunk(k, sp):
        return sum_ref if k == 0 else acc[k].at[sp]

    def make(k, sp):
        at = pl.ds(pl.multiple_of(sp * deep, deep), deep)
        left = h1_ref[:, :, at].reshape(-1, deep)
        columns_at = slice(0, wide) if k == 1 else slice(wide, None)
        right = dproj_ref[:, :, columns_at]
        right = right.reshape(-1, right.shape[-1])
        got = lax.dot_general(left, right, tn, preferred_element_type=FULL).astype(LOW)
        got = got.reshape(2, half, got.shape[-1])
        if k == 1:
            acc_head[sp] = got
        else:
            acc_rest[sp, :, :, : got.shape[-1]] = got
            at = pl.ds(pl.multiple_of(sp * deep, deep), deep)
            row = jnp.sum(dh1_ref[:, at] * unit_ref[:, at], axis=0, keepdims=True)
            column[GAIN_ONE : GAIN_ONE + 1, :] = row
            extra = column[...].T.reshape(2, half, TAIL)
            acc_rest[sp, :, :, got.shape[-1] :] = (tail_ref[sp].astype(FULL) + extra).astype(LOW)

    def up(k, sp):
        return send(
            chunk(k, sp), up_in[k].at[sp], z_send.at[k, 0, sp], z_recv.at[k, 0, sp], (e, s + 1)
        )

    def down(k, sp):
        return send(
            chunk(k, sp), down_in[k].at[sp], z_send.at[k, 1, sp], z_recv.at[k, 1, sp], (e, s - 1)
        )

    def line(k, sp):
        make(k, sp)

        @pl.when((sp >= s) & (s > 0))
        def _():
            arrived(up_in[k].at[sp], z_recv.at[k, 0, sp])
            add_blocks(chunk(k, sp), up_in[k].at[sp])

        @pl.when((sp <= s) & (s < planes - 1))
        def _():
            arrived(down_in[k].at[sp], z_recv.at[k, 1, sp])
            add_blocks(chunk(k, sp), down_in[k].at[sp])

        @pl.when(sp > s)
        def _():
            up(k, sp).start()

        @pl.when(sp < s)
        def _():
            down(k, sp).start()

    def pair(k, n):
        for i in (2 * n, 2 * n - 1):
            sp = s + (2 * (i % 2) - 1) * n

            @pl.when((sp >= 0) & (sp < planes))
            def _(sp=sp):
                line(k, sp)

    def steps(k):
        count = outs[k].shape[1] // 2
        return gather_steps(
            lambda lane: outs[k].at[lane],
            lambda lane, at: outs[k].at[lane, pl.ds(at * count, count)],
            chunk(k, s),
            lambda n: x_send.at[k, n],
            lambda n: x_recv.at[k, n],
            lambda n: y_send.at[k, n],
            lambda n: y_recv.at[k, n],
            lambda n: c_send.at[k, n],
            lambda n: c_recv.at[k, n],
        )

    def keep(k):
        return pltpu.make_async_copy(chunk(k, s), outs[k].at[e], own_sem.at[k])

    def share(k):
        steps(k)[0]()
        keep(k).start()

    p_begin, p_middle, p_finish, p_sent = project_steps(
        True, dproj_ref, w_ref, dh1_ref, mine, away, c_in, x_in, y_in, x_half, y_half,
        pc_send, pc_recv, px_send, px_recv, py_send, py_recv,
    )
    share(0)
    column[...] = jnp.zeros_like(column)
    pair(1, planes - 1)
    p_begin()
    for n in range(planes - 2, 1, -1):
        pair(1, n)
    p_middle()
    pair(1, 1)
    p_finish()
    pair(2, planes - 1)
    steps(0)[1]()
    line(1, s)
    share(1)
    for n in range(planes - 2, 1, -1):
        pair(2, n)
    steps(0)[2]()
    pair(2, 1)
    steps(1)[1]()
    line(2, s)
    share(2)
    steps(1)[2]()
    steps(2)[1]()
    steps(2)[2]()
    for k in range(3):
        keep(k).wait()
        steps(k)[3]()
        steps(k)[4]()
    p_sent()

    def drain(sp, carry):
        for k in (1, 2):

            @pl.when(sp > s)
            def _(k=k):
                up(k, sp).wait_send()

            @pl.when(sp < s)
            def _(k=k):
                down(k, sp).wait_send()

        return carry

    lax.fori_loop(0, planes, drain, 0)


def share_grads(h1, dproj, w_all, units, tail, row_sum, planes, owners, identity):
    length = h1.shape[1]
    deep = MODEL_WIDTH // planes
    query_cols = dproj.shape[2] - 2 * HEAD_SIZE
    head = (2, deep // 2, query_cols)
    rest = (2, deep // 2, 2 * HEAD_SIZE + tail.shape[-1])
    tail = tail.reshape(planes, 2, deep // 2, -1)
    block = (length, MODEL_WIDTH)
    part = (length // 2, MODEL_WIDTH)

    def per_plane(*shapes):
        return [pltpu.VMEM((planes,) + shape, LOW) for shape in shapes]

    return pl.pallas_call(
        functools.partial(share_kernel, planes, owners),
        out_shape=[
            jax.ShapeDtypeStruct((owners,) + shape, LOW)
            for shape in (row_sum.shape, head, rest)
        ]
        + [jax.ShapeDtypeStruct(block, FULL)],
        in_specs=[VM] * 6,
        out_specs=[ANY, ANY, ANY, VM],
        scratch_shapes=per_plane(head, rest)
        + per_plane(head, rest)
        + per_plane(head, rest)
        + [
            pltpu.VMEM((TAIL, deep), FULL),
            pltpu.VMEM((4,) + block, LOW),
            pltpu.VMEM((4,) + block, LOW),
            pltpu.VMEM((4,) + block, LOW),
            pltpu.VMEM(block, LOW),
            pltpu.VMEM(block, LOW),
            pltpu.VMEM(part, LOW),
            pltpu.VMEM(part, LOW),
            DMA((3, 2, planes)),
            DMA((3, 2, planes)),
            DMA((3, 2)),
            DMA((3, 2)),
            DMA((3, 2)),
            DMA((3, 2)),
            DMA((3, 4)),
            DMA((3, 4)),
            DMA((3,)),
            DMA((4,)),
            DMA((4,)),
            DMA((2,)),
            DMA((2,)),
            DMA((2,)),
            DMA((2,)),
        ],
        compiler_params=pltpu.CompilerParams(
            collective_id=identity, has_side_effects=True, vmem_limit_bytes=VMEM_LIMIT
        ),
    )(h1, dproj, w_all, units, tail, row_sum)


def gathered_layer(
    tokens,
    segments,
    routes,
    attn_gain,
    qkv_weight,
    query_gain,
    k_gain,
    w_out,
    ffn_gain,
    router,
    w_gate,
    w_up,
    w_down,
    d_out,
):
    owners = lax.axis_size("expert")
    planes = lax.axis_size("shard")
    me = lax.axis_index("expert")
    plane = lax.axis_index("shard")
    length = tokens.shape[0]
    blocks = owners * planes
    experts_all = router.shape[1]
    capacity = 3 * length * TOPK // (2 * experts_all)
    heads = QUERY_HEADS // owners
    query_cols = heads * HEAD_SIZE
    scaling = HEAD_SIZE ** (-0.5)
    both = ("expert", "shard")
    rows_in = qkv_weight.shape[0]

    kv_head = me * KEY_VALUE_HEADS // owners
    k_at = QUERY_HEADS * HEAD_SIZE + kv_head * HEAD_SIZE
    v_at = k_at + KEY_VALUE_HEADS * HEAD_SIZE
    gains = columns(
        [
            router,
            attn_gain[:, None],
            ffn_gain[:, None],
            jnp.pad(query_gain, (0, rows_in - query_gain.shape[0]))[:, None],
            jnp.pad(k_gain, (0, rows_in - k_gain.shape[0]))[:, None],
        ],
        rows_in,
    )
    mine = jnp.concatenate(
        [
            lax.dynamic_slice_in_dim(qkv_weight, me * query_cols, query_cols, 1),
            lax.dynamic_slice_in_dim(qkv_weight, k_at, HEAD_SIZE, 1),
            lax.dynamic_slice_in_dim(qkv_weight, v_at, HEAD_SIZE, 1),
            gains,
        ],
        axis=1,
    )
    gathered = lax.all_gather(mine, "shard", axis=0, tiled=True)
    qkv_cols = query_cols + 2 * HEAD_SIZE
    wqkv = gathered[:, :qkv_cols]
    router_full = gathered[:, qkv_cols : qkv_cols + experts_all]
    gain_cols = gathered[:, qkv_cols + experts_all :].astype(FULL)
    gain_one, gain_two = gain_cols[:, 0], gain_cols[:, 1]
    per = query_gain.shape[0]
    by_plane = gain_cols.reshape(planes, rows_in, -1)[:, :per]
    gain_query = by_plane[:, :, 2].reshape(-1)
    gain_key = by_plane[:, :, 3].reshape(-1)

    segment_row = segments[0]
    token_tail = columns(
        [segment_row[:, None], positions_of(segment_row)[:, None]], length
    )
    plane_rows = lax.all_gather(
        jnp.concatenate([tokens, token_tail], axis=1), "expert", axis=0, tiled=False
    )
    plane_tokens = plane_rows[:, :, :MODEL_WIDTH].astype(FULL)
    plane_segments = plane_rows[:, :, MODEL_WIDTH]
    plane_places = plane_rows[:, :, MODEL_WIDTH + 1].astype(FULL)

    out_rows = w_out.shape[0]
    first = me * query_cols
    offset = first - plane * out_rows
    if out_rows >= query_cols:
        held = (offset >= 0) & (offset < out_rows)
        piece = lax.dynamic_slice_in_dim(w_out, jnp.where(held, offset, 0), query_cols, 0)
        w_mine = lax.psum(jnp.where(held, piece, 0).astype(LOW), "shard")
    else:
        parts = query_cols // out_rows
        at = plane - me * parts
        held = (at >= 0) & (at < parts)
        spread = jnp.where(held & (jnp.arange(parts) == at)[:, None, None], w_out[None], 0)
        w_mine = lax.psum(spread.astype(LOW), "shard").reshape(query_cols, MODEL_WIDTH)

    d_tail = columns([routes], length)
    d_all = lax.all_gather(
        jnp.concatenate([d_out, d_tail], axis=1), both, axis=0, tiled=False
    )

    unit_plane, inverse_plane = unit_norm(plane_tokens)
    h1 = (unit_plane * gain_one).astype(LOW)
    projected = dot("bqd,df->bqf", h1, wqkv)
    half = HEAD_SIZE // 2
    frequency = THETA ** (-2.0 * jnp.arange(half, dtype=FULL) / HEAD_SIZE)
    angles = plane_places[:, :, None] * frequency
    cosine, sine = jnp.cos(angles), jnp.sin(angles)
    cosine_q, sine_q = cosine[:, :, None, :], sine[:, :, None, :]
    query_raw = projected[:, :, :query_cols].reshape(owners, length, heads, HEAD_SIZE)
    key_raw = projected[:, :, query_cols : query_cols + HEAD_SIZE]
    value = projected[:, :, query_cols + HEAD_SIZE :].astype(LOW)
    query_unit, query_inverse = unit_norm(query_raw)
    key_unit, key_inverse = unit_norm(key_raw)
    query = rotate(query_unit * gain_query, cosine_q, sine_q).astype(LOW)
    key = rotate(key_unit * gain_key, cosine, sine).astype(LOW)
    places = jnp.arange(length, dtype=jnp.int32)
    allowed = (plane_segments[:, :, None] == plane_segments[:, None, :]) & (
        places[None, :] <= places[:, None]
    )
    scores = dot("bqhd,bkd->bhqk", query, key) * scaling
    scores = jnp.where(allowed[:, None], scores, -1e30)
    highest = jnp.max(scores, axis=-1, keepdims=True)
    exponent = jnp.exp(scores - highest)
    probs = exponent / jnp.sum(exponent, axis=-1, keepdims=True)
    probs_low = probs.astype(LOW)
    mixed = dot("bhqk,bkd->bqhd", probs_low, value).astype(LOW)
    mixed = mixed.reshape(owners, length, query_cols)
    partial = dot("bqf,fd->bqd", mixed, w_mine).astype(LOW)
    branch = lax.psum_scatter(partial, "expert", scatter_dimension=0, tiled=False)

    middle = tokens.astype(FULL) + branch.astype(FULL)
    unit_two, inverse_two = unit_norm(middle)
    h2 = (unit_two * gain_two).astype(LOW)
    logits = dot("nd,de->ne", h2, router_full)
    chance = jax.nn.softmax(logits, axis=-1)
    named = jnp.sum(
        (routes[:, :, None] == jnp.arange(experts_all, dtype=jnp.int32)).astype(FULL), axis=1
    )
    chosen_sum = jnp.sum(named * chance, axis=1, keepdims=True)
    gates = named * chance / chosen_sum
    gates_high = gates.astype(LOW)
    gates_rest = (gates - gates_high.astype(FULL)).astype(LOW)
    h_all = lax.all_gather(
        jnp.concatenate([h2, gates_high, gates_rest], axis=1), both, axis=0, tiled=False
    )

    route_all = d_all[:, :, MODEL_WIDTH : MODEL_WIDTH + TOPK].astype(FULL)
    own_experts = (me * EXP_DEV + jnp.arange(EXP_DEV, dtype=jnp.int32)).astype(FULL)
    match = jnp.sum((route_all[:, :, :, None] == own_experts).astype(FULL), axis=2)
    earlier = (places[None, :] < places[:, None]).astype(LOW)
    rank = dot("ts,bsj->btj", earlier, match.astype(LOW))
    slot_ids = jnp.arange(capacity, dtype=jnp.int32).astype(FULL)
    place = jnp.where(match > 0, rank, -1.0).transpose(0, 2, 1)
    dispatch = (place[:, :, None, :] == slot_ids[:, None]).astype(LOW)

    def experts(h_rows, d_rows, gate_high, gate_rest, put):
        count = h_rows.shape[0]
        flat = put.reshape(count, EXP_DEV * capacity, length)
        x = dot("bst,btd->bsd", flat, h_rows).astype(LOW)
        dy = dot("bst,btd->bsd", flat, d_rows).astype(LOW)

        def by_expert(v):
            v = v.reshape(count, EXP_DEV, capacity, v.shape[-1])
            return v.transpose(1, 0, 2, 3).reshape(EXP_DEV, count * capacity, v.shape[-1])

        def by_block(v):
            v = v.reshape(EXP_DEV, count, capacity, v.shape[-1])
            return v.transpose(1, 0, 2, 3).reshape(count, EXP_DEV * capacity, v.shape[-1])

        x, dy = by_expert(x), by_expert(dy)
        gate_slot = dot("bjct,btj->jbc", put, gate_high) + dot("bjct,btj->jbc", put, gate_rest)
        gate_slot = gate_slot.reshape(EXP_DEV, count * capacity, 1)
        g = dot("erd,efd->erf", x, w_gate)
        u = dot("erd,efd->erf", x, w_up)
        da = dot("erd,edf->erf", dy, w_down)
        sigma = jax.nn.sigmoid(g)
        silu = g * sigma
        act = (silu * u).astype(LOW).astype(FULL)
        d_gate_slot = jnp.sum(act * da, axis=-1)
        act_gated = (act * gate_slot).astype(LOW)
        d_act = da * gate_slot
        dg = (d_act * u * sigma * (1.0 + g * (1.0 - sigma))).astype(LOW)
        du = (d_act * silu).astype(LOW)
        y = dot("erf,edf->erd", act_gated, w_down).astype(LOW)
        d_down = dot("erd,erf->edf", dy, act_gated)
        d_gate = dot("erf,erd->efd", dg, x)
        d_up = dot("erf,erd->efd", du, x)
        dx = (dot("erf,efd->erd", dg, w_gate) + dot("erf,efd->erd", du, w_up)).astype(LOW)
        mix = dot("bst,bsd->btd", flat, by_block(y)).astype(LOW)
        d_h = dot("bst,bsd->btd", flat, by_block(dx)).astype(LOW)
        d_g = dot(
            "bjct,jbc->btj", put.astype(FULL), d_gate_slot.reshape(EXP_DEV, count, capacity)
        )
        return mix, d_h, d_g, d_gate, d_up, d_down

    gate_cols = lax.dynamic_slice_in_dim(h_all, MODEL_WIDTH + me * EXP_DEV, EXP_DEV, 2)
    rest_cols = lax.dynamic_slice_in_dim(
        h_all, MODEL_WIDTH + experts_all + me * EXP_DEV, EXP_DEV, 2
    )
    step = min(blocks, GROUP_BLOCKS)
    mixes, d_hs, d_gs, totals = [], [], [], None
    for at in range(0, blocks, step):
        cut = slice(at, at + step)
        mix, d_h, d_g, *grads = experts(
            h_all[cut, :, :MODEL_WIDTH],
            d_all[cut, :, :MODEL_WIDTH],
            gate_cols[cut],
            rest_cols[cut],
            dispatch[cut],
        )
        mixes.append(mix)
        d_hs.append(d_h)
        d_gs.append(d_g)
        totals = grads if totals is None else [a + b for a, b in zip(totals, grads)]
    d_gate, d_up, d_down = totals
    d_g = jnp.concatenate(d_gs, axis=0)
    spread = jnp.zeros((blocks, length, TAIL), LOW)
    spread = lax.dynamic_update_slice_in_dim(spread, d_g.astype(LOW), me * EXP_DEV, 2)
    d_h_wide = jnp.concatenate([jnp.concatenate(d_hs, axis=0), spread], axis=2)

    def home(v):
        v = v.reshape(owners, planes, length, v.shape[-1])
        v = lax.psum_scatter(v, "expert", scatter_dimension=0, tiled=False)
        return lax.psum_scatter(v, "shard", scatter_dimension=0, tiled=False)

    d_home = home(d_h_wide)
    mixture = home(jnp.concatenate(mixes, axis=0))
    result = (middle + mixture.astype(FULL)).astype(LOW)

    upstream = d_out.astype(FULL)
    d_gates = d_home[:, MODEL_WIDTH : MODEL_WIDTH + experts_all].astype(FULL)
    d_chance = named * (d_gates - jnp.sum(d_gates * gates, axis=1, keepdims=True)) / chosen_sum
    d_logits = chance * (d_chance - jnp.sum(d_chance * chance, axis=1, keepdims=True))
    d_logits = d_logits.astype(LOW)
    d_h2 = d_home[:, :MODEL_WIDTH].astype(FULL) + dot("ne,de->nd", d_logits, router_full)
    d_gain_two = jnp.sum(d_h2 * unit_two, axis=0)
    d_middle = upstream + norm_back(d_h2, unit_two, inverse_two, gain_two)
    d_router = dot("nd,ne->de", h2, d_logits)

    d_branch = lax.all_gather(d_middle.astype(LOW), "expert", axis=0, tiled=False)
    d_w_out = dot("bqf,bqd->fd", mixed, d_branch).astype(LOW)
    d_mixed = dot("bqd,fd->bqf", d_branch, w_mine).astype(LOW)
    d_mixed = d_mixed.reshape(owners, length, heads, HEAD_SIZE)
    d_probs = dot("bqhd,bkd->bhqk", d_mixed, value)
    d_scores = probs * (d_probs - jnp.sum(d_probs * probs, axis=-1, keepdims=True))
    d_scores = d_scores.astype(LOW)
    d_query = dot("bhqk,bkd->bqhd", d_scores, key) * scaling
    d_key = dot("bhqk,bqhd->bkd", d_scores, query) * scaling
    d_value = dot("bhqk,bqhd->bkd", probs_low, d_mixed)
    d_query = rotate_back(d_query, cosine_q, sine_q)
    d_key = rotate_back(d_key, cosine, sine)
    d_gain_query = jnp.sum(d_query * query_unit, axis=(0, 1, 2))
    d_gain_key = jnp.sum(d_key * key_unit, axis=(0, 1))
    d_query = norm_back(d_query, query_unit, query_inverse, gain_query)
    d_key = norm_back(d_key, key_unit, key_inverse, gain_key)
    d_projected = jnp.concatenate(
        [d_query.reshape(owners, length, query_cols), d_key, d_value], axis=2
    ).astype(LOW)
    d_h1_part = dot("bqf,df->bqd", d_projected, wqkv).astype(LOW)
    d_h1 = lax.psum_scatter(d_h1_part, "expert", scatter_dimension=0, tiled=False).astype(FULL)
    resident = tokens.astype(FULL)
    unit_one, inverse_one = unit_norm(resident)
    d_gain_one = jnp.sum(d_h1 * unit_one, axis=0)
    d_tokens = (d_middle + norm_back(d_h1, unit_one, inverse_one, gain_one)).astype(LOW)

    d_wqkv = dot("bqd,bqf->df", h1, d_projected).astype(LOW)

    def by_rows(v):
        v = v.reshape(planes, per)
        return jnp.pad(v, ((0, 0), (0, rows_in - per))).reshape(-1)[:, None]

    d_tail = columns(
        [
            d_router,
            d_gain_one[:, None],
            d_gain_two[:, None],
            by_rows(d_gain_query),
            by_rows(d_gain_key),
        ],
        MODEL_WIDTH,
    )
    d_pack = lax.psum_scatter(
        jnp.concatenate([d_wqkv, d_tail], axis=1), "shard", scatter_dimension=0, tiled=True
    )
    d_pack = lax.all_gather(d_pack, "expert", axis=0, tiled=False).astype(FULL)
    d_q_cols = d_pack[:, :, :query_cols].transpose(1, 0, 2).reshape(rows_in, -1)
    d_kv = d_pack[:, :, query_cols:qkv_cols]
    d_kv = jnp.sum(d_kv.reshape(KEY_VALUE_HEADS, -1, rows_in, 2, HEAD_SIZE), axis=1)
    d_kv = d_kv.transpose(1, 2, 0, 3).reshape(rows_in, -1)
    d_qkv_weight = jnp.concatenate([d_q_cols, d_kv], axis=1)
    d_rest = jnp.sum(d_pack[:, :, qkv_cols:], axis=0)
    d_router_out = d_rest[:, :experts_all]
    d_gain_out = d_rest[:, experts_all:]

    d_w_out = d_w_out.reshape(query_cols, owners, -1)
    d_w_out = lax.all_to_all(d_w_out, "expert", split_axis=1, concat_axis=0, tiled=False)
    d_w_out = d_w_out.reshape(QUERY_HEADS * HEAD_SIZE, -1)
    d_w_out = lax.psum_scatter(d_w_out, "shard", scatter_dimension=0, tiled=True)
    d_w_out = lax.all_gather(d_w_out, "expert", axis=1, tiled=True).astype(FULL)

    return (
        result,
        d_tokens,
        d_gain_out[:, 0],
        d_qkv_weight,
        d_gain_out[:per, 2],
        d_gain_out[:per, 3],
        d_w_out,
        d_gain_out[:, 1],
        d_router_out,
        d_gate,
        d_up,
        d_down,
    )


def resident_layer(
    tokens,
    segments,
    routes,
    attn_gain,
    qkv_weight,
    query_gain,
    k_gain,
    w_out,
    ffn_gain,
    router,
    w_gate,
    w_up,
    w_down,
    d_out,
):
    owners = lax.axis_size("expert")
    planes = lax.axis_size("shard")
    me = lax.axis_index("expert")
    plane = lax.axis_index("shard")
    length = tokens.shape[0]
    blocks = owners * planes
    experts_all = router.shape[1]
    capacity = 3 * length * TOPK // (2 * experts_all)
    slots = 2 * capacity
    heads = QUERY_HEADS // owners
    query_cols = heads * HEAD_SIZE
    qkv_cols = query_cols + 2 * HEAD_SIZE
    scaling = HEAD_SIZE ** (-0.5)
    rows_in = qkv_weight.shape[0]
    per = query_gain.shape[0]

    kv_head = me * KEY_VALUE_HEADS // owners
    k_at = QUERY_HEADS * HEAD_SIZE + kv_head * HEAD_SIZE
    v_at = k_at + KEY_VALUE_HEADS * HEAD_SIZE
    mine = jnp.concatenate(
        [
            lax.dynamic_slice_in_dim(qkv_weight, me * query_cols, query_cols, 1),
            lax.dynamic_slice_in_dim(qkv_weight, k_at, HEAD_SIZE, 1),
            lax.dynamic_slice_in_dim(qkv_weight, v_at, HEAD_SIZE, 1),
            columns([router], rows_in),
        ],
        axis=1,
    )
    gain_rows = jnp.zeros((16, rows_in), LOW).at[0].set(attn_gain).at[1].set(ffn_gain)
    gain_rows = lax.dynamic_update_slice(gain_rows, query_gain[None], (2, plane * per))
    gain_rows = lax.dynamic_update_slice(gain_rows, k_gain[None], (3, plane * per))
    segment_row = segments[0]
    token_tail = columns([segment_row[:, None], positions_of(segment_row)[:, None]], length)
    token_rows = jnp.concatenate([tokens, token_tail], axis=1)
    d_rows = jnp.concatenate([d_out, columns([routes], length)], axis=1)
    half = HEAD_SIZE // 2
    frequency = THETA ** (-2.0 * jnp.arange(half, dtype=FULL) / HEAD_SIZE)
    frequency = jnp.broadcast_to(jnp.tile(frequency, 2)[None, :], (8, HEAD_SIZE))
    d_all, w_mine, w_all, gain_all, tail, h1, projected, probs_low, mixed, branch = front(
        mine, gain_rows, token_rows, w_out, d_rows, frequency, planes, owners, 5
    )
    gains = gain_all.astype(FULL)
    gain_one, gain_two = gains[:, 0].reshape(-1), gains[:, 1].reshape(-1)
    router_full = w_all[:, :, qkv_cols : qkv_cols + experts_all].reshape(MODEL_WIDTH, -1)

    places = jnp.arange(length, dtype=jnp.int32)
    route_all = d_all[..., MODEL_WIDTH : MODEL_WIDTH + TOPK].reshape(blocks, length, TOPK)
    own_experts = (me * EXP_DEV + jnp.arange(EXP_DEV, dtype=jnp.int32)).astype(FULL)
    match = jnp.sum((route_all.astype(FULL)[:, :, :, None] == own_experts).astype(FULL), axis=2)
    earlier = (places[None, :] < places[:, None]).astype(LOW)
    rank = dot("ts,bsj->btj", earlier, match.astype(LOW))
    place = jnp.where(match > 0, rank, -1.0).transpose(0, 2, 1)
    place = place.reshape(owners // 2, 2, planes, EXP_DEV, length)
    offset = (capacity * jnp.arange(2, dtype=jnp.int32)).astype(FULL)
    place = jnp.where(place >= 0, place + offset[:, None, None, None], -1.0)
    place = place.transpose(0, 2, 3, 1, 4).reshape(blocks // 2, EXP_DEV, 2 * length)
    lanes = jnp.arange(2 * experts_all, dtype=jnp.int32) % experts_all
    own = (me * EXP_DEV + jnp.arange(EXP_DEV, dtype=jnp.int32))[:, None] == lanes
    sel = jnp.broadcast_to(own.astype(FULL)[:, None, :], (EXP_DEV, 8, 2 * experts_all))

    middle = tokens.astype(FULL) + branch
    unit_two, inverse_two = unit_norm(middle)
    h2 = (unit_two * gain_two).astype(LOW)
    logits = dot("nd,de->ne", h2, router_full)
    chance = jax.nn.softmax(logits, axis=-1)
    named = jnp.sum(
        (routes[:, :, None] == jnp.arange(experts_all, dtype=jnp.int32)).astype(FULL), axis=1
    )
    chosen_sum = jnp.sum(named * chance, axis=1, keepdims=True)
    gates = named * chance / chosen_sum
    gates_high = gates.astype(LOW)
    gates_rest = (gates - gates_high.astype(FULL)).astype(LOW)
    h_rows = jnp.concatenate([h2, gates_high, gates_rest], axis=1)

    x, dy = gather_dispatch(h_rows, d_all, place, planes, slots, 1)
    y, dx, d_gate, d_up, d_down = expert_pass(sel, x, dy, w_gate, w_up, w_down.swapaxes(1, 2))
    d_down = d_down.swapaxes(1, 2)
    d_home, mixture = combine_home(place, dx, y, length, planes, slots, 2)

    upstream = d_out.astype(FULL)
    d_gates = d_home[:, MODEL_WIDTH:]
    d_gates = d_gates[:, :experts_all] + d_gates[:, experts_all:]
    d_chance = named * (d_gates - jnp.sum(d_gates * gates, axis=1, keepdims=True)) / chosen_sum
    d_logits = chance * (d_chance - jnp.sum(d_chance * chance, axis=1, keepdims=True))
    d_logits = d_logits.astype(LOW)
    d_h2 = d_home[:, :MODEL_WIDTH] + dot("ne,de->nd", d_logits, router_full)
    d_gain_two = jnp.sum(d_h2 * unit_two, axis=0)
    d_middle = upstream + norm_back(d_h2, unit_two, inverse_two, gain_two)
    d_router = dot("nd,ne->de", h2, d_logits)

    d_projected, row_sum, d_gains = back(
        d_middle.astype(LOW), w_mine, mixed, projected, probs_low, tail, gain_all, frequency,
        planes, owners, 7,
    )
    resident = tokens.astype(FULL)
    unit_one, inverse_one = unit_norm(resident)

    def by_rows(v):
        v = v.reshape(planes, per)
        return jnp.pad(v, ((0, 0), (0, rows_in - per))).reshape(-1)[:, None]

    d_tail = columns(
        [d_router, d_gain_two[:, None], by_rows(d_gains[0]), by_rows(d_gains[1])], MODEL_WIDTH
    )
    *parts, d_h1 = share_grads(
        h1, d_projected, w_all, unit_one, d_tail, row_sum, planes, owners, 4
    )
    d_w_out, d_qkv_weight, d_rest = finish_grads(*parts, owners)
    result = (middle + mixture).astype(LOW)
    d_tokens = (d_middle + norm_back(d_h1, unit_one, inverse_one, gain_one)).astype(LOW)
    d_gain_out = d_rest[:, experts_all:]
    return (
        result,
        d_tokens,
        d_gain_out[:, GAIN_ONE - experts_all],
        d_qkv_weight,
        d_gain_out[:per, 1],
        d_gain_out[:per, 2],
        d_w_out,
        d_gain_out[:, 0],
        d_rest[:, :experts_all],
        d_gate,
        d_up,
        d_down,
    )


def per_device(*args):
    blocks = lax.axis_size("expert") * lax.axis_size("shard")
    row_bytes = 2 * (MODEL_WIDTH + TAIL)
    if blocks * args[0].shape[0] * row_bytes <= RESIDENT:
        return resident_layer(*args)
    return gathered_layer(*args)


def solution(mesh):
    placed = (
        P(("expert", "shard"), None),
        P(("expert", "shard"), None),
        P(("expert", "shard"), None),
        P("shard"),
        P("shard", None),
        P("shard"),
        P("shard"),
        P("shard", None),
        P("shard"),
        P("shard", None),
        P("expert", "shard", None),
        P("expert", "shard", None),
        P("expert", None, "shard"),
        P(("expert", "shard"), None),
    )
    return jax.shard_map(
        per_device,
        mesh=mesh,
        in_specs=placed,
        out_specs=(
            P(("expert", "shard"), None),
            P(("expert", "shard"), None),
            P("shard"),
            P("shard", None),
            P("shard"),
            P("shard"),
            P("shard", None),
            P("shard"),
            P("shard", None),
            P("expert", "shard", None),
            P("expert", "shard", None),
            P("expert", None, "shard"),
        ),
        check_vma=False,
    )
```

```python
import functools

import jax
import jax.numpy as jnp
from jax import lax
from jax.experimental import pallas as pl
from jax.experimental.pallas import tpu as pltpu
from jax.sharding import PartitionSpec as P

MODEL_WIDTH = 2048
QUERY_HEADS = 32
KEY_VALUE_HEADS = 4
HEAD_SIZE = 128
TOPK = 8
EXP_DEV = 8
TAIL = 128
GAIN_QUERY, GAIN_KEY, GAIN_ONE = 65, 66, 67
GROUP_BLOCKS = 32
RESIDENT = 20 << 20

EPS = 1e-06
THETA = 1000000.0
LOW = jnp.bfloat16
FULL = jnp.float32


def unit_norm(values):
    inverse = lax.rsqrt(jnp.mean(values * values, axis=-1, keepdims=True) + EPS)
    return values * inverse, inverse


def norm_back(incoming, unit_rows, inverse, gain):
    inner = incoming * gain
    return inverse * (inner - unit_rows * jnp.mean(inner * unit_rows, axis=-1, keepdims=True))


def rotate(values, cosine, sine):
    half = values.shape[-1] // 2
    a, b = values[..., :half], values[..., half:]
    return jnp.concatenate([a * cosine - b * sine, b * cosine + a * sine], axis=-1)


def rotate_back(values, cosine, sine):
    half = values.shape[-1] // 2
    a, b = values[..., :half], values[..., half:]
    return jnp.concatenate([a * cosine + b * sine, b * cosine - a * sine], axis=-1)


def dot(spec, left, right):
    return jnp.einsum(spec, left, right, preferred_element_type=FULL)


def positions_of(segment_row):
    places = jnp.arange(segment_row.shape[0], dtype=jnp.int32)
    before = (segment_row[None, :] == segment_row[:, None]) & (places[None, :] < places[:, None])
    return jnp.sum(before.astype(jnp.int32), axis=1)


def columns(parts, rows):
    wide = jnp.concatenate([part.astype(LOW) for part in parts], axis=1)
    return jnp.pad(wide, ((0, rows - wide.shape[0]), (0, TAIL - wide.shape[1])))


MESH = pl.DeviceIdType.MESH
ANY = pl.BlockSpec(memory_space=pl.ANY)
VM = pl.BlockSpec(memory_space=pltpu.VMEM)
DMA = pltpu.SemaphoreType.DMA
VMEM_LIMIT = 58 << 20
TILE = 512


def neighbours():
    e = lax.axis_index("expert")
    core = e + 1 - 2 * (e % 2)
    flip_x = e + 2 - 4 * ((e // 2) % 2)
    flip_y = e + 4 - 8 * ((e // 4) % 2)
    diagonal = flip_x + flip_y - e
    return e, core, flip_x, flip_y, diagonal


def greet(planes):
    e, core, flip_x, flip_y, _ = neighbours()
    s = lax.axis_index("shard")
    barrier = pltpu.get_barrier_semaphore()
    for other in (core, flip_x, flip_y):
        pl.semaphore_signal(barrier, 1, device_id=(other, s), device_id_type=MESH)

    @pl.when(s > 0)
    def _():
        pl.semaphore_signal(barrier, 1, device_id=(e, s - 1), device_id_type=MESH)

    @pl.when(s < planes - 1)
    def _():
        pl.semaphore_signal(barrier, 1, device_id=(e, s + 1), device_id_type=MESH)

    inner = (s > 0) & (s < planes - 1)

    @pl.when(inner)
    def _():
        pl.semaphore_wait(barrier, 5)

    @pl.when(jnp.logical_not(inner))
    def _():
        pl.semaphore_wait(barrier, 4)


def send(source, target, send_sem, recv_sem, device):
    return pltpu.make_async_remote_copy(
        src_ref=source,
        dst_ref=target,
        send_sem=send_sem,
        recv_sem=recv_sem,
        device_id=device,
        device_id_type=MESH,
    )


def one_hot_pair(place_ref, pair, hot_ref, slots):
    rows = place_ref[pair]
    at = lax.broadcasted_iota(jnp.int32, (slots, rows.shape[1]), 0).astype(FULL)
    for j in range(EXP_DEV):
        hot_ref[pl.ds(j * slots, slots), :] = (at == rows[j : j + 1, :]).astype(LOW)


def gather_dispatch_kernel(
    planes, slots, x_ref, d_ref, place_ref, outx_ref, outd_ref,
    buf, hot, stage_x, stage_d, load_d,
    z_send, z_recv, x_send, x_recv, y_send, y_recv, c_send, c_recv, out_x, out_d, in_d,
):
    e, core, flip_x, flip_y, diagonal = neighbours()
    s = lax.axis_index("shard")
    length = x_ref.shape[0]
    half = length // 2
    width = x_ref.shape[1]
    low_half, high_half = pl.ds(0, half), pl.ds(half, half)
    greet(planes)
    buf[e, s] = x_ref[...]

    def up(sp):
        return send(buf.at[e, sp], buf.at[e, sp], z_send.at[0, sp], z_recv.at[sp], (e, s + 1))

    def down(sp):
        return send(buf.at[e, sp], buf.at[e, sp], z_send.at[1, sp], z_recv.at[sp], (e, s - 1))

    def first(sp):
        block = buf.at[e, sp]
        return [
            send(block, block, x_send.at[0, sp], x_recv.at[0, sp], (flip_x, s)),
            send(block, block, y_send.at[0, sp], y_recv.at[0, sp], (flip_y, s)),
            send(block, block, c_send.at[0, sp], c_recv.at[0, sp], (core, s)),
        ]

    def from_x(sp):
        block = buf.at[flip_x, sp]
        part = buf.at[flip_x, sp, low_half]
        return [
            send(part, part, y_send.at[1, sp], y_recv.at[1, sp], (flip_y, s)),
            send(block, block, c_send.at[1, sp], c_recv.at[1, sp], (core, s)),
        ]

    def from_y(sp):
        block = buf.at[flip_y, sp]
        part = buf.at[flip_y, sp, high_half]
        return [
            send(part, part, x_send.at[1, sp], x_recv.at[1, sp], (flip_x, s)),
            send(block, block, c_send.at[2, sp], c_recv.at[2, sp], (core, s)),
        ]

    def from_diagonal(sp):
        block = buf.at[diagonal, sp]
        return send(block, block, c_send.at[3, sp], c_recv.at[3, sp], (core, s))

    def arrived(block, sem):
        send(block, block, sem, sem, (core, s)).wait_recv()

    def plane_at(i):
        distance = (i + 1) // 2
        sign = 2 * (i % 2) - 1
        sp = s + sign * distance
        return sp, (sp >= 0) & (sp < planes) & (i >= 0) & (i <= 2 * planes - 2)

    def step_first(sp, i):
        @pl.when(i > 0)
        def _():
            arrived(buf.at[e, sp], z_recv.at[sp])

        @pl.when((sp <= s) & (s < planes - 1))
        def _():
            up(sp).start()

        @pl.when((sp >= s) & (s > 0))
        def _():
            down(sp).start()

        for copy in first(sp):
            copy.start()

    def step_second(sp):
        arrived(buf.at[flip_x, sp], x_recv.at[0, sp])
        for copy in from_x(sp):
            copy.start()
        arrived(buf.at[flip_y, sp], y_recv.at[0, sp])
        for copy in from_y(sp):
            copy.start()

    def step_third(sp):
        arrived(buf.at[diagonal, sp, low_half], y_recv.at[1, sp])
        arrived(buf.at[diagonal, sp, high_half], x_recv.at[1, sp])
        from_diagonal(sp).start()

    def copy_out(stage, out, sem, q, sp):
        rows = pl.ds(pl.multiple_of((q * planes + sp) * slots, 16), slots)
        return pltpu.make_async_copy(stage.at[q], out.at[:, rows, :], sem.at[q])

    def load(q, sp, k):
        return pltpu.make_async_copy(
            d_ref.at[2 * q + k, sp, :, pl.ds(0, MODEL_WIDTH)],
            load_d.at[q, pl.ds(k * length, length), :],
            in_d.at[q, k],
        )

    def start_loads(sp):
        for q in range(4):
            for k in range(2):
                load(q, sp, k).start()

    def dispatch(sp, i):
        for k, other in enumerate((core, core + flip_x - e, core + flip_y - e, core + diagonal - e)):
            arrived(buf.at[other, sp], c_recv.at[k, sp])

        def one(q, carry):
            one_hot_pair(place_ref, q * planes + sp, hot, slots)
            d_wide = load_d.shape[2]

            @pl.when(i > 0)
            def _():
                copy_out(stage_x, outx_ref, out_x, q, sp).wait()
                copy_out(stage_d, outd_ref, out_d, q, sp).wait()

            for k in range(2):
                load(q, sp, k).wait()

            def columns_of(at, wide, with_d):
                rows = jnp.concatenate(
                    [buf[2 * q, sp, :, at], buf[2 * q + 1, sp, :, at]], axis=0
                )
                got = jnp.dot(hot[...], rows, preferred_element_type=FULL).astype(LOW)
                stage_x[q, :, :, at] = got.reshape(EXP_DEV, slots, wide)
                if with_d:
                    got = jnp.dot(
                        hot[...], load_d[q, :, at], preferred_element_type=FULL
                    ).astype(LOW)
                    stage_d[q, :, :, at] = got.reshape(EXP_DEV, slots, wide)

            def tile(t, inner):
                columns_of(pl.ds(pl.multiple_of(t * TILE, TILE), TILE), TILE, True)
                return inner

            lax.fori_loop(0, MODEL_WIDTH // TILE, tile, 0)
            if width > MODEL_WIDTH:
                columns_of(pl.ds(MODEL_WIDTH, width - MODEL_WIDTH), width - MODEL_WIDTH, False)
            copy_out(stage_x, outx_ref, out_x, q, sp).start()
            copy_out(stage_d, outd_ref, out_d, q, sp).start()
            return carry

        lax.fori_loop(0, 4, one, 0)

    def step(i, carry):
        for lag, work in ((0, step_first), (1, step_second), (2, step_third), (3, dispatch)):
            sp, there = plane_at(i - lag)

            @pl.when(there)
            def _(sp=sp, lag=lag, work=work):
                if lag in (0, 3):
                    work(sp, i - lag)
                else:
                    work(sp)

        sp, there = plane_at(i - 2)

        @pl.when(there)
        def _():
            start_loads(sp)

        return carry

    lax.fori_loop(0, 2 * planes + 2, step, 0)

    def drain(sp, carry):
        for copy in first(sp) + from_x(sp) + from_y(sp) + [from_diagonal(sp)]:
            copy.wait_send()

        @pl.when((sp <= s) & (s < planes - 1))
        def _():
            up(sp).wait_send()

        @pl.when((sp >= s) & (s > 0))
        def _():
            down(sp).wait_send()

        return carry

    lax.fori_loop(0, planes, drain, 0)
    for q in range(4):
        copy_out(stage_x, outx_ref, out_x, q, 0).wait()
        copy_out(stage_d, outd_ref, out_d, q, 0).wait()


def gather_dispatch(rows, d_all, place, planes, slots, identity):
    owners = lax.axis_size("expert")
    length, width = rows.shape
    total = place.shape[0] * slots
    kernel = functools.partial(gather_dispatch_kernel, planes, slots)
    return pl.pallas_call(
        kernel,
        out_shape=[
            jax.ShapeDtypeStruct((EXP_DEV, total, width), LOW),
            jax.ShapeDtypeStruct((EXP_DEV, total, MODEL_WIDTH), LOW),
        ],
        in_specs=[VM, ANY, VM],
        out_specs=[ANY, ANY],
        scratch_shapes=[
            pltpu.VMEM((owners, planes, length, width), LOW),
            pltpu.VMEM((EXP_DEV * slots, 2 * length), LOW),
            pltpu.VMEM((4, EXP_DEV, slots, width), LOW),
            pltpu.VMEM((4, EXP_DEV, slots, MODEL_WIDTH), LOW),
            pltpu.VMEM((4, 2 * length, MODEL_WIDTH), LOW),
            DMA((2, planes)),
            DMA((planes,)),
            DMA((2, planes)),
            DMA((2, planes)),
            DMA((2, planes)),
            DMA((2, planes)),
            DMA((4, planes)),
            DMA((4, planes)),
            DMA((4,)),
            DMA((4,)),
            DMA((4, 2)),
        ],
        compiler_params=pltpu.CompilerParams(
            collective_id=identity, has_side_effects=True, vmem_limit_bytes=VMEM_LIMIT
        ),
    )(rows, d_all, place)


def expert_kernel(
    sel_ref, x_ref, dy_ref, wg_ref, wu_ref, wd_ref,
    y_ref, dx_ref, dwg_ref, dwu_ref, dwd_ref, a_all, dg_all, du_all, a_t, d_t,
):
    rows = x_ref.shape[1]
    step = rows
    experts = sel_ref.shape[2] // 2
    sel = sel_ref[0, 0:1, :]
    lane = lax.broadcasted_iota(jnp.int32, sel.shape, 1)
    high_sel = jnp.where(lane < experts, sel, 0.0)
    rest_sel = sel - high_sel
    nt = (((1,), (1,)), ((), ()))

    def chunk(r, carry):
        at = pl.ds(pl.multiple_of(r * step, step), step)
        x = x_ref[0, at, :MODEL_WIDTH]
        tail = x_ref[0, at, MODEL_WIDTH:].astype(FULL)
        dy = dy_ref[0, at, :]
        gate = jnp.sum(tail * sel, axis=1, keepdims=True)
        g = lax.dot_general(x, wg_ref[0], nt, preferred_element_type=FULL)
        u = lax.dot_general(x, wu_ref[0], nt, preferred_element_type=FULL)
        da = lax.dot_general(dy, wd_ref[0], nt, preferred_element_type=FULL)
        sigma = 1.0 / (1.0 + jnp.exp(-g))
        silu = g * sigma
        act = (silu * u).astype(LOW).astype(FULL)
        d_gate = jnp.sum(act * da, axis=1, keepdims=True)
        d_act = da * gate
        a_all[at, :] = (act * gate).astype(LOW)
        dg_all[at, :] = (d_act * u * sigma * (1.0 + g * (1.0 - sigma))).astype(LOW)
        du_all[at, :] = (d_act * silu).astype(LOW)
        high = d_gate.astype(LOW).astype(FULL)
        dx_ref[0, at, MODEL_WIDTH:] = (high * high_sel + (d_gate - high) * rest_sel).astype(LOW)
        y_ref[0, at, :] = jnp.dot(
            a_all[at, :], wd_ref[0], preferred_element_type=FULL
        ).astype(LOW)
        dx_ref[0, at, :MODEL_WIDTH] = (
            jnp.dot(dg_all[at, :], wg_ref[0], preferred_element_type=FULL)
            + jnp.dot(du_all[at, :], wu_ref[0], preferred_element_type=FULL)
        ).astype(LOW)
        return carry

    lax.fori_loop(0, rows // step, chunk, 0)
    hidden = a_t.shape[0]
    a_t[...] = a_all[...].T
    d_t[:hidden, :] = dg_all[...].T
    d_t[hidden:, :] = du_all[...].T

    def tile(t, carry):
        at = pl.ds(pl.multiple_of(t * TILE, TILE), TILE)
        x = x_ref[0, :, at]
        got = jnp.dot(d_t[...], x, preferred_element_type=FULL)
        dwg_ref[0, :, at] = got[:hidden]
        dwu_ref[0, :, at] = got[hidden:]
        dwd_ref[0, :, at] = jnp.dot(a_t[...], dy_ref[0, :, at], preferred_element_type=FULL)
        return carry

    lax.fori_loop(0, MODEL_WIDTH // TILE, tile, 0)


def expert_pass(sel, x, dy, w_gate, w_up, w_down):
    rows, width = x.shape[1:]
    hidden = w_gate.shape[1]

    def spec(*shape):
        return pl.BlockSpec((1,) + shape, lambda j: (j, 0, 0))

    def out(*shape, dtype=LOW):
        return jax.ShapeDtypeStruct((EXP_DEV,) + shape, dtype)

    return pl.pallas_call(
        expert_kernel,
        grid=(EXP_DEV,),
        in_specs=[
            spec(*sel.shape[1:]),
            spec(rows, width),
            spec(rows, MODEL_WIDTH),
            spec(hidden, MODEL_WIDTH),
            spec(hidden, MODEL_WIDTH),
            spec(hidden, MODEL_WIDTH),
        ],
        out_specs=[
            spec(rows, MODEL_WIDTH),
            spec(rows, width),
            spec(hidden, MODEL_WIDTH),
            spec(hidden, MODEL_WIDTH),
            spec(hidden, MODEL_WIDTH),
        ],
        out_shape=[
            out(rows, MODEL_WIDTH),
            out(rows, width),
            out(hidden, MODEL_WIDTH, dtype=FULL),
            out(hidden, MODEL_WIDTH, dtype=FULL),
            out(hidden, MODEL_WIDTH, dtype=FULL),
        ],
        scratch_shapes=[pltpu.VMEM((rows, hidden), LOW)] * 3
        + [pltpu.VMEM((hidden, rows), LOW), pltpu.VMEM((2 * hidden, rows), LOW)],
        compiler_params=pltpu.CompilerParams(vmem_limit_bytes=VMEM_LIMIT),
        cost_estimate=pl.CostEstimate(
            flops=EXP_DEV * rows * MODEL_WIDTH * hidden * 18,
            bytes_accessed=160 << 20,
            transcendentals=EXP_DEV * rows * hidden,
        ),
    )(sel, x, dy, w_gate, w_up, w_down)


def combine_home_kernel(
    planes, slots, hot_ref, v_ref, m_ref, out_ref, mix_ref,
    hot, load, mine, away, c_in, x_in, y_in, x_half, y_half, u_in, d_in,
    hot_sem, in_sem, free, c_send, c_recv, x_send, x_recv, y_send, y_recv, z_send, z_recv,
):
    e, core, flip_x, flip_y, diagonal = neighbours()
    s = lax.axis_index("shard")
    q_own, q_x, q_y, q_d = e // 2, flip_x // 2, flip_y // 2, diagonal // 2
    parity = e % 2
    length, width = out_ref.shape
    half = length // 2
    low_half, high_half = pl.ds(0, half), pl.ds(half, half)
    order = (q_d, q_x, q_y, q_own)
    spans = (pl.ds(0, width), pl.ds(0, MODEL_WIDTH))

    def fetch(kind, k, sp):
        rows = pl.ds(pl.multiple_of((order[k] * planes + sp) * slots, 16), slots)
        if kind == 0:
            return pltpu.make_async_copy(v_ref.at[:, rows, :], load.at[k % 2], in_sem.at[k % 2])
        return pltpu.make_async_copy(
            m_ref.at[:, rows, :], load.at[k % 2, :, :, pl.ds(0, MODEL_WIDTH)], in_sem.at[k % 2]
        )

    def fetch_hot(k, sp):
        return pltpu.make_async_copy(
            hot_ref.at[order[k] * planes + sp], hot.at[k % 2], hot_sem.at[k % 2]
        )

    def to_core(kind, q, sp):
        return send(
            away.at[q, sp, :, spans[kind]], c_in.at[q, sp, :, spans[kind]], c_send.at[kind, q, sp], c_recv.at[kind, q, sp],
            (core, s),
        )

    def halves(kind, sp):
        return [
            send(
                mine.at[q_d, sp, low_half, spans[kind]], y_half.at[kind, sp, :, spans[kind]],
                y_send.at[kind, 0, sp], y_recv.at[kind, 0, sp], (flip_y, s),
            ),
            send(
                mine.at[q_d, sp, high_half, spans[kind]], x_half.at[kind, sp, :, spans[kind]],
                x_send.at[kind, 0, sp], x_recv.at[kind, 0, sp], (flip_x, s),
            ),
        ]

    def to_x(kind, sp):
        return send(
            mine.at[q_x, sp, :, spans[kind]], x_in.at[kind, sp, :, spans[kind]], x_send.at[kind, 1, sp], x_recv.at[kind, 1, sp],
            (flip_x, s),
        )

    def to_y(kind, sp):
        return send(
            mine.at[q_y, sp, :, spans[kind]], y_in.at[kind, sp, :, spans[kind]], y_send.at[kind, 1, sp], y_recv.at[kind, 1, sp],
            (flip_y, s),
        )

    def up(kind, sp):
        return send(
            mine.at[q_own, sp, :, spans[kind]], u_in.at[kind, sp, :, spans[kind]], z_send.at[kind, 0, sp], z_recv.at[kind, 0, sp],
            (e, s + 1),
        )

    def down(kind, sp):
        return send(
            mine.at[q_own, sp, :, spans[kind]], d_in.at[kind, sp, :, spans[kind]], z_send.at[kind, 1, sp], z_recv.at[kind, 1, sp],
            (e, s - 1),
        )

    def settled(kind, sp):
        for q in range(4):
            to_core(kind, q, sp).wait_send()
        for copy in halves(kind, sp) + [to_x(kind, sp), to_y(kind, sp)]:
            copy.wait_send()

        @pl.when(sp > s)
        def _():
            up(kind, sp).wait_send()

        @pl.when(sp < s)
        def _():
            down(kind, sp).wait_send()

    def arrived(block, sem):
        send(block, block, sem, sem, (core, s)).wait_recv()

    def plane_at(i):
        back = 2 * planes - 2 - i
        sp = s + (2 * (back % 2) - 1) * ((back + 1) // 2)
        return sp, (sp >= 0) & (sp < planes) & (i >= 0) & (back >= 0)

    def add(target, *others):
        if len(others) == 1:
            target[...] = target[...] + others[0][...]
            return
        total = target[...].astype(FULL)
        for other in others:
            total = total + other[...].astype(FULL)
        target[...] = total.astype(LOW)

    def work(kind, sp):
        if kind == 1:
            settled(0, sp)
            pl.semaphore_wait(free.at[sp], 1)
        for k in range(2):
            fetch_hot(k, sp).start()
            fetch(kind, k, sp).start()
        for k, q in enumerate(order):
            fetch_hot(k, sp).wait()
            fetch(kind, k, sp).wait()

            def part(at, wide, q=q, k=k):
                rows = load[k % 2, :, :, at].reshape(EXP_DEV * slots, wide)
                got = jnp.dot(hot[k % 2], rows, preferred_element_type=FULL).astype(LOW)
                got = got.reshape(2, length, wide)

                @pl.when(parity == 0)
                def _():
                    mine[q, sp, :, at] = got[0]
                    away[q, sp, :, at] = got[1]

                @pl.when(parity == 1)
                def _():
                    mine[q, sp, :, at] = got[1]
                    away[q, sp, :, at] = got[0]

            def tile(t, inner, part=part):
                part(pl.ds(pl.multiple_of(t * TILE, TILE), TILE), TILE)
                return inner

            lax.fori_loop(0, MODEL_WIDTH // TILE, tile, 0)
            if kind == 0 and width > MODEL_WIDTH:
                part(pl.ds(MODEL_WIDTH, width - MODEL_WIDTH), width - MODEL_WIDTH)
            to_core(kind, q, sp).start()
            if k < 2:
                fetch_hot(k + 2, sp).start()
                fetch(kind, k + 2, sp).start()

    def pairs(kind, sp):
        for k, q in enumerate(order):
            arrived(c_in.at[q, sp, :, spans[kind]], c_recv.at[kind, q, sp])
            add(mine.at[q, sp, :, spans[kind]], c_in.at[q, sp, :, spans[kind]])
            if k == 0:
                for copy in halves(kind, sp):
                    copy.start()
        if kind == 0:
            pl.semaphore_signal(free.at[sp], 1, device_id=(core, s), device_id_type=MESH)

    def sides(kind, sp):
        arrived(y_half.at[kind, sp, :, spans[kind]], y_recv.at[kind, 0, sp])
        add(mine.at[q_x, sp, low_half, spans[kind]], y_half.at[kind, sp, :, spans[kind]])
        to_x(kind, sp).start()
        arrived(x_half.at[kind, sp, :, spans[kind]], x_recv.at[kind, 0, sp])
        add(mine.at[q_y, sp, high_half, spans[kind]], x_half.at[kind, sp, :, spans[kind]])
        to_y(kind, sp).start()

    def line(kind, sp):
        arrived(x_in.at[kind, sp, :, spans[kind]], x_recv.at[kind, 1, sp])
        arrived(y_in.at[kind, sp, :, spans[kind]], y_recv.at[kind, 1, sp])
        add(
            mine.at[q_own, sp, :, spans[kind]],
            x_in.at[kind, sp, :, spans[kind]],
            y_in.at[kind, sp, :, spans[kind]],
        )

        @pl.when((sp >= s) & (s > 0))
        def _():
            arrived(u_in.at[kind, sp, :, spans[kind]], z_recv.at[kind, 0, sp])
            add(mine.at[q_own, sp, :, spans[kind]], u_in.at[kind, sp, :, spans[kind]])

        @pl.when((sp <= s) & (s < planes - 1))
        def _():
            arrived(d_in.at[kind, sp, :, spans[kind]], z_recv.at[kind, 1, sp])
            add(mine.at[q_own, sp, :, spans[kind]], d_in.at[kind, sp, :, spans[kind]])

        @pl.when(sp > s)
        def _():
            up(kind, sp).start()

        @pl.when(sp < s)
        def _():
            down(kind, sp).start()

        @pl.when(sp == s)
        def _():
            if kind == 0:
                out_ref[...] = mine[q_own, sp].astype(FULL)
            else:
                mix_ref[...] = mine[q_own, sp, :, :MODEL_WIDTH].astype(FULL)

    greet(planes)
    span = 2 * planes - 1

    def step(t, carry):
        for lag, job in ((0, work), (1, pairs), (2, sides), (3, line)):
            for kind in range(2):
                sp, there = plane_at(t - lag - kind * span)

                @pl.when(there)
                def _(sp=sp, job=job, kind=kind):
                    job(kind, sp)

        return carry

    lax.fori_loop(0, 2 * span + 3, step, 0)

    def drain(sp, carry):
        settled(1, sp)
        return carry

    lax.fori_loop(0, planes, drain, 0)


def combine_home(hot, v, m, length, planes, slots, identity):
    width = v.shape[2]
    block = (planes, length, width)
    part = (planes, length // 2, width)
    return pl.pallas_call(
        functools.partial(combine_home_kernel, planes, slots),
        out_shape=[
            jax.ShapeDtypeStruct((length, width), FULL),
            jax.ShapeDtypeStruct((length, MODEL_WIDTH), FULL),
        ],
        in_specs=[ANY, ANY, ANY],
        out_specs=[VM, VM],
        scratch_shapes=[
            pltpu.VMEM((2,) + hot.shape[1:], LOW),
            pltpu.VMEM((2, EXP_DEV, slots, width), LOW),
            pltpu.VMEM((4,) + block, LOW),
            pltpu.VMEM((4,) + block, LOW),
            pltpu.VMEM((4,) + block, LOW),
            pltpu.VMEM((2,) + block, LOW),
            pltpu.VMEM((2,) + block, LOW),
            pltpu.VMEM((2,) + part, LOW),
            pltpu.VMEM((2,) + part, LOW),
            pltpu.VMEM((2,) + block, LOW),
            pltpu.VMEM((2,) + block, LOW),
            DMA((2,)),
            DMA((2,)),
            pltpu.SemaphoreType.REGULAR((planes,)),
            DMA((2, 4, planes)),
            DMA((2, 4, planes)),
            DMA((2, 2, planes)),
            DMA((2, 2, planes)),
            DMA((2, 2, planes)),
            DMA((2, 2, planes)),
            DMA((2, 2, planes)),
            DMA((2, 2, planes)),
        ],
        compiler_params=pltpu.CompilerParams(
            collective_id=identity, has_side_effects=True, vmem_limit_bytes=VMEM_LIMIT
        ),
    )(hot, v, m)


def greet_plane(planes, owners):
    e, s = lax.axis_index("expert"), lax.axis_index("shard")
    barrier = pltpu.get_barrier_semaphore()
    for o in range(1, owners):
        pl.semaphore_signal(
            barrier, 1, device_id=(lax.rem(e + o, owners), s), device_id_type=MESH
        )

    @pl.when(s > 0)
    def _():
        pl.semaphore_signal(barrier, 1, device_id=(e, s - 1), device_id_type=MESH)

    @pl.when(s < planes - 1)
    def _():
        pl.semaphore_signal(barrier, 1, device_id=(e, s + 1), device_id_type=MESH)

    inner = (s > 0) & (s < planes - 1)

    @pl.when(inner)
    def _():
        pl.semaphore_wait(barrier, owners + 1)

    @pl.when(jnp.logical_not(inner))
    def _():
        pl.semaphore_wait(barrier, owners)


def gather_steps(at, cut, source, x_send, x_recv, y_send, y_recv, c_send, c_recv):
    e, core, flip_x, flip_y, diagonal = neighbours()
    s = lax.axis_index("shard")

    def arrived(block, sem):
        send(block, block, sem, sem, (core, s)).wait_recv()

    def first():
        return [
            send(source, at(e), x_send(0), x_recv(0), (flip_x, s)),
            send(source, at(e), y_send(0), y_recv(0), (flip_y, s)),
            send(source, at(e), c_send(0), c_recv(0), (core, s)),
        ]

    def from_x():
        return [
            send(cut(flip_x, 0), cut(flip_x, 0), y_send(1), y_recv(1), (flip_y, s)),
            send(at(flip_x), at(flip_x), c_send(1), c_recv(1), (core, s)),
        ]

    def from_y():
        return [
            send(cut(flip_y, 1), cut(flip_y, 1), x_send(1), x_recv(1), (flip_x, s)),
            send(at(flip_y), at(flip_y), c_send(2), c_recv(2), (core, s)),
        ]

    def from_diagonal():
        return [send(at(diagonal), at(diagonal), c_send(3), c_recv(3), (core, s))]

    def begin():
        for copy in first():
            copy.start()

    def second():
        arrived(at(flip_x), x_recv(0))
        for copy in from_x():
            copy.start()
        arrived(at(flip_y), y_recv(0))
        for copy in from_y():
            copy.start()

    def third():
        arrived(cut(diagonal, 0), y_recv(1))
        arrived(cut(diagonal, 1), x_recv(1))
        for copy in from_diagonal():
            copy.start()

    def last():
        for k, lane in enumerate((core, core + flip_x - e, core + flip_y - e, core + diagonal - e)):
            arrived(at(lane), c_recv(k))

    def sent():
        for copy in first() + from_x() + from_y() + from_diagonal():
            copy.wait_send()

    return begin, second, third, last, sent


def rope_tables(places, frequency):
    angles = places * frequency
    lane = lax.broadcasted_iota(jnp.int32, angles.shape, 1)
    sine = jnp.sin(angles)
    return jnp.cos(angles), jnp.where(lane < HEAD_SIZE // 2, -sine, sine)


def half_turn(v):
    return pltpu.roll(v, HEAD_SIZE // 2, 1)


def front_kernel(
    planes, owners, w_ref, router_ref, gain_ref, tok_ref, d_ref, freq_ref, out_ref,
    d_all, w_out_all, w_all_out, r_all, gains, tail_ref, h1_ref, proj_ref, probs_ref, mixed_ref, branch_ref,
    w_all, tok_all, w_mine, q_rows, mine, away, c_in, x_in, y_in, x_half, y_half,
    keep_sem, w_send, w_recv, v_send, v_recv, k_send, k_recv, r_send, r_recv, g_send, g_recv,
    o_send, o_recv, z_send, z_recv, rx_send, rx_recv, ry_send, ry_recv, rc_send, rc_recv,
    tx_send, tx_recv, ty_send, ty_recv, tc_send, tc_recv,
    dx_send, dx_recv, dy_send, dy_recv, dc_send, dc_recv,
    px_send, px_recv, py_send, py_recv, pc_send, pc_recv,
):
    e, core, flip_x, flip_y, diagonal = neighbours()
    s = lax.axis_index("shard")
    lanes = owners // planes
    home = e // lanes
    length = tok_ref.shape[0]
    half = length // 2
    count = w_mine.shape[0]
    heads = count // HEAD_SIZE
    pieces = 8
    out_part = count // pieces
    deep = w_ref.shape[0]
    query_cols = count
    kv_at = pl.ds(pl.multiple_of(count + HEAD_SIZE * (e % 2), HEAD_SIZE), HEAD_SIZE)

    def arrived(block, sem):
        send(block, block, sem, sem, (core, s)).wait_recv()

    def w_copy(sp, way):
        block = w_all.at[sp, :, pl.ds(0, query_cols)]
        return send(block, block, w_send.at[way, sp], w_recv.at[sp], (e, s + 1 - 2 * way))

    def v_copy(sp, way):
        block = w_all.at[sp, :, kv_at]
        return send(block, block, v_send.at[way, sp], v_recv.at[sp], (e, s + 1 - 2 * way))

    def r_copy(sp, way):
        block = r_all.at[e, sp]
        return send(block, block, r_send.at[way, sp], r_recv.at[sp], (e, s + 1 - 2 * way))

    def k_copy(sp):
        block = w_all.at[sp, :, kv_at]
        return send(block, block, k_send.at[sp], k_recv.at[sp], (core, s))

    def g_copy(sp, way):
        block = gains.at[sp]
        return send(block, block, g_send.at[way, sp], g_recv.at[sp], (e, s + 1 - 2 * way))

    def d_copy(sp, way):
        block = d_all.at[e, sp]
        return send(block, block, z_send.at[way, sp], z_recv.at[sp], (e, s + 1 - 2 * way))

    def o_copy(k, way):
        block = w_mine.at[pl.ds(k * out_part, out_part)]
        return send(block, block, o_send.at[way, k], o_recv.at[k], (e, s + 1 - 2 * way))

    t_begin, t_second, t_third, t_last, t_sent = gather_steps(
        lambda lane: tok_all.at[lane],
        lambda lane, k: tok_all.at[lane, pl.ds(k * half, half)],
        tok_ref,
        lambda k: tx_send.at[k],
        lambda k: tx_recv.at[k],
        lambda k: ty_send.at[k],
        lambda k: ty_recv.at[k],
        lambda k: tc_send.at[k],
        lambda k: tc_recv.at[k],
    )

    r_half = planes // 2
    r_begin, r_second, r_third, r_last, r_sent = gather_steps(
        lambda lane: r_all.at[lane],
        lambda lane, k: r_all.at[lane, pl.ds(k * r_half, r_half)],
        r_all.at[e],
        lambda k: rx_send.at[k],
        lambda k: rx_recv.at[k],
        lambda k: ry_send.at[k],
        lambda k: ry_recv.at[k],
        lambda k: rc_send.at[k],
        lambda k: rc_recv.at[k],
    )

    def d_rows(sp):
        return gather_steps(
            lambda lane: d_all.at[lane, sp],
            lambda lane, k: d_all.at[lane, sp, pl.ds(k * half, half)],
            d_all.at[e, sp],
            lambda k: dx_send.at[k, sp],
            lambda k: dx_recv.at[k, sp],
            lambda k: dy_send.at[k, sp],
            lambda k: dy_recv.at[k, sp],
            lambda k: dc_send.at[k, sp],
            lambda k: dc_recv.at[k, sp],
        )

    keep_d = pltpu.make_async_copy(d_ref, d_all.at[e, s], keep_sem.at[0])
    rows = pl.ds(pl.multiple_of((e - home * lanes) * count, 16), count)
    load_o = pltpu.make_async_copy(out_ref.at[rows], w_mine, keep_sem.at[1])
    keep_w = pltpu.make_async_copy(w_all, w_all_out, keep_sem.at[2])
    keep_o = pltpu.make_async_copy(w_mine, w_out_all, keep_sem.at[3])
    keep_d.start()

    @pl.when(s == home)
    def _():
        load_o.start()

    w_all[s, :, :query_cols] = w_ref[:, :query_cols]
    w_all[s, :, kv_at] = w_ref[:, query_cols:]
    r_all[e, s] = router_ref[...]
    gains[s] = gain_ref[...]
    tok_all[e] = tok_ref[...]
    greet(planes)

    def both_ways(copy, sp):
        @pl.when((sp <= s) & (s < planes - 1))
        def _():
            copy(sp, 0).start()

        @pl.when((sp >= s) & (s > 0))
        def _():
            copy(sp, 1).start()

    def plane_at(i):
        sp = s + (2 * (i % 2) - 1) * ((i + 1) // 2)
        return sp, (sp >= 0) & (sp < planes) & (i >= 0) & (i <= 2 * planes - 2)

    def out_step(k):
        @pl.when(s != home)
        def _():
            arrived(w_mine.at[pl.ds(k * out_part, out_part)], o_recv.at[k])

        @pl.when((s >= home) & (s < planes - 1))
        def _():
            o_copy(k, 0).start()

        @pl.when((s <= home) & (s > 0))
        def _():
            o_copy(k, 1).start()

    t_begin()
    both_ways(g_copy, s)
    keep_d.wait()
    both_ways(d_copy, s)
    both_ways(w_copy, s)
    both_ways(v_copy, s)
    both_ways(r_copy, s)
    k_copy(s).start()
    d_rows(s)[0]()

    def weights(i, carry):
        sp, there = plane_at(i)

        @pl.when(there & (i > 0))
        def _():
            arrived(gains.at[sp], g_recv.at[sp])
            both_ways(g_copy, sp)
            arrived(d_all.at[e, sp], z_recv.at[sp])
            both_ways(d_copy, sp)
            d_rows(sp)[0]()
            arrived(w_all.at[sp, :, pl.ds(0, query_cols)], w_recv.at[sp])
            both_ways(w_copy, sp)
            arrived(w_all.at[sp, :, kv_at], v_recv.at[sp])
            both_ways(v_copy, sp)
            k_copy(sp).start()
            arrived(r_all.at[e, sp], r_recv.at[sp])
            both_ways(r_copy, sp)

        @pl.when(i == 1)
        def _():
            t_second()

        @pl.when(i == 2)
        def _():
            t_third()

        @pl.when((i == 4) & (s == home))
        def _():
            load_o.wait()
            for k in range(pieces):
                out_step(k)

        return carry

    lax.fori_loop(1, 2 * planes - 1, weights, 0)
    r_begin()
    t_last()
    other_kv = pl.ds(pl.multiple_of(count + HEAD_SIZE * (1 - e % 2), HEAD_SIZE), HEAD_SIZE)
    for sp in range(planes):
        arrived(w_all.at[sp, :, other_kv], k_recv.at[sp])
    keep_w.start()

    def distant(n):
        return (s - home == n) | (home - s == n)

    gain_query = gains[0, 2:3, :HEAD_SIZE].astype(FULL)
    gain_key = gains[0, 3:4, :HEAD_SIZE].astype(FULL)
    for sp in range(1, planes):
        gain_query = gain_query + gains[sp, 2:3, :HEAD_SIZE].astype(FULL)
        gain_key = gain_key + gains[sp, 3:4, :HEAD_SIZE].astype(FULL)
    row = lax.broadcasted_iota(jnp.int32, (length, length), 0).astype(FULL)
    column = lax.broadcasted_iota(jnp.int32, (length, length), 1).astype(FULL)

    def attend(b, carry):
        x = tok_all[b, :, :MODEL_WIDTH].astype(FULL)
        inverse = lax.rsqrt(jnp.mean(x * x, axis=1, keepdims=True) + EPS)
        total = jnp.zeros((length, w_all.shape[2]), FULL)
        for sp in range(planes):
            at = slice(sp * deep, (sp + 1) * deep)
            part = x[:, at] * inverse * gains[sp, 0:1, :].astype(FULL)
            part = part.astype(LOW)
            h1_ref[b, :, at] = part
            total = total + jnp.dot(part, w_all[sp], preferred_element_type=FULL)
        proj_ref[b] = total
        tail_ref[b] = tok_all[b, :, MODEL_WIDTH:]
        places = tok_all[b, :, MODEL_WIDTH:].astype(FULL)[:, 1:2]
        cosine, sine = rope_tables(places, freq_ref[0:1, :])

        def normed(v, gain):
            v = v * lax.rsqrt(jnp.mean(v * v, axis=1, keepdims=True) + EPS) * gain
            return (v * cosine + half_turn(v) * sine).astype(LOW)

        for h in range(heads):
            at = slice(h * HEAD_SIZE, (h + 1) * HEAD_SIZE)
            q_rows[h * length : (h + 1) * length, :] = normed(total[:, at], gain_query)
        key = normed(total[:, count : count + HEAD_SIZE], gain_key)
        value = total[:, count + HEAD_SIZE :].astype(LOW)
        scores = lax.dot_general(
            q_rows[...], key, (((1,), (1,)), ((), ())), preferred_element_type=FULL
        ) * (HEAD_SIZE**-0.5)
        allowed = (column <= row) & (column >= row - places)
        scores = jnp.where(jnp.concatenate([allowed] * heads, axis=0), scores, -1e30)
        exponent = jnp.exp(scores - jnp.max(scores, axis=1, keepdims=True))
        probs = (exponent / jnp.sum(exponent, axis=1, keepdims=True)).astype(LOW)
        probs_ref[b] = probs
        mixed = jnp.dot(probs, value, preferred_element_type=FULL).astype(LOW)
        for h in range(heads):
            at = slice(h * HEAD_SIZE, (h + 1) * HEAD_SIZE)
            mixed_ref[b, :, at] = mixed[h * length : (h + 1) * length]

        for lag, stage in ((0, 1), (2, 2)):
            sp, there = plane_at(b - lag)

            @pl.when(there)
            def _(sp=sp, stage=stage):
                d_rows(sp)[stage]()

        for k in range(pieces):

            @pl.when((b == k) & distant(1))
            def _(k=k):
                out_step(k)

        for k in range(5):

            @pl.when((b == 3 + k) & distant(2))
            def _(k=k):
                out_step(k)

        return carry

    lax.fori_loop(0, owners, attend, 0)
    for i in range(owners - 2, 2 * planes - 1):
        sp, there = plane_at(i)

        @pl.when(there)
        def _(sp=sp):
            d_rows(sp)[2]()


    @pl.when(distant(2))
    def _():
        for k in range(5, pieces):
            out_step(k)

    r_second()
    for n in range(3, planes):

        @pl.when(distant(n))
        def _():
            for k in range(pieces):
                out_step(k)

    keep_o.start()
    begin, middle, finish, sent = project_steps(
        False, mixed_ref, w_mine, branch_ref, mine, away, c_in, x_in, y_in, x_half, y_half,
        pc_send, pc_recv, px_send, px_recv, py_send, py_recv,
    )
    begin()
    r_third()
    middle()
    finish()
    r_last()
    t_sent()
    r_sent()
    sent()

    def settled(copy, sp):
        @pl.when((sp <= s) & (s < planes - 1))
        def _():
            copy(sp, 0).wait_send()

        @pl.when((sp >= s) & (s > 0))
        def _():
            copy(sp, 1).wait_send()

    def drain(sp, carry):
        d_rows(sp)[3]()
        d_rows(sp)[4]()
        settled(w_copy, sp)
        settled(v_copy, sp)
        settled(r_copy, sp)
        k_copy(sp).wait_send()
        settled(g_copy, sp)
        settled(d_copy, sp)
        return carry

    lax.fori_loop(0, planes, drain, 0)
    for k in range(pieces):

        @pl.when((s >= home) & (s < planes - 1))
        def _(k=k):
            o_copy(k, 0).wait_send()

        @pl.when((s <= home) & (s > 0))
        def _(k=k):
            o_copy(k, 1).wait_send()

    keep_w.wait()
    keep_o.wait()


def front(w, router, gain_rows, tokens, w_out, d_rows, frequency, planes, owners, identity):
    def out(*shape, dtype=LOW):
        return jax.ShapeDtypeStruct(shape, dtype)

    length = tokens.shape[0]
    count = w_out.shape[0] * planes // owners
    qkv_cols = count + 2 * HEAD_SIZE
    block = (length, MODEL_WIDTH)
    part = (length // 2, MODEL_WIDTH)
    return pl.pallas_call(
        functools.partial(front_kernel, planes, owners),
        out_shape=[
            out(owners, planes, *d_rows.shape),
            out(count, MODEL_WIDTH),
            out(planes, w.shape[0], qkv_cols),
            out(owners, planes, *router.shape),
            out(planes, *gain_rows.shape),
            out(owners, length, TAIL),
            out(owners, length, MODEL_WIDTH),
            out(owners, length, qkv_cols, dtype=FULL),
            out(owners, length * count // HEAD_SIZE, length),
            out(owners, length, count),
            out(length, MODEL_WIDTH, dtype=FULL),
        ],
        in_specs=[VM, VM, VM, VM, VM, VM, ANY],
        out_specs=[ANY, ANY, ANY, VM, VM, VM, VM, VM, VM, VM, VM],
        scratch_shapes=[
            pltpu.VMEM((planes, w.shape[0], qkv_cols), LOW),
            pltpu.VMEM((owners,) + tokens.shape, LOW),
            pltpu.VMEM((count, MODEL_WIDTH), LOW),
            pltpu.VMEM((length * count // HEAD_SIZE, HEAD_SIZE), LOW),
            pltpu.VMEM((4,) + block, LOW),
            pltpu.VMEM((4,) + block, LOW),
            pltpu.VMEM((4,) + block, LOW),
            pltpu.VMEM(block, LOW),
            pltpu.VMEM(block, LOW),
            pltpu.VMEM(part, LOW),
            pltpu.VMEM(part, LOW),
            DMA((4,)),
            DMA((2, planes)),
            DMA((planes,)),
            DMA((2, planes)),
            DMA((planes,)),
            DMA((planes,)),
            DMA((planes,)),
            DMA((2, planes)),
            DMA((planes,)),
            DMA((2, planes)),
            DMA((planes,)),
            DMA((2, 8)),
            DMA((8,)),
            DMA((2, planes)),
            DMA((planes,)),
            DMA((2,)),
            DMA((2,)),
            DMA((2,)),
            DMA((2,)),
            DMA((4,)),
            DMA((4,)),
            DMA((2,)),
            DMA((2,)),
            DMA((2,)),
            DMA((2,)),
            DMA((4,)),
            DMA((4,)),
            DMA((2, planes)),
            DMA((2, planes)),
            DMA((2, planes)),
            DMA((2, planes)),
            DMA((4, planes)),
            DMA((4, planes)),
            DMA((2,)),
            DMA((2,)),
            DMA((2,)),
            DMA((2,)),
            DMA((4,)),
            DMA((4,)),
        ],
        compiler_params=pltpu.CompilerParams(
            collective_id=identity, has_side_effects=True, vmem_limit_bytes=VMEM_LIMIT
        ),
    )(w, router, gain_rows, tokens, d_rows, frequency, w_out)


def project_steps(
    turned, rows_ref, w_ref, out_ref, mine, away, c_in, x_in, y_in, x_half, y_half,
    cs, cr, xs, xr, ys, yr,
):
    e, core, flip_x, flip_y, diagonal = neighbours()
    s = lax.axis_index("shard")
    q_own, q_x, q_y, q_d = e // 2, flip_x // 2, flip_y // 2, diagonal // 2
    parity = e % 2
    half = out_ref.shape[0] // 2
    low_half, high_half = pl.ds(0, half), pl.ds(half, half)
    across = (((1,), (1 if turned else 0,)), ((), ()))
    order = (q_d, q_x, q_y, q_own)

    def arrived(block, sem):
        send(block, block, sem, sem, (core, s)).wait_recv()

    def add(target, *others):
        total = target[...].astype(FULL)
        for other in others:
            total = total + other[...].astype(FULL)
        target[...] = total.astype(LOW)

    def to_core(q):
        return send(away.at[q], c_in.at[q], cs.at[q], cr.at[q], (core, s))

    def compute(q, lane, into):
        rows = rows_ref[2 * q + lane]

        def tile(t, carry):
            at = pl.ds(pl.multiple_of(t * TILE, TILE), TILE)
            if turned:
                deep = w_ref.shape[1]
                w = w_ref[t * TILE // deep, :, : rows.shape[1]]
            else:
                w = w_ref[:, at]
            into[q, :, at] = lax.dot_general(
                rows, w, across, preferred_element_type=FULL
            ).astype(LOW)
            return carry

        lax.fori_loop(0, MODEL_WIDTH // TILE, tile, 0)

    halves = [
        send(mine.at[q_d, low_half], y_half, ys.at[0], yr.at[0], (flip_y, s)),
        send(mine.at[q_d, high_half], x_half, xs.at[0], xr.at[0], (flip_x, s)),
    ]
    to_x = send(mine.at[q_x], x_in, xs.at[1], xr.at[1], (flip_x, s))
    to_y = send(mine.at[q_y], y_in, ys.at[1], yr.at[1], (flip_y, s))

    def joined(q):
        arrived(c_in.at[q], cr.at[q])
        add(mine.at[q], c_in.at[q])

    def begin():
        for q in order:
            compute(q, 1 - parity, away)
            to_core(q).start()
        for k, q in enumerate(order):
            compute(q, parity, mine)
            if k == 0:
                joined(q_d)
                for copy in halves:
                    copy.start()

    def middle():
        joined(q_x)
        arrived(y_half, yr.at[0])
        add(mine.at[q_x, low_half], y_half)
        to_x.start()
        joined(q_y)
        arrived(x_half, xr.at[0])
        add(mine.at[q_y, high_half], x_half)
        to_y.start()

    def finish():
        joined(q_own)
        arrived(x_in, xr.at[1])
        arrived(y_in, yr.at[1])
        out_ref[...] = (
            mine[q_own].astype(FULL) + x_in[...].astype(FULL) + y_in[...].astype(FULL)
        )

    def sent():
        for q in order:
            to_core(q).wait_send()
        for copy in halves + [to_x, to_y]:
            copy.wait_send()

    return begin, middle, finish, sent


def add_blocks(target, other):
    step = min(128, target.shape[1])
    for lead in range(target.shape[0]):

        def one(r, carry, lead=lead):
            at = pl.ds(pl.multiple_of(r * step, step), step)
            target[lead, at, :] = (
                target[lead, at, :].astype(FULL) + other[lead, at, :].astype(FULL)
            ).astype(LOW)
            return carry

        lax.fori_loop(0, target.shape[1] // step, one, 0)


def back_kernel(
    planes, owners, dm_ref, w_out_ref, mixed_ref, proj_ref, probs_ref, places_ref, gain_ref,
    freq_ref, h1_ref, w_ref, unit_ref, tail_ref,
    out_rows, out_head, out_rest, dh1_ref,
    dm_all, mixed_t, rows, q_rows, dm_rows, dproj, column,
    acc_rows, acc_head, acc_rest, sibling, u_rows, u_head, u_rest, d_rows, d_head, d_rest, pair_in,
    mine, away, c_in, x_in, y_in, x_half, y_half,
    gxs, gxr, gys, gyr, gcs, gcr, a_send, a_recv, s_send, s_recv, z_send, z_recv,
    x_send, x_recv, y_send, y_recv, c_send, c_recv, own_sem,
    pc_send, pc_recv, px_send, px_recv, py_send, py_recv,
):
    e, core, _, _, _ = neighbours()
    s = lax.axis_index("shard")
    parity = e % 2
    lanes = owners // planes
    length = dm_ref.shape[0]
    half = length // 2
    count = w_out_ref.shape[0]
    heads = count // HEAD_SIZE
    share_cols = acc_rows.shape[2]
    deep = acc_head.shape[1] * acc_head.shape[2]
    scaling = HEAD_SIZE**-0.5
    nt = (((1,), (1,)), ((), ()))
    tn = (((0,), (0,)), ((), ()))
    up_in, down_in = (u_rows, u_head, u_rest), (d_rows, d_head, d_rest)
    outs = (out_rows, out_head, out_rest)

    def arrived(block, sem):
        send(block, block, sem, sem, (core, s)).wait_recv()

    greet_plane(planes, owners)
    begin, second, third, last, sent = gather_steps(
        lambda lane: dm_all.at[lane],
        lambda lane, k: dm_all.at[lane, pl.ds(k * half, half)],
        dm_ref,
        lambda k: gxs.at[k],
        lambda k: gxr.at[k],
        lambda k: gys.at[k],
        lambda k: gyr.at[k],
        lambda k: gcs.at[k],
        lambda k: gcr.at[k],
    )
    begin()
    dm_all[e] = dm_ref[...]
    for b in range(owners):
        mixed_t[:, b * length : (b + 1) * length] = mixed_ref[b].T
    second()
    third()
    last()

    def spread(other):
        return send(
            rows.at[:, pl.ds(other * share_cols, share_cols)], acc_rows.at[e],
            a_send.at[other], a_recv.at[e], (other, s),
        )

    for other in range(owners):
        at = pl.ds(other * share_cols, share_cols)
        got = jnp.dot(
            mixed_t[...],
            dm_all[:, :, at].reshape(owners * length, share_cols),
            preferred_element_type=FULL,
        ).astype(LOW)
        rows[:, at] = got

        @pl.when(other != e)
        def _(other=other):
            spread(other).start()

        @pl.when(other == e)
        def _(got=got):
            acc_rows[e] = got

    column[...] = jnp.zeros_like(column)
    gain_query = gain_ref[0, 2:3, :HEAD_SIZE].astype(FULL)
    gain_key = gain_ref[0, 3:4, :HEAD_SIZE].astype(FULL)
    for sp in range(1, planes):
        gain_query = gain_query + gain_ref[sp, 2:3, :HEAD_SIZE].astype(FULL)
        gain_key = gain_key + gain_ref[sp, 3:4, :HEAD_SIZE].astype(FULL)

    def attend(b, carry):
        places = places_ref[b].astype(FULL)[:, 1:2]
        cosine, sine = rope_tables(places, freq_ref[0:1, :])

        def unit(v):
            inverse = lax.rsqrt(jnp.mean(v * v, axis=1, keepdims=True) + EPS)
            return v * inverse, inverse

        def turned(v):
            return (v * cosine + half_turn(v) * sine).astype(LOW)

        def back(v, units, inverse, gain, row):
            v = v * cosine - half_turn(v) * sine
            column[row : row + 1, :HEAD_SIZE] += jnp.sum(v * units, axis=0, keepdims=True)
            v = v * gain
            return inverse * (v - units * jnp.mean(v * units, axis=1, keepdims=True))

        d_mixed = lax.dot_general(
            dm_all[b], w_out_ref[...], nt, preferred_element_type=FULL
        ).astype(LOW)
        for h in range(heads):
            at = slice(h * HEAD_SIZE, (h + 1) * HEAD_SIZE)
            here = slice(h * length, (h + 1) * length)
            dm_rows[here, :] = d_mixed[:, at]
            units, _ = unit(proj_ref[b, :, at])
            q_rows[here, :] = turned(units * gain_query)
        key_units, key_inverse = unit(proj_ref[b, :, count : count + HEAD_SIZE])
        key = turned(key_units * gain_key)
        value = proj_ref[b, :, count + HEAD_SIZE :].astype(LOW)
        probs = probs_ref[b]
        wide = probs.astype(FULL)
        d_probs = lax.dot_general(dm_rows[...], value, nt, preferred_element_type=FULL)
        d_scores = wide * (d_probs - jnp.sum(d_probs * wide, axis=1, keepdims=True))
        d_scores = d_scores.astype(LOW)
        d_query = jnp.dot(d_scores, key, preferred_element_type=FULL) * scaling
        d_key = lax.dot_general(d_scores, q_rows[...], tn, preferred_element_type=FULL) * scaling
        d_value = lax.dot_general(probs, dm_rows[...], tn, preferred_element_type=FULL)
        for h in range(heads):
            at = slice(h * HEAD_SIZE, (h + 1) * HEAD_SIZE)
            units, inverse = unit(proj_ref[b, :, at])
            got = back(
                d_query[h * length : (h + 1) * length], units, inverse, gain_query, GAIN_QUERY
            )
            dproj[b, :, at] = got.astype(LOW)
        got = back(d_key, key_units, key_inverse, gain_key, GAIN_KEY)
        dproj[b, :, count : count + HEAD_SIZE] = got.astype(LOW)
        dproj[b, :, count + HEAD_SIZE :] = d_value.astype(LOW)
        return carry

    lax.fori_loop(0, owners, attend, 0)

    def left_of(sp):
        at = pl.ds(pl.multiple_of(sp * deep, deep), deep)
        return h1_ref[:, :, at].reshape(-1, deep)

    def make_head(sp):
        right = dproj[:, :, :count].reshape(-1, count)
        got = lax.dot_general(left_of(sp), right, tn, preferred_element_type=FULL).astype(LOW)
        acc_head[sp] = got.reshape(acc_head.shape[1:])

    def to_sibling(sp):
        return send(sibling.at[sp], pair_in.at[sp], s_send.at[sp], s_recv.at[sp], (core, s))

    def make_rest(sp):
        right = dproj[:, :, count:].reshape(-1, 2 * HEAD_SIZE)
        got = lax.dot_general(left_of(sp), right, tn, preferred_element_type=FULL).astype(LOW)
        key, value = got[:, :HEAD_SIZE], got[:, HEAD_SIZE:]
        at = pl.ds(pl.multiple_of(sp * deep, deep), deep)
        column[GAIN_ONE : GAIN_ONE + 1, :] = jnp.sum(
            dh1_ref[:, at] * unit_ref[:, at], axis=0, keepdims=True
        )
        extra = (tail_ref[sp].astype(FULL) + column[...].T).astype(LOW)
        top, low = extra[: deep // 2], extra[deep // 2 :]

        def put(into, kv, part):
            into[sp, :4] = kv.reshape(4, deep // 4, HEAD_SIZE)
            into[sp, 4:] = part.reshape(2, deep // 4, HEAD_SIZE)

        @pl.when(parity == 0)
        def _():
            put(acc_rest, key, top)
            put(sibling, value, low)

        @pl.when(parity == 1)
        def _():
            put(acc_rest, value, low)
            put(sibling, key, top)

        to_sibling(sp).start()

    def chunk(k, sp):
        if k == 0:
            return acc_rows.at[pl.ds(sp * lanes, lanes)]
        return acc_head.at[sp] if k == 1 else acc_rest.at[sp]

    def ready(k, sp):
        if k == 0:
            for lane in range(lanes):
                source = sp * lanes + lane

                @pl.when(source != e)
                def _(source=source):
                    arrived(acc_rows.at[source], a_recv.at[source])

        elif k == 1:
            make_head(sp)
        else:
            arrived(pair_in.at[sp], s_recv.at[sp])
            add_blocks(acc_rest.at[sp], pair_in.at[sp])

    def up(k, sp):
        return send(
            chunk(k, sp), up_in[k].at[sp], z_send.at[k, 0, sp], z_recv.at[k, 0, sp], (e, s + 1)
        )

    def down(k, sp):
        return send(
            chunk(k, sp), down_in[k].at[sp], z_send.at[k, 1, sp], z_recv.at[k, 1, sp], (e, s - 1)
        )

    def line(k, sp):
        ready(k, sp)

        @pl.when((sp >= s) & (s > 0))
        def _():
            arrived(up_in[k].at[sp], z_recv.at[k, 0, sp])
            add_blocks(chunk(k, sp), up_in[k].at[sp])

        @pl.when((sp <= s) & (s < planes - 1))
        def _():
            arrived(down_in[k].at[sp], z_recv.at[k, 1, sp])
            add_blocks(chunk(k, sp), down_in[k].at[sp])

        @pl.when(sp > s)
        def _():
            up(k, sp).start()

        @pl.when(sp < s)
        def _():
            down(k, sp).start()

    def pair(k, n):
        for i in (2 * n, 2 * n - 1):
            sp = s + (2 * (i % 2) - 1) * n

            @pl.when((sp >= 0) & (sp < planes))
            def _(sp=sp):
                line(k, sp)

    def steps(k):
        size = outs[k].shape[1] // 2
        return gather_steps(
            lambda lane: outs[k].at[lane],
            lambda lane, at: outs[k].at[lane, pl.ds(at * size, size)],
            chunk(k, s),
            lambda n: x_send.at[k, n],
            lambda n: x_recv.at[k, n],
            lambda n: y_send.at[k, n],
            lambda n: y_recv.at[k, n],
            lambda n: c_send.at[k, n],
            lambda n: c_recv.at[k, n],
        )

    def keep(k):
        return pltpu.make_async_copy(chunk(k, s), outs[k].at[e], own_sem.at[k])

    def own(k):
        line(k, s)
        steps(k)[0]()
        keep(k).start()

    p_begin, p_middle, p_finish, p_sent = project_steps(
        True, dproj, w_ref, dh1_ref, mine, away, c_in, x_in, y_in, x_half, y_half,
        pc_send, pc_recv, px_send, px_recv, py_send, py_recv,
    )
    pair(1, planes - 1)
    p_begin()
    for n in range(planes - 2, 0, -1):
        pair(1, n)
    p_middle()
    pair(0, planes - 1)
    p_finish()
    for sp in range(planes):
        make_rest(sp)
    for n in range(planes - 2, 0, -1):
        pair(0, n)
    own(1)
    pair(2, planes - 1)
    steps(1)[1]()
    for n in range(planes - 2, 0, -1):
        pair(2, n)
    own(0)
    steps(1)[2]()
    own(2)
    steps(0)[1]()
    steps(2)[1]()
    steps(0)[2]()
    steps(2)[2]()
    for k in range(3):
        keep(k).wait()
        steps(k)[3]()
        steps(k)[4]()
    p_sent()
    sent()
    for other in range(owners):

        @pl.when(other != e)
        def _(other=other):
            spread(other).wait_send()

    def drain(sp, carry):
        to_sibling(sp).wait_send()
        for k in range(3):

            @pl.when(sp > s)
            def _(k=k):
                up(k, sp).wait_send()

            @pl.when(sp < s)
            def _(k=k):
                down(k, sp).wait_send()

        return carry

    lax.fori_loop(0, planes, drain, 0)


def back(dm, w_out, mixed, proj, probs, places, gains, frequency, h1, w, units, tail, planes, owners, identity):
    length = dm.shape[0]
    count = w_out.shape[0]
    share_cols = MODEL_WIDTH // owners
    deep = MODEL_WIDTH // planes
    shapes = (
        (owners // planes, count, share_cols),
        (2, deep // 2, count),
        (6, deep // 4, HEAD_SIZE),
    )
    stack = (length * count // HEAD_SIZE, HEAD_SIZE)
    block = (length, MODEL_WIDTH)
    part = (length // 2, MODEL_WIDTH)

    def vmem(*shape, dtype=LOW):
        return pltpu.VMEM(shape, dtype)

    per_plane = [vmem(planes, *shape) for shape in shapes]
    return pl.pallas_call(
        functools.partial(back_kernel, planes, owners),
        out_shape=[jax.ShapeDtypeStruct((owners,) + shape, LOW) for shape in shapes]
        + [jax.ShapeDtypeStruct(block, FULL)],
        in_specs=[VM] * 12,
        out_specs=[ANY, ANY, ANY, VM],
        scratch_shapes=[
            vmem(owners, *block),
            vmem(count, owners * length),
            vmem(count, MODEL_WIDTH),
            vmem(*stack),
            vmem(*stack),
            vmem(*proj.shape),
            vmem(TAIL, deep, dtype=FULL),
            vmem(owners, count, share_cols),
            per_plane[1],
            per_plane[2],
            per_plane[2],
        ]
        + per_plane
        + per_plane
        + [
            per_plane[2],
            vmem(4, *block),
            vmem(4, *block),
            vmem(4, *block),
            vmem(*block),
            vmem(*block),
            vmem(*part),
            vmem(*part),
            DMA((2,)),
            DMA((2,)),
            DMA((2,)),
            DMA((2,)),
            DMA((4,)),
            DMA((4,)),
            DMA((owners,)),
            DMA((owners,)),
            DMA((planes,)),
            DMA((planes,)),
            DMA((3, 2, planes)),
            DMA((3, 2, planes)),
            DMA((3, 2)),
            DMA((3, 2)),
            DMA((3, 2)),
            DMA((3, 2)),
            DMA((3, 4)),
            DMA((3, 4)),
            DMA((3,)),
            DMA((4,)),
            DMA((4,)),
            DMA((2,)),
            DMA((2,)),
            DMA((2,)),
            DMA((2,)),
        ],
        compiler_params=pltpu.CompilerParams(
            collective_id=identity, has_side_effects=True, vmem_limit_bytes=VMEM_LIMIT
        ),
    )(dm, w_out, mixed, proj, probs, places, gains, frequency, h1, w, units, tail)


def finish_kernel(owners, rows_ref, head_ref, rest_ref, out_rows, out_qkv, out_tail):
    i = pl.program_id(0)

    @pl.when(i < owners)
    def _():
        out_rows[...] = rows_ref[0].astype(FULL)
        out_qkv[...] = head_ref[0].astype(FULL)

    for at in range(2):

        @pl.when(i == owners + at)
        def _(at=at):
            for h in range(KEY_VALUE_HEADS):
                got = rest_ref[2 * h + at, :4].reshape(-1, HEAD_SIZE)
                out_qkv[:, h * HEAD_SIZE : (h + 1) * HEAD_SIZE] = got.astype(FULL)

    @pl.when(i == 0)
    def _():
        height = out_tail.shape[0] // 2
        for at in range(2):
            total = jnp.zeros((height, TAIL), FULL)
            for lane in range(at, owners, 2):
                total = total + rest_ref[lane, 4:].reshape(-1, TAIL).astype(FULL)
            out_tail[at * height : (at + 1) * height, :] = total


def finish_grads(rows, head, rest, owners):
    rows = rows.reshape(owners, -1, rows.shape[-1])
    head = head.reshape(owners, -1, head.shape[-1])
    count, share = rows.shape[1:]
    height, wide = head.shape[1:]
    last = owners - 1
    return pl.pallas_call(
        functools.partial(finish_kernel, owners),
        grid=(owners + 2,),
        in_specs=[
            pl.BlockSpec((1, count, share), lambda i: (jnp.minimum(i, last), 0, 0)),
            pl.BlockSpec((1, height, wide), lambda i: (jnp.minimum(i, last), 0, 0)),
            pl.BlockSpec(rest.shape, lambda i: (0, 0, 0, 0)),
        ],
        out_specs=[
            pl.BlockSpec((count, share), lambda i: (0, jnp.minimum(i, last))),
            pl.BlockSpec((height, wide), lambda i: (0, i)),
            pl.BlockSpec((height, TAIL), lambda i: (0, 0)),
        ],
        out_shape=[
            jax.ShapeDtypeStruct((count, owners * share), FULL),
            jax.ShapeDtypeStruct((height, (owners + 2) * wide), FULL),
            jax.ShapeDtypeStruct((height, TAIL), FULL),
        ],
        compiler_params=pltpu.CompilerParams(vmem_limit_bytes=VMEM_LIMIT),
    )(rows, head, rest)


def gathered_layer(
    tokens,
    segments,
    routes,
    attn_gain,
    qkv_weight,
    query_gain,
    k_gain,
    w_out,
    ffn_gain,
    router,
    w_gate,
    w_up,
    w_down,
    d_out,
):
    owners = lax.axis_size("expert")
    planes = lax.axis_size("shard")
    me = lax.axis_index("expert")
    plane = lax.axis_index("shard")
    length = tokens.shape[0]
    blocks = owners * planes
    experts_all = router.shape[1]
    capacity = 3 * length * TOPK // (2 * experts_all)
    heads = QUERY_HEADS // owners
    query_cols = heads * HEAD_SIZE
    scaling = HEAD_SIZE ** (-0.5)
    both = ("expert", "shard")
    rows_in = qkv_weight.shape[0]

    kv_head = me * KEY_VALUE_HEADS // owners
    k_at = QUERY_HEADS * HEAD_SIZE + kv_head * HEAD_SIZE
    v_at = k_at + KEY_VALUE_HEADS * HEAD_SIZE
    gains = columns(
        [
            router,
            attn_gain[:, None],
            ffn_gain[:, None],
            jnp.pad(query_gain, (0, rows_in - query_gain.shape[0]))[:, None],
            jnp.pad(k_gain, (0, rows_in - k_gain.shape[0]))[:, None],
        ],
        rows_in,
    )
    mine = jnp.concatenate(
        [
            lax.dynamic_slice_in_dim(qkv_weight, me * query_cols, query_cols, 1),
            lax.dynamic_slice_in_dim(qkv_weight, k_at, HEAD_SIZE, 1),
            lax.dynamic_slice_in_dim(qkv_weight, v_at, HEAD_SIZE, 1),
            gains,
        ],
        axis=1,
    )
    gathered = lax.all_gather(mine, "shard", axis=0, tiled=True)
    qkv_cols = query_cols + 2 * HEAD_SIZE
    wqkv = gathered[:, :qkv_cols]
    router_full = gathered[:, qkv_cols : qkv_cols + experts_all]
    gain_cols = gathered[:, qkv_cols + experts_all :].astype(FULL)
    gain_one, gain_two = gain_cols[:, 0], gain_cols[:, 1]
    per = query_gain.shape[0]
    by_plane = gain_cols.reshape(planes, rows_in, -1)[:, :per]
    gain_query = by_plane[:, :, 2].reshape(-1)
    gain_key = by_plane[:, :, 3].reshape(-1)

    segment_row = segments[0]
    token_tail = columns(
        [segment_row[:, None], positions_of(segment_row)[:, None]], length
    )
    plane_rows = lax.all_gather(
        jnp.concatenate([tokens, token_tail], axis=1), "expert", axis=0, tiled=False
    )
    plane_tokens = plane_rows[:, :, :MODEL_WIDTH].astype(FULL)
    plane_segments = plane_rows[:, :, MODEL_WIDTH]
    plane_places = plane_rows[:, :, MODEL_WIDTH + 1].astype(FULL)

    out_rows = w_out.shape[0]
    first = me * query_cols
    offset = first - plane * out_rows
    if out_rows >= query_cols:
        held = (offset >= 0) & (offset < out_rows)
        piece = lax.dynamic_slice_in_dim(w_out, jnp.where(held, offset, 0), query_cols, 0)
        w_mine = lax.psum(jnp.where(held, piece, 0).astype(LOW), "shard")
    else:
        parts = query_cols // out_rows
        at = plane - me * parts
        held = (at >= 0) & (at < parts)
        spread = jnp.where(held & (jnp.arange(parts) == at)[:, None, None], w_out[None], 0)
        w_mine = lax.psum(spread.astype(LOW), "shard").reshape(query_cols, MODEL_WIDTH)

    d_tail = columns([routes], length)
    d_all = lax.all_gather(
        jnp.concatenate([d_out, d_tail], axis=1), both, axis=0, tiled=False
    )

    unit_plane, inverse_plane = unit_norm(plane_tokens)
    h1 = (unit_plane * gain_one).astype(LOW)
    projected = dot("bqd,df->bqf", h1, wqkv)
    half = HEAD_SIZE // 2
    frequency = THETA ** (-2.0 * jnp.arange(half, dtype=FULL) / HEAD_SIZE)
    angles = plane_places[:, :, None] * frequency
    cosine, sine = jnp.cos(angles), jnp.sin(angles)
    cosine_q, sine_q = cosine[:, :, None, :], sine[:, :, None, :]
    query_raw = projected[:, :, :query_cols].reshape(owners, length, heads, HEAD_SIZE)
    key_raw = projected[:, :, query_cols : query_cols + HEAD_SIZE]
    value = projected[:, :, query_cols + HEAD_SIZE :].astype(LOW)
    query_unit, query_inverse = unit_norm(query_raw)
    key_unit, key_inverse = unit_norm(key_raw)
    query = rotate(query_unit * gain_query, cosine_q, sine_q).astype(LOW)
    key = rotate(key_unit * gain_key, cosine, sine).astype(LOW)
    places = jnp.arange(length, dtype=jnp.int32)
    allowed = (plane_segments[:, :, None] == plane_segments[:, None, :]) & (
        places[None, :] <= places[:, None]
    )
    scores = dot("bqhd,bkd->bhqk", query, key) * scaling
    scores = jnp.where(allowed[:, None], scores, -1e30)
    highest = jnp.max(scores, axis=-1, keepdims=True)
    exponent = jnp.exp(scores - highest)
    probs = exponent / jnp.sum(exponent, axis=-1, keepdims=True)
    probs_low = probs.astype(LOW)
    mixed = dot("bhqk,bkd->bqhd", probs_low, value).astype(LOW)
    mixed = mixed.reshape(owners, length, query_cols)
    partial = dot("bqf,fd->bqd", mixed, w_mine).astype(LOW)
    branch = lax.psum_scatter(partial, "expert", scatter_dimension=0, tiled=False)

    middle = tokens.astype(FULL) + branch.astype(FULL)
    unit_two, inverse_two = unit_norm(middle)
    h2 = (unit_two * gain_two).astype(LOW)
    logits = dot("nd,de->ne", h2, router_full)
    chance = jax.nn.softmax(logits, axis=-1)
    named = jnp.sum(
        (routes[:, :, None] == jnp.arange(experts_all, dtype=jnp.int32)).astype(FULL), axis=1
    )
    chosen_sum = jnp.sum(named * chance, axis=1, keepdims=True)
    gates = named * chance / chosen_sum
    gates_high = gates.astype(LOW)
    gates_rest = (gates - gates_high.astype(FULL)).astype(LOW)
    h_all = lax.all_gather(
        jnp.concatenate([h2, gates_high, gates_rest], axis=1), both, axis=0, tiled=False
    )

    route_all = d_all[:, :, MODEL_WIDTH : MODEL_WIDTH + TOPK].astype(FULL)
    own_experts = (me * EXP_DEV + jnp.arange(EXP_DEV, dtype=jnp.int32)).astype(FULL)
    match = jnp.sum((route_all[:, :, :, None] == own_experts).astype(FULL), axis=2)
    earlier = (places[None, :] < places[:, None]).astype(LOW)
    rank = dot("ts,bsj->btj", earlier, match.astype(LOW))
    slot_ids = jnp.arange(capacity, dtype=jnp.int32).astype(FULL)
    place = jnp.where(match > 0, rank, -1.0).transpose(0, 2, 1)
    dispatch = (place[:, :, None, :] == slot_ids[:, None]).astype(LOW)

    def experts(h_rows, d_rows, gate_high, gate_rest, put):
        count = h_rows.shape[0]
        flat = put.reshape(count, EXP_DEV * capacity, length)
        x = dot("bst,btd->bsd", flat, h_rows).astype(LOW)
        dy = dot("bst,btd->bsd", flat, d_rows).astype(LOW)

        def by_expert(v):
            v = v.reshape(count, EXP_DEV, capacity, v.shape[-1])
            return v.transpose(1, 0, 2, 3).reshape(EXP_DEV, count * capacity, v.shape[-1])

        def by_block(v):
            v = v.reshape(EXP_DEV, count, capacity, v.shape[-1])
            return v.transpose(1, 0, 2, 3).reshape(count, EXP_DEV * capacity, v.shape[-1])

        x, dy = by_expert(x), by_expert(dy)
        gate_slot = dot("bjct,btj->jbc", put, gate_high) + dot("bjct,btj->jbc", put, gate_rest)
        gate_slot = gate_slot.reshape(EXP_DEV, count * capacity, 1)
        g = dot("erd,efd->erf", x, w_gate)
        u = dot("erd,efd->erf", x, w_up)
        da = dot("erd,edf->erf", dy, w_down)
        sigma = jax.nn.sigmoid(g)
        silu = g * sigma
        act = (silu * u).astype(LOW).astype(FULL)
        d_gate_slot = jnp.sum(act * da, axis=-1)
        act_gated = (act * gate_slot).astype(LOW)
        d_act = da * gate_slot
        dg = (d_act * u * sigma * (1.0 + g * (1.0 - sigma))).astype(LOW)
        du = (d_act * silu).astype(LOW)
        y = dot("erf,edf->erd", act_gated, w_down).astype(LOW)
        d_down = dot("erd,erf->edf", dy, act_gated)
        d_gate = dot("erf,erd->efd", dg, x)
        d_up = dot("erf,erd->efd", du, x)
        dx = (dot("erf,efd->erd", dg, w_gate) + dot("erf,efd->erd", du, w_up)).astype(LOW)
        mix = dot("bst,bsd->btd", flat, by_block(y)).astype(LOW)
        d_h = dot("bst,bsd->btd", flat, by_block(dx)).astype(LOW)
        d_g = dot(
            "bjct,jbc->btj", put.astype(FULL), d_gate_slot.reshape(EXP_DEV, count, capacity)
        )
        return mix, d_h, d_g, d_gate, d_up, d_down

    gate_cols = lax.dynamic_slice_in_dim(h_all, MODEL_WIDTH + me * EXP_DEV, EXP_DEV, 2)
    rest_cols = lax.dynamic_slice_in_dim(
        h_all, MODEL_WIDTH + experts_all + me * EXP_DEV, EXP_DEV, 2
    )
    step = min(blocks, GROUP_BLOCKS)
    mixes, d_hs, d_gs, totals = [], [], [], None
    for at in range(0, blocks, step):
        cut = slice(at, at + step)
        mix, d_h, d_g, *grads = experts(
            h_all[cut, :, :MODEL_WIDTH],
            d_all[cut, :, :MODEL_WIDTH],
            gate_cols[cut],
            rest_cols[cut],
            dispatch[cut],
        )
        mixes.append(mix)
        d_hs.append(d_h)
        d_gs.append(d_g)
        totals = grads if totals is None else [a + b for a, b in zip(totals, grads)]
    d_gate, d_up, d_down = totals
    d_g = jnp.concatenate(d_gs, axis=0)
    spread = jnp.zeros((blocks, length, TAIL), LOW)
    spread = lax.dynamic_update_slice_in_dim(spread, d_g.astype(LOW), me * EXP_DEV, 2)
    d_h_wide = jnp.concatenate([jnp.concatenate(d_hs, axis=0), spread], axis=2)

    def home(v):
        v = v.reshape(owners, planes, length, v.shape[-1])
        v = lax.psum_scatter(v, "expert", scatter_dimension=0, tiled=False)
        return lax.psum_scatter(v, "shard", scatter_dimension=0, tiled=False)

    d_home = home(d_h_wide)
    mixture = home(jnp.concatenate(mixes, axis=0))
    result = (middle + mixture.astype(FULL)).astype(LOW)

    upstream = d_out.astype(FULL)
    d_gates = d_home[:, MODEL_WIDTH : MODEL_WIDTH + experts_all].astype(FULL)
    d_chance = named * (d_gates - jnp.sum(d_gates * gates, axis=1, keepdims=True)) / chosen_sum
    d_logits = chance * (d_chance - jnp.sum(d_chance * chance, axis=1, keepdims=True))
    d_logits = d_logits.astype(LOW)
    d_h2 = d_home[:, :MODEL_WIDTH].astype(FULL) + dot("ne,de->nd", d_logits, router_full)
    d_gain_two = jnp.sum(d_h2 * unit_two, axis=0)
    d_middle = upstream + norm_back(d_h2, unit_two, inverse_two, gain_two)
    d_router = dot("nd,ne->de", h2, d_logits)

    d_branch = lax.all_gather(d_middle.astype(LOW), "expert", axis=0, tiled=False)
    d_w_out = dot("bqf,bqd->fd", mixed, d_branch).astype(LOW)
    d_mixed = dot("bqd,fd->bqf", d_branch, w_mine).astype(LOW)
    d_mixed = d_mixed.reshape(owners, length, heads, HEAD_SIZE)
    d_probs = dot("bqhd,bkd->bhqk", d_mixed, value)
    d_scores = probs * (d_probs - jnp.sum(d_probs * probs, axis=-1, keepdims=True))
    d_scores = d_scores.astype(LOW)
    d_query = dot("bhqk,bkd->bqhd", d_scores, key) * scaling
    d_key = dot("bhqk,bqhd->bkd", d_scores, query) * scaling
    d_value = dot("bhqk,bqhd->bkd", probs_low, d_mixed)
    d_query = rotate_back(d_query, cosine_q, sine_q)
    d_key = rotate_back(d_key, cosine, sine)
    d_gain_query = jnp.sum(d_query * query_unit, axis=(0, 1, 2))
    d_gain_key = jnp.sum(d_key * key_unit, axis=(0, 1))
    d_query = norm_back(d_query, query_unit, query_inverse, gain_query)
    d_key = norm_back(d_key, key_unit, key_inverse, gain_key)
    d_projected = jnp.concatenate(
        [d_query.reshape(owners, length, query_cols), d_key, d_value], axis=2
    ).astype(LOW)
    d_h1_part = dot("bqf,df->bqd", d_projected, wqkv).astype(LOW)
    d_h1 = lax.psum_scatter(d_h1_part, "expert", scatter_dimension=0, tiled=False).astype(FULL)
    resident = tokens.astype(FULL)
    unit_one, inverse_one = unit_norm(resident)
    d_gain_one = jnp.sum(d_h1 * unit_one, axis=0)
    d_tokens = (d_middle + norm_back(d_h1, unit_one, inverse_one, gain_one)).astype(LOW)

    d_wqkv = dot("bqd,bqf->df", h1, d_projected).astype(LOW)

    def by_rows(v):
        v = v.reshape(planes, per)
        return jnp.pad(v, ((0, 0), (0, rows_in - per))).reshape(-1)[:, None]

    d_tail = columns(
        [
            d_router,
            d_gain_one[:, None],
            d_gain_two[:, None],
            by_rows(d_gain_query),
            by_rows(d_gain_key),
        ],
        MODEL_WIDTH,
    )
    d_pack = lax.psum_scatter(
        jnp.concatenate([d_wqkv, d_tail], axis=1), "shard", scatter_dimension=0, tiled=True
    )
    d_pack = lax.all_gather(d_pack, "expert", axis=0, tiled=False).astype(FULL)
    d_q_cols = d_pack[:, :, :query_cols].transpose(1, 0, 2).reshape(rows_in, -1)
    d_kv = d_pack[:, :, query_cols:qkv_cols]
    d_kv = jnp.sum(d_kv.reshape(KEY_VALUE_HEADS, -1, rows_in, 2, HEAD_SIZE), axis=1)
    d_kv = d_kv.transpose(1, 2, 0, 3).reshape(rows_in, -1)
    d_qkv_weight = jnp.concatenate([d_q_cols, d_kv], axis=1)
    d_rest = jnp.sum(d_pack[:, :, qkv_cols:], axis=0)
    d_router_out = d_rest[:, :experts_all]
    d_gain_out = d_rest[:, experts_all:]

    d_w_out = d_w_out.reshape(query_cols, owners, -1)
    d_w_out = lax.all_to_all(d_w_out, "expert", split_axis=1, concat_axis=0, tiled=False)
    d_w_out = d_w_out.reshape(QUERY_HEADS * HEAD_SIZE, -1)
    d_w_out = lax.psum_scatter(d_w_out, "shard", scatter_dimension=0, tiled=True)
    d_w_out = lax.all_gather(d_w_out, "expert", axis=1, tiled=True).astype(FULL)

    return (
        result,
        d_tokens,
        d_gain_out[:, 0],
        d_qkv_weight,
        d_gain_out[:per, 2],
        d_gain_out[:per, 3],
        d_w_out,
        d_gain_out[:, 1],
        d_router_out,
        d_gate,
        d_up,
        d_down,
    )


def resident_layer(
    tokens,
    segments,
    routes,
    attn_gain,
    qkv_weight,
    query_gain,
    k_gain,
    w_out,
    ffn_gain,
    router,
    w_gate,
    w_up,
    w_down,
    d_out,
):
    owners = lax.axis_size("expert")
    planes = lax.axis_size("shard")
    me = lax.axis_index("expert")
    plane = lax.axis_index("shard")
    length = tokens.shape[0]
    blocks = owners * planes
    experts_all = router.shape[1]
    capacity = 3 * length * TOPK // (2 * experts_all)
    slots = 2 * capacity
    heads = QUERY_HEADS // owners
    query_cols = heads * HEAD_SIZE
    scaling = HEAD_SIZE ** (-0.5)
    rows_in = qkv_weight.shape[0]
    per = query_gain.shape[0]

    kv_head = me * KEY_VALUE_HEADS // owners
    k_at = QUERY_HEADS * HEAD_SIZE + kv_head * HEAD_SIZE
    v_at = k_at + KEY_VALUE_HEADS * HEAD_SIZE
    mine = jnp.concatenate(
        [
            lax.dynamic_slice_in_dim(qkv_weight, me * query_cols, query_cols, 1),
            lax.dynamic_slice_in_dim(qkv_weight, jnp.where(me % 2 == 0, k_at, v_at), HEAD_SIZE, 1),
        ],
        axis=1,
    )
    router_rows = rows_in // owners
    router_part = lax.dynamic_slice_in_dim(router, me * router_rows, router_rows, 0)
    router_part = columns([router_part], router_rows)
    gain_rows = jnp.zeros((16, rows_in), LOW).at[0].set(attn_gain).at[1].set(ffn_gain)
    gain_rows = lax.dynamic_update_slice(gain_rows, query_gain[None], (2, plane * per))
    gain_rows = lax.dynamic_update_slice(gain_rows, k_gain[None], (3, plane * per))
    segment_row = segments[0]
    token_tail = columns([segment_row[:, None], positions_of(segment_row)[:, None]], length)
    token_rows = jnp.concatenate([tokens, token_tail], axis=1)
    d_rows = jnp.concatenate([d_out, columns([routes], length)], axis=1)
    half = HEAD_SIZE // 2
    frequency = THETA ** (-2.0 * jnp.arange(half, dtype=FULL) / HEAD_SIZE)
    frequency = jnp.broadcast_to(jnp.tile(frequency, 2)[None, :], (8, HEAD_SIZE))
    d_all, w_mine, w_all, router_all, gain_all, tail, h1, projected, probs_low, mixed, branch = front(
        mine, router_part, gain_rows, token_rows, w_out, d_rows, frequency, planes, owners, 5
    )
    gains = gain_all.astype(FULL)
    gain_one, gain_two = gains[:, 0].reshape(-1), gains[:, 1].reshape(-1)
    router_full = router_all.transpose(1, 0, 2, 3).reshape(MODEL_WIDTH, -1)[:, :experts_all]

    places = jnp.arange(length, dtype=jnp.int32)
    route_all = d_all[..., MODEL_WIDTH : MODEL_WIDTH + TOPK].reshape(blocks, length, TOPK)
    own_experts = (me * EXP_DEV + jnp.arange(EXP_DEV, dtype=jnp.int32)).astype(FULL)
    match = jnp.sum((route_all.astype(FULL)[:, :, :, None] == own_experts).astype(FULL), axis=2)
    earlier = (places[None, :] < places[:, None]).astype(LOW)
    rank = dot("ts,bsj->btj", earlier, match.astype(LOW))
    offset = (capacity * jnp.arange(2, dtype=jnp.int32)).astype(FULL)
    place = jnp.where(match > 0, rank, -1.0).reshape(owners // 2, 2, planes, length, EXP_DEV)
    place = jnp.where(place >= 0, place + offset[:, None, None, None], -1.0)
    by_token = place.transpose(0, 2, 1, 3, 4).reshape(blocks // 2, 2 * length, EXP_DEV)
    place = by_token.transpose(0, 2, 1)
    slot_ids = jnp.arange(EXP_DEV * slots, dtype=jnp.int32)
    widen = (slot_ids // slots == jnp.arange(EXP_DEV, dtype=jnp.int32)[:, None]).astype(LOW)
    hot = dot("ptj,js->pts", by_token.astype(LOW), widen)
    hot = (hot == (slot_ids % slots).astype(FULL)).astype(LOW)
    lanes = jnp.arange(2 * experts_all, dtype=jnp.int32) % experts_all
    own = (me * EXP_DEV + jnp.arange(EXP_DEV, dtype=jnp.int32))[:, None] == lanes
    sel = jnp.broadcast_to(own.astype(FULL)[:, None, :], (EXP_DEV, 8, 2 * experts_all))

    middle = tokens.astype(FULL) + branch
    unit_two, inverse_two = unit_norm(middle)
    h2 = (unit_two * gain_two).astype(LOW)
    logits = dot("nd,de->ne", h2, router_full)
    chance = jax.nn.softmax(logits, axis=-1)
    named = jnp.sum(
        (routes[:, :, None] == jnp.arange(experts_all, dtype=jnp.int32)).astype(FULL), axis=1
    )
    chosen_sum = jnp.sum(named * chance, axis=1, keepdims=True)
    gates = named * chance / chosen_sum
    gates_high = gates.astype(LOW)
    gates_rest = (gates - gates_high.astype(FULL)).astype(LOW)
    h_rows = jnp.concatenate([h2, gates_high, gates_rest], axis=1)

    x, dy = gather_dispatch(h_rows, d_all, place, planes, slots, 1)
    y, dx, d_gate, d_up, d_down = expert_pass(sel, x, dy, w_gate, w_up, w_down.swapaxes(1, 2))
    d_down = d_down.swapaxes(1, 2)
    d_home, mixture = combine_home(hot, dx, y, length, planes, slots, 2)

    upstream = d_out.astype(FULL)
    d_gates = d_home[:, MODEL_WIDTH:]
    d_gates = d_gates[:, :experts_all] + d_gates[:, experts_all:]
    d_chance = named * (d_gates - jnp.sum(d_gates * gates, axis=1, keepdims=True)) / chosen_sum
    d_logits = chance * (d_chance - jnp.sum(d_chance * chance, axis=1, keepdims=True))
    d_logits = d_logits.astype(LOW)
    d_h2 = d_home[:, :MODEL_WIDTH] + dot("ne,de->nd", d_logits, router_full)
    d_gain_two = jnp.sum(d_h2 * unit_two, axis=0)
    d_middle = upstream + norm_back(d_h2, unit_two, inverse_two, gain_two)
    d_router = dot("nd,ne->de", h2, d_logits)

    resident = tokens.astype(FULL)
    unit_one, inverse_one = unit_norm(resident)
    d_tail = columns([d_router, d_gain_two[:, None]], MODEL_WIDTH)
    *parts, d_h1 = back(
        d_middle.astype(LOW), w_mine, mixed, projected, probs_low, tail, gain_all, frequency, h1,
        w_all, unit_one, d_tail.reshape(planes, rows_in, -1), planes, owners, 4,
    )
    d_w_out, d_qkv_weight, d_rest = finish_grads(*parts, owners)
    result = (middle + mixture).astype(LOW)
    d_tokens = (d_middle + norm_back(d_h1, unit_one, inverse_one, gain_one)).astype(LOW)
    return (
        result,
        d_tokens,
        d_rest[:, GAIN_ONE],
        d_qkv_weight,
        lax.dynamic_slice_in_dim(d_rest[:, GAIN_QUERY], plane * per, per, 0),
        lax.dynamic_slice_in_dim(d_rest[:, GAIN_KEY], plane * per, per, 0),
        d_w_out,
        d_rest[:, experts_all],
        d_rest[:, :experts_all],
        d_gate,
        d_up,
        d_down,
    )


def per_device(*args):
    blocks = lax.axis_size("expert") * lax.axis_size("shard")
    row_bytes = 2 * (MODEL_WIDTH + TAIL)
    if blocks * args[0].shape[0] * row_bytes <= RESIDENT:
        return resident_layer(*args)
    return gathered_layer(*args)


def solution(mesh):
    placed = (
        P(("expert", "shard"), None),
        P(("expert", "shard"), None),
        P(("expert", "shard"), None),
        P("shard"),
        P("shard", None),
        P("shard"),
        P("shard"),
        P("shard", None),
        P("shard"),
        P("shard", None),
        P("expert", "shard", None),
        P("expert", "shard", None),
        P("expert", None, "shard"),
        P(("expert", "shard"), None),
    )
    return jax.shard_map(
        per_device,
        mesh=mesh,
        in_specs=placed,
        out_specs=(
            P(("expert", "shard"), None),
            P(("expert", "shard"), None),
            P("shard"),
            P("shard", None),
            P("shard"),
            P("shard"),
            P("shard", None),
            P("shard"),
            P("shard", None),
            P("expert", "shard", None),
            P("expert", "shard", None),
            P("expert", None, "shard"),
        ),
        check_vma=False,
    )
```

```python
import functools

import jax
import jax.numpy as jnp
from jax import lax
from jax.experimental import pallas as pl
from jax.experimental.pallas import tpu as pltpu
from jax.sharding import PartitionSpec as P

MODEL_WIDTH = 2048
QUERY_HEADS = 32
KEY_VALUE_HEADS = 4
HEAD_SIZE = 128
TOPK = 8
EXP_DEV = 8
TAIL = 128
GAIN_TWO, GAIN_QUERY, GAIN_KEY, GAIN_ONE = 64, 65, 66, 67
GROUP_BLOCKS = 32
RESIDENT = 20 << 20

EPS = 1e-06
THETA = 1000000.0
LOW = jnp.bfloat16
FULL = jnp.float32


def unit_norm(values):
    inverse = lax.rsqrt(jnp.mean(values * values, axis=-1, keepdims=True) + EPS)
    return values * inverse, inverse


def norm_back(incoming, unit_rows, inverse, gain):
    inner = incoming * gain
    return inverse * (inner - unit_rows * jnp.mean(inner * unit_rows, axis=-1, keepdims=True))


def rotate(values, cosine, sine):
    half = values.shape[-1] // 2
    a, b = values[..., :half], values[..., half:]
    return jnp.concatenate([a * cosine - b * sine, b * cosine + a * sine], axis=-1)


def rotate_back(values, cosine, sine):
    half = values.shape[-1] // 2
    a, b = values[..., :half], values[..., half:]
    return jnp.concatenate([a * cosine + b * sine, b * cosine - a * sine], axis=-1)


def dot(spec, left, right):
    return jnp.einsum(spec, left, right, preferred_element_type=FULL)


def positions_of(segment_row):
    places = jnp.arange(segment_row.shape[0], dtype=jnp.int32)
    before = (segment_row[None, :] == segment_row[:, None]) & (places[None, :] < places[:, None])
    return jnp.sum(before.astype(jnp.int32), axis=1)


def columns(parts, rows):
    wide = jnp.concatenate([part.astype(LOW) for part in parts], axis=1)
    return jnp.pad(wide, ((0, rows - wide.shape[0]), (0, TAIL - wide.shape[1])))


MESH = pl.DeviceIdType.MESH
ANY = pl.BlockSpec(memory_space=pl.ANY)
VM = pl.BlockSpec(memory_space=pltpu.VMEM)
DMA = pltpu.SemaphoreType.DMA
VMEM_LIMIT = 58 << 20
TILE = 512


def neighbours():
    e = lax.axis_index("expert")
    core = e + 1 - 2 * (e % 2)
    flip_x = e + 2 - 4 * ((e // 2) % 2)
    flip_y = e + 4 - 8 * ((e // 4) % 2)
    diagonal = flip_x + flip_y - e
    return e, core, flip_x, flip_y, diagonal


def greet(planes):
    e, core, flip_x, flip_y, _ = neighbours()
    s = lax.axis_index("shard")
    barrier = pltpu.get_barrier_semaphore()
    for other in (core, flip_x, flip_y):
        pl.semaphore_signal(barrier, 1, device_id=(other, s), device_id_type=MESH)

    @pl.when(s > 0)
    def _():
        pl.semaphore_signal(barrier, 1, device_id=(e, s - 1), device_id_type=MESH)

    @pl.when(s < planes - 1)
    def _():
        pl.semaphore_signal(barrier, 1, device_id=(e, s + 1), device_id_type=MESH)

    inner = (s > 0) & (s < planes - 1)

    @pl.when(inner)
    def _():
        pl.semaphore_wait(barrier, 5)

    @pl.when(jnp.logical_not(inner))
    def _():
        pl.semaphore_wait(barrier, 4)


def send(source, target, send_sem, recv_sem, device):
    return pltpu.make_async_remote_copy(
        src_ref=source,
        dst_ref=target,
        send_sem=send_sem,
        recv_sem=recv_sem,
        device_id=device,
        device_id_type=MESH,
    )


def gather_dispatch_kernel(
    planes, slots, x_ref, d_ref, outx_ref, outd_ref, outh_ref,
    buf, hot, place, stage_x, stage_d, stage_h, load_d,
    z_send, z_recv, x_send, x_recv, y_send, y_recv, c_send, c_recv, out_x, out_d, out_h, in_d,
):
    e, core, flip_x, flip_y, diagonal = neighbours()
    s = lax.axis_index("shard")
    length = x_ref.shape[0]
    half = length // 2
    width = x_ref.shape[1]
    low_half, high_half = pl.ds(0, half), pl.ds(half, half)
    greet(planes)
    buf[e, s] = x_ref[...]

    def up(sp):
        return send(buf.at[e, sp], buf.at[e, sp], z_send.at[0, sp], z_recv.at[sp], (e, s + 1))

    def down(sp):
        return send(buf.at[e, sp], buf.at[e, sp], z_send.at[1, sp], z_recv.at[sp], (e, s - 1))

    def first(sp):
        block = buf.at[e, sp]
        return [
            send(block, block, x_send.at[0, sp], x_recv.at[0, sp], (flip_x, s)),
            send(block, block, y_send.at[0, sp], y_recv.at[0, sp], (flip_y, s)),
            send(block, block, c_send.at[0, sp], c_recv.at[0, sp], (core, s)),
        ]

    def from_x(sp):
        block = buf.at[flip_x, sp]
        part = buf.at[flip_x, sp, low_half]
        return [
            send(part, part, y_send.at[1, sp], y_recv.at[1, sp], (flip_y, s)),
            send(block, block, c_send.at[1, sp], c_recv.at[1, sp], (core, s)),
        ]

    def from_y(sp):
        block = buf.at[flip_y, sp]
        part = buf.at[flip_y, sp, high_half]
        return [
            send(part, part, x_send.at[1, sp], x_recv.at[1, sp], (flip_x, s)),
            send(block, block, c_send.at[2, sp], c_recv.at[2, sp], (core, s)),
        ]

    def from_diagonal(sp):
        block = buf.at[diagonal, sp]
        return send(block, block, c_send.at[3, sp], c_recv.at[3, sp], (core, s))

    def arrived(block, sem):
        send(block, block, sem, sem, (core, s)).wait_recv()

    def plane_at(i):
        distance = (i + 1) // 2
        sign = 2 * (i % 2) - 1
        sp = s + sign * distance
        return sp, (sp >= 0) & (sp < planes) & (i >= 0) & (i <= 2 * planes - 2)

    def step_first(sp, i):
        @pl.when(i > 0)
        def _():
            arrived(buf.at[e, sp], z_recv.at[sp])

        @pl.when((sp <= s) & (s < planes - 1))
        def _():
            up(sp).start()

        @pl.when((sp >= s) & (s > 0))
        def _():
            down(sp).start()

        for copy in first(sp):
            copy.start()

    def step_second(sp):
        arrived(buf.at[flip_x, sp], x_recv.at[0, sp])
        for copy in from_x(sp):
            copy.start()
        arrived(buf.at[flip_y, sp], y_recv.at[0, sp])
        for copy in from_y(sp):
            copy.start()

    def step_third(sp):
        arrived(buf.at[diagonal, sp, low_half], y_recv.at[1, sp])
        arrived(buf.at[diagonal, sp, high_half], x_recv.at[1, sp])
        from_diagonal(sp).start()

    def copy_out(stage, out, sem, q, sp):
        rows = pl.ds(pl.multiple_of((q * planes + sp) * slots, 16), slots)
        return pltpu.make_async_copy(stage.at[q], out.at[:, rows, :], sem.at[q])

    def load(q, sp, k):
        return pltpu.make_async_copy(
            d_ref.at[2 * q + k, sp],
            load_d.at[q, pl.ds(k * length, length), :],
            in_d.at[q, k],
        )

    def start_loads(sp):
        for q in range(4):
            for k in range(2):
                load(q, sp, k).start()

    def copy_hot(q, sp):
        return pltpu.make_async_copy(
            stage_h.at[q], outh_ref.at[q * planes + sp], out_h.at[q]
        )

    row = lax.broadcasted_iota(jnp.int32, (length, length), 0)
    earlier = (lax.broadcasted_iota(jnp.int32, (length, length), 1) < row).astype(LOW)
    lane = lax.broadcasted_iota(jnp.int32, (2 * length, TAIL), 1).astype(FULL)
    slot = lax.broadcasted_iota(jnp.int32, (slots, 2 * length), 0).astype(FULL)

    def one_hot(q, sp):
        routes = load_d[q, :, MODEL_WIDTH:].astype(FULL)
        named = (routes[:, 0:1] == lane).astype(FULL)
        for k in range(1, TOPK):
            named = named + (routes[:, k : k + 1] == lane).astype(FULL)
        for k in range(2):
            here = slice(k * length, (k + 1) * length)
            rank = jnp.dot(earlier, named[here].astype(LOW), preferred_element_type=FULL)
            rank = jnp.where(named[here] > 0, rank + k * (slots // 2), -1.0)
            place[:, here] = rank.T
        rows = place[pl.ds(pl.multiple_of(e * EXP_DEV, EXP_DEV), EXP_DEV), :]
        for j in range(EXP_DEV):
            hot[q, sp, pl.ds(j * slots, slots), :] = (slot == rows[j : j + 1, :]).astype(LOW)

    def dispatch_d(sp, i):
        def one(q, carry):
            @pl.when(i > 0)
            def _():
                copy_out(stage_d, outd_ref, out_d, q, sp).wait()
                copy_hot(q, sp).wait()

            for k in range(2):
                load(q, sp, k).wait()
            one_hot(q, sp)
            stage_h[q] = hot[q, sp].T
            copy_hot(q, sp).start()

            def tile(t, inner):
                at = pl.ds(pl.multiple_of(t * TILE, TILE), TILE)
                got = jnp.dot(
                    hot[q, sp], load_d[q, :, at], preferred_element_type=FULL
                ).astype(LOW)
                stage_d[q, :, :, at] = got.reshape(EXP_DEV, slots, TILE)
                return inner

            lax.fori_loop(0, MODEL_WIDTH // TILE, tile, 0)
            copy_out(stage_d, outd_ref, out_d, q, sp).start()
            return carry

        lax.fori_loop(0, 4, one, 0)

    def dispatch(sp, i):
        for k, other in enumerate((core, core + flip_x - e, core + flip_y - e, core + diagonal - e)):
            arrived(buf.at[other, sp], c_recv.at[k, sp])

        def one(q, carry):
            @pl.when(i > 0)
            def _():
                copy_out(stage_x, outx_ref, out_x, q, sp).wait()

            def columns_of(at, wide):
                rows = jnp.concatenate(
                    [buf[2 * q, sp, :, at], buf[2 * q + 1, sp, :, at]], axis=0
                )
                got = jnp.dot(hot[q, sp], rows, preferred_element_type=FULL).astype(LOW)
                stage_x[q, :, :, at] = got.reshape(EXP_DEV, slots, wide)

            def tile(t, inner):
                columns_of(pl.ds(pl.multiple_of(t * TILE, TILE), TILE), TILE)
                return inner

            lax.fori_loop(0, MODEL_WIDTH // TILE, tile, 0)
            if width > MODEL_WIDTH:
                columns_of(pl.ds(MODEL_WIDTH, width - MODEL_WIDTH), width - MODEL_WIDTH)
            copy_out(stage_x, outx_ref, out_x, q, sp).start()
            return carry

        lax.fori_loop(0, 4, one, 0)

    def step(i, carry):
        for lag, work in ((0, step_first), (1, step_second), (2, step_third), (0, dispatch_d), (3, dispatch)):
            sp, there = plane_at(i - lag)

            @pl.when(there)
            def _(sp=sp, lag=lag, work=work):
                if work in (step_second, step_third):
                    work(sp)
                else:
                    work(sp, i - lag)

        sp, there = plane_at(i + 1)

        @pl.when(there)
        def _():
            start_loads(sp)

        return carry

    start_loads(s)
    lax.fori_loop(0, 2 * planes + 2, step, 0)

    def drain(sp, carry):
        for copy in first(sp) + from_x(sp) + from_y(sp) + [from_diagonal(sp)]:
            copy.wait_send()

        @pl.when((sp <= s) & (s < planes - 1))
        def _():
            up(sp).wait_send()

        @pl.when((sp >= s) & (s > 0))
        def _():
            down(sp).wait_send()

        return carry

    lax.fori_loop(0, planes, drain, 0)
    for q in range(4):
        copy_out(stage_x, outx_ref, out_x, q, 0).wait()
        copy_out(stage_d, outd_ref, out_d, q, 0).wait()
        copy_hot(q, 0).wait()


def gather_dispatch(rows, d_all, planes, slots, identity):
    owners = lax.axis_size("expert")
    length, width = rows.shape
    pairs = owners * planes // 2
    total = pairs * slots
    kernel = functools.partial(gather_dispatch_kernel, planes, slots)
    return pl.pallas_call(
        kernel,
        out_shape=[
            jax.ShapeDtypeStruct((EXP_DEV, total, width), LOW),
            jax.ShapeDtypeStruct((EXP_DEV, total, MODEL_WIDTH), LOW),
            jax.ShapeDtypeStruct((pairs, 2 * length, EXP_DEV * slots), LOW),
        ],
        in_specs=[VM, ANY],
        out_specs=[ANY, ANY, ANY],
        scratch_shapes=[
            pltpu.VMEM((owners, planes, length, width), LOW),
            pltpu.VMEM((4, planes, EXP_DEV * slots, 2 * length), LOW),
            pltpu.VMEM((TAIL, 2 * length), FULL),
            pltpu.VMEM((4, EXP_DEV, slots, width), LOW),
            pltpu.VMEM((4, EXP_DEV, slots, MODEL_WIDTH), LOW),
            pltpu.VMEM((4, 2 * length, EXP_DEV * slots), LOW),
            pltpu.VMEM((4, 2 * length, MODEL_WIDTH + TAIL), LOW),
            DMA((2, planes)),
            DMA((planes,)),
            DMA((2, planes)),
            DMA((2, planes)),
            DMA((2, planes)),
            DMA((2, planes)),
            DMA((4, planes)),
            DMA((4, planes)),
            DMA((4,)),
            DMA((4,)),
            DMA((4,)),
            DMA((4, 2)),
        ],
        compiler_params=pltpu.CompilerParams(
            collective_id=identity, has_side_effects=True, vmem_limit_bytes=VMEM_LIMIT
        ),
    )(rows, d_all)


def expert_kernel(
    sel_ref, x_ref, dy_ref, wg_ref, wu_ref, wd_ref,
    y_ref, dx_ref, dwg_ref, dwu_ref, dwd_ref, a_all, dg_all, du_all, a_t, d_t,
):
    rows = x_ref.shape[1]
    step = rows
    experts = sel_ref.shape[2] // 2
    sel = sel_ref[0, 0:1, :]
    lane = lax.broadcasted_iota(jnp.int32, sel.shape, 1)
    high_sel = jnp.where(lane < experts, sel, 0.0)
    rest_sel = sel - high_sel
    nt = (((1,), (1,)), ((), ()))

    def chunk(r, carry):
        at = pl.ds(pl.multiple_of(r * step, step), step)
        x = x_ref[0, at, :MODEL_WIDTH]
        tail = x_ref[0, at, MODEL_WIDTH:].astype(FULL)
        dy = dy_ref[0, at, :]
        gate = jnp.sum(tail * sel, axis=1, keepdims=True)
        g = lax.dot_general(x, wg_ref[0], nt, preferred_element_type=FULL)
        u = lax.dot_general(x, wu_ref[0], nt, preferred_element_type=FULL)
        da = lax.dot_general(dy, wd_ref[0], nt, preferred_element_type=FULL)
        sigma = 1.0 / (1.0 + jnp.exp(-g))
        silu = g * sigma
        act = (silu * u).astype(LOW).astype(FULL)
        d_gate = jnp.sum(act * da, axis=1, keepdims=True)
        d_act = da * gate
        a_all[at, :] = (act * gate).astype(LOW)
        dg_all[at, :] = (d_act * u * sigma * (1.0 + g * (1.0 - sigma))).astype(LOW)
        du_all[at, :] = (d_act * silu).astype(LOW)
        high = d_gate.astype(LOW).astype(FULL)
        dx_ref[0, at, MODEL_WIDTH:] = (high * high_sel + (d_gate - high) * rest_sel).astype(LOW)
        y_ref[0, at, :] = jnp.dot(
            a_all[at, :], wd_ref[0], preferred_element_type=FULL
        ).astype(LOW)
        dx_ref[0, at, :MODEL_WIDTH] = (
            jnp.dot(dg_all[at, :], wg_ref[0], preferred_element_type=FULL)
            + jnp.dot(du_all[at, :], wu_ref[0], preferred_element_type=FULL)
        ).astype(LOW)
        return carry

    lax.fori_loop(0, rows // step, chunk, 0)
    hidden = a_t.shape[0]
    a_t[...] = a_all[...].T
    d_t[:hidden, :] = dg_all[...].T
    d_t[hidden:, :] = du_all[...].T

    def tile(t, carry):
        at = pl.ds(pl.multiple_of(t * TILE, TILE), TILE)
        x = x_ref[0, :, at]
        got = jnp.dot(d_t[...], x, preferred_element_type=FULL)
        dwg_ref[0, :, at] = got[:hidden]
        dwu_ref[0, :, at] = got[hidden:]
        dwd_ref[0, :, at] = jnp.dot(a_t[...], dy_ref[0, :, at], preferred_element_type=FULL)
        return carry

    lax.fori_loop(0, MODEL_WIDTH // TILE, tile, 0)


def expert_pass(sel, x, dy, w_gate, w_up, w_down):
    rows, width = x.shape[1:]
    hidden = w_gate.shape[1]

    def spec(*shape):
        return pl.BlockSpec((1,) + shape, lambda j: (j, 0, 0))

    def out(*shape, dtype=LOW):
        return jax.ShapeDtypeStruct((EXP_DEV,) + shape, dtype)

    return pl.pallas_call(
        expert_kernel,
        grid=(EXP_DEV,),
        in_specs=[
            spec(*sel.shape[1:]),
            spec(rows, width),
            spec(rows, MODEL_WIDTH),
            spec(hidden, MODEL_WIDTH),
            spec(hidden, MODEL_WIDTH),
            spec(hidden, MODEL_WIDTH),
        ],
        out_specs=[
            spec(rows, MODEL_WIDTH),
            spec(rows, width),
            spec(hidden, MODEL_WIDTH),
            spec(hidden, MODEL_WIDTH),
            spec(hidden, MODEL_WIDTH),
        ],
        out_shape=[
            out(rows, MODEL_WIDTH),
            out(rows, width),
            out(hidden, MODEL_WIDTH, dtype=FULL),
            out(hidden, MODEL_WIDTH, dtype=FULL),
            out(hidden, MODEL_WIDTH, dtype=FULL),
        ],
        scratch_shapes=[pltpu.VMEM((rows, hidden), LOW)] * 3
        + [pltpu.VMEM((hidden, rows), LOW), pltpu.VMEM((2 * hidden, rows), LOW)],
        compiler_params=pltpu.CompilerParams(vmem_limit_bytes=VMEM_LIMIT),
        cost_estimate=pl.CostEstimate(
            flops=EXP_DEV * rows * MODEL_WIDTH * hidden * 18,
            bytes_accessed=160 << 20,
            transcendentals=EXP_DEV * rows * hidden,
        ),
    )(sel, x, dy, w_gate, w_up, w_down)


def combine_home_kernel(
    planes, slots, hot_ref, v_ref, m_ref, out_ref, mix_ref,
    hot, load, mine, away, c_in, x_in, y_in, x_half, y_half, u_in, d_in,
    hot_sem, in_sem, free, c_send, c_recv, x_send, x_recv, y_send, y_recv, z_send, z_recv,
):
    e, core, flip_x, flip_y, diagonal = neighbours()
    s = lax.axis_index("shard")
    q_own, q_x, q_y, q_d = e // 2, flip_x // 2, flip_y // 2, diagonal // 2
    parity = e % 2
    length, width = out_ref.shape
    half = length // 2
    low_half, high_half = pl.ds(0, half), pl.ds(half, half)
    order = (q_d, q_x, q_y, q_own)
    spans = (pl.ds(0, width), pl.ds(0, MODEL_WIDTH))

    def fetch(kind, k, sp):
        rows = pl.ds(pl.multiple_of((order[k] * planes + sp) * slots, 16), slots)
        if kind == 0:
            return pltpu.make_async_copy(v_ref.at[:, rows, :], load.at[k % 2], in_sem.at[k % 2])
        return pltpu.make_async_copy(
            m_ref.at[:, rows, :], load.at[k % 2, :, :, pl.ds(0, MODEL_WIDTH)], in_sem.at[k % 2]
        )

    def fetch_hot(k, sp):
        return pltpu.make_async_copy(
            hot_ref.at[order[k] * planes + sp], hot.at[k % 2], hot_sem.at[k % 2]
        )

    def to_core(kind, q, sp):
        return send(
            away.at[q, sp, :, spans[kind]], c_in.at[q, sp, :, spans[kind]], c_send.at[kind, q, sp], c_recv.at[kind, q, sp],
            (core, s),
        )

    def halves(kind, sp):
        return [
            send(
                mine.at[q_d, sp, low_half, spans[kind]], y_half.at[kind, sp, :, spans[kind]],
                y_send.at[kind, 0, sp], y_recv.at[kind, 0, sp], (flip_y, s),
            ),
            send(
                mine.at[q_d, sp, high_half, spans[kind]], x_half.at[kind, sp, :, spans[kind]],
                x_send.at[kind, 0, sp], x_recv.at[kind, 0, sp], (flip_x, s),
            ),
        ]

    def to_x(kind, sp):
        return send(
            mine.at[q_x, sp, :, spans[kind]], x_in.at[kind, sp, :, spans[kind]], x_send.at[kind, 1, sp], x_recv.at[kind, 1, sp],
            (flip_x, s),
        )

    def to_y(kind, sp):
        return send(
            mine.at[q_y, sp, :, spans[kind]], y_in.at[kind, sp, :, spans[kind]], y_send.at[kind, 1, sp], y_recv.at[kind, 1, sp],
            (flip_y, s),
        )

    def up(kind, sp):
        return send(
            mine.at[q_own, sp, :, spans[kind]], u_in.at[kind, sp, :, spans[kind]], z_send.at[kind, 0, sp], z_recv.at[kind, 0, sp],
            (e, s + 1),
        )

    def down(kind, sp):
        return send(
            mine.at[q_own, sp, :, spans[kind]], d_in.at[kind, sp, :, spans[kind]], z_send.at[kind, 1, sp], z_recv.at[kind, 1, sp],
            (e, s - 1),
        )

    def settled(kind, sp):
        for q in range(4):
            to_core(kind, q, sp).wait_send()
        for copy in halves(kind, sp) + [to_x(kind, sp), to_y(kind, sp)]:
            copy.wait_send()

        @pl.when(sp > s)
        def _():
            up(kind, sp).wait_send()

        @pl.when(sp < s)
        def _():
            down(kind, sp).wait_send()

    def arrived(block, sem):
        send(block, block, sem, sem, (core, s)).wait_recv()

    def plane_at(i):
        back = 2 * planes - 2 - i
        sp = s + (2 * (back % 2) - 1) * ((back + 1) // 2)
        return sp, (sp >= 0) & (sp < planes) & (i >= 0) & (back >= 0)

    def add(target, *others):
        if len(others) == 1:
            target[...] = target[...] + others[0][...]
            return
        total = target[...].astype(FULL)
        for other in others:
            total = total + other[...].astype(FULL)
        target[...] = total.astype(LOW)

    def work(kind, sp):
        if kind == 1:
            settled(0, sp)
            pl.semaphore_wait(free.at[sp], 1)
        for k, q in enumerate(order):
            fetch_hot(k, sp).wait()
            fetch(kind, k, sp).wait()

            def part(at, wide, q=q, k=k):
                rows = load[k % 2, :, :, at].reshape(EXP_DEV * slots, wide)
                got = jnp.dot(hot[k % 2], rows, preferred_element_type=FULL).astype(LOW)
                got = got.reshape(2, length, wide)

                @pl.when(parity == 0)
                def _():
                    mine[q, sp, :, at] = got[0]
                    away[q, sp, :, at] = got[1]

                @pl.when(parity == 1)
                def _():
                    mine[q, sp, :, at] = got[1]
                    away[q, sp, :, at] = got[0]

            def tile(t, inner, part=part):
                part(pl.ds(pl.multiple_of(t * TILE, TILE), TILE), TILE)
                return inner

            lax.fori_loop(0, MODEL_WIDTH // TILE, tile, 0)
            if kind == 0 and width > MODEL_WIDTH:
                part(pl.ds(MODEL_WIDTH, width - MODEL_WIDTH), width - MODEL_WIDTH)
            to_core(kind, q, sp).start()
            if k < 2:
                fetch_hot(k + 2, sp).start()
                fetch(kind, k + 2, sp).start()

    def fetch_first(kind, sp):
        for k in range(2):
            fetch_hot(k, sp).start()
            fetch(kind, k, sp).start()

    def pairs(kind, sp):
        for k, q in enumerate(order):
            arrived(c_in.at[q, sp, :, spans[kind]], c_recv.at[kind, q, sp])
            add(mine.at[q, sp, :, spans[kind]], c_in.at[q, sp, :, spans[kind]])
            if k == 0:
                for copy in halves(kind, sp):
                    copy.start()
        if kind == 0:
            pl.semaphore_signal(free.at[sp], 1, device_id=(core, s), device_id_type=MESH)

    def sides(kind, sp):
        arrived(y_half.at[kind, sp, :, spans[kind]], y_recv.at[kind, 0, sp])
        add(mine.at[q_x, sp, low_half, spans[kind]], y_half.at[kind, sp, :, spans[kind]])
        to_x(kind, sp).start()
        arrived(x_half.at[kind, sp, :, spans[kind]], x_recv.at[kind, 0, sp])
        add(mine.at[q_y, sp, high_half, spans[kind]], x_half.at[kind, sp, :, spans[kind]])
        to_y(kind, sp).start()

    def line(kind, sp):
        arrived(x_in.at[kind, sp, :, spans[kind]], x_recv.at[kind, 1, sp])
        arrived(y_in.at[kind, sp, :, spans[kind]], y_recv.at[kind, 1, sp])
        add(
            mine.at[q_own, sp, :, spans[kind]],
            x_in.at[kind, sp, :, spans[kind]],
            y_in.at[kind, sp, :, spans[kind]],
        )

        @pl.when((sp >= s) & (s > 0))
        def _():
            arrived(u_in.at[kind, sp, :, spans[kind]], z_recv.at[kind, 0, sp])
            add(mine.at[q_own, sp, :, spans[kind]], u_in.at[kind, sp, :, spans[kind]])

        @pl.when((sp <= s) & (s < planes - 1))
        def _():
            arrived(d_in.at[kind, sp, :, spans[kind]], z_recv.at[kind, 1, sp])
            add(mine.at[q_own, sp, :, spans[kind]], d_in.at[kind, sp, :, spans[kind]])

        @pl.when(sp > s)
        def _():
            up(kind, sp).start()

        @pl.when(sp < s)
        def _():
            down(kind, sp).start()

        @pl.when(sp == s)
        def _():
            if kind == 0:
                out_ref[...] = mine[q_own, sp].astype(FULL)
            else:
                mix_ref[...] = mine[q_own, sp, :, :MODEL_WIDTH].astype(FULL)

    greet(planes)
    span = 2 * planes - 1

    def step(t, carry):
        for lag, job in ((0, fetch_first), (1, pairs), (2, sides), (0, work), (3, line)):
            for kind in range(2):
                sp, there = plane_at(t - lag - kind * span)

                @pl.when(there)
                def _(sp=sp, job=job, kind=kind):
                    job(kind, sp)

        return carry

    lax.fori_loop(0, 2 * span + 3, step, 0)

    def drain(sp, carry):
        settled(1, sp)
        return carry

    lax.fori_loop(0, planes, drain, 0)


def combine_home(hot, v, m, length, planes, slots, identity):
    width = v.shape[2]
    block = (planes, length, width)
    part = (planes, length // 2, width)
    return pl.pallas_call(
        functools.partial(combine_home_kernel, planes, slots),
        out_shape=[
            jax.ShapeDtypeStruct((length, width), FULL),
            jax.ShapeDtypeStruct((length, MODEL_WIDTH), FULL),
        ],
        in_specs=[ANY, ANY, ANY],
        out_specs=[VM, VM],
        scratch_shapes=[
            pltpu.VMEM((2,) + hot.shape[1:], LOW),
            pltpu.VMEM((2, EXP_DEV, slots, width), LOW),
            pltpu.VMEM((4,) + block, LOW),
            pltpu.VMEM((4,) + block, LOW),
            pltpu.VMEM((4,) + block, LOW),
            pltpu.VMEM((2,) + block, LOW),
            pltpu.VMEM((2,) + block, LOW),
            pltpu.VMEM((2,) + part, LOW),
            pltpu.VMEM((2,) + part, LOW),
            pltpu.VMEM((2,) + block, LOW),
            pltpu.VMEM((2,) + block, LOW),
            DMA((2,)),
            DMA((2,)),
            pltpu.SemaphoreType.REGULAR((planes,)),
            DMA((2, 4, planes)),
            DMA((2, 4, planes)),
            DMA((2, 2, planes)),
            DMA((2, 2, planes)),
            DMA((2, 2, planes)),
            DMA((2, 2, planes)),
            DMA((2, 2, planes)),
            DMA((2, 2, planes)),
        ],
        compiler_params=pltpu.CompilerParams(
            collective_id=identity, has_side_effects=True, vmem_limit_bytes=VMEM_LIMIT
        ),
    )(hot, v, m)


def greet_plane(planes, owners):
    e, s = lax.axis_index("expert"), lax.axis_index("shard")
    barrier = pltpu.get_barrier_semaphore()
    for o in range(1, owners):
        pl.semaphore_signal(
            barrier, 1, device_id=(lax.rem(e + o, owners), s), device_id_type=MESH
        )

    @pl.when(s > 0)
    def _():
        pl.semaphore_signal(barrier, 1, device_id=(e, s - 1), device_id_type=MESH)

    @pl.when(s < planes - 1)
    def _():
        pl.semaphore_signal(barrier, 1, device_id=(e, s + 1), device_id_type=MESH)

    inner = (s > 0) & (s < planes - 1)

    @pl.when(inner)
    def _():
        pl.semaphore_wait(barrier, owners + 1)

    @pl.when(jnp.logical_not(inner))
    def _():
        pl.semaphore_wait(barrier, owners)


def gather_steps(at, cut, source, x_send, x_recv, y_send, y_recv, c_send, c_recv):
    e, core, flip_x, flip_y, diagonal = neighbours()
    s = lax.axis_index("shard")

    def arrived(block, sem):
        send(block, block, sem, sem, (core, s)).wait_recv()

    def first():
        return [
            send(source, at(e), x_send(0), x_recv(0), (flip_x, s)),
            send(source, at(e), y_send(0), y_recv(0), (flip_y, s)),
            send(source, at(e), c_send(0), c_recv(0), (core, s)),
        ]

    def from_x():
        return [
            send(cut(flip_x, 0), cut(flip_x, 0), y_send(1), y_recv(1), (flip_y, s)),
            send(at(flip_x), at(flip_x), c_send(1), c_recv(1), (core, s)),
        ]

    def from_y():
        return [
            send(cut(flip_y, 1), cut(flip_y, 1), x_send(1), x_recv(1), (flip_x, s)),
            send(at(flip_y), at(flip_y), c_send(2), c_recv(2), (core, s)),
        ]

    def from_diagonal():
        return [send(at(diagonal), at(diagonal), c_send(3), c_recv(3), (core, s))]

    def begin():
        for copy in first():
            copy.start()

    def second():
        arrived(at(flip_x), x_recv(0))
        for copy in from_x():
            copy.start()
        arrived(at(flip_y), y_recv(0))
        for copy in from_y():
            copy.start()

    def third():
        arrived(cut(diagonal, 0), y_recv(1))
        arrived(cut(diagonal, 1), x_recv(1))
        for copy in from_diagonal():
            copy.start()

    def last():
        for k, lane in enumerate((core, core + flip_x - e, core + flip_y - e, core + diagonal - e)):
            arrived(at(lane), c_recv(k))

    def sent():
        for copy in first() + from_x() + from_y() + from_diagonal():
            copy.wait_send()

    return begin, second, third, last, sent


def rope_tables(places, frequency):
    angles = places * frequency
    lane = lax.broadcasted_iota(jnp.int32, angles.shape, 1)
    sine = jnp.sin(angles)
    return jnp.cos(angles), jnp.where(lane < HEAD_SIZE // 2, -sine, sine)


def half_turn(v):
    return pltpu.roll(v, HEAD_SIZE // 2, 1)


def head_gains(rows, planes):
    total = rows[0, :, :HEAD_SIZE].astype(FULL)
    for sp in range(1, planes):
        part = rows[sp, :, :HEAD_SIZE].astype(FULL)
        total = total + pltpu.roll(part, sp * (HEAD_SIZE // planes), 1)
    return total[2:3], total[3:4]


def front_kernel(
    planes, owners, qkv_ref, router_ref, gain_ref, tok_ref, d_ref, freq_ref, out_ref,
    d_all, w_out_all, w_all_out, r_all, gains, tail_ref, h1_ref, proj_ref, probs_ref, mixed_ref, branch_ref,
    w_all, tok_all, w_mine, q_rows, mine, away, c_in, x_in, y_in, x_half, y_half,
    keep_sem, w_send, w_recv, v_send, v_recv, k_send, k_recv, r_send, r_recv, g_send, g_recv,
    o_send, o_recv, z_send, z_recv, rx_send, rx_recv, ry_send, ry_recv, rc_send, rc_recv,
    tx_send, tx_recv, ty_send, ty_recv, tc_send, tc_recv,
    dx_send, dx_recv, dy_send, dy_recv, dc_send, dc_recv,
    px_send, px_recv, py_send, py_recv, pc_send, pc_recv,
):
    e, core, flip_x, flip_y, diagonal = neighbours()
    s = lax.axis_index("shard")
    lanes = owners // planes
    home = e // lanes
    length = tok_ref.shape[0]
    half = length // 2
    count = w_mine.shape[0]
    heads = count // HEAD_SIZE
    pieces = 8
    out_part = count // pieces
    deep = qkv_ref.shape[0]
    query_cols = count
    kv_at = pl.ds(pl.multiple_of(count + HEAD_SIZE * (e % 2), HEAD_SIZE), HEAD_SIZE)

    def arrived(block, sem):
        send(block, block, sem, sem, (core, s)).wait_recv()

    def w_copy(sp, way):
        block = w_all.at[sp, :, pl.ds(0, query_cols)]
        return send(block, block, w_send.at[way, sp], w_recv.at[sp], (e, s + 1 - 2 * way))

    def v_copy(sp, way):
        block = w_all.at[sp, :, kv_at]
        return send(block, block, v_send.at[way, sp], v_recv.at[sp], (e, s + 1 - 2 * way))

    def r_copy(sp, way):
        block = r_all.at[e, sp]
        return send(block, block, r_send.at[way, sp], r_recv.at[sp], (e, s + 1 - 2 * way))

    def k_copy(sp):
        block = w_all.at[sp, :, kv_at]
        return send(block, block, k_send.at[sp], k_recv.at[sp], (core, s))

    def g_copy(sp, way):
        block = gains.at[sp]
        return send(block, block, g_send.at[way, sp], g_recv.at[sp], (e, s + 1 - 2 * way))

    def d_copy(sp, way):
        block = d_all.at[e, sp]
        return send(block, block, z_send.at[way, sp], z_recv.at[sp], (e, s + 1 - 2 * way))

    def o_copy(k, way):
        block = w_mine.at[pl.ds(k * out_part, out_part)]
        return send(block, block, o_send.at[way, k], o_recv.at[k], (e, s + 1 - 2 * way))

    t_begin, t_second, t_third, t_last, t_sent = gather_steps(
        lambda lane: tok_all.at[lane],
        lambda lane, k: tok_all.at[lane, pl.ds(k * half, half)],
        tok_ref,
        lambda k: tx_send.at[k],
        lambda k: tx_recv.at[k],
        lambda k: ty_send.at[k],
        lambda k: ty_recv.at[k],
        lambda k: tc_send.at[k],
        lambda k: tc_recv.at[k],
    )

    r_half = planes // 2
    r_begin, r_second, r_third, r_last, r_sent = gather_steps(
        lambda lane: r_all.at[lane],
        lambda lane, k: r_all.at[lane, pl.ds(k * r_half, r_half)],
        r_all.at[e],
        lambda k: rx_send.at[k],
        lambda k: rx_recv.at[k],
        lambda k: ry_send.at[k],
        lambda k: ry_recv.at[k],
        lambda k: rc_send.at[k],
        lambda k: rc_recv.at[k],
    )

    def d_rows(sp):
        return gather_steps(
            lambda lane: d_all.at[lane, sp],
            lambda lane, k: d_all.at[lane, sp, pl.ds(k * half, half)],
            d_all.at[e, sp],
            lambda k: dx_send.at[k, sp],
            lambda k: dx_recv.at[k, sp],
            lambda k: dy_send.at[k, sp],
            lambda k: dy_recv.at[k, sp],
            lambda k: dc_send.at[k, sp],
            lambda k: dc_recv.at[k, sp],
        )

    keep_d = pltpu.make_async_copy(d_ref, d_all.at[e, s], keep_sem.at[0])
    rows = pl.ds(pl.multiple_of((e - home * lanes) * count, 16), count)
    load_o = pltpu.make_async_copy(out_ref.at[rows], w_mine, keep_sem.at[1])
    keep_w = pltpu.make_async_copy(w_all, w_all_out, keep_sem.at[2])
    keep_o = pltpu.make_async_copy(w_mine, w_out_all, keep_sem.at[3])
    at = pl.ds(pl.multiple_of(e * count, count), count)
    load_w = pltpu.make_async_copy(
        qkv_ref.at[:, at], w_all.at[s, :, pl.ds(0, query_cols)], keep_sem.at[4]
    )
    kv_from = (QUERY_HEADS + e % 2 * KEY_VALUE_HEADS + e * KEY_VALUE_HEADS // owners) * HEAD_SIZE
    at = pl.ds(pl.multiple_of(kv_from, HEAD_SIZE), HEAD_SIZE)
    load_v = pltpu.make_async_copy(qkv_ref.at[:, at], w_all.at[s, :, kv_at], keep_sem.at[5])
    keep_d.start()

    @pl.when(s == home)
    def _():
        load_o.start()

    load_w.start()
    load_v.start()
    r_all[e, s] = router_ref[...]
    gains[s] = gain_ref[...]
    tok_all[e] = tok_ref[...]
    greet(planes)

    def both_ways(copy, sp):
        @pl.when((sp <= s) & (s < planes - 1))
        def _():
            copy(sp, 0).start()

        @pl.when((sp >= s) & (s > 0))
        def _():
            copy(sp, 1).start()

    def plane_at(i):
        sp = s + (2 * (i % 2) - 1) * ((i + 1) // 2)
        return sp, (sp >= 0) & (sp < planes) & (i >= 0) & (i <= 2 * planes - 2)

    def out_step(k):
        @pl.when(s != home)
        def _():
            arrived(w_mine.at[pl.ds(k * out_part, out_part)], o_recv.at[k])

        @pl.when((s >= home) & (s < planes - 1))
        def _():
            o_copy(k, 0).start()

        @pl.when((s <= home) & (s > 0))
        def _():
            o_copy(k, 1).start()

    t_begin()
    both_ways(g_copy, s)
    keep_d.wait()
    both_ways(d_copy, s)
    load_w.wait()
    both_ways(w_copy, s)
    load_v.wait()
    both_ways(v_copy, s)
    both_ways(r_copy, s)
    k_copy(s).start()
    d_rows(s)[0]()

    def weights(i, carry):
        sp, there = plane_at(i)

        @pl.when(there & (i > 0))
        def _():
            arrived(gains.at[sp], g_recv.at[sp])
            both_ways(g_copy, sp)
            arrived(d_all.at[e, sp], z_recv.at[sp])
            both_ways(d_copy, sp)
            d_rows(sp)[0]()
            arrived(w_all.at[sp, :, pl.ds(0, query_cols)], w_recv.at[sp])
            both_ways(w_copy, sp)
            arrived(w_all.at[sp, :, kv_at], v_recv.at[sp])
            both_ways(v_copy, sp)
            k_copy(sp).start()
            arrived(r_all.at[e, sp], r_recv.at[sp])
            both_ways(r_copy, sp)

        @pl.when(i == 1)
        def _():
            t_second()

        @pl.when(i == 2)
        def _():
            t_third()

        @pl.when((i == 4) & (s == home))
        def _():
            load_o.wait()
            for k in range(pieces):
                out_step(k)

        return carry

    lax.fori_loop(1, 2 * planes - 1, weights, 0)
    r_begin()
    t_last()
    other_kv = pl.ds(pl.multiple_of(count + HEAD_SIZE * (1 - e % 2), HEAD_SIZE), HEAD_SIZE)
    for sp in range(planes):
        arrived(w_all.at[sp, :, other_kv], k_recv.at[sp])
    keep_w.start()

    def distant(n):
        return (s - home == n) | (home - s == n)

    gain_query, gain_key = head_gains(gains, planes)
    row = lax.broadcasted_iota(jnp.int32, (length, length), 0).astype(FULL)
    column = lax.broadcasted_iota(jnp.int32, (length, length), 1).astype(FULL)

    def attend(b, carry):
        x = tok_all[b, :, :MODEL_WIDTH].astype(FULL)
        inverse = lax.rsqrt(jnp.mean(x * x, axis=1, keepdims=True) + EPS)
        total = jnp.zeros((length, w_all.shape[2]), FULL)
        for sp in range(planes):
            at = slice(sp * deep, (sp + 1) * deep)
            part = x[:, at] * inverse * gains[sp, 0:1, :].astype(FULL)
            part = part.astype(LOW)
            h1_ref[b, :, at] = part
            total = total + jnp.dot(part, w_all[sp], preferred_element_type=FULL)
        proj_ref[b] = total
        tail_ref[b] = tok_all[b, :, MODEL_WIDTH:]
        places = tok_all[b, :, MODEL_WIDTH:].astype(FULL)[:, 1:2]
        cosine, sine = rope_tables(places, freq_ref[0:1, :])

        def normed(v, gain):
            v = v * lax.rsqrt(jnp.mean(v * v, axis=1, keepdims=True) + EPS) * gain
            return (v * cosine + half_turn(v) * sine).astype(LOW)

        for h in range(heads):
            at = slice(h * HEAD_SIZE, (h + 1) * HEAD_SIZE)
            q_rows[h * length : (h + 1) * length, :] = normed(total[:, at], gain_query)
        key = normed(total[:, count : count + HEAD_SIZE], gain_key)
        value = total[:, count + HEAD_SIZE :].astype(LOW)
        scores = lax.dot_general(
            q_rows[...], key, (((1,), (1,)), ((), ())), preferred_element_type=FULL
        ) * (HEAD_SIZE**-0.5)
        allowed = (column <= row) & (column >= row - places)
        scores = jnp.where(jnp.concatenate([allowed] * heads, axis=0), scores, -1e30)
        exponent = jnp.exp(scores - jnp.max(scores, axis=1, keepdims=True))
        probs = (exponent / jnp.sum(exponent, axis=1, keepdims=True)).astype(LOW)
        probs_ref[b] = probs
        mixed = jnp.dot(probs, value, preferred_element_type=FULL).astype(LOW)
        for h in range(heads):
            at = slice(h * HEAD_SIZE, (h + 1) * HEAD_SIZE)
            mixed_ref[b, :, at] = mixed[h * length : (h + 1) * length]

        for lag, stage in ((0, 1), (2, 2)):
            sp, there = plane_at(b - lag)

            @pl.when(there)
            def _(sp=sp, stage=stage):
                d_rows(sp)[stage]()

        for k in range(pieces):

            @pl.when((b == k) & distant(1))
            def _(k=k):
                out_step(k)

        for k in range(5):

            @pl.when((b == 3 + k) & distant(2))
            def _(k=k):
                out_step(k)

        return carry

    lax.fori_loop(0, owners, attend, 0)
    for i in range(owners - 2, 2 * planes - 1):
        sp, there = plane_at(i)

        @pl.when(there)
        def _(sp=sp):
            d_rows(sp)[2]()


    @pl.when(distant(2))
    def _():
        for k in range(5, pieces):
            out_step(k)

    r_second()
    for n in range(3, planes):

        @pl.when(distant(n))
        def _():
            for k in range(pieces):
                out_step(k)

    keep_o.start()
    begin, middle, finish, sent = project_steps(
        False, mixed_ref, w_mine, branch_ref, mine, away, c_in, x_in, y_in, x_half, y_half,
        pc_send, pc_recv, px_send, px_recv, py_send, py_recv,
    )
    begin()
    r_third()
    middle()
    finish()
    r_last()
    t_sent()
    r_sent()
    sent()

    def settled(copy, sp):
        @pl.when((sp <= s) & (s < planes - 1))
        def _():
            copy(sp, 0).wait_send()

        @pl.when((sp >= s) & (s > 0))
        def _():
            copy(sp, 1).wait_send()

    def drain(sp, carry):
        d_rows(sp)[3]()
        d_rows(sp)[4]()
        settled(w_copy, sp)
        settled(v_copy, sp)
        settled(r_copy, sp)
        k_copy(sp).wait_send()
        settled(g_copy, sp)
        settled(d_copy, sp)
        return carry

    lax.fori_loop(0, planes, drain, 0)
    for k in range(pieces):

        @pl.when((s >= home) & (s < planes - 1))
        def _(k=k):
            o_copy(k, 0).wait_send()

        @pl.when((s <= home) & (s > 0))
        def _(k=k):
            o_copy(k, 1).wait_send()

    keep_w.wait()
    keep_o.wait()


def front(w, router, gain_rows, tokens, w_out, d_rows, frequency, planes, owners, identity):
    def out(*shape, dtype=LOW):
        return jax.ShapeDtypeStruct(shape, dtype)

    length = tokens.shape[0]
    count = w_out.shape[0] * planes // owners
    qkv_cols = count + 2 * HEAD_SIZE
    block = (length, MODEL_WIDTH)
    part = (length // 2, MODEL_WIDTH)
    return pl.pallas_call(
        functools.partial(front_kernel, planes, owners),
        out_shape=[
            out(owners, planes, *d_rows.shape),
            out(count, MODEL_WIDTH),
            out(planes, w.shape[0], qkv_cols),
            out(owners, planes, *router.shape),
            out(planes, *gain_rows.shape),
            out(owners, length, TAIL),
            out(owners, length, MODEL_WIDTH),
            out(owners, length, qkv_cols, dtype=FULL),
            out(owners, length * count // HEAD_SIZE, length),
            out(owners, length, count),
            out(length, MODEL_WIDTH, dtype=FULL),
        ],
        in_specs=[ANY, VM, VM, VM, VM, VM, ANY],
        out_specs=[ANY, ANY, ANY, VM, VM, VM, VM, VM, VM, VM, VM],
        scratch_shapes=[
            pltpu.VMEM((planes, w.shape[0], qkv_cols), LOW),
            pltpu.VMEM((owners,) + tokens.shape, LOW),
            pltpu.VMEM((count, MODEL_WIDTH), LOW),
            pltpu.VMEM((length * count // HEAD_SIZE, HEAD_SIZE), LOW),
            pltpu.VMEM((4,) + block, LOW),
            pltpu.VMEM((4,) + block, LOW),
            pltpu.VMEM((4,) + block, LOW),
            pltpu.VMEM(block, LOW),
            pltpu.VMEM(block, LOW),
            pltpu.VMEM(part, LOW),
            pltpu.VMEM(part, LOW),
            DMA((6,)),
            DMA((2, planes)),
            DMA((planes,)),
            DMA((2, planes)),
            DMA((planes,)),
            DMA((planes,)),
            DMA((planes,)),
            DMA((2, planes)),
            DMA((planes,)),
            DMA((2, planes)),
            DMA((planes,)),
            DMA((2, 8)),
            DMA((8,)),
            DMA((2, planes)),
            DMA((planes,)),
            DMA((2,)),
            DMA((2,)),
            DMA((2,)),
            DMA((2,)),
            DMA((4,)),
            DMA((4,)),
            DMA((2,)),
            DMA((2,)),
            DMA((2,)),
            DMA((2,)),
            DMA((4,)),
            DMA((4,)),
            DMA((2, planes)),
            DMA((2, planes)),
            DMA((2, planes)),
            DMA((2, planes)),
            DMA((4, planes)),
            DMA((4, planes)),
            DMA((2,)),
            DMA((2,)),
            DMA((2,)),
            DMA((2,)),
            DMA((4,)),
            DMA((4,)),
        ],
        compiler_params=pltpu.CompilerParams(
            collective_id=identity, has_side_effects=True, vmem_limit_bytes=VMEM_LIMIT
        ),
    )(w, router, gain_rows, tokens, d_rows, frequency, w_out)


def project_steps(
    turned, rows_ref, w_ref, out_ref, mine, away, c_in, x_in, y_in, x_half, y_half,
    cs, cr, xs, xr, ys, yr,
):
    e, core, flip_x, flip_y, diagonal = neighbours()
    s = lax.axis_index("shard")
    q_own, q_x, q_y, q_d = e // 2, flip_x // 2, flip_y // 2, diagonal // 2
    parity = e % 2
    half = out_ref.shape[0] // 2
    low_half, high_half = pl.ds(0, half), pl.ds(half, half)
    across = (((1,), (1 if turned else 0,)), ((), ()))
    order = (q_d, q_x, q_y, q_own)

    def arrived(block, sem):
        send(block, block, sem, sem, (core, s)).wait_recv()

    def add(target, *others):
        total = target[...].astype(FULL)
        for other in others:
            total = total + other[...].astype(FULL)
        target[...] = total.astype(LOW)

    def to_core(q):
        return send(away.at[q], c_in.at[q], cs.at[q], cr.at[q], (core, s))

    def compute(q, lane, into):
        rows = rows_ref[2 * q + lane]

        def tile(t, carry):
            at = pl.ds(pl.multiple_of(t * TILE, TILE), TILE)
            if turned:
                deep = w_ref.shape[1]
                w = w_ref[t * TILE // deep, :, : rows.shape[1]]
            else:
                w = w_ref[:, at]
            into[q, :, at] = lax.dot_general(
                rows, w, across, preferred_element_type=FULL
            ).astype(LOW)
            return carry

        lax.fori_loop(0, MODEL_WIDTH // TILE, tile, 0)

    halves = [
        send(mine.at[q_d, low_half], y_half, ys.at[0], yr.at[0], (flip_y, s)),
        send(mine.at[q_d, high_half], x_half, xs.at[0], xr.at[0], (flip_x, s)),
    ]
    to_x = send(mine.at[q_x], x_in, xs.at[1], xr.at[1], (flip_x, s))
    to_y = send(mine.at[q_y], y_in, ys.at[1], yr.at[1], (flip_y, s))

    def joined(q):
        arrived(c_in.at[q], cr.at[q])
        add(mine.at[q], c_in.at[q])

    def begin():
        for q in order:
            compute(q, 1 - parity, away)
            to_core(q).start()
        for k, q in enumerate(order):
            compute(q, parity, mine)
            if k == 0:
                joined(q_d)
                for copy in halves:
                    copy.start()

    def middle():
        joined(q_x)
        arrived(y_half, yr.at[0])
        add(mine.at[q_x, low_half], y_half)
        to_x.start()
        joined(q_y)
        arrived(x_half, xr.at[0])
        add(mine.at[q_y, high_half], x_half)
        to_y.start()

    def finish():
        joined(q_own)
        arrived(x_in, xr.at[1])
        arrived(y_in, yr.at[1])
        out_ref[...] = (
            mine[q_own].astype(FULL) + x_in[...].astype(FULL) + y_in[...].astype(FULL)
        )

    def sent():
        for q in order:
            to_core(q).wait_send()
        for copy in halves + [to_x, to_y]:
            copy.wait_send()

    return begin, middle, finish, sent


def add_blocks(target, other):
    step = min(128, target.shape[1])
    for lead in range(target.shape[0]):

        def one(r, carry, lead=lead):
            at = pl.ds(pl.multiple_of(r * step, step), step)
            target[lead, at, :] = (
                target[lead, at, :].astype(FULL) + other[lead, at, :].astype(FULL)
            ).astype(LOW)
            return carry

        lax.fori_loop(0, target.shape[1] // step, one, 0)


def back_kernel(
    planes, owners, dm_ref, w_out_ref, mixed_ref, proj_ref, probs_ref, places_ref, gain_ref,
    freq_ref, h1_ref, w_ref, tok_ref, h2_ref, dl_ref, gain_two_ref,
    out_rows, out_head, out_rest, dh1_ref,
    dm_all, mixed_t, rows, q_rows, dm_rows, dproj, column,
    acc_rows, acc_head, acc_rest, sibling, u_rows, u_head, u_rest, d_rows, d_head, d_rest, pair_in,
    mine, away, c_in, x_in, y_in, x_half, y_half,
    gxs, gxr, gys, gyr, gcs, gcr, a_send, a_recv, s_send, s_recv, z_send, z_recv,
    x_send, x_recv, y_send, y_recv, c_send, c_recv, own_sem,
    pc_send, pc_recv, px_send, px_recv, py_send, py_recv,
):
    e, core, _, _, _ = neighbours()
    s = lax.axis_index("shard")
    parity = e % 2
    lanes = owners // planes
    length = dm_ref.shape[0]
    half = length // 2
    count = w_out_ref.shape[0]
    heads = count // HEAD_SIZE
    share_cols = acc_rows.shape[2]
    deep = acc_head.shape[1] * acc_head.shape[2]
    scaling = HEAD_SIZE**-0.5
    nt = (((1,), (1,)), ((), ()))
    tn = (((0,), (0,)), ((), ()))
    up_in, down_in = (u_rows, u_head, u_rest), (d_rows, d_head, d_rest)
    outs = (out_rows, out_head, out_rest)

    def arrived(block, sem):
        send(block, block, sem, sem, (core, s)).wait_recv()

    greet_plane(planes, owners)
    begin, second, third, last, sent = gather_steps(
        lambda lane: dm_all.at[lane],
        lambda lane, k: dm_all.at[lane, pl.ds(k * half, half)],
        dm_ref,
        lambda k: gxs.at[k],
        lambda k: gxr.at[k],
        lambda k: gys.at[k],
        lambda k: gyr.at[k],
        lambda k: gcs.at[k],
        lambda k: gcr.at[k],
    )
    begin()
    dm_all[e] = dm_ref[...]
    for b in range(owners):
        mixed_t[:, b * length : (b + 1) * length] = mixed_ref[b].T

    def lane_at(j):
        flipped = [(e // bit + j // bit) % 2 * bit for bit in (1, 2, 4)]
        return flipped[0] + flipped[1] + flipped[2]

    def spread(other):
        return send(
            rows.at[:, pl.ds(other * share_cols, share_cols)], acc_rows.at[e],
            a_send.at[other], a_recv.at[e], (other, s),
        )

    column[...] = jnp.zeros_like(column)
    gain_query, gain_key = head_gains(gain_ref, planes)

    def attend(j, carry):
        b = lane_at(j)
        for at, step in ((2, second), (6, third)):

            @pl.when(j == at)
            def _(step=step):
                step()

        @pl.when(j % 2 == 1)
        def _():
            arrived(dm_all.at[b], gcr.at[j // 2])

        places = places_ref[b].astype(FULL)[:, 1:2]
        cosine, sine = rope_tables(places, freq_ref[0:1, :])

        def unit(v):
            inverse = lax.rsqrt(jnp.mean(v * v, axis=1, keepdims=True) + EPS)
            return v * inverse, inverse

        def turned(v):
            return (v * cosine + half_turn(v) * sine).astype(LOW)

        def back(v, units, inverse, gain, row):
            v = v * cosine - half_turn(v) * sine
            column[row : row + 1, :HEAD_SIZE] += jnp.sum(v * units, axis=0, keepdims=True)
            v = v * gain
            return inverse * (v - units * jnp.mean(v * units, axis=1, keepdims=True))

        d_mixed = lax.dot_general(
            dm_all[b], w_out_ref[...], nt, preferred_element_type=FULL
        ).astype(LOW)
        for h in range(heads):
            at = slice(h * HEAD_SIZE, (h + 1) * HEAD_SIZE)
            here = slice(h * length, (h + 1) * length)
            dm_rows[here, :] = d_mixed[:, at]
            units, _ = unit(proj_ref[b, :, at])
            q_rows[here, :] = turned(units * gain_query)
        key_units, key_inverse = unit(proj_ref[b, :, count : count + HEAD_SIZE])
        key = turned(key_units * gain_key)
        value = proj_ref[b, :, count + HEAD_SIZE :].astype(LOW)
        probs = probs_ref[b]
        wide = probs.astype(FULL)
        d_probs = lax.dot_general(dm_rows[...], value, nt, preferred_element_type=FULL)
        d_scores = wide * (d_probs - jnp.sum(d_probs * wide, axis=1, keepdims=True))
        d_scores = d_scores.astype(LOW)
        d_query = jnp.dot(d_scores, key, preferred_element_type=FULL) * scaling
        d_key = lax.dot_general(d_scores, q_rows[...], tn, preferred_element_type=FULL) * scaling
        d_value = lax.dot_general(probs, dm_rows[...], tn, preferred_element_type=FULL)
        for h in range(heads):
            at = slice(h * HEAD_SIZE, (h + 1) * HEAD_SIZE)
            units, inverse = unit(proj_ref[b, :, at])
            got = back(
                d_query[h * length : (h + 1) * length], units, inverse, gain_query, GAIN_QUERY
            )
            dproj[b, :, at] = got.astype(LOW)
        got = back(d_key, key_units, key_inverse, gain_key, GAIN_KEY)
        dproj[b, :, count : count + HEAD_SIZE] = got.astype(LOW)
        dproj[b, :, count + HEAD_SIZE :] = d_value.astype(LOW)
        return carry

    lax.fori_loop(0, owners, attend, 0)
    for other in range(owners):
        at = pl.ds(other * share_cols, share_cols)
        got = jnp.dot(
            mixed_t[...],
            dm_all[:, :, at].reshape(owners * length, share_cols),
            preferred_element_type=FULL,
        ).astype(LOW)
        rows[:, at] = got

        @pl.when(other != e)
        def _(other=other):
            spread(other).start()

        @pl.when(other == e)
        def _(got=got):
            acc_rows[e] = got


    resident = tok_ref[...].astype(FULL)
    inverse_one = lax.rsqrt(jnp.mean(resident * resident, axis=1, keepdims=True) + EPS)

    def left_of(sp):
        at = pl.ds(pl.multiple_of(sp * deep, deep), deep)
        return h1_ref[:, :, at].reshape(-1, deep)

    def make_head(sp):
        right = dproj[:, :, :count].reshape(-1, count)
        got = lax.dot_general(left_of(sp), right, tn, preferred_element_type=FULL).astype(LOW)
        acc_head[sp] = got.reshape(acc_head.shape[1:])

    def to_sibling(sp):
        return send(sibling.at[sp], pair_in.at[sp], s_send.at[sp], s_recv.at[sp], (core, s))

    def make_rest(sp):
        right = dproj[:, :, count:].reshape(-1, 2 * HEAD_SIZE)
        got = lax.dot_general(left_of(sp), right, tn, preferred_element_type=FULL).astype(LOW)
        key, value = got[:, :HEAD_SIZE], got[:, HEAD_SIZE:]
        at = pl.ds(pl.multiple_of(sp * deep, deep), deep)
        column[GAIN_ONE : GAIN_ONE + 1, :] = jnp.sum(
            dh1_ref[:, at] * (tok_ref[:, at].astype(FULL) * inverse_one), axis=0, keepdims=True
        )
        column[GAIN_TWO : GAIN_TWO + 1, :] = gain_two_ref[:, at]
        extra = lax.dot_general(h2_ref[:, at], dl_ref[...], tn, preferred_element_type=FULL)
        extra = (extra + column[...].T).astype(LOW)
        top, low = extra[: deep // 2], extra[deep // 2 :]

        def put(into, kv, part):
            into[sp, :4] = kv.reshape(4, deep // 4, HEAD_SIZE)
            into[sp, 4:] = part.reshape(2, deep // 4, HEAD_SIZE)

        @pl.when(parity == 0)
        def _():
            put(acc_rest, key, top)
            put(sibling, value, low)

        @pl.when(parity == 1)
        def _():
            put(acc_rest, value, low)
            put(sibling, key, top)

        to_sibling(sp).start()

    def chunk(k, sp):
        if k == 0:
            return acc_rows.at[pl.ds(sp * lanes, lanes)]
        return acc_head.at[sp] if k == 1 else acc_rest.at[sp]

    def ready(k, sp):
        if k == 0:
            for lane in range(lanes):
                source = sp * lanes + lane

                @pl.when(source != e)
                def _(source=source):
                    arrived(acc_rows.at[source], a_recv.at[source])

        elif k == 1:
            make_head(sp)
        else:
            arrived(pair_in.at[sp], s_recv.at[sp])
            add_blocks(acc_rest.at[sp], pair_in.at[sp])

    def up(k, sp):
        return send(
            chunk(k, sp), up_in[k].at[sp], z_send.at[k, 0, sp], z_recv.at[k, 0, sp], (e, s + 1)
        )

    def down(k, sp):
        return send(
            chunk(k, sp), down_in[k].at[sp], z_send.at[k, 1, sp], z_recv.at[k, 1, sp], (e, s - 1)
        )

    def line(k, sp):
        ready(k, sp)

        @pl.when((sp >= s) & (s > 0))
        def _():
            arrived(up_in[k].at[sp], z_recv.at[k, 0, sp])
            add_blocks(chunk(k, sp), up_in[k].at[sp])

        @pl.when((sp <= s) & (s < planes - 1))
        def _():
            arrived(down_in[k].at[sp], z_recv.at[k, 1, sp])
            add_blocks(chunk(k, sp), down_in[k].at[sp])

        @pl.when(sp > s)
        def _():
            up(k, sp).start()

        @pl.when(sp < s)
        def _():
            down(k, sp).start()

    def pair(k, n):
        for i in (2 * n, 2 * n - 1):
            sp = s + (2 * (i % 2) - 1) * n

            @pl.when((sp >= 0) & (sp < planes))
            def _(sp=sp):
                line(k, sp)

    def steps(k):
        size = outs[k].shape[1] // 2
        return gather_steps(
            lambda lane: outs[k].at[lane],
            lambda lane, at: outs[k].at[lane, pl.ds(at * size, size)],
            chunk(k, s),
            lambda n: x_send.at[k, n],
            lambda n: x_recv.at[k, n],
            lambda n: y_send.at[k, n],
            lambda n: y_recv.at[k, n],
            lambda n: c_send.at[k, n],
            lambda n: c_recv.at[k, n],
        )

    def keep(k):
        return pltpu.make_async_copy(chunk(k, s), outs[k].at[e], own_sem.at[k])

    def own(k):
        line(k, s)
        steps(k)[0]()
        keep(k).start()

    p_begin, p_middle, p_finish, p_sent = project_steps(
        True, dproj, w_ref, dh1_ref, mine, away, c_in, x_in, y_in, x_half, y_half,
        pc_send, pc_recv, px_send, px_recv, py_send, py_recv,
    )
    pair(1, planes - 1)
    p_begin()
    for n in range(planes - 2, 0, -1):
        pair(1, n)
    p_middle()
    pair(0, planes - 1)
    p_finish()
    for sp in range(planes):
        make_rest(sp)
    for n in range(planes - 2, 0, -1):
        pair(0, n)
    own(1)
    pair(2, planes - 1)
    steps(1)[1]()
    for n in range(planes - 2, 0, -1):
        pair(2, n)
    own(0)
    steps(1)[2]()
    own(2)
    steps(0)[1]()
    steps(2)[1]()
    steps(0)[2]()
    steps(2)[2]()
    for k in range(3):
        keep(k).wait()
        steps(k)[3]()
        steps(k)[4]()
    p_sent()
    sent()
    for other in range(owners):

        @pl.when(other != e)
        def _(other=other):
            spread(other).wait_send()

    def drain(sp, carry):
        to_sibling(sp).wait_send()
        for k in range(3):

            @pl.when(sp > s)
            def _(k=k):
                up(k, sp).wait_send()

            @pl.when(sp < s)
            def _(k=k):
                down(k, sp).wait_send()

        return carry

    lax.fori_loop(0, planes, drain, 0)


def back(
    dm, w_out, mixed, proj, probs, places, gains, frequency, h1, w, tokens, h2, d_logits, gain_two,
    planes, owners, identity,
):
    length = dm.shape[0]
    count = w_out.shape[0]
    share_cols = MODEL_WIDTH // owners
    deep = MODEL_WIDTH // planes
    shapes = (
        (owners // planes, count, share_cols),
        (2, deep // 2, count),
        (6, deep // 4, HEAD_SIZE),
    )
    stack = (length * count // HEAD_SIZE, HEAD_SIZE)
    block = (length, MODEL_WIDTH)
    part = (length // 2, MODEL_WIDTH)

    def vmem(*shape, dtype=LOW):
        return pltpu.VMEM(shape, dtype)

    per_plane = [vmem(planes, *shape) for shape in shapes]
    return pl.pallas_call(
        functools.partial(back_kernel, planes, owners),
        out_shape=[jax.ShapeDtypeStruct((owners,) + shape, LOW) for shape in shapes]
        + [jax.ShapeDtypeStruct(block, FULL)],
        in_specs=[VM] * 14,
        out_specs=[ANY, ANY, ANY, VM],
        scratch_shapes=[
            vmem(owners, *block),
            vmem(count, owners * length),
            vmem(count, MODEL_WIDTH),
            vmem(*stack),
            vmem(*stack),
            vmem(*proj.shape),
            vmem(TAIL, deep, dtype=FULL),
            vmem(owners, count, share_cols),
            per_plane[1],
            per_plane[2],
            per_plane[2],
        ]
        + per_plane
        + per_plane
        + [
            per_plane[2],
            vmem(4, *block),
            vmem(4, *block),
            vmem(4, *block),
            vmem(*block),
            vmem(*block),
            vmem(*part),
            vmem(*part),
            DMA((2,)),
            DMA((2,)),
            DMA((2,)),
            DMA((2,)),
            DMA((4,)),
            DMA((4,)),
            DMA((owners,)),
            DMA((owners,)),
            DMA((planes,)),
            DMA((planes,)),
            DMA((3, 2, planes)),
            DMA((3, 2, planes)),
            DMA((3, 2)),
            DMA((3, 2)),
            DMA((3, 2)),
            DMA((3, 2)),
            DMA((3, 4)),
            DMA((3, 4)),
            DMA((3,)),
            DMA((4,)),
            DMA((4,)),
            DMA((2,)),
            DMA((2,)),
            DMA((2,)),
            DMA((2,)),
        ],
        compiler_params=pltpu.CompilerParams(
            collective_id=identity, has_side_effects=True, vmem_limit_bytes=VMEM_LIMIT
        ),
    )(
        dm, w_out, mixed, proj, probs, places, gains, frequency, h1, w, tokens, h2, d_logits,
        gain_two,
    )


def finish_kernel(
    owners, rows_ref, head_ref, rest_ref, tok_ref, middle_ref, mix_ref, dm_ref, dh1_ref, gain_ref,
    out_rows, out_qkv, out_router, out_gains, result_ref, dtok_ref,
):
    i = pl.program_id(0)

    @pl.when(i < owners)
    def _():
        out_rows[...] = rows_ref[0].astype(FULL)
        out_qkv[...] = head_ref[0].astype(FULL)

    for at in range(2):

        @pl.when(i == owners + at)
        def _(at=at):
            for h in range(KEY_VALUE_HEADS):
                got = rest_ref[2 * h + at, :4].reshape(-1, HEAD_SIZE)
                out_qkv[:, h * HEAD_SIZE : (h + 1) * HEAD_SIZE] = got.astype(FULL)

    @pl.when(i == 0)
    def _():
        height = out_router.shape[0] // 2
        experts = out_router.shape[1]
        for at in range(2):
            total = jnp.zeros((height, TAIL), FULL)
            for lane in range(at, owners, 2):
                total = total + rest_ref[lane, 4:].reshape(-1, TAIL).astype(FULL)
            here = slice(at * height, (at + 1) * height)
            out_router[here, :] = total[:, :experts]
            out_gains[:, here] = total.T[experts : experts + 8]

    @pl.when(i == 1)
    def _():
        result_ref[...] = (middle_ref[...] + mix_ref[...]).astype(LOW)

    @pl.when(i == 2)
    def _():
        resident = tok_ref[...].astype(FULL)
        units, inverse = unit_norm(resident)
        back = norm_back(dh1_ref[...], units, inverse, gain_ref[...])
        dtok_ref[...] = (dm_ref[...] + back).astype(LOW)


def finish_grads(rows, head, rest, tokens, middle, mix, d_middle, d_h1, gain, owners):
    rows = rows.reshape(owners, -1, rows.shape[-1])
    head = head.reshape(owners, -1, head.shape[-1])
    count, share = rows.shape[1:]
    height, wide = head.shape[1:]
    last = owners - 1

    def whole(shape):
        return pl.BlockSpec(shape, lambda i: (0,) * len(shape))

    block = tokens.shape
    return pl.pallas_call(
        functools.partial(finish_kernel, owners),
        grid=(owners + 2,),
        in_specs=[
            pl.BlockSpec((1, count, share), lambda i: (jnp.minimum(i, last), 0, 0)),
            pl.BlockSpec((1, height, wide), lambda i: (jnp.minimum(i, last), 0, 0)),
            whole(rest.shape),
        ]
        + [whole(block)] * 5
        + [whole(gain.shape)],
        out_specs=[
            pl.BlockSpec((count, share), lambda i: (0, jnp.minimum(i, last))),
            pl.BlockSpec((height, wide), lambda i: (0, i)),
            whole((height, TAIL // 2)),
            whole((8, height)),
            whole(block),
            whole(block),
        ],
        out_shape=[
            jax.ShapeDtypeStruct((count, owners * share), FULL),
            jax.ShapeDtypeStruct((height, (owners + 2) * wide), FULL),
            jax.ShapeDtypeStruct((height, TAIL // 2), FULL),
            jax.ShapeDtypeStruct((8, height), FULL),
            jax.ShapeDtypeStruct(block, LOW),
            jax.ShapeDtypeStruct(block, LOW),
        ],
        compiler_params=pltpu.CompilerParams(vmem_limit_bytes=VMEM_LIMIT),
    )(rows, head, rest, tokens, middle, mix, d_middle, d_h1, gain)


def gathered_layer(
    tokens,
    segments,
    routes,
    attn_gain,
    qkv_weight,
    query_gain,
    k_gain,
    w_out,
    ffn_gain,
    router,
    w_gate,
    w_up,
    w_down,
    d_out,
):
    owners = lax.axis_size("expert")
    planes = lax.axis_size("shard")
    me = lax.axis_index("expert")
    plane = lax.axis_index("shard")
    length = tokens.shape[0]
    blocks = owners * planes
    experts_all = router.shape[1]
    capacity = 3 * length * TOPK // (2 * experts_all)
    heads = QUERY_HEADS // owners
    query_cols = heads * HEAD_SIZE
    scaling = HEAD_SIZE ** (-0.5)
    both = ("expert", "shard")
    rows_in = qkv_weight.shape[0]

    kv_head = me * KEY_VALUE_HEADS // owners
    k_at = QUERY_HEADS * HEAD_SIZE + kv_head * HEAD_SIZE
    v_at = k_at + KEY_VALUE_HEADS * HEAD_SIZE
    gains = columns(
        [
            router,
            attn_gain[:, None],
            ffn_gain[:, None],
            jnp.pad(query_gain, (0, rows_in - query_gain.shape[0]))[:, None],
            jnp.pad(k_gain, (0, rows_in - k_gain.shape[0]))[:, None],
        ],
        rows_in,
    )
    mine = jnp.concatenate(
        [
            lax.dynamic_slice_in_dim(qkv_weight, me * query_cols, query_cols, 1),
            lax.dynamic_slice_in_dim(qkv_weight, k_at, HEAD_SIZE, 1),
            lax.dynamic_slice_in_dim(qkv_weight, v_at, HEAD_SIZE, 1),
            gains,
        ],
        axis=1,
    )
    gathered = lax.all_gather(mine, "shard", axis=0, tiled=True)
    qkv_cols = query_cols + 2 * HEAD_SIZE
    wqkv = gathered[:, :qkv_cols]
    router_full = gathered[:, qkv_cols : qkv_cols + experts_all]
    gain_cols = gathered[:, qkv_cols + experts_all :].astype(FULL)
    gain_one, gain_two = gain_cols[:, 0], gain_cols[:, 1]
    per = query_gain.shape[0]
    by_plane = gain_cols.reshape(planes, rows_in, -1)[:, :per]
    gain_query = by_plane[:, :, 2].reshape(-1)
    gain_key = by_plane[:, :, 3].reshape(-1)

    segment_row = segments[0]
    token_tail = columns(
        [segment_row[:, None], positions_of(segment_row)[:, None]], length
    )
    plane_rows = lax.all_gather(
        jnp.concatenate([tokens, token_tail], axis=1), "expert", axis=0, tiled=False
    )
    plane_tokens = plane_rows[:, :, :MODEL_WIDTH].astype(FULL)
    plane_segments = plane_rows[:, :, MODEL_WIDTH]
    plane_places = plane_rows[:, :, MODEL_WIDTH + 1].astype(FULL)

    out_rows = w_out.shape[0]
    first = me * query_cols
    offset = first - plane * out_rows
    if out_rows >= query_cols:
        held = (offset >= 0) & (offset < out_rows)
        piece = lax.dynamic_slice_in_dim(w_out, jnp.where(held, offset, 0), query_cols, 0)
        w_mine = lax.psum(jnp.where(held, piece, 0).astype(LOW), "shard")
    else:
        parts = query_cols // out_rows
        at = plane - me * parts
        held = (at >= 0) & (at < parts)
        spread = jnp.where(held & (jnp.arange(parts) == at)[:, None, None], w_out[None], 0)
        w_mine = lax.psum(spread.astype(LOW), "shard").reshape(query_cols, MODEL_WIDTH)

    d_tail = columns([routes], length)
    d_all = lax.all_gather(
        jnp.concatenate([d_out, d_tail], axis=1), both, axis=0, tiled=False
    )

    unit_plane, inverse_plane = unit_norm(plane_tokens)
    h1 = (unit_plane * gain_one).astype(LOW)
    projected = dot("bqd,df->bqf", h1, wqkv)
    half = HEAD_SIZE // 2
    frequency = THETA ** (-2.0 * jnp.arange(half, dtype=FULL) / HEAD_SIZE)
    angles = plane_places[:, :, None] * frequency
    cosine, sine = jnp.cos(angles), jnp.sin(angles)
    cosine_q, sine_q = cosine[:, :, None, :], sine[:, :, None, :]
    query_raw = projected[:, :, :query_cols].reshape(owners, length, heads, HEAD_SIZE)
    key_raw = projected[:, :, query_cols : query_cols + HEAD_SIZE]
    value = projected[:, :, query_cols + HEAD_SIZE :].astype(LOW)
    query_unit, query_inverse = unit_norm(query_raw)
    key_unit, key_inverse = unit_norm(key_raw)
    query = rotate(query_unit * gain_query, cosine_q, sine_q).astype(LOW)
    key = rotate(key_unit * gain_key, cosine, sine).astype(LOW)
    places = jnp.arange(length, dtype=jnp.int32)
    allowed = (plane_segments[:, :, None] == plane_segments[:, None, :]) & (
        places[None, :] <= places[:, None]
    )
    scores = dot("bqhd,bkd->bhqk", query, key) * scaling
    scores = jnp.where(allowed[:, None], scores, -1e30)
    highest = jnp.max(scores, axis=-1, keepdims=True)
    exponent = jnp.exp(scores - highest)
    probs = exponent / jnp.sum(exponent, axis=-1, keepdims=True)
    probs_low = probs.astype(LOW)
    mixed = dot("bhqk,bkd->bqhd", probs_low, value).astype(LOW)
    mixed = mixed.reshape(owners, length, query_cols)
    partial = dot("bqf,fd->bqd", mixed, w_mine).astype(LOW)
    branch = lax.psum_scatter(partial, "expert", scatter_dimension=0, tiled=False)

    middle = tokens.astype(FULL) + branch.astype(FULL)
    unit_two, inverse_two = unit_norm(middle)
    h2 = (unit_two * gain_two).astype(LOW)
    logits = dot("nd,de->ne", h2, router_full)
    chance = jax.nn.softmax(logits, axis=-1)
    named = jnp.sum(
        (routes[:, :, None] == jnp.arange(experts_all, dtype=jnp.int32)).astype(FULL), axis=1
    )
    chosen_sum = jnp.sum(named * chance, axis=1, keepdims=True)
    gates = named * chance / chosen_sum
    gates_high = gates.astype(LOW)
    gates_rest = (gates - gates_high.astype(FULL)).astype(LOW)
    h_all = lax.all_gather(
        jnp.concatenate([h2, gates_high, gates_rest], axis=1), both, axis=0, tiled=False
    )

    route_all = d_all[:, :, MODEL_WIDTH : MODEL_WIDTH + TOPK].astype(FULL)
    own_experts = (me * EXP_DEV + jnp.arange(EXP_DEV, dtype=jnp.int32)).astype(FULL)
    match = jnp.sum((route_all[:, :, :, None] == own_experts).astype(FULL), axis=2)
    earlier = (places[None, :] < places[:, None]).astype(LOW)
    rank = dot("ts,bsj->btj", earlier, match.astype(LOW))
    slot_ids = jnp.arange(capacity, dtype=jnp.int32).astype(FULL)
    place = jnp.where(match > 0, rank, -1.0).transpose(0, 2, 1)
    dispatch = (place[:, :, None, :] == slot_ids[:, None]).astype(LOW)

    def experts(h_rows, d_rows, gate_high, gate_rest, put):
        count = h_rows.shape[0]
        flat = put.reshape(count, EXP_DEV * capacity, length)
        x = dot("bst,btd->bsd", flat, h_rows).astype(LOW)
        dy = dot("bst,btd->bsd", flat, d_rows).astype(LOW)

        def by_expert(v):
            v = v.reshape(count, EXP_DEV, capacity, v.shape[-1])
            return v.transpose(1, 0, 2, 3).reshape(EXP_DEV, count * capacity, v.shape[-1])

        def by_block(v):
            v = v.reshape(EXP_DEV, count, capacity, v.shape[-1])
            return v.transpose(1, 0, 2, 3).reshape(count, EXP_DEV * capacity, v.shape[-1])

        x, dy = by_expert(x), by_expert(dy)
        gate_slot = dot("bjct,btj->jbc", put, gate_high) + dot("bjct,btj->jbc", put, gate_rest)
        gate_slot = gate_slot.reshape(EXP_DEV, count * capacity, 1)
        g = dot("erd,efd->erf", x, w_gate)
        u = dot("erd,efd->erf", x, w_up)
        da = dot("erd,edf->erf", dy, w_down)
        sigma = jax.nn.sigmoid(g)
        silu = g * sigma
        act = (silu * u).astype(LOW).astype(FULL)
        d_gate_slot = jnp.sum(act * da, axis=-1)
        act_gated = (act * gate_slot).astype(LOW)
        d_act = da * gate_slot
        dg = (d_act * u * sigma * (1.0 + g * (1.0 - sigma))).astype(LOW)
        du = (d_act * silu).astype(LOW)
        y = dot("erf,edf->erd", act_gated, w_down).astype(LOW)
        d_down = dot("erd,erf->edf", dy, act_gated)
        d_gate = dot("erf,erd->efd", dg, x)
        d_up = dot("erf,erd->efd", du, x)
        dx = (dot("erf,efd->erd", dg, w_gate) + dot("erf,efd->erd", du, w_up)).astype(LOW)
        mix = dot("bst,bsd->btd", flat, by_block(y)).astype(LOW)
        d_h = dot("bst,bsd->btd", flat, by_block(dx)).astype(LOW)
        d_g = dot(
            "bjct,jbc->btj", put.astype(FULL), d_gate_slot.reshape(EXP_DEV, count, capacity)
        )
        return mix, d_h, d_g, d_gate, d_up, d_down

    gate_cols = lax.dynamic_slice_in_dim(h_all, MODEL_WIDTH + me * EXP_DEV, EXP_DEV, 2)
    rest_cols = lax.dynamic_slice_in_dim(
        h_all, MODEL_WIDTH + experts_all + me * EXP_DEV, EXP_DEV, 2
    )
    step = min(blocks, GROUP_BLOCKS)
    mixes, d_hs, d_gs, totals = [], [], [], None
    for at in range(0, blocks, step):
        cut = slice(at, at + step)
        mix, d_h, d_g, *grads = experts(
            h_all[cut, :, :MODEL_WIDTH],
            d_all[cut, :, :MODEL_WIDTH],
            gate_cols[cut],
            rest_cols[cut],
            dispatch[cut],
        )
        mixes.append(mix)
        d_hs.append(d_h)
        d_gs.append(d_g)
        totals = grads if totals is None else [a + b for a, b in zip(totals, grads)]
    d_gate, d_up, d_down = totals
    d_g = jnp.concatenate(d_gs, axis=0)
    spread = jnp.zeros((blocks, length, TAIL), LOW)
    spread = lax.dynamic_update_slice_in_dim(spread, d_g.astype(LOW), me * EXP_DEV, 2)
    d_h_wide = jnp.concatenate([jnp.concatenate(d_hs, axis=0), spread], axis=2)

    def home(v):
        v = v.reshape(owners, planes, length, v.shape[-1])
        v = lax.psum_scatter(v, "expert", scatter_dimension=0, tiled=False)
        return lax.psum_scatter(v, "shard", scatter_dimension=0, tiled=False)

    d_home = home(d_h_wide)
    mixture = home(jnp.concatenate(mixes, axis=0))
    result = (middle + mixture.astype(FULL)).astype(LOW)

    upstream = d_out.astype(FULL)
    d_gates = d_home[:, MODEL_WIDTH : MODEL_WIDTH + experts_all].astype(FULL)
    d_chance = named * (d_gates - jnp.sum(d_gates * gates, axis=1, keepdims=True)) / chosen_sum
    d_logits = chance * (d_chance - jnp.sum(d_chance * chance, axis=1, keepdims=True))
    d_logits = d_logits.astype(LOW)
    d_h2 = d_home[:, :MODEL_WIDTH].astype(FULL) + dot("ne,de->nd", d_logits, router_full)
    d_gain_two = jnp.sum(d_h2 * unit_two, axis=0)
    d_middle = upstream + norm_back(d_h2, unit_two, inverse_two, gain_two)
    d_router = dot("nd,ne->de", h2, d_logits)

    d_branch = lax.all_gather(d_middle.astype(LOW), "expert", axis=0, tiled=False)
    d_w_out = dot("bqf,bqd->fd", mixed, d_branch).astype(LOW)
    d_mixed = dot("bqd,fd->bqf", d_branch, w_mine).astype(LOW)
    d_mixed = d_mixed.reshape(owners, length, heads, HEAD_SIZE)
    d_probs = dot("bqhd,bkd->bhqk", d_mixed, value)
    d_scores = probs * (d_probs - jnp.sum(d_probs * probs, axis=-1, keepdims=True))
    d_scores = d_scores.astype(LOW)
    d_query = dot("bhqk,bkd->bqhd", d_scores, key) * scaling
    d_key = dot("bhqk,bqhd->bkd", d_scores, query) * scaling
    d_value = dot("bhqk,bqhd->bkd", probs_low, d_mixed)
    d_query = rotate_back(d_query, cosine_q, sine_q)
    d_key = rotate_back(d_key, cosine, sine)
    d_gain_query = jnp.sum(d_query * query_unit, axis=(0, 1, 2))
    d_gain_key = jnp.sum(d_key * key_unit, axis=(0, 1))
    d_query = norm_back(d_query, query_unit, query_inverse, gain_query)
    d_key = norm_back(d_key, key_unit, key_inverse, gain_key)
    d_projected = jnp.concatenate(
        [d_query.reshape(owners, length, query_cols), d_key, d_value], axis=2
    ).astype(LOW)
    d_h1_part = dot("bqf,df->bqd", d_projected, wqkv).astype(LOW)
    d_h1 = lax.psum_scatter(d_h1_part, "expert", scatter_dimension=0, tiled=False).astype(FULL)
    resident = tokens.astype(FULL)
    unit_one, inverse_one = unit_norm(resident)
    d_gain_one = jnp.sum(d_h1 * unit_one, axis=0)
    d_tokens = (d_middle + norm_back(d_h1, unit_one, inverse_one, gain_one)).astype(LOW)

    d_wqkv = dot("bqd,bqf->df", h1, d_projected).astype(LOW)

    def by_rows(v):
        v = v.reshape(planes, per)
        return jnp.pad(v, ((0, 0), (0, rows_in - per))).reshape(-1)[:, None]

    d_tail = columns(
        [
            d_router,
            d_gain_one[:, None],
            d_gain_two[:, None],
            by_rows(d_gain_query),
            by_rows(d_gain_key),
        ],
        MODEL_WIDTH,
    )
    d_pack = lax.psum_scatter(
        jnp.concatenate([d_wqkv, d_tail], axis=1), "shard", scatter_dimension=0, tiled=True
    )
    d_pack = lax.all_gather(d_pack, "expert", axis=0, tiled=False).astype(FULL)
    d_q_cols = d_pack[:, :, :query_cols].transpose(1, 0, 2).reshape(rows_in, -1)
    d_kv = d_pack[:, :, query_cols:qkv_cols]
    d_kv = jnp.sum(d_kv.reshape(KEY_VALUE_HEADS, -1, rows_in, 2, HEAD_SIZE), axis=1)
    d_kv = d_kv.transpose(1, 2, 0, 3).reshape(rows_in, -1)
    d_qkv_weight = jnp.concatenate([d_q_cols, d_kv], axis=1)
    d_rest = jnp.sum(d_pack[:, :, qkv_cols:], axis=0)
    d_router_out = d_rest[:, :experts_all]
    d_gain_out = d_rest[:, experts_all:]

    d_w_out = d_w_out.reshape(query_cols, owners, -1)
    d_w_out = lax.all_to_all(d_w_out, "expert", split_axis=1, concat_axis=0, tiled=False)
    d_w_out = d_w_out.reshape(QUERY_HEADS * HEAD_SIZE, -1)
    d_w_out = lax.psum_scatter(d_w_out, "shard", scatter_dimension=0, tiled=True)
    d_w_out = lax.all_gather(d_w_out, "expert", axis=1, tiled=True).astype(FULL)

    return (
        result,
        d_tokens,
        d_gain_out[:, 0],
        d_qkv_weight,
        d_gain_out[:per, 2],
        d_gain_out[:per, 3],
        d_w_out,
        d_gain_out[:, 1],
        d_router_out,
        d_gate,
        d_up,
        d_down,
    )


def resident_layer(
    tokens,
    segments,
    routes,
    attn_gain,
    qkv_weight,
    query_gain,
    k_gain,
    w_out,
    ffn_gain,
    router,
    w_gate,
    w_up,
    w_down,
    d_out,
):
    owners = lax.axis_size("expert")
    planes = lax.axis_size("shard")
    me = lax.axis_index("expert")
    plane = lax.axis_index("shard")
    length = tokens.shape[0]
    blocks = owners * planes
    experts_all = router.shape[1]
    capacity = 3 * length * TOPK // (2 * experts_all)
    slots = 2 * capacity
    heads = QUERY_HEADS // owners
    query_cols = heads * HEAD_SIZE
    scaling = HEAD_SIZE ** (-0.5)
    rows_in = qkv_weight.shape[0]
    per = query_gain.shape[0]

    router_rows = rows_in // owners
    router_part = lax.dynamic_slice_in_dim(router, me * router_rows, router_rows, 0)
    router_part = columns([router_part], router_rows)
    gain_rows = [attn_gain, ffn_gain]
    gain_rows += [jnp.pad(gain, (0, rows_in - per)) for gain in (query_gain, k_gain)]
    gain_rows = jnp.pad(jnp.stack(gain_rows), ((0, 12), (0, 0)))
    segment_row = segments[0]
    token_tail = columns([segment_row[:, None], positions_of(segment_row)[:, None]], length)
    token_rows = jnp.concatenate([tokens, token_tail], axis=1)
    d_rows = jnp.concatenate([d_out, columns([routes], length)], axis=1)
    half = HEAD_SIZE // 2
    frequency = THETA ** (-2.0 * jnp.arange(half, dtype=FULL) / HEAD_SIZE)
    frequency = jnp.broadcast_to(jnp.tile(frequency, 2)[None, :], (8, HEAD_SIZE))
    d_all, w_mine, w_all, router_all, gain_all, tail, h1, projected, probs_low, mixed, branch = front(
        qkv_weight, router_part, gain_rows, token_rows, w_out, d_rows, frequency, planes, owners, 5
    )
    gains = gain_all.astype(FULL)
    gain_one, gain_two = gains[:, 0].reshape(-1), gains[:, 1].reshape(-1)
    router_full = router_all.transpose(1, 0, 2, 3).reshape(MODEL_WIDTH, -1)[:, :experts_all]

    lanes = jnp.arange(2 * experts_all, dtype=jnp.int32) % experts_all
    own = (me * EXP_DEV + jnp.arange(EXP_DEV, dtype=jnp.int32))[:, None] == lanes
    sel = jnp.broadcast_to(own.astype(FULL)[:, None, :], (EXP_DEV, 8, 2 * experts_all))

    middle = tokens.astype(FULL) + branch
    unit_two, inverse_two = unit_norm(middle)
    h2 = (unit_two * gain_two).astype(LOW)
    logits = dot("nd,de->ne", h2, router_full)
    chance = jax.nn.softmax(logits, axis=-1)
    named = jnp.sum(
        (routes[:, :, None] == jnp.arange(experts_all, dtype=jnp.int32)).astype(FULL), axis=1
    )
    chosen_sum = jnp.sum(named * chance, axis=1, keepdims=True)
    gates = named * chance / chosen_sum
    gates_high = gates.astype(LOW)
    gates_rest = (gates - gates_high.astype(FULL)).astype(LOW)
    h_rows = jnp.concatenate([h2, gates_high, gates_rest], axis=1)

    x, dy, hot = gather_dispatch(h_rows, d_all, planes, slots, 1)
    y, dx, d_gate, d_up, d_down = expert_pass(sel, x, dy, w_gate, w_up, w_down.swapaxes(1, 2))
    d_down = d_down.swapaxes(1, 2)
    d_home, mixture = combine_home(hot, dx, y, length, planes, slots, 2)

    upstream = d_out.astype(FULL)
    d_gates = d_home[:, MODEL_WIDTH:]
    d_gates = d_gates[:, :experts_all] + d_gates[:, experts_all:]
    d_chance = named * (d_gates - jnp.sum(d_gates * gates, axis=1, keepdims=True)) / chosen_sum
    d_logits = chance * (d_chance - jnp.sum(d_chance * chance, axis=1, keepdims=True))
    d_logits = d_logits.astype(LOW)
    d_h2 = d_home[:, :MODEL_WIDTH] + dot("ne,de->nd", d_logits, router_full)
    d_gain_two = jnp.sum(d_h2 * unit_two, axis=0, keepdims=True)
    d_middle = upstream + norm_back(d_h2, unit_two, inverse_two, gain_two)

    *parts, d_h1 = back(
        d_middle.astype(LOW), w_mine, mixed, projected, probs_low, tail, gain_all, frequency, h1,
        w_all, tokens, h2, columns([d_logits], length), d_gain_two, planes, owners, 4,
    )
    d_w_out, d_qkv_weight, d_router, d_gains, result, d_tokens = finish_grads(
        *parts, tokens, middle, mixture, d_middle, d_h1, gain_one[None], owners
    )
    return (
        result,
        d_tokens,
        d_gains[GAIN_ONE - experts_all],
        d_qkv_weight,
        lax.dynamic_slice_in_dim(d_gains[GAIN_QUERY - experts_all], plane * per, per, 0),
        lax.dynamic_slice_in_dim(d_gains[GAIN_KEY - experts_all], plane * per, per, 0),
        d_w_out,
        d_gains[0],
        d_router,
        d_gate,
        d_up,
        d_down,
    )


def per_device(*args):
    blocks = lax.axis_size("expert") * lax.axis_size("shard")
    row_bytes = 2 * (MODEL_WIDTH + TAIL)
    if blocks * args[0].shape[0] * row_bytes <= RESIDENT:
        return resident_layer(*args)
    return gathered_layer(*args)


def solution(mesh):
    placed = (
        P(("expert", "shard"), None),
        P(("expert", "shard"), None),
        P(("expert", "shard"), None),
        P("shard"),
        P("shard", None),
        P("shard"),
        P("shard"),
        P("shard", None),
        P("shard"),
        P("shard", None),
        P("expert", "shard", None),
        P("expert", "shard", None),
        P("expert", None, "shard"),
        P(("expert", "shard"), None),
    )
    return jax.shard_map(
        per_device,
        mesh=mesh,
        in_specs=placed,
        out_specs=(
            P(("expert", "shard"), None),
            P(("expert", "shard"), None),
            P("shard"),
            P("shard", None),
            P("shard"),
            P("shard"),
            P("shard", None),
            P("shard"),
            P("shard", None),
            P("expert", "shard", None),
            P("expert", "shard", None),
            P("expert", None, "shard"),
        ),
        check_vma=False,
    )
```

```python
import functools

import jax
import jax.numpy as jnp
from jax import lax
from jax.experimental import pallas as pl
from jax.experimental.pallas import tpu as pltpu
from jax.sharding import PartitionSpec as P

MODEL_WIDTH = 2048
QUERY_HEADS = 32
KEY_VALUE_HEADS = 4
HEAD_SIZE = 128
TOPK = 8
EXP_DEV = 8
TAIL = 128
GAIN_TWO, GAIN_QUERY, GAIN_KEY, GAIN_ONE = 64, 65, 66, 67
GROUP_BLOCKS = 32
RESIDENT = 20 << 20

EPS = 1e-06
THETA = 1000000.0
LOW = jnp.bfloat16
FULL = jnp.float32


def unit_norm(values):
    inverse = lax.rsqrt(jnp.mean(values * values, axis=-1, keepdims=True) + EPS)
    return values * inverse, inverse


def norm_back(incoming, unit_rows, inverse, gain):
    inner = incoming * gain
    return inverse * (inner - unit_rows * jnp.mean(inner * unit_rows, axis=-1, keepdims=True))


def rotate(values, cosine, sine):
    half = values.shape[-1] // 2
    a, b = values[..., :half], values[..., half:]
    return jnp.concatenate([a * cosine - b * sine, b * cosine + a * sine], axis=-1)


def rotate_back(values, cosine, sine):
    half = values.shape[-1] // 2
    a, b = values[..., :half], values[..., half:]
    return jnp.concatenate([a * cosine + b * sine, b * cosine - a * sine], axis=-1)


def dot(spec, left, right):
    return jnp.einsum(spec, left, right, preferred_element_type=FULL)


def positions_of(segment_row):
    places = jnp.arange(segment_row.shape[0], dtype=jnp.int32)
    before = (segment_row[None, :] == segment_row[:, None]) & (places[None, :] < places[:, None])
    return jnp.sum(before.astype(jnp.int32), axis=1)


def columns(parts, rows):
    wide = jnp.concatenate([part.astype(LOW) for part in parts], axis=1)
    return jnp.pad(wide, ((0, rows - wide.shape[0]), (0, TAIL - wide.shape[1])))


MESH = pl.DeviceIdType.MESH
ANY = pl.BlockSpec(memory_space=pl.ANY)
VM = pl.BlockSpec(memory_space=pltpu.VMEM)
DMA = pltpu.SemaphoreType.DMA
VMEM_LIMIT = 58 << 20
TILE = 512


def neighbours():
    e = lax.axis_index("expert")
    core = e + 1 - 2 * (e % 2)
    flip_x = e + 2 - 4 * ((e // 2) % 2)
    flip_y = e + 4 - 8 * ((e // 4) % 2)
    diagonal = flip_x + flip_y - e
    return e, core, flip_x, flip_y, diagonal


def greet(planes):
    e, core, flip_x, flip_y, _ = neighbours()
    s = lax.axis_index("shard")
    barrier = pltpu.get_barrier_semaphore()
    for other in (core, flip_x, flip_y):
        pl.semaphore_signal(barrier, 1, device_id=(other, s), device_id_type=MESH)

    @pl.when(s > 0)
    def _():
        pl.semaphore_signal(barrier, 1, device_id=(e, s - 1), device_id_type=MESH)

    @pl.when(s < planes - 1)
    def _():
        pl.semaphore_signal(barrier, 1, device_id=(e, s + 1), device_id_type=MESH)

    inner = (s > 0) & (s < planes - 1)

    @pl.when(inner)
    def _():
        pl.semaphore_wait(barrier, 5)

    @pl.when(jnp.logical_not(inner))
    def _():
        pl.semaphore_wait(barrier, 4)


def send(source, target, send_sem, recv_sem, device):
    return pltpu.make_async_remote_copy(
        src_ref=source,
        dst_ref=target,
        send_sem=send_sem,
        recv_sem=recv_sem,
        device_id=device,
        device_id_type=MESH,
    )


def gather_dispatch_kernel(
    planes, slots, x_ref, d_ref, outx_ref, outd_ref, outh_ref,
    buf, hot, place, stage_x, stage_d, stage_h, load_d,
    z_send, z_recv, x_send, x_recv, y_send, y_recv, c_send, c_recv, out_x, out_d, out_h, in_d,
):
    e, core, flip_x, flip_y, diagonal = neighbours()
    s = lax.axis_index("shard")
    length = x_ref.shape[0]
    half = length // 2
    width = x_ref.shape[1]
    low_half, high_half = pl.ds(0, half), pl.ds(half, half)
    greet(planes)
    buf[e, s] = x_ref[...]

    def up(sp):
        return send(buf.at[e, sp], buf.at[e, sp], z_send.at[0, sp], z_recv.at[sp], (e, s + 1))

    def down(sp):
        return send(buf.at[e, sp], buf.at[e, sp], z_send.at[1, sp], z_recv.at[sp], (e, s - 1))

    def first(sp):
        block = buf.at[e, sp]
        return [
            send(block, block, x_send.at[0, sp], x_recv.at[0, sp], (flip_x, s)),
            send(block, block, y_send.at[0, sp], y_recv.at[0, sp], (flip_y, s)),
            send(block, block, c_send.at[0, sp], c_recv.at[0, sp], (core, s)),
        ]

    def from_x(sp):
        block = buf.at[flip_x, sp]
        part = buf.at[flip_x, sp, low_half]
        return [
            send(part, part, y_send.at[1, sp], y_recv.at[1, sp], (flip_y, s)),
            send(block, block, c_send.at[1, sp], c_recv.at[1, sp], (core, s)),
        ]

    def from_y(sp):
        block = buf.at[flip_y, sp]
        part = buf.at[flip_y, sp, high_half]
        return [
            send(part, part, x_send.at[1, sp], x_recv.at[1, sp], (flip_x, s)),
            send(block, block, c_send.at[2, sp], c_recv.at[2, sp], (core, s)),
        ]

    def from_diagonal(sp):
        block = buf.at[diagonal, sp]
        return send(block, block, c_send.at[3, sp], c_recv.at[3, sp], (core, s))

    def arrived(block, sem):
        send(block, block, sem, sem, (core, s)).wait_recv()

    def plane_at(i):
        distance = (i + 1) // 2
        sign = 2 * (i % 2) - 1
        sp = s + sign * distance
        return sp, (sp >= 0) & (sp < planes) & (i >= 0) & (i <= 2 * planes - 2)

    def step_first(sp, i):
        @pl.when(i > 0)
        def _():
            arrived(buf.at[e, sp], z_recv.at[sp])

        @pl.when((sp <= s) & (s < planes - 1))
        def _():
            up(sp).start()

        @pl.when((sp >= s) & (s > 0))
        def _():
            down(sp).start()

        for copy in first(sp):
            copy.start()

    def step_second(sp):
        arrived(buf.at[flip_x, sp], x_recv.at[0, sp])
        for copy in from_x(sp):
            copy.start()
        arrived(buf.at[flip_y, sp], y_recv.at[0, sp])
        for copy in from_y(sp):
            copy.start()

    def step_third(sp):
        arrived(buf.at[diagonal, sp, low_half], y_recv.at[1, sp])
        arrived(buf.at[diagonal, sp, high_half], x_recv.at[1, sp])
        from_diagonal(sp).start()

    def copy_out(stage, out, sem, q, sp):
        rows = pl.ds(pl.multiple_of((q * planes + sp) * slots, 16), slots)
        return pltpu.make_async_copy(stage.at[q], out.at[:, rows, :], sem.at[q])

    def load(q, sp, k):
        return pltpu.make_async_copy(
            d_ref.at[2 * q + k, sp],
            load_d.at[q, pl.ds(k * length, length), :],
            in_d.at[q, k],
        )

    def start_loads(sp):
        for q in range(4):
            for k in range(2):
                load(q, sp, k).start()

    def copy_hot(q, sp):
        return pltpu.make_async_copy(
            stage_h.at[q], outh_ref.at[q * planes + sp], out_h.at[q]
        )

    row = lax.broadcasted_iota(jnp.int32, (length, length), 0)
    earlier = (lax.broadcasted_iota(jnp.int32, (length, length), 1) < row).astype(LOW)
    lane = lax.broadcasted_iota(jnp.int32, (2 * length, TAIL), 1).astype(FULL)
    slot = lax.broadcasted_iota(jnp.int32, (slots, 2 * length), 0).astype(FULL)

    def one_hot(q, sp):
        routes = load_d[q, :, MODEL_WIDTH:].astype(FULL)
        named = (routes[:, 0:1] == lane).astype(FULL)
        for k in range(1, TOPK):
            named = named + (routes[:, k : k + 1] == lane).astype(FULL)
        for k in range(2):
            here = slice(k * length, (k + 1) * length)
            rank = jnp.dot(earlier, named[here].astype(LOW), preferred_element_type=FULL)
            rank = jnp.where(named[here] > 0, rank + k * (slots // 2), -1.0)
            place[:, here] = rank.T
        rows = place[pl.ds(pl.multiple_of(e * EXP_DEV, EXP_DEV), EXP_DEV), :]
        for j in range(EXP_DEV):
            hot[q, sp, pl.ds(j * slots, slots), :] = (slot == rows[j : j + 1, :]).astype(LOW)

    def dispatch_d(sp, i):
        def one(q, carry):
            @pl.when(i > 0)
            def _():
                copy_out(stage_d, outd_ref, out_d, q, sp).wait()
                copy_hot(q, sp).wait()

            for k in range(2):
                load(q, sp, k).wait()
            one_hot(q, sp)
            stage_h[q] = hot[q, sp].T
            copy_hot(q, sp).start()

            def tile(t, inner):
                at = pl.ds(pl.multiple_of(t * TILE, TILE), TILE)
                got = jnp.dot(
                    hot[q, sp], load_d[q, :, at], preferred_element_type=FULL
                ).astype(LOW)
                stage_d[q, :, :, at] = got.reshape(EXP_DEV, slots, TILE)
                return inner

            lax.fori_loop(0, MODEL_WIDTH // TILE, tile, 0)
            copy_out(stage_d, outd_ref, out_d, q, sp).start()
            return carry

        lax.fori_loop(0, 4, one, 0)

    def dispatch(sp, i):
        for k, other in enumerate((core, core + flip_x - e, core + flip_y - e, core + diagonal - e)):
            arrived(buf.at[other, sp], c_recv.at[k, sp])

        def one(q, carry):
            @pl.when(i > 0)
            def _():
                copy_out(stage_x, outx_ref, out_x, q, sp).wait()

            def columns_of(at, wide):
                rows = jnp.concatenate(
                    [buf[2 * q, sp, :, at], buf[2 * q + 1, sp, :, at]], axis=0
                )
                got = jnp.dot(hot[q, sp], rows, preferred_element_type=FULL).astype(LOW)
                stage_x[q, :, :, at] = got.reshape(EXP_DEV, slots, wide)

            def tile(t, inner):
                columns_of(pl.ds(pl.multiple_of(t * TILE, TILE), TILE), TILE)
                return inner

            lax.fori_loop(0, MODEL_WIDTH // TILE, tile, 0)
            if width > MODEL_WIDTH:
                columns_of(pl.ds(MODEL_WIDTH, width - MODEL_WIDTH), width - MODEL_WIDTH)
            copy_out(stage_x, outx_ref, out_x, q, sp).start()
            return carry

        lax.fori_loop(0, 4, one, 0)

    def step(i, carry):
        for lag, work in ((0, step_first), (2, step_second), (4, step_third), (0, dispatch_d), (5, dispatch)):
            sp, there = plane_at(i - lag)

            @pl.when(there)
            def _(sp=sp, lag=lag, work=work):
                if work in (step_second, step_third):
                    work(sp)
                else:
                    work(sp, i - lag)

        sp, there = plane_at(i + 1)

        @pl.when(there)
        def _():
            start_loads(sp)

        return carry

    start_loads(s)
    lax.fori_loop(0, 2 * planes + 4, step, 0)

    def drain(sp, carry):
        for copy in first(sp) + from_x(sp) + from_y(sp) + [from_diagonal(sp)]:
            copy.wait_send()

        @pl.when((sp <= s) & (s < planes - 1))
        def _():
            up(sp).wait_send()

        @pl.when((sp >= s) & (s > 0))
        def _():
            down(sp).wait_send()

        return carry

    lax.fori_loop(0, planes, drain, 0)
    for q in range(4):
        copy_out(stage_x, outx_ref, out_x, q, 0).wait()
        copy_out(stage_d, outd_ref, out_d, q, 0).wait()
        copy_hot(q, 0).wait()


def gather_dispatch(rows, d_all, planes, slots, identity):
    owners = lax.axis_size("expert")
    length, width = rows.shape
    pairs = owners * planes // 2
    total = pairs * slots
    kernel = functools.partial(gather_dispatch_kernel, planes, slots)
    return pl.pallas_call(
        kernel,
        out_shape=[
            jax.ShapeDtypeStruct((EXP_DEV, total, width), LOW),
            jax.ShapeDtypeStruct((EXP_DEV, total, MODEL_WIDTH), LOW),
            jax.ShapeDtypeStruct((pairs, 2 * length, EXP_DEV * slots), LOW),
        ],
        in_specs=[VM, ANY],
        out_specs=[ANY, ANY, ANY],
        scratch_shapes=[
            pltpu.VMEM((owners, planes, length, width), LOW),
            pltpu.VMEM((4, planes, EXP_DEV * slots, 2 * length), LOW),
            pltpu.VMEM((TAIL, 2 * length), FULL),
            pltpu.VMEM((4, EXP_DEV, slots, width), LOW),
            pltpu.VMEM((4, EXP_DEV, slots, MODEL_WIDTH), LOW),
            pltpu.VMEM((4, 2 * length, EXP_DEV * slots), LOW),
            pltpu.VMEM((4, 2 * length, MODEL_WIDTH + TAIL), LOW),
            DMA((2, planes)),
            DMA((planes,)),
            DMA((2, planes)),
            DMA((2, planes)),
            DMA((2, planes)),
            DMA((2, planes)),
            DMA((4, planes)),
            DMA((4, planes)),
            DMA((4,)),
            DMA((4,)),
            DMA((4,)),
            DMA((4, 2)),
        ],
        compiler_params=pltpu.CompilerParams(
            collective_id=identity, has_side_effects=True, vmem_limit_bytes=VMEM_LIMIT
        ),
    )(rows, d_all)


def expert_kernel(
    sel_ref, x_ref, dy_ref, wg_ref, wu_ref, wd_ref,
    y_ref, dx_ref, dwg_ref, dwu_ref, dwd_ref, a_all, dg_all, du_all, a_t, d_t,
):
    rows = x_ref.shape[1]
    step = rows
    experts = sel_ref.shape[2] // 2
    sel = sel_ref[0, 0:1, :]
    lane = lax.broadcasted_iota(jnp.int32, sel.shape, 1)
    high_sel = jnp.where(lane < experts, sel, 0.0)
    rest_sel = sel - high_sel
    nt = (((1,), (1,)), ((), ()))

    def chunk(r, carry):
        at = pl.ds(pl.multiple_of(r * step, step), step)
        x = x_ref[0, at, :MODEL_WIDTH]
        tail = x_ref[0, at, MODEL_WIDTH:].astype(FULL)
        dy = dy_ref[0, at, :]
        gate = jnp.sum(tail * sel, axis=1, keepdims=True)
        g = lax.dot_general(x, wg_ref[0], nt, preferred_element_type=FULL)
        u = lax.dot_general(x, wu_ref[0], nt, preferred_element_type=FULL)
        da = lax.dot_general(dy, wd_ref[0], nt, preferred_element_type=FULL)
        sigma = 1.0 / (1.0 + jnp.exp(-g))
        silu = g * sigma
        act = (silu * u).astype(LOW).astype(FULL)
        d_gate = jnp.sum(act * da, axis=1, keepdims=True)
        d_act = da * gate
        a_all[at, :] = (act * gate).astype(LOW)
        dg_all[at, :] = (d_act * u * sigma * (1.0 + g * (1.0 - sigma))).astype(LOW)
        du_all[at, :] = (d_act * silu).astype(LOW)
        high = d_gate.astype(LOW).astype(FULL)
        dx_ref[0, at, MODEL_WIDTH:] = (high * high_sel + (d_gate - high) * rest_sel).astype(LOW)
        y_ref[0, at, :] = jnp.dot(
            a_all[at, :], wd_ref[0], preferred_element_type=FULL
        ).astype(LOW)
        dx_ref[0, at, :MODEL_WIDTH] = (
            jnp.dot(dg_all[at, :], wg_ref[0], preferred_element_type=FULL)
            + jnp.dot(du_all[at, :], wu_ref[0], preferred_element_type=FULL)
        ).astype(LOW)
        return carry

    lax.fori_loop(0, rows // step, chunk, 0)
    hidden = a_t.shape[0]
    a_t[...] = a_all[...].T
    d_t[:hidden, :] = dg_all[...].T
    d_t[hidden:, :] = du_all[...].T

    def tile(t, carry):
        at = pl.ds(pl.multiple_of(t * TILE, TILE), TILE)
        x = x_ref[0, :, at]
        got = jnp.dot(d_t[...], x, preferred_element_type=FULL)
        dwg_ref[0, :, at] = got[:hidden]
        dwu_ref[0, :, at] = got[hidden:]
        dwd_ref[0, :, at] = jnp.dot(a_t[...], dy_ref[0, :, at], preferred_element_type=FULL)
        return carry

    lax.fori_loop(0, MODEL_WIDTH // TILE, tile, 0)


def expert_pass(sel, x, dy, w_gate, w_up, w_down):
    rows, width = x.shape[1:]
    hidden = w_gate.shape[1]

    def spec(*shape):
        return pl.BlockSpec((1,) + shape, lambda j: (j, 0, 0))

    def out(*shape, dtype=LOW):
        return jax.ShapeDtypeStruct((EXP_DEV,) + shape, dtype)

    return pl.pallas_call(
        expert_kernel,
        grid=(EXP_DEV,),
        in_specs=[
            spec(*sel.shape[1:]),
            spec(rows, width),
            spec(rows, MODEL_WIDTH),
            spec(hidden, MODEL_WIDTH),
            spec(hidden, MODEL_WIDTH),
            spec(hidden, MODEL_WIDTH),
        ],
        out_specs=[
            spec(rows, MODEL_WIDTH),
            spec(rows, width),
            spec(hidden, MODEL_WIDTH),
            spec(hidden, MODEL_WIDTH),
            spec(hidden, MODEL_WIDTH),
        ],
        out_shape=[
            out(rows, MODEL_WIDTH),
            out(rows, width),
            out(hidden, MODEL_WIDTH, dtype=FULL),
            out(hidden, MODEL_WIDTH, dtype=FULL),
            out(hidden, MODEL_WIDTH, dtype=FULL),
        ],
        scratch_shapes=[pltpu.VMEM((rows, hidden), LOW)] * 3
        + [pltpu.VMEM((hidden, rows), LOW), pltpu.VMEM((2 * hidden, rows), LOW)],
        compiler_params=pltpu.CompilerParams(vmem_limit_bytes=VMEM_LIMIT),
        cost_estimate=pl.CostEstimate(
            flops=EXP_DEV * rows * MODEL_WIDTH * hidden * 18,
            bytes_accessed=160 << 20,
            transcendentals=EXP_DEV * rows * hidden,
        ),
    )(sel, x, dy, w_gate, w_up, w_down)


def combine_home_kernel(
    planes, slots, hot_ref, v_ref, m_ref, out_ref, mix_ref,
    hot, load, mine, away, c_in, x_in, y_in, x_half, y_half, u_in, d_in,
    hot_sem, in_sem, free, c_send, c_recv, x_send, x_recv, y_send, y_recv, z_send, z_recv,
):
    e, core, flip_x, flip_y, diagonal = neighbours()
    s = lax.axis_index("shard")
    q_own, q_x, q_y, q_d = e // 2, flip_x // 2, flip_y // 2, diagonal // 2
    parity = e % 2
    length, width = out_ref.shape
    half = length // 2
    low_half, high_half = pl.ds(0, half), pl.ds(half, half)
    order = (q_d, q_x, q_y, q_own)
    spans = (pl.ds(0, width), pl.ds(0, MODEL_WIDTH))

    def fetch(kind, k, sp):
        rows = pl.ds(pl.multiple_of((order[k] * planes + sp) * slots, 16), slots)
        if kind == 0:
            return pltpu.make_async_copy(v_ref.at[:, rows, :], load.at[k % 2], in_sem.at[k % 2])
        return pltpu.make_async_copy(
            m_ref.at[:, rows, :], load.at[k % 2, :, :, pl.ds(0, MODEL_WIDTH)], in_sem.at[k % 2]
        )

    def fetch_hot(k, sp):
        return pltpu.make_async_copy(
            hot_ref.at[order[k] * planes + sp], hot.at[k % 2], hot_sem.at[k % 2]
        )

    def to_core(kind, q, sp):
        return send(
            away.at[q, sp, :, spans[kind]], c_in.at[q, sp, :, spans[kind]], c_send.at[kind, q, sp], c_recv.at[kind, q, sp],
            (core, s),
        )

    def halves(kind, sp):
        return [
            send(
                mine.at[q_d, sp, low_half, spans[kind]], y_half.at[kind, sp, :, spans[kind]],
                y_send.at[kind, 0, sp], y_recv.at[kind, 0, sp], (flip_y, s),
            ),
            send(
                mine.at[q_d, sp, high_half, spans[kind]], x_half.at[kind, sp, :, spans[kind]],
                x_send.at[kind, 0, sp], x_recv.at[kind, 0, sp], (flip_x, s),
            ),
        ]

    def to_x(kind, sp):
        return send(
            mine.at[q_x, sp, :, spans[kind]], x_in.at[kind, sp, :, spans[kind]], x_send.at[kind, 1, sp], x_recv.at[kind, 1, sp],
            (flip_x, s),
        )

    def to_y(kind, sp):
        return send(
            mine.at[q_y, sp, :, spans[kind]], y_in.at[kind, sp, :, spans[kind]], y_send.at[kind, 1, sp], y_recv.at[kind, 1, sp],
            (flip_y, s),
        )

    def up(kind, sp):
        return send(
            mine.at[q_own, sp, :, spans[kind]], u_in.at[kind, sp, :, spans[kind]], z_send.at[kind, 0, sp], z_recv.at[kind, 0, sp],
            (e, s + 1),
        )

    def down(kind, sp):
        return send(
            mine.at[q_own, sp, :, spans[kind]], d_in.at[kind, sp, :, spans[kind]], z_send.at[kind, 1, sp], z_recv.at[kind, 1, sp],
            (e, s - 1),
        )

    def settled(kind, sp):
        for q in range(4):
            to_core(kind, q, sp).wait_send()
        for copy in halves(kind, sp) + [to_x(kind, sp), to_y(kind, sp)]:
            copy.wait_send()

        @pl.when(sp > s)
        def _():
            up(kind, sp).wait_send()

        @pl.when(sp < s)
        def _():
            down(kind, sp).wait_send()

    def arrived(block, sem):
        send(block, block, sem, sem, (core, s)).wait_recv()

    def plane_at(i):
        back = 2 * planes - 2 - i
        sp = s + (2 * (back % 2) - 1) * ((back + 1) // 2)
        return sp, (sp >= 0) & (sp < planes) & (i >= 0) & (back >= 0)

    def add(target, *others):
        if len(others) == 1:
            target[...] = target[...] + others[0][...]
            return
        total = target[...].astype(FULL)
        for other in others:
            total = total + other[...].astype(FULL)
        target[...] = total.astype(LOW)

    def work(kind, sp):
        if kind == 1:
            settled(0, sp)
            pl.semaphore_wait(free.at[sp], 1)
        for k, q in enumerate(order):
            fetch_hot(k, sp).wait()
            fetch(kind, k, sp).wait()

            def part(at, wide, q=q, k=k):
                rows = load[k % 2, :, :, at].reshape(EXP_DEV * slots, wide)
                got = jnp.dot(hot[k % 2], rows, preferred_element_type=FULL).astype(LOW)
                got = got.reshape(2, length, wide)

                @pl.when(parity == 0)
                def _():
                    mine[q, sp, :, at] = got[0]
                    away[q, sp, :, at] = got[1]

                @pl.when(parity == 1)
                def _():
                    mine[q, sp, :, at] = got[1]
                    away[q, sp, :, at] = got[0]

            def tile(t, inner, part=part):
                part(pl.ds(pl.multiple_of(t * TILE, TILE), TILE), TILE)
                return inner

            lax.fori_loop(0, MODEL_WIDTH // TILE, tile, 0)
            if kind == 0 and width > MODEL_WIDTH:
                part(pl.ds(MODEL_WIDTH, width - MODEL_WIDTH), width - MODEL_WIDTH)
            to_core(kind, q, sp).start()
            if k < 2:
                fetch_hot(k + 2, sp).start()
                fetch(kind, k + 2, sp).start()

    def fetch_first(kind, sp):
        for k in range(2):
            fetch_hot(k, sp).start()
            fetch(kind, k, sp).start()

    def pairs(kind, sp):
        for k, q in enumerate(order):
            arrived(c_in.at[q, sp, :, spans[kind]], c_recv.at[kind, q, sp])
            add(mine.at[q, sp, :, spans[kind]], c_in.at[q, sp, :, spans[kind]])
            if k == 0:
                for copy in halves(kind, sp):
                    copy.start()
        if kind == 0:
            pl.semaphore_signal(free.at[sp], 1, device_id=(core, s), device_id_type=MESH)

    def sides(kind, sp):
        arrived(y_half.at[kind, sp, :, spans[kind]], y_recv.at[kind, 0, sp])
        add(mine.at[q_x, sp, low_half, spans[kind]], y_half.at[kind, sp, :, spans[kind]])
        to_x(kind, sp).start()
        arrived(x_half.at[kind, sp, :, spans[kind]], x_recv.at[kind, 0, sp])
        add(mine.at[q_y, sp, high_half, spans[kind]], x_half.at[kind, sp, :, spans[kind]])
        to_y(kind, sp).start()

    def line(kind, sp):
        arrived(x_in.at[kind, sp, :, spans[kind]], x_recv.at[kind, 1, sp])
        arrived(y_in.at[kind, sp, :, spans[kind]], y_recv.at[kind, 1, sp])
        add(
            mine.at[q_own, sp, :, spans[kind]],
            x_in.at[kind, sp, :, spans[kind]],
            y_in.at[kind, sp, :, spans[kind]],
        )

        @pl.when((sp >= s) & (s > 0))
        def _():
            arrived(u_in.at[kind, sp, :, spans[kind]], z_recv.at[kind, 0, sp])
            add(mine.at[q_own, sp, :, spans[kind]], u_in.at[kind, sp, :, spans[kind]])

        @pl.when((sp <= s) & (s < planes - 1))
        def _():
            arrived(d_in.at[kind, sp, :, spans[kind]], z_recv.at[kind, 1, sp])
            add(mine.at[q_own, sp, :, spans[kind]], d_in.at[kind, sp, :, spans[kind]])

        @pl.when(sp > s)
        def _():
            up(kind, sp).start()

        @pl.when(sp < s)
        def _():
            down(kind, sp).start()

        @pl.when(sp == s)
        def _():
            if kind == 0:
                out_ref[...] = mine[q_own, sp].astype(FULL)
            else:
                mix_ref[...] = mine[q_own, sp, :, :MODEL_WIDTH].astype(FULL)

    greet(planes)
    span = 2 * planes - 1

    def step(t, carry):
        for lag, job in ((0, fetch_first), (1, pairs), (3, sides), (0, work), (5, line)):
            for kind in range(2):
                sp, there = plane_at(t - lag - kind * span)

                @pl.when(there)
                def _(sp=sp, job=job, kind=kind):
                    job(kind, sp)

        return carry

    lax.fori_loop(0, 2 * span + 5, step, 0)

    def drain(sp, carry):
        settled(1, sp)
        return carry

    lax.fori_loop(0, planes, drain, 0)


def combine_home(hot, v, m, length, planes, slots, identity):
    width = v.shape[2]
    block = (planes, length, width)
    part = (planes, length // 2, width)
    return pl.pallas_call(
        functools.partial(combine_home_kernel, planes, slots),
        out_shape=[
            jax.ShapeDtypeStruct((length, width), FULL),
            jax.ShapeDtypeStruct((length, MODEL_WIDTH), FULL),
        ],
        in_specs=[ANY, ANY, ANY],
        out_specs=[VM, VM],
        scratch_shapes=[
            pltpu.VMEM((2,) + hot.shape[1:], LOW),
            pltpu.VMEM((2, EXP_DEV, slots, width), LOW),
            pltpu.VMEM((4,) + block, LOW),
            pltpu.VMEM((4,) + block, LOW),
            pltpu.VMEM((4,) + block, LOW),
            pltpu.VMEM((2,) + block, LOW),
            pltpu.VMEM((2,) + block, LOW),
            pltpu.VMEM((2,) + part, LOW),
            pltpu.VMEM((2,) + part, LOW),
            pltpu.VMEM((2,) + block, LOW),
            pltpu.VMEM((2,) + block, LOW),
            DMA((2,)),
            DMA((2,)),
            pltpu.SemaphoreType.REGULAR((planes,)),
            DMA((2, 4, planes)),
            DMA((2, 4, planes)),
            DMA((2, 2, planes)),
            DMA((2, 2, planes)),
            DMA((2, 2, planes)),
            DMA((2, 2, planes)),
            DMA((2, 2, planes)),
            DMA((2, 2, planes)),
        ],
        compiler_params=pltpu.CompilerParams(
            collective_id=identity, has_side_effects=True, vmem_limit_bytes=VMEM_LIMIT
        ),
    )(hot, v, m)


def greet_plane(planes, owners):
    e, s = lax.axis_index("expert"), lax.axis_index("shard")
    barrier = pltpu.get_barrier_semaphore()
    for o in range(1, owners):
        pl.semaphore_signal(
            barrier, 1, device_id=(lax.rem(e + o, owners), s), device_id_type=MESH
        )

    @pl.when(s > 0)
    def _():
        pl.semaphore_signal(barrier, 1, device_id=(e, s - 1), device_id_type=MESH)

    @pl.when(s < planes - 1)
    def _():
        pl.semaphore_signal(barrier, 1, device_id=(e, s + 1), device_id_type=MESH)

    inner = (s > 0) & (s < planes - 1)

    @pl.when(inner)
    def _():
        pl.semaphore_wait(barrier, owners + 1)

    @pl.when(jnp.logical_not(inner))
    def _():
        pl.semaphore_wait(barrier, owners)


def gather_steps(at, cut, source, x_send, x_recv, y_send, y_recv, c_send, c_recv):
    e, core, flip_x, flip_y, diagonal = neighbours()
    s = lax.axis_index("shard")

    def arrived(block, sem):
        send(block, block, sem, sem, (core, s)).wait_recv()

    def first():
        return [
            send(source, at(e), x_send(0), x_recv(0), (flip_x, s)),
            send(source, at(e), y_send(0), y_recv(0), (flip_y, s)),
            send(source, at(e), c_send(0), c_recv(0), (core, s)),
        ]

    def from_x():
        return [
            send(cut(flip_x, 0), cut(flip_x, 0), y_send(1), y_recv(1), (flip_y, s)),
            send(at(flip_x), at(flip_x), c_send(1), c_recv(1), (core, s)),
        ]

    def from_y():
        return [
            send(cut(flip_y, 1), cut(flip_y, 1), x_send(1), x_recv(1), (flip_x, s)),
            send(at(flip_y), at(flip_y), c_send(2), c_recv(2), (core, s)),
        ]

    def from_diagonal():
        return [send(at(diagonal), at(diagonal), c_send(3), c_recv(3), (core, s))]

    def begin():
        for copy in first():
            copy.start()

    def second():
        arrived(at(flip_x), x_recv(0))
        for copy in from_x():
            copy.start()
        arrived(at(flip_y), y_recv(0))
        for copy in from_y():
            copy.start()

    def third():
        arrived(cut(diagonal, 0), y_recv(1))
        arrived(cut(diagonal, 1), x_recv(1))
        for copy in from_diagonal():
            copy.start()

    def last():
        for k, lane in enumerate((core, core + flip_x - e, core + flip_y - e, core + diagonal - e)):
            arrived(at(lane), c_recv(k))

    def sent():
        for copy in first() + from_x() + from_y() + from_diagonal():
            copy.wait_send()

    return begin, second, third, last, sent


def rope_tables(places, frequency):
    angles = places * frequency
    lane = lax.broadcasted_iota(jnp.int32, angles.shape, 1)
    sine = jnp.sin(angles)
    return jnp.cos(angles), jnp.where(lane < HEAD_SIZE // 2, -sine, sine)


def half_turn(v):
    return pltpu.roll(v, HEAD_SIZE // 2, 1)


def head_gains(rows, planes):
    total = rows[0, :, :HEAD_SIZE].astype(FULL)
    for sp in range(1, planes):
        part = rows[sp, :, :HEAD_SIZE].astype(FULL)
        total = total + pltpu.roll(part, sp * (HEAD_SIZE // planes), 1)
    return total[2:3], total[3:4]


def front_kernel(
    planes, owners, qkv_ref, router_ref, gain_ref, tok_ref, d_ref, freq_ref, out_ref,
    d_all, w_out_all, w_all_out, r_all, gains, tail_ref, h1_ref, proj_ref, probs_ref, mixed_ref, branch_ref,
    w_all, tok_all, w_mine, q_rows, mine, away, c_in, x_in, y_in, x_half, y_half,
    keep_sem, w_send, w_recv, v_send, v_recv, k_send, k_recv, r_send, r_recv, g_send, g_recv,
    o_send, o_recv, z_send, z_recv, rx_send, rx_recv, ry_send, ry_recv, rc_send, rc_recv,
    tx_send, tx_recv, ty_send, ty_recv, tc_send, tc_recv,
    dx_send, dx_recv, dy_send, dy_recv, dc_send, dc_recv,
    px_send, px_recv, py_send, py_recv, pc_send, pc_recv,
):
    e, core, flip_x, flip_y, diagonal = neighbours()
    s = lax.axis_index("shard")
    lanes = owners // planes
    home = e // lanes
    length = tok_ref.shape[0]
    half = length // 2
    count = w_mine.shape[0]
    heads = count // HEAD_SIZE
    pieces = 8
    out_part = count // pieces
    deep = qkv_ref.shape[0]
    query_cols = count
    kv_at = pl.ds(pl.multiple_of(count + HEAD_SIZE * (e % 2), HEAD_SIZE), HEAD_SIZE)

    def arrived(block, sem):
        send(block, block, sem, sem, (core, s)).wait_recv()

    def w_copy(sp, way):
        block = w_all.at[sp, :, pl.ds(0, query_cols)]
        return send(block, block, w_send.at[way, sp], w_recv.at[sp], (e, s + 1 - 2 * way))

    def v_copy(sp, way):
        block = w_all.at[sp, :, kv_at]
        return send(block, block, v_send.at[way, sp], v_recv.at[sp], (e, s + 1 - 2 * way))

    def r_copy(sp, way):
        block = r_all.at[e, sp]
        return send(block, block, r_send.at[way, sp], r_recv.at[sp], (e, s + 1 - 2 * way))

    def k_copy(sp):
        block = w_all.at[sp, :, kv_at]
        return send(block, block, k_send.at[sp], k_recv.at[sp], (core, s))

    def g_copy(sp, way):
        block = gains.at[sp]
        return send(block, block, g_send.at[way, sp], g_recv.at[sp], (e, s + 1 - 2 * way))

    def d_copy(sp, way):
        block = d_all.at[e, sp]
        return send(block, block, z_send.at[way, sp], z_recv.at[sp], (e, s + 1 - 2 * way))

    def o_copy(k, way):
        block = w_mine.at[pl.ds(k * out_part, out_part)]
        return send(block, block, o_send.at[way, k], o_recv.at[k], (e, s + 1 - 2 * way))

    t_begin, t_second, t_third, t_last, t_sent = gather_steps(
        lambda lane: tok_all.at[lane],
        lambda lane, k: tok_all.at[lane, pl.ds(k * half, half)],
        tok_ref,
        lambda k: tx_send.at[k],
        lambda k: tx_recv.at[k],
        lambda k: ty_send.at[k],
        lambda k: ty_recv.at[k],
        lambda k: tc_send.at[k],
        lambda k: tc_recv.at[k],
    )

    r_half = planes // 2
    r_begin, r_second, r_third, r_last, r_sent = gather_steps(
        lambda lane: r_all.at[lane],
        lambda lane, k: r_all.at[lane, pl.ds(k * r_half, r_half)],
        r_all.at[e],
        lambda k: rx_send.at[k],
        lambda k: rx_recv.at[k],
        lambda k: ry_send.at[k],
        lambda k: ry_recv.at[k],
        lambda k: rc_send.at[k],
        lambda k: rc_recv.at[k],
    )

    def d_rows(sp):
        return gather_steps(
            lambda lane: d_all.at[lane, sp],
            lambda lane, k: d_all.at[lane, sp, pl.ds(k * half, half)],
            d_all.at[e, sp],
            lambda k: dx_send.at[k, sp],
            lambda k: dx_recv.at[k, sp],
            lambda k: dy_send.at[k, sp],
            lambda k: dy_recv.at[k, sp],
            lambda k: dc_send.at[k, sp],
            lambda k: dc_recv.at[k, sp],
        )

    keep_d = pltpu.make_async_copy(d_ref, d_all.at[e, s], keep_sem.at[0])
    rows = pl.ds(pl.multiple_of((e - home * lanes) * count, 16), count)
    load_o = pltpu.make_async_copy(out_ref.at[rows], w_mine, keep_sem.at[1])
    keep_w = pltpu.make_async_copy(w_all, w_all_out, keep_sem.at[2])
    keep_o = pltpu.make_async_copy(w_mine, w_out_all, keep_sem.at[3])
    at = pl.ds(pl.multiple_of(e * count, count), count)
    load_w = pltpu.make_async_copy(
        qkv_ref.at[:, at], w_all.at[s, :, pl.ds(0, query_cols)], keep_sem.at[4]
    )
    kv_from = (QUERY_HEADS + e % 2 * KEY_VALUE_HEADS + e * KEY_VALUE_HEADS // owners) * HEAD_SIZE
    at = pl.ds(pl.multiple_of(kv_from, HEAD_SIZE), HEAD_SIZE)
    load_v = pltpu.make_async_copy(qkv_ref.at[:, at], w_all.at[s, :, kv_at], keep_sem.at[5])
    keep_d.start()

    @pl.when(s == home)
    def _():
        load_o.start()

    load_w.start()
    load_v.start()
    r_all[e, s] = router_ref[...]
    gains[s] = gain_ref[...]
    tok_all[e] = tok_ref[...]
    greet(planes)

    def both_ways(copy, sp):
        @pl.when((sp <= s) & (s < planes - 1))
        def _():
            copy(sp, 0).start()

        @pl.when((sp >= s) & (s > 0))
        def _():
            copy(sp, 1).start()

    def plane_at(i):
        sp = s + (2 * (i % 2) - 1) * ((i + 1) // 2)
        return sp, (sp >= 0) & (sp < planes) & (i >= 0) & (i <= 2 * planes - 2)

    def out_step(k):
        @pl.when(s != home)
        def _():
            arrived(w_mine.at[pl.ds(k * out_part, out_part)], o_recv.at[k])

        @pl.when((s >= home) & (s < planes - 1))
        def _():
            o_copy(k, 0).start()

        @pl.when((s <= home) & (s > 0))
        def _():
            o_copy(k, 1).start()

    t_begin()
    both_ways(g_copy, s)
    keep_d.wait()
    both_ways(d_copy, s)
    load_w.wait()
    both_ways(w_copy, s)
    load_v.wait()
    both_ways(v_copy, s)
    both_ways(r_copy, s)
    k_copy(s).start()
    d_rows(s)[0]()

    def weights(i, carry):
        sp, there = plane_at(i)

        @pl.when(there & (i > 0))
        def _():
            arrived(gains.at[sp], g_recv.at[sp])
            both_ways(g_copy, sp)
            arrived(d_all.at[e, sp], z_recv.at[sp])
            both_ways(d_copy, sp)
            d_rows(sp)[0]()
            arrived(w_all.at[sp, :, pl.ds(0, query_cols)], w_recv.at[sp])
            both_ways(w_copy, sp)
            arrived(w_all.at[sp, :, kv_at], v_recv.at[sp])
            both_ways(v_copy, sp)
            k_copy(sp).start()
            arrived(r_all.at[e, sp], r_recv.at[sp])
            both_ways(r_copy, sp)

        @pl.when(i == 1)
        def _():
            t_second()

        @pl.when(i == 2)
        def _():
            t_third()

        @pl.when((i == 4) & (s == home))
        def _():
            load_o.wait()
            for k in range(pieces):
                out_step(k)

        return carry

    lax.fori_loop(1, 2 * planes - 1, weights, 0)
    r_begin()
    t_last()
    other_kv = pl.ds(pl.multiple_of(count + HEAD_SIZE * (1 - e % 2), HEAD_SIZE), HEAD_SIZE)
    for sp in range(planes):
        arrived(w_all.at[sp, :, other_kv], k_recv.at[sp])
    keep_w.start()

    def distant(n):
        return (s - home == n) | (home - s == n)

    gain_query, gain_key = head_gains(gains, planes)
    row = lax.broadcasted_iota(jnp.int32, (length, length), 0).astype(FULL)
    column = lax.broadcasted_iota(jnp.int32, (length, length), 1).astype(FULL)

    def attend(b, carry):
        x = tok_all[b, :, :MODEL_WIDTH].astype(FULL)
        inverse = lax.rsqrt(jnp.mean(x * x, axis=1, keepdims=True) + EPS)
        total = jnp.zeros((length, w_all.shape[2]), FULL)
        for sp in range(planes):
            at = slice(sp * deep, (sp + 1) * deep)
            part = x[:, at] * inverse * gains[sp, 0:1, :].astype(FULL)
            part = part.astype(LOW)
            h1_ref[b, :, at] = part
            total = total + jnp.dot(part, w_all[sp], preferred_element_type=FULL)
        proj_ref[b] = total
        tail_ref[b] = tok_all[b, :, MODEL_WIDTH:]
        places = tok_all[b, :, MODEL_WIDTH:].astype(FULL)[:, 1:2]
        cosine, sine = rope_tables(places, freq_ref[0:1, :])

        def normed(v, gain):
            v = v * lax.rsqrt(jnp.mean(v * v, axis=1, keepdims=True) + EPS) * gain
            return (v * cosine + half_turn(v) * sine).astype(LOW)

        for h in range(heads):
            at = slice(h * HEAD_SIZE, (h + 1) * HEAD_SIZE)
            q_rows[h * length : (h + 1) * length, :] = normed(total[:, at], gain_query)
        key = normed(total[:, count : count + HEAD_SIZE], gain_key)
        value = total[:, count + HEAD_SIZE :].astype(LOW)
        scores = lax.dot_general(
            q_rows[...], key, (((1,), (1,)), ((), ())), preferred_element_type=FULL
        ) * (HEAD_SIZE**-0.5)
        allowed = (column <= row) & (column >= row - places)
        scores = jnp.where(jnp.concatenate([allowed] * heads, axis=0), scores, -1e30)
        exponent = jnp.exp(scores - jnp.max(scores, axis=1, keepdims=True))
        probs = (exponent / jnp.sum(exponent, axis=1, keepdims=True)).astype(LOW)
        probs_ref[b] = probs
        mixed = jnp.dot(probs, value, preferred_element_type=FULL).astype(LOW)
        for h in range(heads):
            at = slice(h * HEAD_SIZE, (h + 1) * HEAD_SIZE)
            mixed_ref[b, :, at] = mixed[h * length : (h + 1) * length]

        for lag, stage in ((0, 1), (2, 2)):
            sp, there = plane_at(b - lag)

            @pl.when(there)
            def _(sp=sp, stage=stage):
                d_rows(sp)[stage]()

        for k in range(pieces):

            @pl.when((b == k) & distant(1))
            def _(k=k):
                out_step(k)

        for k in range(5):

            @pl.when((b == 3 + k) & distant(2))
            def _(k=k):
                out_step(k)

        return carry

    lax.fori_loop(0, owners, attend, 0)
    for i in range(owners - 2, 2 * planes - 1):
        sp, there = plane_at(i)

        @pl.when(there)
        def _(sp=sp):
            d_rows(sp)[2]()


    @pl.when(distant(2))
    def _():
        for k in range(5, pieces):
            out_step(k)

    r_second()
    for n in range(3, planes):

        @pl.when(distant(n))
        def _():
            for k in range(pieces):
                out_step(k)

    keep_o.start()
    begin, middle, finish, sent = project_steps(
        False, mixed_ref, w_mine, branch_ref, mine, away, c_in, x_in, y_in, x_half, y_half,
        pc_send, pc_recv, px_send, px_recv, py_send, py_recv,
    )
    begin()
    r_third()
    middle()
    finish()
    r_last()
    t_sent()
    r_sent()
    sent()

    def settled(copy, sp):
        @pl.when((sp <= s) & (s < planes - 1))
        def _():
            copy(sp, 0).wait_send()

        @pl.when((sp >= s) & (s > 0))
        def _():
            copy(sp, 1).wait_send()

    def drain(sp, carry):
        d_rows(sp)[3]()
        d_rows(sp)[4]()
        settled(w_copy, sp)
        settled(v_copy, sp)
        settled(r_copy, sp)
        k_copy(sp).wait_send()
        settled(g_copy, sp)
        settled(d_copy, sp)
        return carry

    lax.fori_loop(0, planes, drain, 0)
    for k in range(pieces):

        @pl.when((s >= home) & (s < planes - 1))
        def _(k=k):
            o_copy(k, 0).wait_send()

        @pl.when((s <= home) & (s > 0))
        def _(k=k):
            o_copy(k, 1).wait_send()

    keep_w.wait()
    keep_o.wait()


def front(w, router, gain_rows, tokens, w_out, d_rows, frequency, planes, owners, identity):
    def out(*shape, dtype=LOW):
        return jax.ShapeDtypeStruct(shape, dtype)

    length = tokens.shape[0]
    count = w_out.shape[0] * planes // owners
    qkv_cols = count + 2 * HEAD_SIZE
    block = (length, MODEL_WIDTH)
    part = (length // 2, MODEL_WIDTH)
    return pl.pallas_call(
        functools.partial(front_kernel, planes, owners),
        out_shape=[
            out(owners, planes, *d_rows.shape),
            out(count, MODEL_WIDTH),
            out(planes, w.shape[0], qkv_cols),
            out(owners, planes, *router.shape),
            out(planes, *gain_rows.shape),
            out(owners, length, TAIL),
            out(owners, length, MODEL_WIDTH),
            out(owners, length, qkv_cols, dtype=FULL),
            out(owners, length * count // HEAD_SIZE, length),
            out(owners, length, count),
            out(length, MODEL_WIDTH, dtype=FULL),
        ],
        in_specs=[ANY, VM, VM, VM, VM, VM, ANY],
        out_specs=[ANY, ANY, ANY, VM, VM, VM, VM, VM, VM, VM, VM],
        scratch_shapes=[
            pltpu.VMEM((planes, w.shape[0], qkv_cols), LOW),
            pltpu.VMEM((owners,) + tokens.shape, LOW),
            pltpu.VMEM((count, MODEL_WIDTH), LOW),
            pltpu.VMEM((length * count // HEAD_SIZE, HEAD_SIZE), LOW),
            pltpu.VMEM((4,) + block, LOW),
            pltpu.VMEM((4,) + block, LOW),
            pltpu.VMEM((4,) + block, LOW),
            pltpu.VMEM(block, LOW),
            pltpu.VMEM(block, LOW),
            pltpu.VMEM(part, LOW),
            pltpu.VMEM(part, LOW),
            DMA((6,)),
            DMA((2, planes)),
            DMA((planes,)),
            DMA((2, planes)),
            DMA((planes,)),
            DMA((planes,)),
            DMA((planes,)),
            DMA((2, planes)),
            DMA((planes,)),
            DMA((2, planes)),
            DMA((planes,)),
            DMA((2, 8)),
            DMA((8,)),
            DMA((2, planes)),
            DMA((planes,)),
            DMA((2,)),
            DMA((2,)),
            DMA((2,)),
            DMA((2,)),
            DMA((4,)),
            DMA((4,)),
            DMA((2,)),
            DMA((2,)),
            DMA((2,)),
            DMA((2,)),
            DMA((4,)),
            DMA((4,)),
            DMA((2, planes)),
            DMA((2, planes)),
            DMA((2, planes)),
            DMA((2, planes)),
            DMA((4, planes)),
            DMA((4, planes)),
            DMA((2,)),
            DMA((2,)),
            DMA((2,)),
            DMA((2,)),
            DMA((4,)),
            DMA((4,)),
        ],
        compiler_params=pltpu.CompilerParams(
            collective_id=identity, has_side_effects=True, vmem_limit_bytes=VMEM_LIMIT
        ),
    )(w, router, gain_rows, tokens, d_rows, frequency, w_out)


def project_steps(
    turned, rows_ref, w_ref, out_ref, mine, away, c_in, x_in, y_in, x_half, y_half,
    cs, cr, xs, xr, ys, yr,
):
    e, core, flip_x, flip_y, diagonal = neighbours()
    s = lax.axis_index("shard")
    q_own, q_x, q_y, q_d = e // 2, flip_x // 2, flip_y // 2, diagonal // 2
    parity = e % 2
    half = out_ref.shape[0] // 2
    low_half, high_half = pl.ds(0, half), pl.ds(half, half)
    across = (((1,), (1 if turned else 0,)), ((), ()))
    order = (q_d, q_x, q_y, q_own)

    def arrived(block, sem):
        send(block, block, sem, sem, (core, s)).wait_recv()

    def add(target, *others):
        total = target[...].astype(FULL)
        for other in others:
            total = total + other[...].astype(FULL)
        target[...] = total.astype(LOW)

    def to_core(q):
        return send(away.at[q], c_in.at[q], cs.at[q], cr.at[q], (core, s))

    def compute(q, lane, into):
        rows = rows_ref[2 * q + lane]

        def tile(t, carry):
            at = pl.ds(pl.multiple_of(t * TILE, TILE), TILE)
            if turned:
                deep = w_ref.shape[1]
                w = w_ref[t * TILE // deep, :, : rows.shape[1]]
            else:
                w = w_ref[:, at]
            into[q, :, at] = lax.dot_general(
                rows, w, across, preferred_element_type=FULL
            ).astype(LOW)
            return carry

        lax.fori_loop(0, MODEL_WIDTH // TILE, tile, 0)

    halves = [
        send(mine.at[q_d, low_half], y_half, ys.at[0], yr.at[0], (flip_y, s)),
        send(mine.at[q_d, high_half], x_half, xs.at[0], xr.at[0], (flip_x, s)),
    ]
    to_x = send(mine.at[q_x], x_in, xs.at[1], xr.at[1], (flip_x, s))
    to_y = send(mine.at[q_y], y_in, ys.at[1], yr.at[1], (flip_y, s))

    def joined(q):
        arrived(c_in.at[q], cr.at[q])
        add(mine.at[q], c_in.at[q])

    def begin():
        for q in order:
            compute(q, 1 - parity, away)
            to_core(q).start()
        for k, q in enumerate(order):
            compute(q, parity, mine)
            if k == 0:
                joined(q_d)
                for copy in halves:
                    copy.start()

    def middle():
        joined(q_x)
        arrived(y_half, yr.at[0])
        add(mine.at[q_x, low_half], y_half)
        to_x.start()
        joined(q_y)
        arrived(x_half, xr.at[0])
        add(mine.at[q_y, high_half], x_half)
        to_y.start()

    def finish():
        joined(q_own)
        arrived(x_in, xr.at[1])
        arrived(y_in, yr.at[1])
        out_ref[...] = (
            mine[q_own].astype(FULL) + x_in[...].astype(FULL) + y_in[...].astype(FULL)
        )

    def sent():
        for q in order:
            to_core(q).wait_send()
        for copy in halves + [to_x, to_y]:
            copy.wait_send()

    return begin, middle, finish, sent


def add_blocks(target, other):
    step = min(128, target.shape[1])
    for lead in range(target.shape[0]):

        def one(r, carry, lead=lead):
            at = pl.ds(pl.multiple_of(r * step, step), step)
            target[lead, at, :] = (
                target[lead, at, :].astype(FULL) + other[lead, at, :].astype(FULL)
            ).astype(LOW)
            return carry

        lax.fori_loop(0, target.shape[1] // step, one, 0)


def back_kernel(
    planes, owners, dm_ref, w_out_ref, mixed_ref, proj_ref, probs_ref, places_ref, gain_ref,
    freq_ref, h1_ref, w_ref, tok_ref, h2_ref, dl_ref, gain_two_ref,
    out_rows, out_head, out_rest, dh1_ref,
    dm_all, mixed_t, rows, q_rows, dm_rows, dproj, column,
    acc_rows, acc_head, acc_rest, sibling, u_rows, u_head, u_rest, d_rows, d_head, d_rest, pair_in,
    mine, away, c_in, x_in, y_in, x_half, y_half,
    gxs, gxr, gys, gyr, gcs, gcr, a_send, a_recv, s_send, s_recv, z_send, z_recv,
    x_send, x_recv, y_send, y_recv, c_send, c_recv, own_sem,
    pc_send, pc_recv, px_send, px_recv, py_send, py_recv,
):
    e, core, _, _, _ = neighbours()
    s = lax.axis_index("shard")
    parity = e % 2
    lanes = owners // planes
    length = dm_ref.shape[0]
    half = length // 2
    count = w_out_ref.shape[0]
    heads = count // HEAD_SIZE
    share_cols = acc_rows.shape[2]
    deep = acc_head.shape[1] * acc_head.shape[2]
    scaling = HEAD_SIZE**-0.5
    nt = (((1,), (1,)), ((), ()))
    tn = (((0,), (0,)), ((), ()))
    up_in, down_in = (u_rows, u_head, u_rest), (d_rows, d_head, d_rest)
    outs = (out_rows, out_head, out_rest)

    def arrived(block, sem):
        send(block, block, sem, sem, (core, s)).wait_recv()

    greet_plane(planes, owners)
    begin, second, third, last, sent = gather_steps(
        lambda lane: dm_all.at[lane],
        lambda lane, k: dm_all.at[lane, pl.ds(k * half, half)],
        dm_ref,
        lambda k: gxs.at[k],
        lambda k: gxr.at[k],
        lambda k: gys.at[k],
        lambda k: gyr.at[k],
        lambda k: gcs.at[k],
        lambda k: gcr.at[k],
    )
    begin()
    dm_all[e] = dm_ref[...]
    for b in range(owners):
        mixed_t[:, b * length : (b + 1) * length] = mixed_ref[b].T

    def lane_at(j):
        flipped = [(e // bit + j // bit) % 2 * bit for bit in (1, 2, 4)]
        return flipped[0] + flipped[1] + flipped[2]

    def spread(other):
        return send(
            rows.at[:, pl.ds(other * share_cols, share_cols)], acc_rows.at[e],
            a_send.at[other], a_recv.at[e], (other, s),
        )

    column[...] = jnp.zeros_like(column)
    gain_query, gain_key = head_gains(gain_ref, planes)

    def attend(j, carry):
        b = lane_at(j)
        for at, step in ((2, second), (6, third)):

            @pl.when(j == at)
            def _(step=step):
                step()

        @pl.when(j % 2 == 1)
        def _():
            arrived(dm_all.at[b], gcr.at[j // 2])

        places = places_ref[b].astype(FULL)[:, 1:2]
        cosine, sine = rope_tables(places, freq_ref[0:1, :])

        def unit(v):
            inverse = lax.rsqrt(jnp.mean(v * v, axis=1, keepdims=True) + EPS)
            return v * inverse, inverse

        def turned(v):
            return (v * cosine + half_turn(v) * sine).astype(LOW)

        def back(v, units, inverse, gain, row):
            v = v * cosine - half_turn(v) * sine
            column[row : row + 1, :HEAD_SIZE] += jnp.sum(v * units, axis=0, keepdims=True)
            v = v * gain
            return inverse * (v - units * jnp.mean(v * units, axis=1, keepdims=True))

        d_mixed = lax.dot_general(
            dm_all[b], w_out_ref[...], nt, preferred_element_type=FULL
        ).astype(LOW)
        for h in range(heads):
            at = slice(h * HEAD_SIZE, (h + 1) * HEAD_SIZE)
            here = slice(h * length, (h + 1) * length)
            dm_rows[here, :] = d_mixed[:, at]
            units, _ = unit(proj_ref[b, :, at])
            q_rows[here, :] = turned(units * gain_query)
        key_units, key_inverse = unit(proj_ref[b, :, count : count + HEAD_SIZE])
        key = turned(key_units * gain_key)
        value = proj_ref[b, :, count + HEAD_SIZE :].astype(LOW)
        probs = probs_ref[b]
        wide = probs.astype(FULL)
        d_probs = lax.dot_general(dm_rows[...], value, nt, preferred_element_type=FULL)
        d_scores = wide * (d_probs - jnp.sum(d_probs * wide, axis=1, keepdims=True))
        d_scores = d_scores.astype(LOW)
        d_query = jnp.dot(d_scores, key, preferred_element_type=FULL) * scaling
        d_key = lax.dot_general(d_scores, q_rows[...], tn, preferred_element_type=FULL) * scaling
        d_value = lax.dot_general(probs, dm_rows[...], tn, preferred_element_type=FULL)
        for h in range(heads):
            at = slice(h * HEAD_SIZE, (h + 1) * HEAD_SIZE)
            units, inverse = unit(proj_ref[b, :, at])
            got = back(
                d_query[h * length : (h + 1) * length], units, inverse, gain_query, GAIN_QUERY
            )
            dproj[b, :, at] = got.astype(LOW)
        got = back(d_key, key_units, key_inverse, gain_key, GAIN_KEY)
        dproj[b, :, count : count + HEAD_SIZE] = got.astype(LOW)
        dproj[b, :, count + HEAD_SIZE :] = d_value.astype(LOW)
        return carry

    lax.fori_loop(0, owners, attend, 0)
    resident = tok_ref[...].astype(FULL)
    inverse_one = lax.rsqrt(jnp.mean(resident * resident, axis=1, keepdims=True) + EPS)

    def left_of(sp):
        at = pl.ds(pl.multiple_of(sp * deep, deep), deep)
        return h1_ref[:, :, at].reshape(-1, deep)

    def make_head(sp):
        right = dproj[:, :, :count].reshape(-1, count)
        got = lax.dot_general(left_of(sp), right, tn, preferred_element_type=FULL).astype(LOW)
        acc_head[sp] = got.reshape(acc_head.shape[1:])

    def to_sibling(sp):
        return send(sibling.at[sp], pair_in.at[sp], s_send.at[sp], s_recv.at[sp], (core, s))

    def make_rest(sp):
        right = dproj[:, :, count:].reshape(-1, 2 * HEAD_SIZE)
        got = lax.dot_general(left_of(sp), right, tn, preferred_element_type=FULL).astype(LOW)
        key, value = got[:, :HEAD_SIZE], got[:, HEAD_SIZE:]
        at = pl.ds(pl.multiple_of(sp * deep, deep), deep)
        column[GAIN_ONE : GAIN_ONE + 1, :] = jnp.sum(
            dh1_ref[:, at] * (tok_ref[:, at].astype(FULL) * inverse_one), axis=0, keepdims=True
        )
        column[GAIN_TWO : GAIN_TWO + 1, :] = gain_two_ref[:, at]
        extra = lax.dot_general(h2_ref[:, at], dl_ref[...], tn, preferred_element_type=FULL)
        extra = (extra + column[...].T).astype(LOW)
        top, low = extra[: deep // 2], extra[deep // 2 :]

        def put(into, kv, part):
            into[sp, :4] = kv.reshape(4, deep // 4, HEAD_SIZE)
            into[sp, 4:] = part.reshape(2, deep // 4, HEAD_SIZE)

        @pl.when(parity == 0)
        def _():
            put(acc_rest, key, top)
            put(sibling, value, low)

        @pl.when(parity == 1)
        def _():
            put(acc_rest, value, low)
            put(sibling, key, top)

        to_sibling(sp).start()

    def chunk(k, sp):
        if k == 0:
            return acc_rows.at[pl.ds(sp * lanes, lanes)]
        return acc_head.at[sp] if k == 1 else acc_rest.at[sp]

    def ready(k, sp):
        if k == 0:
            for lane in range(lanes):
                source = sp * lanes + lane

                @pl.when(source != e)
                def _(source=source):
                    arrived(acc_rows.at[source], a_recv.at[source])

        elif k == 1:
            make_head(sp)
        else:
            arrived(pair_in.at[sp], s_recv.at[sp])
            add_blocks(acc_rest.at[sp], pair_in.at[sp])

    def up(k, sp):
        return send(
            chunk(k, sp), up_in[k].at[sp], z_send.at[k, 0, sp], z_recv.at[k, 0, sp], (e, s + 1)
        )

    def down(k, sp):
        return send(
            chunk(k, sp), down_in[k].at[sp], z_send.at[k, 1, sp], z_recv.at[k, 1, sp], (e, s - 1)
        )

    def line(k, sp):
        ready(k, sp)

        @pl.when((sp >= s) & (s > 0))
        def _():
            arrived(up_in[k].at[sp], z_recv.at[k, 0, sp])
            add_blocks(chunk(k, sp), up_in[k].at[sp])

        @pl.when((sp <= s) & (s < planes - 1))
        def _():
            arrived(down_in[k].at[sp], z_recv.at[k, 1, sp])
            add_blocks(chunk(k, sp), down_in[k].at[sp])

        @pl.when(sp > s)
        def _():
            up(k, sp).start()

        @pl.when(sp < s)
        def _():
            down(k, sp).start()

    def pair(k, n):
        for i in (2 * n, 2 * n - 1):
            sp = s + (2 * (i % 2) - 1) * n

            @pl.when((sp >= 0) & (sp < planes))
            def _(sp=sp):
                line(k, sp)

    def steps(k):
        size = outs[k].shape[1] // 2
        return gather_steps(
            lambda lane: outs[k].at[lane],
            lambda lane, at: outs[k].at[lane, pl.ds(at * size, size)],
            chunk(k, s),
            lambda n: x_send.at[k, n],
            lambda n: x_recv.at[k, n],
            lambda n: y_send.at[k, n],
            lambda n: y_recv.at[k, n],
            lambda n: c_send.at[k, n],
            lambda n: c_recv.at[k, n],
        )

    def keep(k):
        return pltpu.make_async_copy(chunk(k, s), outs[k].at[e], own_sem.at[k])

    def own(k):
        line(k, s)
        steps(k)[0]()
        keep(k).start()

    p_begin, p_middle, p_finish, p_sent = project_steps(
        True, dproj, w_ref, dh1_ref, mine, away, c_in, x_in, y_in, x_half, y_half,
        pc_send, pc_recv, px_send, px_recv, py_send, py_recv,
    )
    pair(1, planes - 1)
    for other in range(owners):
        at = pl.ds(other * share_cols, share_cols)
        got = jnp.dot(
            mixed_t[...],
            dm_all[:, :, at].reshape(owners * length, share_cols),
            preferred_element_type=FULL,
        ).astype(LOW)
        rows[:, at] = got

        @pl.when(other != e)
        def _(other=other):
            spread(other).start()

        @pl.when(other == e)
        def _(got=got):
            acc_rows[e] = got
    for n in range(planes - 2, 0, -1):
        pair(1, n)
        if n == planes - 2:
            p_begin()
    pair(0, planes - 1)
    p_middle()
    own(1)
    for n in range(planes - 2, 1, -1):
        pair(0, n)
    p_finish()
    for sp in range(planes):
        make_rest(sp)
    pair(0, 1)
    steps(1)[1]()
    pair(2, planes - 1)
    own(0)
    steps(1)[2]()
    for n in range(planes - 2, 0, -1):
        pair(2, n)
    steps(0)[1]()
    own(2)
    steps(0)[2]()
    steps(2)[1]()
    steps(2)[2]()
    for k in range(3):
        keep(k).wait()
        steps(k)[3]()
        steps(k)[4]()
    p_sent()
    sent()
    for other in range(owners):

        @pl.when(other != e)
        def _(other=other):
            spread(other).wait_send()

    def drain(sp, carry):
        to_sibling(sp).wait_send()
        for k in range(3):

            @pl.when(sp > s)
            def _(k=k):
                up(k, sp).wait_send()

            @pl.when(sp < s)
            def _(k=k):
                down(k, sp).wait_send()

        return carry

    lax.fori_loop(0, planes, drain, 0)


def back(
    dm, w_out, mixed, proj, probs, places, gains, frequency, h1, w, tokens, h2, d_logits, gain_two,
    planes, owners, identity,
):
    length = dm.shape[0]
    count = w_out.shape[0]
    share_cols = MODEL_WIDTH // owners
    deep = MODEL_WIDTH // planes
    shapes = (
        (owners // planes, count, share_cols),
        (2, deep // 2, count),
        (6, deep // 4, HEAD_SIZE),
    )
    stack = (length * count // HEAD_SIZE, HEAD_SIZE)
    block = (length, MODEL_WIDTH)
    part = (length // 2, MODEL_WIDTH)

    def vmem(*shape, dtype=LOW):
        return pltpu.VMEM(shape, dtype)

    per_plane = [vmem(planes, *shape) for shape in shapes]
    return pl.pallas_call(
        functools.partial(back_kernel, planes, owners),
        out_shape=[jax.ShapeDtypeStruct((owners,) + shape, LOW) for shape in shapes]
        + [jax.ShapeDtypeStruct(block, FULL)],
        in_specs=[VM] * 14,
        out_specs=[ANY, ANY, ANY, VM],
        scratch_shapes=[
            vmem(owners, *block),
            vmem(count, owners * length),
            vmem(count, MODEL_WIDTH),
            vmem(*stack),
            vmem(*stack),
            vmem(*proj.shape),
            vmem(TAIL, deep, dtype=FULL),
            vmem(owners, count, share_cols),
            per_plane[1],
            per_plane[2],
            per_plane[2],
        ]
        + per_plane
        + per_plane
        + [
            per_plane[2],
            vmem(4, *block),
            vmem(4, *block),
            vmem(4, *block),
            vmem(*block),
            vmem(*block),
            vmem(*part),
            vmem(*part),
            DMA((2,)),
            DMA((2,)),
            DMA((2,)),
            DMA((2,)),
            DMA((4,)),
            DMA((4,)),
            DMA((owners,)),
            DMA((owners,)),
            DMA((planes,)),
            DMA((planes,)),
            DMA((3, 2, planes)),
            DMA((3, 2, planes)),
            DMA((3, 2)),
            DMA((3, 2)),
            DMA((3, 2)),
            DMA((3, 2)),
            DMA((3, 4)),
            DMA((3, 4)),
            DMA((3,)),
            DMA((4,)),
            DMA((4,)),
            DMA((2,)),
            DMA((2,)),
            DMA((2,)),
            DMA((2,)),
        ],
        compiler_params=pltpu.CompilerParams(
            collective_id=identity, has_side_effects=True, vmem_limit_bytes=VMEM_LIMIT
        ),
    )(
        dm, w_out, mixed, proj, probs, places, gains, frequency, h1, w, tokens, h2, d_logits,
        gain_two,
    )


def finish_kernel(
    owners, rows_ref, head_ref, rest_ref, tok_ref, middle_ref, mix_ref, dm_ref, dh1_ref, gain_ref,
    out_rows, out_qkv, out_router, out_gains, result_ref, dtok_ref,
):
    i = pl.program_id(0)

    @pl.when(i < owners)
    def _():
        out_rows[...] = rows_ref[0].astype(FULL)
        out_qkv[...] = head_ref[0].astype(FULL)

    for at in range(2):

        @pl.when(i == owners + at)
        def _(at=at):
            for h in range(KEY_VALUE_HEADS):
                got = rest_ref[2 * h + at, :4].reshape(-1, HEAD_SIZE)
                out_qkv[:, h * HEAD_SIZE : (h + 1) * HEAD_SIZE] = got.astype(FULL)

    @pl.when(i == 0)
    def _():
        height = out_router.shape[0] // 2
        experts = out_router.shape[1]
        for at in range(2):
            total = jnp.zeros((height, TAIL), FULL)
            for lane in range(at, owners, 2):
                total = total + rest_ref[lane, 4:].reshape(-1, TAIL).astype(FULL)
            here = slice(at * height, (at + 1) * height)
            out_router[here, :] = total[:, :experts]
            out_gains[:, here] = total.T[experts : experts + 8]

    @pl.when(i == 1)
    def _():
        result_ref[...] = (middle_ref[...] + mix_ref[...]).astype(LOW)

    @pl.when(i == 2)
    def _():
        resident = tok_ref[...].astype(FULL)
        units, inverse = unit_norm(resident)
        back = norm_back(dh1_ref[...], units, inverse, gain_ref[...])
        dtok_ref[...] = (dm_ref[...] + back).astype(LOW)


def finish_grads(rows, head, rest, tokens, middle, mix, d_middle, d_h1, gain, owners):
    rows = rows.reshape(owners, -1, rows.shape[-1])
    head = head.reshape(owners, -1, head.shape[-1])
    count, share = rows.shape[1:]
    height, wide = head.shape[1:]
    last = owners - 1

    def whole(shape):
        return pl.BlockSpec(shape, lambda i: (0,) * len(shape))

    block = tokens.shape
    return pl.pallas_call(
        functools.partial(finish_kernel, owners),
        grid=(owners + 2,),
        in_specs=[
            pl.BlockSpec((1, count, share), lambda i: (jnp.minimum(i, last), 0, 0)),
            pl.BlockSpec((1, height, wide), lambda i: (jnp.minimum(i, last), 0, 0)),
            whole(rest.shape),
        ]
        + [whole(block)] * 5
        + [whole(gain.shape)],
        out_specs=[
            pl.BlockSpec((count, share), lambda i: (0, jnp.minimum(i, last))),
            pl.BlockSpec((height, wide), lambda i: (0, i)),
            whole((height, TAIL // 2)),
            whole((8, height)),
            whole(block),
            whole(block),
        ],
        out_shape=[
            jax.ShapeDtypeStruct((count, owners * share), FULL),
            jax.ShapeDtypeStruct((height, (owners + 2) * wide), FULL),
            jax.ShapeDtypeStruct((height, TAIL // 2), FULL),
            jax.ShapeDtypeStruct((8, height), FULL),
            jax.ShapeDtypeStruct(block, LOW),
            jax.ShapeDtypeStruct(block, LOW),
        ],
        compiler_params=pltpu.CompilerParams(vmem_limit_bytes=VMEM_LIMIT),
    )(rows, head, rest, tokens, middle, mix, d_middle, d_h1, gain)


def gathered_layer(
    tokens,
    segments,
    routes,
    attn_gain,
    qkv_weight,
    query_gain,
    k_gain,
    w_out,
    ffn_gain,
    router,
    w_gate,
    w_up,
    w_down,
    d_out,
):
    owners = lax.axis_size("expert")
    planes = lax.axis_size("shard")
    me = lax.axis_index("expert")
    plane = lax.axis_index("shard")
    length = tokens.shape[0]
    blocks = owners * planes
    experts_all = router.shape[1]
    capacity = 3 * length * TOPK // (2 * experts_all)
    heads = QUERY_HEADS // owners
    query_cols = heads * HEAD_SIZE
    scaling = HEAD_SIZE ** (-0.5)
    both = ("expert", "shard")
    rows_in = qkv_weight.shape[0]

    kv_head = me * KEY_VALUE_HEADS // owners
    k_at = QUERY_HEADS * HEAD_SIZE + kv_head * HEAD_SIZE
    v_at = k_at + KEY_VALUE_HEADS * HEAD_SIZE
    gains = columns(
        [
            router,
            attn_gain[:, None],
            ffn_gain[:, None],
            jnp.pad(query_gain, (0, rows_in - query_gain.shape[0]))[:, None],
            jnp.pad(k_gain, (0, rows_in - k_gain.shape[0]))[:, None],
        ],
        rows_in,
    )
    mine = jnp.concatenate(
        [
            lax.dynamic_slice_in_dim(qkv_weight, me * query_cols, query_cols, 1),
            lax.dynamic_slice_in_dim(qkv_weight, k_at, HEAD_SIZE, 1),
            lax.dynamic_slice_in_dim(qkv_weight, v_at, HEAD_SIZE, 1),
            gains,
        ],
        axis=1,
    )
    gathered = lax.all_gather(mine, "shard", axis=0, tiled=True)
    qkv_cols = query_cols + 2 * HEAD_SIZE
    wqkv = gathered[:, :qkv_cols]
    router_full = gathered[:, qkv_cols : qkv_cols + experts_all]
    gain_cols = gathered[:, qkv_cols + experts_all :].astype(FULL)
    gain_one, gain_two = gain_cols[:, 0], gain_cols[:, 1]
    per = query_gain.shape[0]
    by_plane = gain_cols.reshape(planes, rows_in, -1)[:, :per]
    gain_query = by_plane[:, :, 2].reshape(-1)
    gain_key = by_plane[:, :, 3].reshape(-1)

    segment_row = segments[0]
    token_tail = columns(
        [segment_row[:, None], positions_of(segment_row)[:, None]], length
    )
    plane_rows = lax.all_gather(
        jnp.concatenate([tokens, token_tail], axis=1), "expert", axis=0, tiled=False
    )
    plane_tokens = plane_rows[:, :, :MODEL_WIDTH].astype(FULL)
    plane_segments = plane_rows[:, :, MODEL_WIDTH]
    plane_places = plane_rows[:, :, MODEL_WIDTH + 1].astype(FULL)

    out_rows = w_out.shape[0]
    first = me * query_cols
    offset = first - plane * out_rows
    if out_rows >= query_cols:
        held = (offset >= 0) & (offset < out_rows)
        piece = lax.dynamic_slice_in_dim(w_out, jnp.where(held, offset, 0), query_cols, 0)
        w_mine = lax.psum(jnp.where(held, piece, 0).astype(LOW), "shard")
    else:
        parts = query_cols // out_rows
        at = plane - me * parts
        held = (at >= 0) & (at < parts)
        spread = jnp.where(held & (jnp.arange(parts) == at)[:, None, None], w_out[None], 0)
        w_mine = lax.psum(spread.astype(LOW), "shard").reshape(query_cols, MODEL_WIDTH)

    d_tail = columns([routes], length)
    d_all = lax.all_gather(
        jnp.concatenate([d_out, d_tail], axis=1), both, axis=0, tiled=False
    )

    unit_plane, inverse_plane = unit_norm(plane_tokens)
    h1 = (unit_plane * gain_one).astype(LOW)
    projected = dot("bqd,df->bqf", h1, wqkv)
    half = HEAD_SIZE // 2
    frequency = THETA ** (-2.0 * jnp.arange(half, dtype=FULL) / HEAD_SIZE)
    angles = plane_places[:, :, None] * frequency
    cosine, sine = jnp.cos(angles), jnp.sin(angles)
    cosine_q, sine_q = cosine[:, :, None, :], sine[:, :, None, :]
    query_raw = projected[:, :, :query_cols].reshape(owners, length, heads, HEAD_SIZE)
    key_raw = projected[:, :, query_cols : query_cols + HEAD_SIZE]
    value = projected[:, :, query_cols + HEAD_SIZE :].astype(LOW)
    query_unit, query_inverse = unit_norm(query_raw)
    key_unit, key_inverse = unit_norm(key_raw)
    query = rotate(query_unit * gain_query, cosine_q, sine_q).astype(LOW)
    key = rotate(key_unit * gain_key, cosine, sine).astype(LOW)
    places = jnp.arange(length, dtype=jnp.int32)
    allowed = (plane_segments[:, :, None] == plane_segments[:, None, :]) & (
        places[None, :] <= places[:, None]
    )
    scores = dot("bqhd,bkd->bhqk", query, key) * scaling
    scores = jnp.where(allowed[:, None], scores, -1e30)
    highest = jnp.max(scores, axis=-1, keepdims=True)
    exponent = jnp.exp(scores - highest)
    probs = exponent / jnp.sum(exponent, axis=-1, keepdims=True)
    probs_low = probs.astype(LOW)
    mixed = dot("bhqk,bkd->bqhd", probs_low, value).astype(LOW)
    mixed = mixed.reshape(owners, length, query_cols)
    partial = dot("bqf,fd->bqd", mixed, w_mine).astype(LOW)
    branch = lax.psum_scatter(partial, "expert", scatter_dimension=0, tiled=False)

    middle = tokens.astype(FULL) + branch.astype(FULL)
    unit_two, inverse_two = unit_norm(middle)
    h2 = (unit_two * gain_two).astype(LOW)
    logits = dot("nd,de->ne", h2, router_full)
    chance = jax.nn.softmax(logits, axis=-1)
    named = jnp.sum(
        (routes[:, :, None] == jnp.arange(experts_all, dtype=jnp.int32)).astype(FULL), axis=1
    )
    chosen_sum = jnp.sum(named * chance, axis=1, keepdims=True)
    gates = named * chance / chosen_sum
    gates_high = gates.astype(LOW)
    gates_rest = (gates - gates_high.astype(FULL)).astype(LOW)
    h_all = lax.all_gather(
        jnp.concatenate([h2, gates_high, gates_rest], axis=1), both, axis=0, tiled=False
    )

    route_all = d_all[:, :, MODEL_WIDTH : MODEL_WIDTH + TOPK].astype(FULL)
    own_experts = (me * EXP_DEV + jnp.arange(EXP_DEV, dtype=jnp.int32)).astype(FULL)
    match = jnp.sum((route_all[:, :, :, None] == own_experts).astype(FULL), axis=2)
    earlier = (places[None, :] < places[:, None]).astype(LOW)
    rank = dot("ts,bsj->btj", earlier, match.astype(LOW))
    slot_ids = jnp.arange(capacity, dtype=jnp.int32).astype(FULL)
    place = jnp.where(match > 0, rank, -1.0).transpose(0, 2, 1)
    dispatch = (place[:, :, None, :] == slot_ids[:, None]).astype(LOW)

    def experts(h_rows, d_rows, gate_high, gate_rest, put):
        count = h_rows.shape[0]
        flat = put.reshape(count, EXP_DEV * capacity, length)
        x = dot("bst,btd->bsd", flat, h_rows).astype(LOW)
        dy = dot("bst,btd->bsd", flat, d_rows).astype(LOW)

        def by_expert(v):
            v = v.reshape(count, EXP_DEV, capacity, v.shape[-1])
            return v.transpose(1, 0, 2, 3).reshape(EXP_DEV, count * capacity, v.shape[-1])

        def by_block(v):
            v = v.reshape(EXP_DEV, count, capacity, v.shape[-1])
            return v.transpose(1, 0, 2, 3).reshape(count, EXP_DEV * capacity, v.shape[-1])

        x, dy = by_expert(x), by_expert(dy)
        gate_slot = dot("bjct,btj->jbc", put, gate_high) + dot("bjct,btj->jbc", put, gate_rest)
        gate_slot = gate_slot.reshape(EXP_DEV, count * capacity, 1)
        g = dot("erd,efd->erf", x, w_gate)
        u = dot("erd,efd->erf", x, w_up)
        da = dot("erd,edf->erf", dy, w_down)
        sigma = jax.nn.sigmoid(g)
        silu = g * sigma
        act = (silu * u).astype(LOW).astype(FULL)
        d_gate_slot = jnp.sum(act * da, axis=-1)
        act_gated = (act * gate_slot).astype(LOW)
        d_act = da * gate_slot
        dg = (d_act * u * sigma * (1.0 + g * (1.0 - sigma))).astype(LOW)
        du = (d_act * silu).astype(LOW)
        y = dot("erf,edf->erd", act_gated, w_down).astype(LOW)
        d_down = dot("erd,erf->edf", dy, act_gated)
        d_gate = dot("erf,erd->efd", dg, x)
        d_up = dot("erf,erd->efd", du, x)
        dx = (dot("erf,efd->erd", dg, w_gate) + dot("erf,efd->erd", du, w_up)).astype(LOW)
        mix = dot("bst,bsd->btd", flat, by_block(y)).astype(LOW)
        d_h = dot("bst,bsd->btd", flat, by_block(dx)).astype(LOW)
        d_g = dot(
            "bjct,jbc->btj", put.astype(FULL), d_gate_slot.reshape(EXP_DEV, count, capacity)
        )
        return mix, d_h, d_g, d_gate, d_up, d_down

    gate_cols = lax.dynamic_slice_in_dim(h_all, MODEL_WIDTH + me * EXP_DEV, EXP_DEV, 2)
    rest_cols = lax.dynamic_slice_in_dim(
        h_all, MODEL_WIDTH + experts_all + me * EXP_DEV, EXP_DEV, 2
    )
    step = min(blocks, GROUP_BLOCKS)
    mixes, d_hs, d_gs, totals = [], [], [], None
    for at in range(0, blocks, step):
        cut = slice(at, at + step)
        mix, d_h, d_g, *grads = experts(
            h_all[cut, :, :MODEL_WIDTH],
            d_all[cut, :, :MODEL_WIDTH],
            gate_cols[cut],
            rest_cols[cut],
            dispatch[cut],
        )
        mixes.append(mix)
        d_hs.append(d_h)
        d_gs.append(d_g)
        totals = grads if totals is None else [a + b for a, b in zip(totals, grads)]
    d_gate, d_up, d_down = totals
    d_g = jnp.concatenate(d_gs, axis=0)
    spread = jnp.zeros((blocks, length, TAIL), LOW)
    spread = lax.dynamic_update_slice_in_dim(spread, d_g.astype(LOW), me * EXP_DEV, 2)
    d_h_wide = jnp.concatenate([jnp.concatenate(d_hs, axis=0), spread], axis=2)

    def home(v):
        v = v.reshape(owners, planes, length, v.shape[-1])
        v = lax.psum_scatter(v, "expert", scatter_dimension=0, tiled=False)
        return lax.psum_scatter(v, "shard", scatter_dimension=0, tiled=False)

    d_home = home(d_h_wide)
    mixture = home(jnp.concatenate(mixes, axis=0))
    result = (middle + mixture.astype(FULL)).astype(LOW)

    upstream = d_out.astype(FULL)
    d_gates = d_home[:, MODEL_WIDTH : MODEL_WIDTH + experts_all].astype(FULL)
    d_chance = named * (d_gates - jnp.sum(d_gates * gates, axis=1, keepdims=True)) / chosen_sum
    d_logits = chance * (d_chance - jnp.sum(d_chance * chance, axis=1, keepdims=True))
    d_logits = d_logits.astype(LOW)
    d_h2 = d_home[:, :MODEL_WIDTH].astype(FULL) + dot("ne,de->nd", d_logits, router_full)
    d_gain_two = jnp.sum(d_h2 * unit_two, axis=0)
    d_middle = upstream + norm_back(d_h2, unit_two, inverse_two, gain_two)
    d_router = dot("nd,ne->de", h2, d_logits)

    d_branch = lax.all_gather(d_middle.astype(LOW), "expert", axis=0, tiled=False)
    d_w_out = dot("bqf,bqd->fd", mixed, d_branch).astype(LOW)
    d_mixed = dot("bqd,fd->bqf", d_branch, w_mine).astype(LOW)
    d_mixed = d_mixed.reshape(owners, length, heads, HEAD_SIZE)
    d_probs = dot("bqhd,bkd->bhqk", d_mixed, value)
    d_scores = probs * (d_probs - jnp.sum(d_probs * probs, axis=-1, keepdims=True))
    d_scores = d_scores.astype(LOW)
    d_query = dot("bhqk,bkd->bqhd", d_scores, key) * scaling
    d_key = dot("bhqk,bqhd->bkd", d_scores, query) * scaling
    d_value = dot("bhqk,bqhd->bkd", probs_low, d_mixed)
    d_query = rotate_back(d_query, cosine_q, sine_q)
    d_key = rotate_back(d_key, cosine, sine)
    d_gain_query = jnp.sum(d_query * query_unit, axis=(0, 1, 2))
    d_gain_key = jnp.sum(d_key * key_unit, axis=(0, 1))
    d_query = norm_back(d_query, query_unit, query_inverse, gain_query)
    d_key = norm_back(d_key, key_unit, key_inverse, gain_key)
    d_projected = jnp.concatenate(
        [d_query.reshape(owners, length, query_cols), d_key, d_value], axis=2
    ).astype(LOW)
    d_h1_part = dot("bqf,df->bqd", d_projected, wqkv).astype(LOW)
    d_h1 = lax.psum_scatter(d_h1_part, "expert", scatter_dimension=0, tiled=False).astype(FULL)
    resident = tokens.astype(FULL)
    unit_one, inverse_one = unit_norm(resident)
    d_gain_one = jnp.sum(d_h1 * unit_one, axis=0)
    d_tokens = (d_middle + norm_back(d_h1, unit_one, inverse_one, gain_one)).astype(LOW)

    d_wqkv = dot("bqd,bqf->df", h1, d_projected).astype(LOW)

    def by_rows(v):
        v = v.reshape(planes, per)
        return jnp.pad(v, ((0, 0), (0, rows_in - per))).reshape(-1)[:, None]

    d_tail = columns(
        [
            d_router,
            d_gain_one[:, None],
            d_gain_two[:, None],
            by_rows(d_gain_query),
            by_rows(d_gain_key),
        ],
        MODEL_WIDTH,
    )
    d_pack = lax.psum_scatter(
        jnp.concatenate([d_wqkv, d_tail], axis=1), "shard", scatter_dimension=0, tiled=True
    )
    d_pack = lax.all_gather(d_pack, "expert", axis=0, tiled=False).astype(FULL)
    d_q_cols = d_pack[:, :, :query_cols].transpose(1, 0, 2).reshape(rows_in, -1)
    d_kv = d_pack[:, :, query_cols:qkv_cols]
    d_kv = jnp.sum(d_kv.reshape(KEY_VALUE_HEADS, -1, rows_in, 2, HEAD_SIZE), axis=1)
    d_kv = d_kv.transpose(1, 2, 0, 3).reshape(rows_in, -1)
    d_qkv_weight = jnp.concatenate([d_q_cols, d_kv], axis=1)
    d_rest = jnp.sum(d_pack[:, :, qkv_cols:], axis=0)
    d_router_out = d_rest[:, :experts_all]
    d_gain_out = d_rest[:, experts_all:]

    d_w_out = d_w_out.reshape(query_cols, owners, -1)
    d_w_out = lax.all_to_all(d_w_out, "expert", split_axis=1, concat_axis=0, tiled=False)
    d_w_out = d_w_out.reshape(QUERY_HEADS * HEAD_SIZE, -1)
    d_w_out = lax.psum_scatter(d_w_out, "shard", scatter_dimension=0, tiled=True)
    d_w_out = lax.all_gather(d_w_out, "expert", axis=1, tiled=True).astype(FULL)

    return (
        result,
        d_tokens,
        d_gain_out[:, 0],
        d_qkv_weight,
        d_gain_out[:per, 2],
        d_gain_out[:per, 3],
        d_w_out,
        d_gain_out[:, 1],
        d_router_out,
        d_gate,
        d_up,
        d_down,
    )


def resident_layer(
    tokens,
    segments,
    routes,
    attn_gain,
    qkv_weight,
    query_gain,
    k_gain,
    w_out,
    ffn_gain,
    router,
    w_gate,
    w_up,
    w_down,
    d_out,
):
    owners = lax.axis_size("expert")
    planes = lax.axis_size("shard")
    me = lax.axis_index("expert")
    plane = lax.axis_index("shard")
    length = tokens.shape[0]
    blocks = owners * planes
    experts_all = router.shape[1]
    capacity = 3 * length * TOPK // (2 * experts_all)
    slots = 2 * capacity
    heads = QUERY_HEADS // owners
    query_cols = heads * HEAD_SIZE
    scaling = HEAD_SIZE ** (-0.5)
    rows_in = qkv_weight.shape[0]
    per = query_gain.shape[0]

    router_rows = rows_in // owners
    router_part = lax.dynamic_slice_in_dim(router, me * router_rows, router_rows, 0)
    router_part = columns([router_part], router_rows)
    gain_rows = [attn_gain, ffn_gain]
    gain_rows += [jnp.pad(gain, (0, rows_in - per)) for gain in (query_gain, k_gain)]
    gain_rows = jnp.pad(jnp.stack(gain_rows), ((0, 12), (0, 0)))
    segment_row = segments[0]
    token_tail = columns([segment_row[:, None], positions_of(segment_row)[:, None]], length)
    token_rows = jnp.concatenate([tokens, token_tail], axis=1)
    d_rows = jnp.concatenate([d_out, columns([routes], length)], axis=1)
    half = HEAD_SIZE // 2
    frequency = THETA ** (-2.0 * jnp.arange(half, dtype=FULL) / HEAD_SIZE)
    frequency = jnp.broadcast_to(jnp.tile(frequency, 2)[None, :], (8, HEAD_SIZE))
    d_all, w_mine, w_all, router_all, gain_all, tail, h1, projected, probs_low, mixed, branch = front(
        qkv_weight, router_part, gain_rows, token_rows, w_out, d_rows, frequency, planes, owners, 5
    )
    gains = gain_all.astype(FULL)
    gain_one, gain_two = gains[:, 0].reshape(-1), gains[:, 1].reshape(-1)
    router_full = router_all.transpose(1, 0, 2, 3).reshape(MODEL_WIDTH, -1)[:, :experts_all]

    lanes = jnp.arange(2 * experts_all, dtype=jnp.int32) % experts_all
    own = (me * EXP_DEV + jnp.arange(EXP_DEV, dtype=jnp.int32))[:, None] == lanes
    sel = jnp.broadcast_to(own.astype(FULL)[:, None, :], (EXP_DEV, 8, 2 * experts_all))

    middle = tokens.astype(FULL) + branch
    unit_two, inverse_two = unit_norm(middle)
    h2 = (unit_two * gain_two).astype(LOW)
    logits = dot("nd,de->ne", h2, router_full)
    chance = jax.nn.softmax(logits, axis=-1)
    named = jnp.sum(
        (routes[:, :, None] == jnp.arange(experts_all, dtype=jnp.int32)).astype(FULL), axis=1
    )
    chosen_sum = jnp.sum(named * chance, axis=1, keepdims=True)
    gates = named * chance / chosen_sum
    gates_high = gates.astype(LOW)
    gates_rest = (gates - gates_high.astype(FULL)).astype(LOW)
    h_rows = jnp.concatenate([h2, gates_high, gates_rest], axis=1)

    x, dy, hot = gather_dispatch(h_rows, d_all, planes, slots, 1)
    y, dx, d_gate, d_up, d_down = expert_pass(sel, x, dy, w_gate, w_up, w_down.swapaxes(1, 2))
    d_down = d_down.swapaxes(1, 2)
    d_home, mixture = combine_home(hot, dx, y, length, planes, slots, 2)

    upstream = d_out.astype(FULL)
    d_gates = d_home[:, MODEL_WIDTH:]
    d_gates = d_gates[:, :experts_all] + d_gates[:, experts_all:]
    d_chance = named * (d_gates - jnp.sum(d_gates * gates, axis=1, keepdims=True)) / chosen_sum
    d_logits = chance * (d_chance - jnp.sum(d_chance * chance, axis=1, keepdims=True))
    d_logits = d_logits.astype(LOW)
    d_h2 = d_home[:, :MODEL_WIDTH] + dot("ne,de->nd", d_logits, router_full)
    d_gain_two = jnp.sum(d_h2 * unit_two, axis=0, keepdims=True)
    d_middle = upstream + norm_back(d_h2, unit_two, inverse_two, gain_two)

    *parts, d_h1 = back(
        d_middle.astype(LOW), w_mine, mixed, projected, probs_low, tail, gain_all, frequency, h1,
        w_all, tokens, h2, columns([d_logits], length), d_gain_two, planes, owners, 4,
    )
    d_w_out, d_qkv_weight, d_router, d_gains, result, d_tokens = finish_grads(
        *parts, tokens, middle, mixture, d_middle, d_h1, gain_one[None], owners
    )
    return (
        result,
        d_tokens,
        d_gains[GAIN_ONE - experts_all],
        d_qkv_weight,
        lax.dynamic_slice_in_dim(d_gains[GAIN_QUERY - experts_all], plane * per, per, 0),
        lax.dynamic_slice_in_dim(d_gains[GAIN_KEY - experts_all], plane * per, per, 0),
        d_w_out,
        d_gains[0],
        d_router,
        d_gate,
        d_up,
        d_down,
    )


def per_device(*args):
    blocks = lax.axis_size("expert") * lax.axis_size("shard")
    row_bytes = 2 * (MODEL_WIDTH + TAIL)
    if blocks * args[0].shape[0] * row_bytes <= RESIDENT:
        return resident_layer(*args)
    return gathered_layer(*args)


def solution(mesh):
    placed = (
        P(("expert", "shard"), None),
        P(("expert", "shard"), None),
        P(("expert", "shard"), None),
        P("shard"),
        P("shard", None),
        P("shard"),
        P("shard"),
        P("shard", None),
        P("shard"),
        P("shard", None),
        P("expert", "shard", None),
        P("expert", "shard", None),
        P("expert", None, "shard"),
        P(("expert", "shard"), None),
    )
    return jax.shard_map(
        per_device,
        mesh=mesh,
        in_specs=placed,
        out_specs=(
            P(("expert", "shard"), None),
            P(("expert", "shard"), None),
            P("shard"),
            P("shard", None),
            P("shard"),
            P("shard"),
            P("shard", None),
            P("shard"),
            P("shard", None),
            P("expert", "shard", None),
            P("expert", "shard", None),
            P("expert", None, "shard"),
        ),
        check_vma=False,
    )
```

```python
import functools

import jax
import jax.numpy as jnp
import numpy as np
from jax import lax
from jax.experimental import pallas as pl
from jax.experimental.pallas import tpu as pltpu
from jax.sharding import PartitionSpec as P

MODEL_WIDTH = 2048
QUERY_HEADS = 32
KEY_VALUE_HEADS = 4
HEAD_SIZE = 128
TOPK = 8
EXP_DEV = 8
TAIL = 128
GAIN_TWO, GAIN_QUERY, GAIN_KEY, GAIN_ONE = 64, 65, 66, 67
GROUP_BLOCKS = 32
RESIDENT = 20 << 20

EPS = 1e-06
THETA = 1000000.0
LOW = jnp.bfloat16
FULL = jnp.float32


def unit_norm(values):
    inverse = lax.rsqrt(jnp.mean(values * values, axis=-1, keepdims=True) + EPS)
    return values * inverse, inverse


def norm_back(incoming, unit_rows, inverse, gain):
    inner = incoming * gain
    return inverse * (inner - unit_rows * jnp.mean(inner * unit_rows, axis=-1, keepdims=True))


def rotate(values, cosine, sine):
    half = values.shape[-1] // 2
    a, b = values[..., :half], values[..., half:]
    return jnp.concatenate([a * cosine - b * sine, b * cosine + a * sine], axis=-1)


def rotate_back(values, cosine, sine):
    half = values.shape[-1] // 2
    a, b = values[..., :half], values[..., half:]
    return jnp.concatenate([a * cosine + b * sine, b * cosine - a * sine], axis=-1)


def dot(spec, left, right):
    return jnp.einsum(spec, left, right, preferred_element_type=FULL)


def positions_of(segment_row):
    places = jnp.arange(segment_row.shape[0], dtype=jnp.int32)
    before = (segment_row[None, :] == segment_row[:, None]) & (places[None, :] < places[:, None])
    return jnp.sum(before.astype(jnp.int32), axis=1)


def columns(parts, rows):
    wide = jnp.concatenate([part.astype(LOW) for part in parts], axis=1)
    return jnp.pad(wide, ((0, rows - wide.shape[0]), (0, TAIL - wide.shape[1])))


MESH = pl.DeviceIdType.MESH
ANY = pl.BlockSpec(memory_space=pl.ANY)
VM = pl.BlockSpec(memory_space=pltpu.VMEM)
DMA = pltpu.SemaphoreType.DMA
VMEM_LIMIT = 58 << 20
TILE = 512


def neighbours():
    e = lax.axis_index("expert")
    core = e + 1 - 2 * (e % 2)
    flip_x = e + 2 - 4 * ((e // 2) % 2)
    flip_y = e + 4 - 8 * ((e // 4) % 2)
    diagonal = flip_x + flip_y - e
    return e, core, flip_x, flip_y, diagonal


def greet(planes):
    e, core, flip_x, flip_y, _ = neighbours()
    s = lax.axis_index("shard")
    barrier = pltpu.get_barrier_semaphore()
    for other in (core, flip_x, flip_y):
        pl.semaphore_signal(barrier, 1, device_id=(other, s), device_id_type=MESH)

    @pl.when(s > 0)
    def _():
        pl.semaphore_signal(barrier, 1, device_id=(e, s - 1), device_id_type=MESH)

    @pl.when(s < planes - 1)
    def _():
        pl.semaphore_signal(barrier, 1, device_id=(e, s + 1), device_id_type=MESH)

    inner = (s > 0) & (s < planes - 1)

    @pl.when(inner)
    def _():
        pl.semaphore_wait(barrier, 5)

    @pl.when(jnp.logical_not(inner))
    def _():
        pl.semaphore_wait(barrier, 4)


def send(source, target, send_sem, recv_sem, device):
    return pltpu.make_async_remote_copy(
        src_ref=source,
        dst_ref=target,
        send_sem=send_sem,
        recv_sem=recv_sem,
        device_id=device,
        device_id_type=MESH,
    )


def gather_dispatch_kernel(
    planes, slots, x_ref, d_ref, outx_ref, outd_ref, outh_ref,
    buf, hot, place, stage_x, stage_d, stage_h, load_d,
    z_send, z_recv, x_send, x_recv, y_send, y_recv, c_send, c_recv, out_x, out_d, out_h, in_d,
):
    e, core, flip_x, flip_y, diagonal = neighbours()
    s = lax.axis_index("shard")
    length = x_ref.shape[0]
    half = length // 2
    width = x_ref.shape[1]
    low_half, high_half = pl.ds(0, half), pl.ds(half, half)
    greet(planes)
    buf[e, s] = x_ref[...]

    def up(sp):
        return send(buf.at[e, sp], buf.at[e, sp], z_send.at[0, sp], z_recv.at[sp], (e, s + 1))

    def down(sp):
        return send(buf.at[e, sp], buf.at[e, sp], z_send.at[1, sp], z_recv.at[sp], (e, s - 1))

    def first(sp):
        block = buf.at[e, sp]
        return [
            send(block, block, x_send.at[0, sp], x_recv.at[0, sp], (flip_x, s)),
            send(block, block, y_send.at[0, sp], y_recv.at[0, sp], (flip_y, s)),
            send(block, block, c_send.at[0, sp], c_recv.at[0, sp], (core, s)),
        ]

    def from_x(sp):
        block = buf.at[flip_x, sp]
        part = buf.at[flip_x, sp, low_half]
        return [
            send(part, part, y_send.at[1, sp], y_recv.at[1, sp], (flip_y, s)),
            send(block, block, c_send.at[1, sp], c_recv.at[1, sp], (core, s)),
        ]

    def from_y(sp):
        block = buf.at[flip_y, sp]
        part = buf.at[flip_y, sp, high_half]
        return [
            send(part, part, x_send.at[1, sp], x_recv.at[1, sp], (flip_x, s)),
            send(block, block, c_send.at[2, sp], c_recv.at[2, sp], (core, s)),
        ]

    def from_diagonal(sp):
        block = buf.at[diagonal, sp]
        return send(block, block, c_send.at[3, sp], c_recv.at[3, sp], (core, s))

    def arrived(block, sem):
        send(block, block, sem, sem, (core, s)).wait_recv()

    def plane_at(i):
        distance = (i + 1) // 2
        sign = 2 * (i % 2) - 1
        sp = s + sign * distance
        return sp, (sp >= 0) & (sp < planes) & (i >= 0) & (i <= 2 * planes - 2)

    def step_first(sp, i):
        @pl.when(i > 0)
        def _():
            arrived(buf.at[e, sp], z_recv.at[sp])

        @pl.when((sp <= s) & (s < planes - 1))
        def _():
            up(sp).start()

        @pl.when((sp >= s) & (s > 0))
        def _():
            down(sp).start()

        for copy in first(sp):
            copy.start()

    def step_second(sp):
        arrived(buf.at[flip_x, sp], x_recv.at[0, sp])
        for copy in from_x(sp):
            copy.start()
        arrived(buf.at[flip_y, sp], y_recv.at[0, sp])
        for copy in from_y(sp):
            copy.start()

    def step_third(sp):
        arrived(buf.at[diagonal, sp, low_half], y_recv.at[1, sp])
        arrived(buf.at[diagonal, sp, high_half], x_recv.at[1, sp])
        from_diagonal(sp).start()

    def copy_out(stage, out, sem, q, sp):
        rows = pl.ds(pl.multiple_of((q * planes + sp) * slots, 16), slots)
        return pltpu.make_async_copy(stage.at[q], out.at[:, rows, :], sem.at[q])

    def load(q, sp, k):
        return pltpu.make_async_copy(
            d_ref.at[2 * q + k, sp],
            load_d.at[q, pl.ds(k * length, length), :],
            in_d.at[q, k],
        )

    def start_loads(sp):
        for q in range(4):
            for k in range(2):
                load(q, sp, k).start()

    def copy_hot(q, sp):
        return pltpu.make_async_copy(
            stage_h.at[q], outh_ref.at[q * planes + sp], out_h.at[q]
        )

    row = lax.broadcasted_iota(jnp.int32, (length, length), 0)
    earlier = (lax.broadcasted_iota(jnp.int32, (length, length), 1) < row).astype(LOW)
    lane = lax.broadcasted_iota(jnp.int32, (2 * length, TAIL), 1).astype(FULL)
    slot = lax.broadcasted_iota(jnp.int32, (slots, 2 * length), 0).astype(FULL)

    def one_hot(q, sp):
        routes = load_d[q, :, MODEL_WIDTH:].astype(FULL)
        named = (routes[:, 0:1] == lane).astype(FULL)
        for k in range(1, TOPK):
            named = named + (routes[:, k : k + 1] == lane).astype(FULL)
        for k in range(2):
            here = slice(k * length, (k + 1) * length)
            rank = jnp.dot(earlier, named[here].astype(LOW), preferred_element_type=FULL)
            rank = jnp.where(named[here] > 0, rank + k * (slots // 2), -1.0)
            place[:, here] = rank.T
        rows = place[pl.ds(pl.multiple_of(e * EXP_DEV, EXP_DEV), EXP_DEV), :]
        for j in range(EXP_DEV):
            hot[q, sp, pl.ds(j * slots, slots), :] = (slot == rows[j : j + 1, :]).astype(LOW)

    def dispatch_d(sp, i):
        def one(q, carry):
            @pl.when(i > 0)
            def _():
                copy_out(stage_d, outd_ref, out_d, q, sp).wait()
                copy_hot(q, sp).wait()

            for k in range(2):
                load(q, sp, k).wait()
            one_hot(q, sp)
            stage_h[q] = hot[q, sp].T
            copy_hot(q, sp).start()

            def tile(t, inner):
                at = pl.ds(pl.multiple_of(t * TILE, TILE), TILE)
                got = jnp.dot(
                    hot[q, sp], load_d[q, :, at], preferred_element_type=FULL
                ).astype(LOW)
                stage_d[q, :, :, at] = got.reshape(EXP_DEV, slots, TILE)
                return inner

            lax.fori_loop(0, MODEL_WIDTH // TILE, tile, 0)
            copy_out(stage_d, outd_ref, out_d, q, sp).start()
            return carry

        lax.fori_loop(0, 4, one, 0)

    def dispatch(sp, i):
        for k, other in enumerate((core, core + flip_x - e, core + flip_y - e, core + diagonal - e)):
            arrived(buf.at[other, sp], c_recv.at[k, sp])

        def one(q, carry):
            @pl.when(i > 0)
            def _():
                copy_out(stage_x, outx_ref, out_x, q, sp).wait()

            def columns_of(at, wide):
                rows = jnp.concatenate(
                    [buf[2 * q, sp, :, at], buf[2 * q + 1, sp, :, at]], axis=0
                )
                got = jnp.dot(hot[q, sp], rows, preferred_element_type=FULL).astype(LOW)
                stage_x[q, :, :, at] = got.reshape(EXP_DEV, slots, wide)

            def tile(t, inner):
                columns_of(pl.ds(pl.multiple_of(t * TILE, TILE), TILE), TILE)
                return inner

            lax.fori_loop(0, MODEL_WIDTH // TILE, tile, 0)
            if width > MODEL_WIDTH:
                columns_of(pl.ds(MODEL_WIDTH, width - MODEL_WIDTH), width - MODEL_WIDTH)
            copy_out(stage_x, outx_ref, out_x, q, sp).start()
            return carry

        lax.fori_loop(0, 4, one, 0)

    def step(i, carry):
        for lag, work in ((0, step_first), (2, step_second), (4, step_third), (0, dispatch_d), (5, dispatch)):
            sp, there = plane_at(i - lag)

            @pl.when(there)
            def _(sp=sp, lag=lag, work=work):
                if work in (step_second, step_third):
                    work(sp)
                else:
                    work(sp, i - lag)

        sp, there = plane_at(i + 1)

        @pl.when(there)
        def _():
            start_loads(sp)

        return carry

    start_loads(s)
    lax.fori_loop(0, 2 * planes + 4, step, 0)

    def drain(sp, carry):
        for copy in first(sp) + from_x(sp) + from_y(sp) + [from_diagonal(sp)]:
            copy.wait_send()

        @pl.when((sp <= s) & (s < planes - 1))
        def _():
            up(sp).wait_send()

        @pl.when((sp >= s) & (s > 0))
        def _():
            down(sp).wait_send()

        return carry

    lax.fori_loop(0, planes, drain, 0)
    for q in range(4):
        copy_out(stage_x, outx_ref, out_x, q, 0).wait()
        copy_out(stage_d, outd_ref, out_d, q, 0).wait()
        copy_hot(q, 0).wait()


def gather_dispatch(rows, d_all, planes, slots, identity):
    owners = lax.axis_size("expert")
    length, width = rows.shape
    pairs = owners * planes // 2
    total = pairs * slots
    kernel = functools.partial(gather_dispatch_kernel, planes, slots)
    return pl.pallas_call(
        kernel,
        out_shape=[
            jax.ShapeDtypeStruct((EXP_DEV, total, width), LOW),
            jax.ShapeDtypeStruct((EXP_DEV, total, MODEL_WIDTH), LOW),
            jax.ShapeDtypeStruct((pairs, 2 * length, EXP_DEV * slots), LOW),
        ],
        in_specs=[VM, ANY],
        out_specs=[ANY, ANY, ANY],
        scratch_shapes=[
            pltpu.VMEM((owners, planes, length, width), LOW),
            pltpu.VMEM((4, planes, EXP_DEV * slots, 2 * length), LOW),
            pltpu.VMEM((TAIL, 2 * length), FULL),
            pltpu.VMEM((4, EXP_DEV, slots, width), LOW),
            pltpu.VMEM((4, EXP_DEV, slots, MODEL_WIDTH), LOW),
            pltpu.VMEM((4, 2 * length, EXP_DEV * slots), LOW),
            pltpu.VMEM((4, 2 * length, MODEL_WIDTH + TAIL), LOW),
            DMA((2, planes)),
            DMA((planes,)),
            DMA((2, planes)),
            DMA((2, planes)),
            DMA((2, planes)),
            DMA((2, planes)),
            DMA((4, planes)),
            DMA((4, planes)),
            DMA((4,)),
            DMA((4,)),
            DMA((4,)),
            DMA((4, 2)),
        ],
        compiler_params=pltpu.CompilerParams(
            collective_id=identity, has_side_effects=True, vmem_limit_bytes=VMEM_LIMIT
        ),
    )(rows, d_all)


def expert_kernel(
    sel_ref, x_ref, dy_ref, wg_ref, wu_ref, wd_ref,
    y_ref, dx_ref, dwg_ref, dwu_ref, dwd_ref, a_all, dg_all, du_all, a_t, d_t,
):
    rows = x_ref.shape[1]
    step = rows
    experts = sel_ref.shape[2] // 2
    sel = sel_ref[0, 0:1, :]
    lane = lax.broadcasted_iota(jnp.int32, sel.shape, 1)
    high_sel = jnp.where(lane < experts, sel, 0.0)
    rest_sel = sel - high_sel
    nt = (((1,), (1,)), ((), ()))

    def chunk(r, carry):
        at = pl.ds(pl.multiple_of(r * step, step), step)
        x = x_ref[0, at, :MODEL_WIDTH]
        tail = x_ref[0, at, MODEL_WIDTH:].astype(FULL)
        dy = dy_ref[0, at, :]
        gate = jnp.sum(tail * sel, axis=1, keepdims=True)
        g = lax.dot_general(x, wg_ref[0], nt, preferred_element_type=FULL)
        u = lax.dot_general(x, wu_ref[0], nt, preferred_element_type=FULL)
        da = lax.dot_general(dy, wd_ref[0], nt, preferred_element_type=FULL)
        sigma = 1.0 / (1.0 + jnp.exp(-g))
        silu = g * sigma
        act = (silu * u).astype(LOW).astype(FULL)
        d_gate = jnp.sum(act * da, axis=1, keepdims=True)
        d_act = da * gate
        a_all[at, :] = (act * gate).astype(LOW)
        dg_all[at, :] = (d_act * u * sigma * (1.0 + g * (1.0 - sigma))).astype(LOW)
        du_all[at, :] = (d_act * silu).astype(LOW)
        high = d_gate.astype(LOW).astype(FULL)
        dx_ref[0, at, MODEL_WIDTH:] = (high * high_sel + (d_gate - high) * rest_sel).astype(LOW)
        y_ref[0, at, :] = jnp.dot(
            a_all[at, :], wd_ref[0], preferred_element_type=FULL
        ).astype(LOW)
        dx_ref[0, at, :MODEL_WIDTH] = (
            jnp.dot(dg_all[at, :], wg_ref[0], preferred_element_type=FULL)
            + jnp.dot(du_all[at, :], wu_ref[0], preferred_element_type=FULL)
        ).astype(LOW)
        return carry

    lax.fori_loop(0, rows // step, chunk, 0)
    hidden = a_t.shape[0]
    a_t[...] = a_all[...].T
    d_t[:hidden, :] = dg_all[...].T
    d_t[hidden:, :] = du_all[...].T

    def tile(t, carry):
        at = pl.ds(pl.multiple_of(t * TILE, TILE), TILE)
        x = x_ref[0, :, at]
        got = jnp.dot(d_t[...], x, preferred_element_type=FULL)
        dwg_ref[0, :, at] = got[:hidden]
        dwu_ref[0, :, at] = got[hidden:]
        dwd_ref[0, :, at] = jnp.dot(a_t[...], dy_ref[0, :, at], preferred_element_type=FULL)
        return carry

    lax.fori_loop(0, MODEL_WIDTH // TILE, tile, 0)


def expert_pass(sel, x, dy, w_gate, w_up, w_down):
    rows, width = x.shape[1:]
    hidden = w_gate.shape[1]

    def spec(*shape):
        return pl.BlockSpec((1,) + shape, lambda j: (j, 0, 0))

    def out(*shape, dtype=LOW):
        return jax.ShapeDtypeStruct((EXP_DEV,) + shape, dtype)

    return pl.pallas_call(
        expert_kernel,
        grid=(EXP_DEV,),
        in_specs=[
            spec(*sel.shape[1:]),
            spec(rows, width),
            spec(rows, MODEL_WIDTH),
            spec(hidden, MODEL_WIDTH),
            spec(hidden, MODEL_WIDTH),
            spec(hidden, MODEL_WIDTH),
        ],
        out_specs=[
            spec(rows, MODEL_WIDTH),
            spec(rows, width),
            spec(hidden, MODEL_WIDTH),
            spec(hidden, MODEL_WIDTH),
            spec(hidden, MODEL_WIDTH),
        ],
        out_shape=[
            out(rows, MODEL_WIDTH),
            out(rows, width),
            out(hidden, MODEL_WIDTH, dtype=FULL),
            out(hidden, MODEL_WIDTH, dtype=FULL),
            out(hidden, MODEL_WIDTH, dtype=FULL),
        ],
        scratch_shapes=[pltpu.VMEM((rows, hidden), LOW)] * 3
        + [pltpu.VMEM((hidden, rows), LOW), pltpu.VMEM((2 * hidden, rows), LOW)],
        compiler_params=pltpu.CompilerParams(vmem_limit_bytes=VMEM_LIMIT),
        cost_estimate=pl.CostEstimate(
            flops=EXP_DEV * rows * MODEL_WIDTH * hidden * 18,
            bytes_accessed=160 << 20,
            transcendentals=EXP_DEV * rows * hidden,
        ),
    )(sel, x, dy, w_gate, w_up, w_down)


def combine_home_kernel(
    planes, slots, hot_ref, v_ref, m_ref, out_ref, mix_ref,
    hot, load, mine, away, c_in, x_in, y_in, x_half, y_half, u_in, d_in,
    hot_sem, in_sem, free, c_send, c_recv, x_send, x_recv, y_send, y_recv, z_send, z_recv,
):
    e, core, flip_x, flip_y, diagonal = neighbours()
    s = lax.axis_index("shard")
    q_own, q_x, q_y, q_d = e // 2, flip_x // 2, flip_y // 2, diagonal // 2
    parity = e % 2
    length, width = out_ref.shape
    half = length // 2
    low_half, high_half = pl.ds(0, half), pl.ds(half, half)
    order = (q_d, q_x, q_y, q_own)
    spans = (pl.ds(0, width), pl.ds(0, MODEL_WIDTH))

    def fetch(kind, k, sp):
        rows = pl.ds(pl.multiple_of((order[k] * planes + sp) * slots, 16), slots)
        if kind == 0:
            return pltpu.make_async_copy(v_ref.at[:, rows, :], load.at[k % 2], in_sem.at[k % 2])
        return pltpu.make_async_copy(
            m_ref.at[:, rows, :], load.at[k % 2, :, :, pl.ds(0, MODEL_WIDTH)], in_sem.at[k % 2]
        )

    def fetch_hot(k, sp):
        return pltpu.make_async_copy(
            hot_ref.at[order[k] * planes + sp], hot.at[k % 2], hot_sem.at[k % 2]
        )

    def to_core(kind, q, sp):
        return send(
            away.at[q, sp, :, spans[kind]], c_in.at[q, sp, :, spans[kind]], c_send.at[kind, q, sp], c_recv.at[kind, q, sp],
            (core, s),
        )

    def halves(kind, sp):
        return [
            send(
                mine.at[q_d, sp, low_half, spans[kind]], y_half.at[kind, sp, :, spans[kind]],
                y_send.at[kind, 0, sp], y_recv.at[kind, 0, sp], (flip_y, s),
            ),
            send(
                mine.at[q_d, sp, high_half, spans[kind]], x_half.at[kind, sp, :, spans[kind]],
                x_send.at[kind, 0, sp], x_recv.at[kind, 0, sp], (flip_x, s),
            ),
        ]

    def to_x(kind, sp):
        return send(
            mine.at[q_x, sp, :, spans[kind]], x_in.at[kind, sp, :, spans[kind]], x_send.at[kind, 1, sp], x_recv.at[kind, 1, sp],
            (flip_x, s),
        )

    def to_y(kind, sp):
        return send(
            mine.at[q_y, sp, :, spans[kind]], y_in.at[kind, sp, :, spans[kind]], y_send.at[kind, 1, sp], y_recv.at[kind, 1, sp],
            (flip_y, s),
        )

    def up(kind, sp):
        return send(
            mine.at[q_own, sp, :, spans[kind]], u_in.at[kind, sp, :, spans[kind]], z_send.at[kind, 0, sp], z_recv.at[kind, 0, sp],
            (e, s + 1),
        )

    def down(kind, sp):
        return send(
            mine.at[q_own, sp, :, spans[kind]], d_in.at[kind, sp, :, spans[kind]], z_send.at[kind, 1, sp], z_recv.at[kind, 1, sp],
            (e, s - 1),
        )

    def settled(kind, sp):
        for q in range(4):
            to_core(kind, q, sp).wait_send()
        for copy in halves(kind, sp) + [to_x(kind, sp), to_y(kind, sp)]:
            copy.wait_send()

        @pl.when(sp > s)
        def _():
            up(kind, sp).wait_send()

        @pl.when(sp < s)
        def _():
            down(kind, sp).wait_send()

    def arrived(block, sem):
        send(block, block, sem, sem, (core, s)).wait_recv()

    def plane_at(i):
        back = 2 * planes - 2 - i
        sp = s + (2 * (back % 2) - 1) * ((back + 1) // 2)
        return sp, (sp >= 0) & (sp < planes) & (i >= 0) & (back >= 0)

    def add(target, *others):
        if len(others) == 1:
            target[...] = target[...] + others[0][...]
            return
        total = target[...].astype(FULL)
        for other in others:
            total = total + other[...].astype(FULL)
        target[...] = total.astype(LOW)

    def work(kind, sp):
        if kind == 1:
            settled(0, sp)
            pl.semaphore_wait(free.at[sp], 1)
        for k, q in enumerate(order):
            fetch_hot(k, sp).wait()
            fetch(kind, k, sp).wait()

            def part(at, wide, q=q, k=k):
                rows = load[k % 2, :, :, at].reshape(EXP_DEV * slots, wide)
                got = jnp.dot(hot[k % 2], rows, preferred_element_type=FULL).astype(LOW)
                got = got.reshape(2, length, wide)

                @pl.when(parity == 0)
                def _():
                    mine[q, sp, :, at] = got[0]
                    away[q, sp, :, at] = got[1]

                @pl.when(parity == 1)
                def _():
                    mine[q, sp, :, at] = got[1]
                    away[q, sp, :, at] = got[0]

            def tile(t, inner, part=part):
                part(pl.ds(pl.multiple_of(t * TILE, TILE), TILE), TILE)
                return inner

            lax.fori_loop(0, MODEL_WIDTH // TILE, tile, 0)
            if kind == 0 and width > MODEL_WIDTH:
                part(pl.ds(MODEL_WIDTH, width - MODEL_WIDTH), width - MODEL_WIDTH)
            to_core(kind, q, sp).start()
            if k < 2:
                fetch_hot(k + 2, sp).start()
                fetch(kind, k + 2, sp).start()

    def fetch_first(kind, sp):
        for k in range(2):
            fetch_hot(k, sp).start()
            fetch(kind, k, sp).start()

    def pairs(kind, sp):
        for k, q in enumerate(order):
            arrived(c_in.at[q, sp, :, spans[kind]], c_recv.at[kind, q, sp])
            add(mine.at[q, sp, :, spans[kind]], c_in.at[q, sp, :, spans[kind]])
            if k == 0:
                for copy in halves(kind, sp):
                    copy.start()
        if kind == 0:
            pl.semaphore_signal(free.at[sp], 1, device_id=(core, s), device_id_type=MESH)

    def sides(kind, sp):
        arrived(y_half.at[kind, sp, :, spans[kind]], y_recv.at[kind, 0, sp])
        add(mine.at[q_x, sp, low_half, spans[kind]], y_half.at[kind, sp, :, spans[kind]])
        to_x(kind, sp).start()
        arrived(x_half.at[kind, sp, :, spans[kind]], x_recv.at[kind, 0, sp])
        add(mine.at[q_y, sp, high_half, spans[kind]], x_half.at[kind, sp, :, spans[kind]])
        to_y(kind, sp).start()

    def line(kind, sp):
        arrived(x_in.at[kind, sp, :, spans[kind]], x_recv.at[kind, 1, sp])
        arrived(y_in.at[kind, sp, :, spans[kind]], y_recv.at[kind, 1, sp])
        add(
            mine.at[q_own, sp, :, spans[kind]],
            x_in.at[kind, sp, :, spans[kind]],
            y_in.at[kind, sp, :, spans[kind]],
        )

        @pl.when((sp >= s) & (s > 0))
        def _():
            arrived(u_in.at[kind, sp, :, spans[kind]], z_recv.at[kind, 0, sp])
            add(mine.at[q_own, sp, :, spans[kind]], u_in.at[kind, sp, :, spans[kind]])

        @pl.when((sp <= s) & (s < planes - 1))
        def _():
            arrived(d_in.at[kind, sp, :, spans[kind]], z_recv.at[kind, 1, sp])
            add(mine.at[q_own, sp, :, spans[kind]], d_in.at[kind, sp, :, spans[kind]])

        @pl.when(sp > s)
        def _():
            up(kind, sp).start()

        @pl.when(sp < s)
        def _():
            down(kind, sp).start()

        @pl.when(sp == s)
        def _():
            if kind == 0:
                out_ref[...] = mine[q_own, sp].astype(FULL)
            else:
                mix_ref[...] = mine[q_own, sp, :, :MODEL_WIDTH].astype(FULL)

    greet(planes)
    span = 2 * planes - 1

    def step(t, carry):
        for lag, job in ((0, fetch_first), (1, pairs), (3, sides), (0, work), (5, line)):
            for kind in range(2):
                sp, there = plane_at(t - lag - kind * span)

                @pl.when(there)
                def _(sp=sp, job=job, kind=kind):
                    job(kind, sp)

        return carry

    lax.fori_loop(0, 2 * span + 5, step, 0)

    def drain(sp, carry):
        settled(1, sp)
        return carry

    lax.fori_loop(0, planes, drain, 0)


def combine_home(hot, v, m, length, planes, slots, identity):
    width = v.shape[2]
    block = (planes, length, width)
    part = (planes, length // 2, width)
    return pl.pallas_call(
        functools.partial(combine_home_kernel, planes, slots),
        out_shape=[
            jax.ShapeDtypeStruct((length, width), FULL),
            jax.ShapeDtypeStruct((length, MODEL_WIDTH), FULL),
        ],
        in_specs=[ANY, ANY, ANY],
        out_specs=[VM, VM],
        scratch_shapes=[
            pltpu.VMEM((2,) + hot.shape[1:], LOW),
            pltpu.VMEM((2, EXP_DEV, slots, width), LOW),
            pltpu.VMEM((4,) + block, LOW),
            pltpu.VMEM((4,) + block, LOW),
            pltpu.VMEM((4,) + block, LOW),
            pltpu.VMEM((2,) + block, LOW),
            pltpu.VMEM((2,) + block, LOW),
            pltpu.VMEM((2,) + part, LOW),
            pltpu.VMEM((2,) + part, LOW),
            pltpu.VMEM((2,) + block, LOW),
            pltpu.VMEM((2,) + block, LOW),
            DMA((2,)),
            DMA((2,)),
            pltpu.SemaphoreType.REGULAR((planes,)),
            DMA((2, 4, planes)),
            DMA((2, 4, planes)),
            DMA((2, 2, planes)),
            DMA((2, 2, planes)),
            DMA((2, 2, planes)),
            DMA((2, 2, planes)),
            DMA((2, 2, planes)),
            DMA((2, 2, planes)),
        ],
        compiler_params=pltpu.CompilerParams(
            collective_id=identity, has_side_effects=True, vmem_limit_bytes=VMEM_LIMIT
        ),
    )(hot, v, m)


def greet_plane(planes, owners):
    e, s = lax.axis_index("expert"), lax.axis_index("shard")
    barrier = pltpu.get_barrier_semaphore()
    for o in range(1, owners):
        pl.semaphore_signal(
            barrier, 1, device_id=(lax.rem(e + o, owners), s), device_id_type=MESH
        )

    @pl.when(s > 0)
    def _():
        pl.semaphore_signal(barrier, 1, device_id=(e, s - 1), device_id_type=MESH)

    @pl.when(s < planes - 1)
    def _():
        pl.semaphore_signal(barrier, 1, device_id=(e, s + 1), device_id_type=MESH)

    inner = (s > 0) & (s < planes - 1)

    @pl.when(inner)
    def _():
        pl.semaphore_wait(barrier, owners + 1)

    @pl.when(jnp.logical_not(inner))
    def _():
        pl.semaphore_wait(barrier, owners)


def gather_steps(at, cut, source, x_send, x_recv, y_send, y_recv, c_send, c_recv):
    e, core, flip_x, flip_y, diagonal = neighbours()
    s = lax.axis_index("shard")

    def arrived(block, sem):
        send(block, block, sem, sem, (core, s)).wait_recv()

    def first():
        return [
            send(source, at(e), x_send(0), x_recv(0), (flip_x, s)),
            send(source, at(e), y_send(0), y_recv(0), (flip_y, s)),
            send(source, at(e), c_send(0), c_recv(0), (core, s)),
        ]

    def from_x():
        return [
            send(cut(flip_x, 0), cut(flip_x, 0), y_send(1), y_recv(1), (flip_y, s)),
            send(at(flip_x), at(flip_x), c_send(1), c_recv(1), (core, s)),
        ]

    def from_y():
        return [
            send(cut(flip_y, 1), cut(flip_y, 1), x_send(1), x_recv(1), (flip_x, s)),
            send(at(flip_y), at(flip_y), c_send(2), c_recv(2), (core, s)),
        ]

    def from_diagonal():
        return [send(at(diagonal), at(diagonal), c_send(3), c_recv(3), (core, s))]

    def begin():
        for copy in first():
            copy.start()

    def second():
        arrived(at(flip_x), x_recv(0))
        for copy in from_x():
            copy.start()
        arrived(at(flip_y), y_recv(0))
        for copy in from_y():
            copy.start()

    def third():
        arrived(cut(diagonal, 0), y_recv(1))
        arrived(cut(diagonal, 1), x_recv(1))
        for copy in from_diagonal():
            copy.start()

    def last():
        for k, lane in enumerate((core, core + flip_x - e, core + flip_y - e, core + diagonal - e)):
            arrived(at(lane), c_recv(k))

    def sent():
        for copy in first() + from_x() + from_y() + from_diagonal():
            copy.wait_send()

    return begin, second, third, last, sent


def rope_tables(places, frequency):
    angles = places * frequency
    lane = lax.broadcasted_iota(jnp.int32, angles.shape, 1)
    sine = jnp.sin(angles)
    return jnp.cos(angles), jnp.where(lane < HEAD_SIZE // 2, -sine, sine)


def half_turn(v):
    return pltpu.roll(v, HEAD_SIZE // 2, 1)


def head_gains(rows, planes):
    total = rows[0, :, :HEAD_SIZE].astype(FULL)
    for sp in range(1, planes):
        part = rows[sp, :, :HEAD_SIZE].astype(FULL)
        total = total + pltpu.roll(part, sp * (HEAD_SIZE // planes), 1)
    return total[2:3], total[3:4]


def front_kernel(
    planes, owners, qkv_ref, router_ref, gain_ref, tok_ref, d_ref, freq_ref, out_ref,
    d_all, w_out_all, w_all_out, r_all, gains, tail_ref, h1_ref, proj_ref, probs_ref, mixed_ref, branch_ref,
    w_all, tok_all, w_mine, q_rows, mine, away, c_in, x_in, y_in, x_half, y_half,
    keep_sem, w_send, w_recv, v_send, v_recv, k_send, k_recv, r_send, r_recv, g_send, g_recv,
    o_send, o_recv, z_send, z_recv, rx_send, rx_recv, ry_send, ry_recv, rc_send, rc_recv,
    tx_send, tx_recv, ty_send, ty_recv, tc_send, tc_recv,
    dx_send, dx_recv, dy_send, dy_recv, dc_send, dc_recv,
    px_send, px_recv, py_send, py_recv, pc_send, pc_recv,
):
    e, core, flip_x, flip_y, diagonal = neighbours()
    s = lax.axis_index("shard")
    lanes = owners // planes
    home = e // lanes
    length = tok_ref.shape[0]
    half = length // 2
    count = w_mine.shape[0]
    heads = count // HEAD_SIZE
    pieces = 8
    out_part = count // pieces
    deep = qkv_ref.shape[0]
    query_cols = count
    kv_at = pl.ds(pl.multiple_of(count + HEAD_SIZE * (e % 2), HEAD_SIZE), HEAD_SIZE)

    def arrived(block, sem):
        send(block, block, sem, sem, (core, s)).wait_recv()

    def w_copy(sp, way):
        block = w_all.at[sp, :, pl.ds(0, query_cols)]
        return send(block, block, w_send.at[way, sp], w_recv.at[sp], (e, s + 1 - 2 * way))

    def v_copy(sp, way):
        block = w_all.at[sp, :, kv_at]
        return send(block, block, v_send.at[way, sp], v_recv.at[sp], (e, s + 1 - 2 * way))

    def r_copy(sp, way):
        block = r_all.at[e, sp]
        return send(block, block, r_send.at[way, sp], r_recv.at[sp], (e, s + 1 - 2 * way))

    def k_copy(sp):
        block = w_all.at[sp, :, kv_at]
        return send(block, block, k_send.at[sp], k_recv.at[sp], (core, s))

    def g_copy(sp, way):
        block = gains.at[sp]
        return send(block, block, g_send.at[way, sp], g_recv.at[sp], (e, s + 1 - 2 * way))

    def d_copy(sp, way):
        block = d_all.at[e, sp]
        return send(block, block, z_send.at[way, sp], z_recv.at[sp], (e, s + 1 - 2 * way))

    def o_copy(k, way):
        block = w_mine.at[pl.ds(k * out_part, out_part)]
        return send(block, block, o_send.at[way, k], o_recv.at[k], (e, s + 1 - 2 * way))

    t_begin, t_second, t_third, t_last, t_sent = gather_steps(
        lambda lane: tok_all.at[lane],
        lambda lane, k: tok_all.at[lane, pl.ds(k * half, half)],
        tok_ref,
        lambda k: tx_send.at[k],
        lambda k: tx_recv.at[k],
        lambda k: ty_send.at[k],
        lambda k: ty_recv.at[k],
        lambda k: tc_send.at[k],
        lambda k: tc_recv.at[k],
    )

    r_half = planes // 2
    r_begin, r_second, r_third, r_last, r_sent = gather_steps(
        lambda lane: r_all.at[lane],
        lambda lane, k: r_all.at[lane, pl.ds(k * r_half, r_half)],
        r_all.at[e],
        lambda k: rx_send.at[k],
        lambda k: rx_recv.at[k],
        lambda k: ry_send.at[k],
        lambda k: ry_recv.at[k],
        lambda k: rc_send.at[k],
        lambda k: rc_recv.at[k],
    )

    def d_rows(sp):
        return gather_steps(
            lambda lane: d_all.at[lane, sp],
            lambda lane, k: d_all.at[lane, sp, pl.ds(k * half, half)],
            d_all.at[e, sp],
            lambda k: dx_send.at[k, sp],
            lambda k: dx_recv.at[k, sp],
            lambda k: dy_send.at[k, sp],
            lambda k: dy_recv.at[k, sp],
            lambda k: dc_send.at[k, sp],
            lambda k: dc_recv.at[k, sp],
        )

    keep_d = pltpu.make_async_copy(d_ref, d_all.at[e, s], keep_sem.at[0])
    rows = pl.ds(pl.multiple_of((e - home * lanes) * count, 16), count)
    load_o = pltpu.make_async_copy(out_ref.at[rows], w_mine, keep_sem.at[1])
    keep_w = pltpu.make_async_copy(w_all, w_all_out, keep_sem.at[2])
    keep_o = pltpu.make_async_copy(w_mine, w_out_all, keep_sem.at[3])
    at = pl.ds(pl.multiple_of(e * count, count), count)
    load_w = pltpu.make_async_copy(
        qkv_ref.at[:, at], w_all.at[s, :, pl.ds(0, query_cols)], keep_sem.at[4]
    )
    kv_from = (QUERY_HEADS + e % 2 * KEY_VALUE_HEADS + e * KEY_VALUE_HEADS // owners) * HEAD_SIZE
    at = pl.ds(pl.multiple_of(kv_from, HEAD_SIZE), HEAD_SIZE)
    load_v = pltpu.make_async_copy(qkv_ref.at[:, at], w_all.at[s, :, kv_at], keep_sem.at[5])
    keep_d.start()

    @pl.when(s == home)
    def _():
        load_o.start()

    load_w.start()
    load_v.start()
    r_all[e, s] = router_ref[...]
    gains[s] = gain_ref[...]
    tok_all[e] = tok_ref[...]
    greet(planes)

    def both_ways(copy, sp):
        @pl.when((sp <= s) & (s < planes - 1))
        def _():
            copy(sp, 0).start()

        @pl.when((sp >= s) & (s > 0))
        def _():
            copy(sp, 1).start()

    def plane_at(i):
        sp = s + (2 * (i % 2) - 1) * ((i + 1) // 2)
        return sp, (sp >= 0) & (sp < planes) & (i >= 0) & (i <= 2 * planes - 2)

    def out_step(k):
        @pl.when(s != home)
        def _():
            arrived(w_mine.at[pl.ds(k * out_part, out_part)], o_recv.at[k])

        @pl.when((s >= home) & (s < planes - 1))
        def _():
            o_copy(k, 0).start()

        @pl.when((s <= home) & (s > 0))
        def _():
            o_copy(k, 1).start()

    t_begin()
    both_ways(g_copy, s)
    keep_d.wait()
    both_ways(d_copy, s)
    load_w.wait()
    both_ways(w_copy, s)
    load_v.wait()
    both_ways(v_copy, s)
    both_ways(r_copy, s)
    k_copy(s).start()
    d_rows(s)[0]()

    def weights(i, carry):
        sp, there = plane_at(i)

        @pl.when(there & (i > 0))
        def _():
            arrived(gains.at[sp], g_recv.at[sp])
            both_ways(g_copy, sp)
            arrived(d_all.at[e, sp], z_recv.at[sp])
            both_ways(d_copy, sp)
            d_rows(sp)[0]()
            arrived(w_all.at[sp, :, pl.ds(0, query_cols)], w_recv.at[sp])
            both_ways(w_copy, sp)
            arrived(w_all.at[sp, :, kv_at], v_recv.at[sp])
            both_ways(v_copy, sp)
            k_copy(sp).start()
            arrived(r_all.at[e, sp], r_recv.at[sp])
            both_ways(r_copy, sp)

        @pl.when(i == 1)
        def _():
            t_second()

        @pl.when(i == 2)
        def _():
            t_third()

        @pl.when((i == 4) & (s == home))
        def _():
            load_o.wait()
            for k in range(pieces):
                out_step(k)

        return carry

    lax.fori_loop(1, 2 * planes - 1, weights, 0)
    r_begin()
    t_last()
    other_kv = pl.ds(pl.multiple_of(count + HEAD_SIZE * (1 - e % 2), HEAD_SIZE), HEAD_SIZE)
    for sp in range(planes):
        arrived(w_all.at[sp, :, other_kv], k_recv.at[sp])
    keep_w.start()

    def distant(n):
        return (s - home == n) | (home - s == n)

    gain_query, gain_key = head_gains(gains, planes)
    row = lax.broadcasted_iota(jnp.int32, (length, length), 0).astype(FULL)
    column = lax.broadcasted_iota(jnp.int32, (length, length), 1).astype(FULL)

    def attend(b, carry):
        x = tok_all[b, :, :MODEL_WIDTH].astype(FULL)
        inverse = lax.rsqrt(jnp.mean(x * x, axis=1, keepdims=True) + EPS)
        total = jnp.zeros((length, w_all.shape[2]), FULL)
        for sp in range(planes):
            at = slice(sp * deep, (sp + 1) * deep)
            part = x[:, at] * inverse * gains[sp, 0:1, :].astype(FULL)
            part = part.astype(LOW)
            h1_ref[b, :, at] = part
            total = total + jnp.dot(part, w_all[sp], preferred_element_type=FULL)
        proj_ref[b] = total
        tail_ref[b] = tok_all[b, :, MODEL_WIDTH:]
        places = tok_all[b, :, MODEL_WIDTH:].astype(FULL)[:, 1:2]
        cosine, sine = rope_tables(places, freq_ref[0:1, :])

        def normed(v, gain):
            v = v * lax.rsqrt(jnp.mean(v * v, axis=1, keepdims=True) + EPS) * gain
            return (v * cosine + half_turn(v) * sine).astype(LOW)

        for h in range(heads):
            at = slice(h * HEAD_SIZE, (h + 1) * HEAD_SIZE)
            q_rows[h * length : (h + 1) * length, :] = normed(total[:, at], gain_query)
        key = normed(total[:, count : count + HEAD_SIZE], gain_key)
        value = total[:, count + HEAD_SIZE :].astype(LOW)
        scores = lax.dot_general(
            q_rows[...], key, (((1,), (1,)), ((), ())), preferred_element_type=FULL
        ) * (HEAD_SIZE**-0.5)
        allowed = (column <= row) & (column >= row - places)
        scores = jnp.where(jnp.concatenate([allowed] * heads, axis=0), scores, -1e30)
        exponent = jnp.exp(scores - jnp.max(scores, axis=1, keepdims=True))
        probs = (exponent / jnp.sum(exponent, axis=1, keepdims=True)).astype(LOW)
        probs_ref[b] = probs
        mixed = jnp.dot(probs, value, preferred_element_type=FULL).astype(LOW)
        for h in range(heads):
            at = slice(h * HEAD_SIZE, (h + 1) * HEAD_SIZE)
            mixed_ref[b, :, at] = mixed[h * length : (h + 1) * length]

        for lag, stage in ((0, 1), (2, 2)):
            sp, there = plane_at(b - lag)

            @pl.when(there)
            def _(sp=sp, stage=stage):
                d_rows(sp)[stage]()

        for k in range(pieces):

            @pl.when((b == k) & distant(1))
            def _(k=k):
                out_step(k)

        for k in range(5):

            @pl.when((b == 3 + k) & distant(2))
            def _(k=k):
                out_step(k)

        return carry

    lax.fori_loop(0, owners, attend, 0)
    for i in range(owners - 2, 2 * planes - 1):
        sp, there = plane_at(i)

        @pl.when(there)
        def _(sp=sp):
            d_rows(sp)[2]()


    @pl.when(distant(2))
    def _():
        for k in range(5, pieces):
            out_step(k)

    r_second()
    for n in range(3, planes):

        @pl.when(distant(n))
        def _():
            for k in range(pieces):
                out_step(k)

    keep_o.start()
    begin, middle, finish, sent = project_steps(
        False, mixed_ref, w_mine, branch_ref, mine, away, c_in, x_in, y_in, x_half, y_half,
        pc_send, pc_recv, px_send, px_recv, py_send, py_recv,
    )
    begin()
    r_third()
    middle()
    finish()
    r_last()
    t_sent()
    r_sent()
    sent()

    def settled(copy, sp):
        @pl.when((sp <= s) & (s < planes - 1))
        def _():
            copy(sp, 0).wait_send()

        @pl.when((sp >= s) & (s > 0))
        def _():
            copy(sp, 1).wait_send()

    def drain(sp, carry):
        d_rows(sp)[3]()
        d_rows(sp)[4]()
        settled(w_copy, sp)
        settled(v_copy, sp)
        settled(r_copy, sp)
        k_copy(sp).wait_send()
        settled(g_copy, sp)
        settled(d_copy, sp)
        return carry

    lax.fori_loop(0, planes, drain, 0)
    for k in range(pieces):

        @pl.when((s >= home) & (s < planes - 1))
        def _(k=k):
            o_copy(k, 0).wait_send()

        @pl.when((s <= home) & (s > 0))
        def _(k=k):
            o_copy(k, 1).wait_send()

    keep_w.wait()
    keep_o.wait()


def front(w, router, gain_rows, tokens, w_out, d_rows, frequency, planes, owners, identity):
    def out(*shape, dtype=LOW):
        return jax.ShapeDtypeStruct(shape, dtype)

    length = tokens.shape[0]
    count = w_out.shape[0] * planes // owners
    qkv_cols = count + 2 * HEAD_SIZE
    block = (length, MODEL_WIDTH)
    part = (length // 2, MODEL_WIDTH)
    return pl.pallas_call(
        functools.partial(front_kernel, planes, owners),
        out_shape=[
            out(owners, planes, *d_rows.shape),
            out(count, MODEL_WIDTH),
            out(planes, w.shape[0], qkv_cols),
            out(owners, planes, *router.shape),
            out(planes, *gain_rows.shape),
            out(owners, length, TAIL),
            out(owners, length, MODEL_WIDTH),
            out(owners, length, qkv_cols, dtype=FULL),
            out(owners, length * count // HEAD_SIZE, length),
            out(owners, length, count),
            out(length, MODEL_WIDTH, dtype=FULL),
        ],
        in_specs=[ANY, VM, VM, VM, VM, VM, ANY],
        out_specs=[ANY, ANY, ANY, VM, VM, VM, VM, VM, VM, VM, VM],
        scratch_shapes=[
            pltpu.VMEM((planes, w.shape[0], qkv_cols), LOW),
            pltpu.VMEM((owners,) + tokens.shape, LOW),
            pltpu.VMEM((count, MODEL_WIDTH), LOW),
            pltpu.VMEM((length * count // HEAD_SIZE, HEAD_SIZE), LOW),
            pltpu.VMEM((4,) + block, LOW),
            pltpu.VMEM((4,) + block, LOW),
            pltpu.VMEM((4,) + block, LOW),
            pltpu.VMEM(block, LOW),
            pltpu.VMEM(block, LOW),
            pltpu.VMEM(part, LOW),
            pltpu.VMEM(part, LOW),
            DMA((6,)),
            DMA((2, planes)),
            DMA((planes,)),
            DMA((2, planes)),
            DMA((planes,)),
            DMA((planes,)),
            DMA((planes,)),
            DMA((2, planes)),
            DMA((planes,)),
            DMA((2, planes)),
            DMA((planes,)),
            DMA((2, 8)),
            DMA((8,)),
            DMA((2, planes)),
            DMA((planes,)),
            DMA((2,)),
            DMA((2,)),
            DMA((2,)),
            DMA((2,)),
            DMA((4,)),
            DMA((4,)),
            DMA((2,)),
            DMA((2,)),
            DMA((2,)),
            DMA((2,)),
            DMA((4,)),
            DMA((4,)),
            DMA((2, planes)),
            DMA((2, planes)),
            DMA((2, planes)),
            DMA((2, planes)),
            DMA((4, planes)),
            DMA((4, planes)),
            DMA((2,)),
            DMA((2,)),
            DMA((2,)),
            DMA((2,)),
            DMA((4,)),
            DMA((4,)),
        ],
        compiler_params=pltpu.CompilerParams(
            collective_id=identity, has_side_effects=True, vmem_limit_bytes=VMEM_LIMIT
        ),
    )(w, router, gain_rows, tokens, d_rows, frequency, w_out)


def project_steps(
    turned, rows_ref, w_ref, out_ref, mine, away, c_in, x_in, y_in, x_half, y_half,
    cs, cr, xs, xr, ys, yr,
):
    e, core, flip_x, flip_y, diagonal = neighbours()
    s = lax.axis_index("shard")
    q_own, q_x, q_y, q_d = e // 2, flip_x // 2, flip_y // 2, diagonal // 2
    parity = e % 2
    half = out_ref.shape[0] // 2
    low_half, high_half = pl.ds(0, half), pl.ds(half, half)
    across = (((1,), (1 if turned else 0,)), ((), ()))
    order = (q_d, q_x, q_y, q_own)

    def arrived(block, sem):
        send(block, block, sem, sem, (core, s)).wait_recv()

    def add(target, *others):
        total = target[...].astype(FULL)
        for other in others:
            total = total + other[...].astype(FULL)
        target[...] = total.astype(LOW)

    def to_core(q):
        return send(away.at[q], c_in.at[q], cs.at[q], cr.at[q], (core, s))

    def compute(q, lane, into):
        rows = rows_ref[2 * q + lane]

        def tile(t, carry):
            at = pl.ds(pl.multiple_of(t * TILE, TILE), TILE)
            if turned:
                deep = w_ref.shape[1]
                w = w_ref[t * TILE // deep, :, : rows.shape[1]]
            else:
                w = w_ref[:, at]
            into[q, :, at] = lax.dot_general(
                rows, w, across, preferred_element_type=FULL
            ).astype(LOW)
            return carry

        lax.fori_loop(0, MODEL_WIDTH // TILE, tile, 0)

    halves = [
        send(mine.at[q_d, low_half], y_half, ys.at[0], yr.at[0], (flip_y, s)),
        send(mine.at[q_d, high_half], x_half, xs.at[0], xr.at[0], (flip_x, s)),
    ]
    to_x = send(mine.at[q_x], x_in, xs.at[1], xr.at[1], (flip_x, s))
    to_y = send(mine.at[q_y], y_in, ys.at[1], yr.at[1], (flip_y, s))

    def joined(q):
        arrived(c_in.at[q], cr.at[q])
        add(mine.at[q], c_in.at[q])

    def begin():
        for q in order:
            compute(q, 1 - parity, away)
            to_core(q).start()
        for k, q in enumerate(order):
            compute(q, parity, mine)
            if k == 0:
                joined(q_d)
                for copy in halves:
                    copy.start()

    def middle():
        joined(q_x)
        arrived(y_half, yr.at[0])
        add(mine.at[q_x, low_half], y_half)
        to_x.start()
        joined(q_y)
        arrived(x_half, xr.at[0])
        add(mine.at[q_y, high_half], x_half)
        to_y.start()

    def finish():
        joined(q_own)
        arrived(x_in, xr.at[1])
        arrived(y_in, yr.at[1])
        out_ref[...] = (
            mine[q_own].astype(FULL) + x_in[...].astype(FULL) + y_in[...].astype(FULL)
        )

    def sent():
        for q in order:
            to_core(q).wait_send()
        for copy in halves + [to_x, to_y]:
            copy.wait_send()

    return begin, middle, finish, sent


def add_blocks(target, other):
    step = min(128, target.shape[1])
    for lead in range(target.shape[0]):

        def one(r, carry, lead=lead):
            at = pl.ds(pl.multiple_of(r * step, step), step)
            target[lead, at, :] = (
                target[lead, at, :].astype(FULL) + other[lead, at, :].astype(FULL)
            ).astype(LOW)
            return carry

        lax.fori_loop(0, target.shape[1] // step, one, 0)


def back_kernel(
    planes, owners, dm_ref, w_out_ref, mixed_ref, proj_ref, probs_ref, places_ref, gain_ref,
    freq_ref, h1_ref, w_ref, tok_ref, h2_ref, dl_ref, gain_two_ref,
    out_rows, out_head, out_rest, dh1_ref,
    dm_all, mixed_t, rows, q_rows, dm_rows, dproj, column,
    acc_rows, acc_head, acc_rest, sibling, u_rows, u_head, u_rest, d_rows, d_head, d_rest, pair_in,
    mine, away, c_in, x_in, y_in, x_half, y_half,
    gxs, gxr, gys, gyr, gcs, gcr, a_send, a_recv, s_send, s_recv, z_send, z_recv,
    x_send, x_recv, y_send, y_recv, c_send, c_recv, own_sem,
    pc_send, pc_recv, px_send, px_recv, py_send, py_recv,
):
    e, core, _, _, _ = neighbours()
    s = lax.axis_index("shard")
    parity = e % 2
    lanes = owners // planes
    length = dm_ref.shape[0]
    half = length // 2
    count = w_out_ref.shape[0]
    heads = count // HEAD_SIZE
    share_cols = acc_rows.shape[2]
    deep = acc_head.shape[1] * acc_head.shape[2]
    scaling = HEAD_SIZE**-0.5
    nt = (((1,), (1,)), ((), ()))
    tn = (((0,), (0,)), ((), ()))
    up_in, down_in = (u_rows, u_head, u_rest), (d_rows, d_head, d_rest)
    outs = (out_rows, out_head, out_rest)

    def arrived(block, sem):
        send(block, block, sem, sem, (core, s)).wait_recv()

    greet_plane(planes, owners)
    begin, second, third, last, sent = gather_steps(
        lambda lane: dm_all.at[lane],
        lambda lane, k: dm_all.at[lane, pl.ds(k * half, half)],
        dm_ref,
        lambda k: gxs.at[k],
        lambda k: gxr.at[k],
        lambda k: gys.at[k],
        lambda k: gyr.at[k],
        lambda k: gcs.at[k],
        lambda k: gcr.at[k],
    )
    begin()
    dm_all[e] = dm_ref[...]
    for b in range(owners):
        mixed_t[:, b * length : (b + 1) * length] = mixed_ref[b].T

    def lane_at(j):
        flipped = [(e // bit + j // bit) % 2 * bit for bit in (1, 2, 4)]
        return flipped[0] + flipped[1] + flipped[2]

    def spread(other):
        return send(
            rows.at[:, pl.ds(other * share_cols, share_cols)], acc_rows.at[e],
            a_send.at[other], a_recv.at[e], (other, s),
        )

    column[...] = jnp.zeros_like(column)
    gain_query, gain_key = head_gains(gain_ref, planes)

    def attend(j, carry):
        b = lane_at(j)
        for at, step in ((2, second), (6, third)):

            @pl.when(j == at)
            def _(step=step):
                step()

        @pl.when(j % 2 == 1)
        def _():
            arrived(dm_all.at[b], gcr.at[j // 2])

        places = places_ref[b].astype(FULL)[:, 1:2]
        cosine, sine = rope_tables(places, freq_ref[0:1, :])

        def unit(v):
            inverse = lax.rsqrt(jnp.mean(v * v, axis=1, keepdims=True) + EPS)
            return v * inverse, inverse

        def turned(v):
            return (v * cosine + half_turn(v) * sine).astype(LOW)

        def back(v, units, inverse, gain, row):
            v = v * cosine - half_turn(v) * sine
            column[row : row + 1, :HEAD_SIZE] += jnp.sum(v * units, axis=0, keepdims=True)
            v = v * gain
            return inverse * (v - units * jnp.mean(v * units, axis=1, keepdims=True))

        d_mixed = lax.dot_general(
            dm_all[b], w_out_ref[...], nt, preferred_element_type=FULL
        ).astype(LOW)
        for h in range(heads):
            at = slice(h * HEAD_SIZE, (h + 1) * HEAD_SIZE)
            here = slice(h * length, (h + 1) * length)
            dm_rows[here, :] = d_mixed[:, at]
            units, _ = unit(proj_ref[b, :, at])
            q_rows[here, :] = turned(units * gain_query)
        key_units, key_inverse = unit(proj_ref[b, :, count : count + HEAD_SIZE])
        key = turned(key_units * gain_key)
        value = proj_ref[b, :, count + HEAD_SIZE :].astype(LOW)
        probs = probs_ref[b]
        wide = probs.astype(FULL)
        d_probs = lax.dot_general(dm_rows[...], value, nt, preferred_element_type=FULL)
        d_scores = wide * (d_probs - jnp.sum(d_probs * wide, axis=1, keepdims=True))
        d_scores = d_scores.astype(LOW)
        d_query = jnp.dot(d_scores, key, preferred_element_type=FULL) * scaling
        d_key = lax.dot_general(d_scores, q_rows[...], tn, preferred_element_type=FULL) * scaling
        d_value = lax.dot_general(probs, dm_rows[...], tn, preferred_element_type=FULL)
        for h in range(heads):
            at = slice(h * HEAD_SIZE, (h + 1) * HEAD_SIZE)
            units, inverse = unit(proj_ref[b, :, at])
            got = back(
                d_query[h * length : (h + 1) * length], units, inverse, gain_query, GAIN_QUERY
            )
            dproj[b, :, at] = got.astype(LOW)
        got = back(d_key, key_units, key_inverse, gain_key, GAIN_KEY)
        dproj[b, :, count : count + HEAD_SIZE] = got.astype(LOW)
        dproj[b, :, count + HEAD_SIZE :] = d_value.astype(LOW)
        return carry

    lax.fori_loop(0, owners, attend, 0)
    resident = tok_ref[...].astype(FULL)
    inverse_one = lax.rsqrt(jnp.mean(resident * resident, axis=1, keepdims=True) + EPS)

    def left_of(sp):
        at = pl.ds(pl.multiple_of(sp * deep, deep), deep)
        return h1_ref[:, :, at].reshape(-1, deep)

    def make_head(sp):
        right = dproj[:, :, :count].reshape(-1, count)
        got = lax.dot_general(left_of(sp), right, tn, preferred_element_type=FULL).astype(LOW)
        acc_head[sp] = got.reshape(acc_head.shape[1:])

    def to_sibling(sp):
        return send(sibling.at[sp], pair_in.at[sp], s_send.at[sp], s_recv.at[sp], (core, s))

    def make_rest(sp):
        right = dproj[:, :, count:].reshape(-1, 2 * HEAD_SIZE)
        got = lax.dot_general(left_of(sp), right, tn, preferred_element_type=FULL).astype(LOW)
        key, value = got[:, :HEAD_SIZE], got[:, HEAD_SIZE:]
        at = pl.ds(pl.multiple_of(sp * deep, deep), deep)
        column[GAIN_ONE : GAIN_ONE + 1, :] = jnp.sum(
            dh1_ref[:, at] * (tok_ref[:, at].astype(FULL) * inverse_one), axis=0, keepdims=True
        )
        column[GAIN_TWO : GAIN_TWO + 1, :] = gain_two_ref[:, at]
        extra = lax.dot_general(h2_ref[:, at], dl_ref[...], tn, preferred_element_type=FULL)
        extra = (extra + column[...].T).astype(LOW)
        top, low = extra[: deep // 2], extra[deep // 2 :]

        def put(into, kv, part):
            into[sp, :4] = kv.reshape(4, deep // 4, HEAD_SIZE)
            into[sp, 4:] = part.reshape(2, deep // 4, HEAD_SIZE)

        @pl.when(parity == 0)
        def _():
            put(acc_rest, key, top)
            put(sibling, value, low)

        @pl.when(parity == 1)
        def _():
            put(acc_rest, value, low)
            put(sibling, key, top)

        to_sibling(sp).start()

    def chunk(k, sp):
        if k == 0:
            return acc_rows.at[pl.ds(sp * lanes, lanes)]
        return acc_head.at[sp] if k == 1 else acc_rest.at[sp]

    def ready(k, sp):
        if k == 0:
            for lane in range(lanes):
                source = sp * lanes + lane

                @pl.when(source != e)
                def _(source=source):
                    arrived(acc_rows.at[source], a_recv.at[source])

        elif k == 1:
            make_head(sp)
        else:
            arrived(pair_in.at[sp], s_recv.at[sp])
            add_blocks(acc_rest.at[sp], pair_in.at[sp])

    def up(k, sp):
        return send(
            chunk(k, sp), up_in[k].at[sp], z_send.at[k, 0, sp], z_recv.at[k, 0, sp], (e, s + 1)
        )

    def down(k, sp):
        return send(
            chunk(k, sp), down_in[k].at[sp], z_send.at[k, 1, sp], z_recv.at[k, 1, sp], (e, s - 1)
        )

    def line(k, sp):
        ready(k, sp)

        @pl.when((sp >= s) & (s > 0))
        def _():
            arrived(up_in[k].at[sp], z_recv.at[k, 0, sp])
            add_blocks(chunk(k, sp), up_in[k].at[sp])

        @pl.when((sp <= s) & (s < planes - 1))
        def _():
            arrived(down_in[k].at[sp], z_recv.at[k, 1, sp])
            add_blocks(chunk(k, sp), down_in[k].at[sp])

        @pl.when(sp > s)
        def _():
            up(k, sp).start()

        @pl.when(sp < s)
        def _():
            down(k, sp).start()

    def pair(k, n):
        for i in (2 * n, 2 * n - 1):
            sp = s + (2 * (i % 2) - 1) * n

            @pl.when((sp >= 0) & (sp < planes))
            def _(sp=sp):
                line(k, sp)

    def steps(k):
        size = outs[k].shape[1] // 2
        return gather_steps(
            lambda lane: outs[k].at[lane],
            lambda lane, at: outs[k].at[lane, pl.ds(at * size, size)],
            chunk(k, s),
            lambda n: x_send.at[k, n],
            lambda n: x_recv.at[k, n],
            lambda n: y_send.at[k, n],
            lambda n: y_recv.at[k, n],
            lambda n: c_send.at[k, n],
            lambda n: c_recv.at[k, n],
        )

    def keep(k):
        return pltpu.make_async_copy(chunk(k, s), outs[k].at[e], own_sem.at[k])

    def own(k):
        line(k, s)
        steps(k)[0]()
        keep(k).start()

    p_begin, p_middle, p_finish, p_sent = project_steps(
        True, dproj, w_ref, dh1_ref, mine, away, c_in, x_in, y_in, x_half, y_half,
        pc_send, pc_recv, px_send, px_recv, py_send, py_recv,
    )
    pair(1, planes - 1)
    for other in range(owners):
        at = pl.ds(other * share_cols, share_cols)
        got = jnp.dot(
            mixed_t[...],
            dm_all[:, :, at].reshape(owners * length, share_cols),
            preferred_element_type=FULL,
        ).astype(LOW)
        rows[:, at] = got

        @pl.when(other != e)
        def _(other=other):
            spread(other).start()

        @pl.when(other == e)
        def _(got=got):
            acc_rows[e] = got
    for n in range(planes - 2, 0, -1):
        pair(1, n)
        if n == planes - 2:
            p_begin()
    pair(0, planes - 1)
    p_middle()
    own(1)
    for n in range(planes - 2, 1, -1):
        pair(0, n)
    p_finish()
    for sp in range(planes):
        make_rest(sp)
    pair(0, 1)
    steps(1)[1]()
    pair(2, planes - 1)
    own(0)
    steps(1)[2]()
    for n in range(planes - 2, 0, -1):
        pair(2, n)
    steps(0)[1]()
    own(2)
    steps(0)[2]()
    steps(2)[1]()
    steps(2)[2]()
    for k in range(3):
        keep(k).wait()
        steps(k)[3]()
        steps(k)[4]()
    p_sent()
    sent()
    for other in range(owners):

        @pl.when(other != e)
        def _(other=other):
            spread(other).wait_send()

    def drain(sp, carry):
        to_sibling(sp).wait_send()
        for k in range(3):

            @pl.when(sp > s)
            def _(k=k):
                up(k, sp).wait_send()

            @pl.when(sp < s)
            def _(k=k):
                down(k, sp).wait_send()

        return carry

    lax.fori_loop(0, planes, drain, 0)


def back(
    dm, w_out, mixed, proj, probs, places, gains, frequency, h1, w, tokens, h2, d_logits, gain_two,
    planes, owners, identity,
):
    length = dm.shape[0]
    count = w_out.shape[0]
    share_cols = MODEL_WIDTH // owners
    deep = MODEL_WIDTH // planes
    shapes = (
        (owners // planes, count, share_cols),
        (2, deep // 2, count),
        (6, deep // 4, HEAD_SIZE),
    )
    stack = (length * count // HEAD_SIZE, HEAD_SIZE)
    block = (length, MODEL_WIDTH)
    part = (length // 2, MODEL_WIDTH)

    def vmem(*shape, dtype=LOW):
        return pltpu.VMEM(shape, dtype)

    per_plane = [vmem(planes, *shape) for shape in shapes]
    return pl.pallas_call(
        functools.partial(back_kernel, planes, owners),
        out_shape=[jax.ShapeDtypeStruct((owners,) + shape, LOW) for shape in shapes]
        + [jax.ShapeDtypeStruct(block, FULL)],
        in_specs=[VM] * 14,
        out_specs=[ANY, ANY, ANY, VM],
        scratch_shapes=[
            vmem(owners, *block),
            vmem(count, owners * length),
            vmem(count, MODEL_WIDTH),
            vmem(*stack),
            vmem(*stack),
            vmem(*proj.shape),
            vmem(TAIL, deep, dtype=FULL),
            vmem(owners, count, share_cols),
            per_plane[1],
            per_plane[2],
            per_plane[2],
        ]
        + per_plane
        + per_plane
        + [
            per_plane[2],
            vmem(4, *block),
            vmem(4, *block),
            vmem(4, *block),
            vmem(*block),
            vmem(*block),
            vmem(*part),
            vmem(*part),
            DMA((2,)),
            DMA((2,)),
            DMA((2,)),
            DMA((2,)),
            DMA((4,)),
            DMA((4,)),
            DMA((owners,)),
            DMA((owners,)),
            DMA((planes,)),
            DMA((planes,)),
            DMA((3, 2, planes)),
            DMA((3, 2, planes)),
            DMA((3, 2)),
            DMA((3, 2)),
            DMA((3, 2)),
            DMA((3, 2)),
            DMA((3, 4)),
            DMA((3, 4)),
            DMA((3,)),
            DMA((4,)),
            DMA((4,)),
            DMA((2,)),
            DMA((2,)),
            DMA((2,)),
            DMA((2,)),
        ],
        compiler_params=pltpu.CompilerParams(
            collective_id=identity, has_side_effects=True, vmem_limit_bytes=VMEM_LIMIT
        ),
    )(
        dm, w_out, mixed, proj, probs, places, gains, frequency, h1, w, tokens, h2, d_logits,
        gain_two,
    )


def finish_kernel(
    owners, rows_ref, head_ref, rest_ref, tok_ref, middle_ref, mix_ref, dm_ref, dh1_ref, gain_ref,
    out_rows, out_qkv, out_router, out_gains, result_ref, dtok_ref,
):
    i = pl.program_id(0)

    @pl.when(i < owners)
    def _():
        out_rows[...] = rows_ref[0].astype(FULL)
        out_qkv[...] = head_ref[0].astype(FULL)

    for at in range(2):

        @pl.when(i == owners + at)
        def _(at=at):
            for h in range(KEY_VALUE_HEADS):
                got = rest_ref[2 * h + at, :4].reshape(-1, HEAD_SIZE)
                out_qkv[:, h * HEAD_SIZE : (h + 1) * HEAD_SIZE] = got.astype(FULL)

    @pl.when(i == 0)
    def _():
        height = out_router.shape[0] // 2
        experts = out_router.shape[1]
        for at in range(2):
            total = jnp.zeros((height, TAIL), FULL)
            for lane in range(at, owners, 2):
                total = total + rest_ref[lane, 4:].reshape(-1, TAIL).astype(FULL)
            here = slice(at * height, (at + 1) * height)
            out_router[here, :] = total[:, :experts]
            out_gains[:, here] = total.T[experts : experts + 8]

    @pl.when(i == 1)
    def _():
        result_ref[...] = (middle_ref[...] + mix_ref[...]).astype(LOW)

    @pl.when(i == 2)
    def _():
        resident = tok_ref[...].astype(FULL)
        units, inverse = unit_norm(resident)
        back = norm_back(dh1_ref[...], units, inverse, gain_ref[...])
        dtok_ref[...] = (dm_ref[...] + back).astype(LOW)


def finish_grads(rows, head, rest, tokens, middle, mix, d_middle, d_h1, gain, owners):
    rows = rows.reshape(owners, -1, rows.shape[-1])
    head = head.reshape(owners, -1, head.shape[-1])
    count, share = rows.shape[1:]
    height, wide = head.shape[1:]
    last = owners - 1

    def whole(shape):
        return pl.BlockSpec(shape, lambda i: (0,) * len(shape))

    block = tokens.shape
    return pl.pallas_call(
        functools.partial(finish_kernel, owners),
        grid=(owners + 2,),
        in_specs=[
            pl.BlockSpec((1, count, share), lambda i: (jnp.minimum(i, last), 0, 0)),
            pl.BlockSpec((1, height, wide), lambda i: (jnp.minimum(i, last), 0, 0)),
            whole(rest.shape),
        ]
        + [whole(block)] * 5
        + [whole(gain.shape)],
        out_specs=[
            pl.BlockSpec((count, share), lambda i: (0, jnp.minimum(i, last))),
            pl.BlockSpec((height, wide), lambda i: (0, i)),
            whole((height, TAIL // 2)),
            whole((8, height)),
            whole(block),
            whole(block),
        ],
        out_shape=[
            jax.ShapeDtypeStruct((count, owners * share), FULL),
            jax.ShapeDtypeStruct((height, (owners + 2) * wide), FULL),
            jax.ShapeDtypeStruct((height, TAIL // 2), FULL),
            jax.ShapeDtypeStruct((8, height), FULL),
            jax.ShapeDtypeStruct(block, LOW),
            jax.ShapeDtypeStruct(block, LOW),
        ],
        compiler_params=pltpu.CompilerParams(vmem_limit_bytes=VMEM_LIMIT),
    )(rows, head, rest, tokens, middle, mix, d_middle, d_h1, gain)


def gathered_layer(
    tokens,
    segments,
    routes,
    attn_gain,
    qkv_weight,
    query_gain,
    k_gain,
    w_out,
    ffn_gain,
    router,
    w_gate,
    w_up,
    w_down,
    d_out,
):
    owners = lax.axis_size("expert")
    planes = lax.axis_size("shard")
    me = lax.axis_index("expert")
    plane = lax.axis_index("shard")
    length = tokens.shape[0]
    blocks = owners * planes
    experts_all = router.shape[1]
    capacity = 3 * length * TOPK // (2 * experts_all)
    heads = QUERY_HEADS // owners
    query_cols = heads * HEAD_SIZE
    scaling = HEAD_SIZE ** (-0.5)
    both = ("expert", "shard")
    rows_in = qkv_weight.shape[0]

    kv_head = me * KEY_VALUE_HEADS // owners
    k_at = QUERY_HEADS * HEAD_SIZE + kv_head * HEAD_SIZE
    v_at = k_at + KEY_VALUE_HEADS * HEAD_SIZE
    gains = columns(
        [
            router,
            attn_gain[:, None],
            ffn_gain[:, None],
            jnp.pad(query_gain, (0, rows_in - query_gain.shape[0]))[:, None],
            jnp.pad(k_gain, (0, rows_in - k_gain.shape[0]))[:, None],
        ],
        rows_in,
    )
    mine = jnp.concatenate(
        [
            lax.dynamic_slice_in_dim(qkv_weight, me * query_cols, query_cols, 1),
            lax.dynamic_slice_in_dim(qkv_weight, k_at, HEAD_SIZE, 1),
            lax.dynamic_slice_in_dim(qkv_weight, v_at, HEAD_SIZE, 1),
            gains,
        ],
        axis=1,
    )
    gathered = lax.all_gather(mine, "shard", axis=0, tiled=True)
    qkv_cols = query_cols + 2 * HEAD_SIZE
    wqkv = gathered[:, :qkv_cols]
    router_full = gathered[:, qkv_cols : qkv_cols + experts_all]
    gain_cols = gathered[:, qkv_cols + experts_all :].astype(FULL)
    gain_one, gain_two = gain_cols[:, 0], gain_cols[:, 1]
    per = query_gain.shape[0]
    by_plane = gain_cols.reshape(planes, rows_in, -1)[:, :per]
    gain_query = by_plane[:, :, 2].reshape(-1)
    gain_key = by_plane[:, :, 3].reshape(-1)

    segment_row = segments[0]
    token_tail = columns(
        [segment_row[:, None], positions_of(segment_row)[:, None]], length
    )
    plane_rows = lax.all_gather(
        jnp.concatenate([tokens, token_tail], axis=1), "expert", axis=0, tiled=False
    )
    plane_tokens = plane_rows[:, :, :MODEL_WIDTH].astype(FULL)
    plane_segments = plane_rows[:, :, MODEL_WIDTH]
    plane_places = plane_rows[:, :, MODEL_WIDTH + 1].astype(FULL)

    out_rows = w_out.shape[0]
    first = me * query_cols
    offset = first - plane * out_rows
    if out_rows >= query_cols:
        held = (offset >= 0) & (offset < out_rows)
        piece = lax.dynamic_slice_in_dim(w_out, jnp.where(held, offset, 0), query_cols, 0)
        w_mine = lax.psum(jnp.where(held, piece, 0).astype(LOW), "shard")
    else:
        parts = query_cols // out_rows
        at = plane - me * parts
        held = (at >= 0) & (at < parts)
        spread = jnp.where(held & (jnp.arange(parts) == at)[:, None, None], w_out[None], 0)
        w_mine = lax.psum(spread.astype(LOW), "shard").reshape(query_cols, MODEL_WIDTH)

    d_tail = columns([routes], length)
    d_all = lax.all_gather(
        jnp.concatenate([d_out, d_tail], axis=1), both, axis=0, tiled=False
    )

    unit_plane, inverse_plane = unit_norm(plane_tokens)
    h1 = (unit_plane * gain_one).astype(LOW)
    projected = dot("bqd,df->bqf", h1, wqkv)
    half = HEAD_SIZE // 2
    frequency = THETA ** (-2.0 * jnp.arange(half, dtype=FULL) / HEAD_SIZE)
    angles = plane_places[:, :, None] * frequency
    cosine, sine = jnp.cos(angles), jnp.sin(angles)
    cosine_q, sine_q = cosine[:, :, None, :], sine[:, :, None, :]
    query_raw = projected[:, :, :query_cols].reshape(owners, length, heads, HEAD_SIZE)
    key_raw = projected[:, :, query_cols : query_cols + HEAD_SIZE]
    value = projected[:, :, query_cols + HEAD_SIZE :].astype(LOW)
    query_unit, query_inverse = unit_norm(query_raw)
    key_unit, key_inverse = unit_norm(key_raw)
    query = rotate(query_unit * gain_query, cosine_q, sine_q).astype(LOW)
    key = rotate(key_unit * gain_key, cosine, sine).astype(LOW)
    places = jnp.arange(length, dtype=jnp.int32)
    allowed = (plane_segments[:, :, None] == plane_segments[:, None, :]) & (
        places[None, :] <= places[:, None]
    )
    scores = dot("bqhd,bkd->bhqk", query, key) * scaling
    scores = jnp.where(allowed[:, None], scores, -1e30)
    highest = jnp.max(scores, axis=-1, keepdims=True)
    exponent = jnp.exp(scores - highest)
    probs = exponent / jnp.sum(exponent, axis=-1, keepdims=True)
    probs_low = probs.astype(LOW)
    mixed = dot("bhqk,bkd->bqhd", probs_low, value).astype(LOW)
    mixed = mixed.reshape(owners, length, query_cols)
    partial = dot("bqf,fd->bqd", mixed, w_mine).astype(LOW)
    branch = lax.psum_scatter(partial, "expert", scatter_dimension=0, tiled=False)

    middle = tokens.astype(FULL) + branch.astype(FULL)
    unit_two, inverse_two = unit_norm(middle)
    h2 = (unit_two * gain_two).astype(LOW)
    logits = dot("nd,de->ne", h2, router_full)
    chance = jax.nn.softmax(logits, axis=-1)
    named = jnp.sum(
        (routes[:, :, None] == jnp.arange(experts_all, dtype=jnp.int32)).astype(FULL), axis=1
    )
    chosen_sum = jnp.sum(named * chance, axis=1, keepdims=True)
    gates = named * chance / chosen_sum
    gates_high = gates.astype(LOW)
    gates_rest = (gates - gates_high.astype(FULL)).astype(LOW)
    h_all = lax.all_gather(
        jnp.concatenate([h2, gates_high, gates_rest], axis=1), both, axis=0, tiled=False
    )

    route_all = d_all[:, :, MODEL_WIDTH : MODEL_WIDTH + TOPK].astype(FULL)
    own_experts = (me * EXP_DEV + jnp.arange(EXP_DEV, dtype=jnp.int32)).astype(FULL)
    match = jnp.sum((route_all[:, :, :, None] == own_experts).astype(FULL), axis=2)
    earlier = (places[None, :] < places[:, None]).astype(LOW)
    rank = dot("ts,bsj->btj", earlier, match.astype(LOW))
    slot_ids = jnp.arange(capacity, dtype=jnp.int32).astype(FULL)
    place = jnp.where(match > 0, rank, -1.0).transpose(0, 2, 1)
    dispatch = (place[:, :, None, :] == slot_ids[:, None]).astype(LOW)

    def experts(h_rows, d_rows, gate_high, gate_rest, put):
        count = h_rows.shape[0]
        flat = put.reshape(count, EXP_DEV * capacity, length)
        x = dot("bst,btd->bsd", flat, h_rows).astype(LOW)
        dy = dot("bst,btd->bsd", flat, d_rows).astype(LOW)

        def by_expert(v):
            v = v.reshape(count, EXP_DEV, capacity, v.shape[-1])
            return v.transpose(1, 0, 2, 3).reshape(EXP_DEV, count * capacity, v.shape[-1])

        def by_block(v):
            v = v.reshape(EXP_DEV, count, capacity, v.shape[-1])
            return v.transpose(1, 0, 2, 3).reshape(count, EXP_DEV * capacity, v.shape[-1])

        x, dy = by_expert(x), by_expert(dy)
        gate_slot = dot("bjct,btj->jbc", put, gate_high) + dot("bjct,btj->jbc", put, gate_rest)
        gate_slot = gate_slot.reshape(EXP_DEV, count * capacity, 1)
        g = dot("erd,efd->erf", x, w_gate)
        u = dot("erd,efd->erf", x, w_up)
        da = dot("erd,edf->erf", dy, w_down)
        sigma = jax.nn.sigmoid(g)
        silu = g * sigma
        act = (silu * u).astype(LOW).astype(FULL)
        d_gate_slot = jnp.sum(act * da, axis=-1)
        act_gated = (act * gate_slot).astype(LOW)
        d_act = da * gate_slot
        dg = (d_act * u * sigma * (1.0 + g * (1.0 - sigma))).astype(LOW)
        du = (d_act * silu).astype(LOW)
        y = dot("erf,edf->erd", act_gated, w_down).astype(LOW)
        d_down = dot("erd,erf->edf", dy, act_gated)
        d_gate = dot("erf,erd->efd", dg, x)
        d_up = dot("erf,erd->efd", du, x)
        dx = (dot("erf,efd->erd", dg, w_gate) + dot("erf,efd->erd", du, w_up)).astype(LOW)
        mix = dot("bst,bsd->btd", flat, by_block(y)).astype(LOW)
        d_h = dot("bst,bsd->btd", flat, by_block(dx)).astype(LOW)
        d_g = dot(
            "bjct,jbc->btj", put.astype(FULL), d_gate_slot.reshape(EXP_DEV, count, capacity)
        )
        return mix, d_h, d_g, d_gate, d_up, d_down

    gate_cols = lax.dynamic_slice_in_dim(h_all, MODEL_WIDTH + me * EXP_DEV, EXP_DEV, 2)
    rest_cols = lax.dynamic_slice_in_dim(
        h_all, MODEL_WIDTH + experts_all + me * EXP_DEV, EXP_DEV, 2
    )
    step = min(blocks, GROUP_BLOCKS)
    mixes, d_hs, d_gs, totals = [], [], [], None
    for at in range(0, blocks, step):
        cut = slice(at, at + step)
        mix, d_h, d_g, *grads = experts(
            h_all[cut, :, :MODEL_WIDTH],
            d_all[cut, :, :MODEL_WIDTH],
            gate_cols[cut],
            rest_cols[cut],
            dispatch[cut],
        )
        mixes.append(mix)
        d_hs.append(d_h)
        d_gs.append(d_g)
        totals = grads if totals is None else [a + b for a, b in zip(totals, grads)]
    d_gate, d_up, d_down = totals
    d_g = jnp.concatenate(d_gs, axis=0)
    spread = jnp.zeros((blocks, length, TAIL), LOW)
    spread = lax.dynamic_update_slice_in_dim(spread, d_g.astype(LOW), me * EXP_DEV, 2)
    d_h_wide = jnp.concatenate([jnp.concatenate(d_hs, axis=0), spread], axis=2)

    def home(v):
        v = v.reshape(owners, planes, length, v.shape[-1])
        v = lax.psum_scatter(v, "expert", scatter_dimension=0, tiled=False)
        return lax.psum_scatter(v, "shard", scatter_dimension=0, tiled=False)

    d_home = home(d_h_wide)
    mixture = home(jnp.concatenate(mixes, axis=0))
    result = (middle + mixture.astype(FULL)).astype(LOW)

    upstream = d_out.astype(FULL)
    d_gates = d_home[:, MODEL_WIDTH : MODEL_WIDTH + experts_all].astype(FULL)
    d_chance = named * (d_gates - jnp.sum(d_gates * gates, axis=1, keepdims=True)) / chosen_sum
    d_logits = chance * (d_chance - jnp.sum(d_chance * chance, axis=1, keepdims=True))
    d_logits = d_logits.astype(LOW)
    d_h2 = d_home[:, :MODEL_WIDTH].astype(FULL) + dot("ne,de->nd", d_logits, router_full)
    d_gain_two = jnp.sum(d_h2 * unit_two, axis=0)
    d_middle = upstream + norm_back(d_h2, unit_two, inverse_two, gain_two)
    d_router = dot("nd,ne->de", h2, d_logits)

    d_branch = lax.all_gather(d_middle.astype(LOW), "expert", axis=0, tiled=False)
    d_w_out = dot("bqf,bqd->fd", mixed, d_branch).astype(LOW)
    d_mixed = dot("bqd,fd->bqf", d_branch, w_mine).astype(LOW)
    d_mixed = d_mixed.reshape(owners, length, heads, HEAD_SIZE)
    d_probs = dot("bqhd,bkd->bhqk", d_mixed, value)
    d_scores = probs * (d_probs - jnp.sum(d_probs * probs, axis=-1, keepdims=True))
    d_scores = d_scores.astype(LOW)
    d_query = dot("bhqk,bkd->bqhd", d_scores, key) * scaling
    d_key = dot("bhqk,bqhd->bkd", d_scores, query) * scaling
    d_value = dot("bhqk,bqhd->bkd", probs_low, d_mixed)
    d_query = rotate_back(d_query, cosine_q, sine_q)
    d_key = rotate_back(d_key, cosine, sine)
    d_gain_query = jnp.sum(d_query * query_unit, axis=(0, 1, 2))
    d_gain_key = jnp.sum(d_key * key_unit, axis=(0, 1))
    d_query = norm_back(d_query, query_unit, query_inverse, gain_query)
    d_key = norm_back(d_key, key_unit, key_inverse, gain_key)
    d_projected = jnp.concatenate(
        [d_query.reshape(owners, length, query_cols), d_key, d_value], axis=2
    ).astype(LOW)
    d_h1_part = dot("bqf,df->bqd", d_projected, wqkv).astype(LOW)
    d_h1 = lax.psum_scatter(d_h1_part, "expert", scatter_dimension=0, tiled=False).astype(FULL)
    resident = tokens.astype(FULL)
    unit_one, inverse_one = unit_norm(resident)
    d_gain_one = jnp.sum(d_h1 * unit_one, axis=0)
    d_tokens = (d_middle + norm_back(d_h1, unit_one, inverse_one, gain_one)).astype(LOW)

    d_wqkv = dot("bqd,bqf->df", h1, d_projected).astype(LOW)

    def by_rows(v):
        v = v.reshape(planes, per)
        return jnp.pad(v, ((0, 0), (0, rows_in - per))).reshape(-1)[:, None]

    d_tail = columns(
        [
            d_router,
            d_gain_one[:, None],
            d_gain_two[:, None],
            by_rows(d_gain_query),
            by_rows(d_gain_key),
        ],
        MODEL_WIDTH,
    )
    d_pack = lax.psum_scatter(
        jnp.concatenate([d_wqkv, d_tail], axis=1), "shard", scatter_dimension=0, tiled=True
    )
    d_pack = lax.all_gather(d_pack, "expert", axis=0, tiled=False).astype(FULL)
    d_q_cols = d_pack[:, :, :query_cols].transpose(1, 0, 2).reshape(rows_in, -1)
    d_kv = d_pack[:, :, query_cols:qkv_cols]
    d_kv = jnp.sum(d_kv.reshape(KEY_VALUE_HEADS, -1, rows_in, 2, HEAD_SIZE), axis=1)
    d_kv = d_kv.transpose(1, 2, 0, 3).reshape(rows_in, -1)
    d_qkv_weight = jnp.concatenate([d_q_cols, d_kv], axis=1)
    d_rest = jnp.sum(d_pack[:, :, qkv_cols:], axis=0)
    d_router_out = d_rest[:, :experts_all]
    d_gain_out = d_rest[:, experts_all:]

    d_w_out = d_w_out.reshape(query_cols, owners, -1)
    d_w_out = lax.all_to_all(d_w_out, "expert", split_axis=1, concat_axis=0, tiled=False)
    d_w_out = d_w_out.reshape(QUERY_HEADS * HEAD_SIZE, -1)
    d_w_out = lax.psum_scatter(d_w_out, "shard", scatter_dimension=0, tiled=True)
    d_w_out = lax.all_gather(d_w_out, "expert", axis=1, tiled=True).astype(FULL)

    return (
        result,
        d_tokens,
        d_gain_out[:, 0],
        d_qkv_weight,
        d_gain_out[:per, 2],
        d_gain_out[:per, 3],
        d_w_out,
        d_gain_out[:, 1],
        d_router_out,
        d_gate,
        d_up,
        d_down,
    )


def resident_layer(
    tokens,
    segments,
    routes,
    attn_gain,
    qkv_weight,
    query_gain,
    k_gain,
    w_out,
    ffn_gain,
    router,
    w_gate,
    w_up,
    w_down,
    d_out,
):
    owners = lax.axis_size("expert")
    planes = lax.axis_size("shard")
    me = lax.axis_index("expert")
    plane = lax.axis_index("shard")
    length = tokens.shape[0]
    blocks = owners * planes
    experts_all = router.shape[1]
    capacity = 3 * length * TOPK // (2 * experts_all)
    slots = 2 * capacity
    heads = QUERY_HEADS // owners
    query_cols = heads * HEAD_SIZE
    scaling = HEAD_SIZE ** (-0.5)
    rows_in = qkv_weight.shape[0]
    per = query_gain.shape[0]

    router_rows = rows_in // owners
    router_part = lax.dynamic_slice_in_dim(router, me * router_rows, router_rows, 0)
    router_part = columns([router_part], router_rows)
    row = lax.broadcasted_iota(jnp.int32, (16, rows_in), 0)
    gain_rows = jnp.zeros((16, rows_in), LOW)
    for at, gain in enumerate((attn_gain, ffn_gain, query_gain, k_gain)):
        gain = jnp.pad(gain, (0, rows_in - gain.shape[0]))
        gain_rows = jnp.where(row == at, gain[None, :], gain_rows)
    segment_row = segments[0]
    token_tail = columns([segment_row[:, None], positions_of(segment_row)[:, None]], length)
    token_rows = jnp.concatenate([tokens, token_tail], axis=1)
    d_rows = jnp.concatenate([d_out, columns([routes], length)], axis=1)
    frequency = THETA ** (-2.0 * np.arange(HEAD_SIZE // 2) / HEAD_SIZE)
    frequency = jnp.asarray(np.tile(frequency, (8, 2)).astype(np.float32))
    d_all, w_mine, w_all, router_all, gain_all, tail, h1, projected, probs_low, mixed, branch = front(
        qkv_weight, router_part, gain_rows, token_rows, w_out, d_rows, frequency, planes, owners, 5
    )
    gains = gain_all.astype(FULL)
    gain_one, gain_two = gains[:, 0].reshape(-1), gains[:, 1].reshape(-1)
    router_full = router_all.transpose(1, 0, 2, 3).reshape(MODEL_WIDTH, -1)[:, :experts_all]

    lanes = jnp.arange(2 * experts_all, dtype=jnp.int32) % experts_all
    own = (me * EXP_DEV + jnp.arange(EXP_DEV, dtype=jnp.int32))[:, None] == lanes
    sel = jnp.broadcast_to(own.astype(FULL)[:, None, :], (EXP_DEV, 8, 2 * experts_all))

    middle = tokens.astype(FULL) + branch
    unit_two, inverse_two = unit_norm(middle)
    h2 = (unit_two * gain_two).astype(LOW)
    logits = dot("nd,de->ne", h2, router_full)
    chance = jax.nn.softmax(logits, axis=-1)
    named = jnp.sum(
        (routes[:, :, None] == jnp.arange(experts_all, dtype=jnp.int32)).astype(FULL), axis=1
    )
    chosen_sum = jnp.sum(named * chance, axis=1, keepdims=True)
    gates = named * chance / chosen_sum
    gates_high = gates.astype(LOW)
    gates_rest = (gates - gates_high.astype(FULL)).astype(LOW)
    h_rows = jnp.concatenate([h2, gates_high, gates_rest], axis=1)

    x, dy, hot = gather_dispatch(h_rows, d_all, planes, slots, 1)
    y, dx, d_gate, d_up, d_down = expert_pass(sel, x, dy, w_gate, w_up, w_down.swapaxes(1, 2))
    d_down = d_down.swapaxes(1, 2)
    d_home, mixture = combine_home(hot, dx, y, length, planes, slots, 2)

    upstream = d_out.astype(FULL)
    d_gates = d_home[:, MODEL_WIDTH:]
    d_gates = d_gates[:, :experts_all] + d_gates[:, experts_all:]
    d_chance = named * (d_gates - jnp.sum(d_gates * gates, axis=1, keepdims=True)) / chosen_sum
    d_logits = chance * (d_chance - jnp.sum(d_chance * chance, axis=1, keepdims=True))
    d_logits = d_logits.astype(LOW)
    d_h2 = d_home[:, :MODEL_WIDTH] + dot("ne,de->nd", d_logits, router_full)
    d_gain_two = jnp.sum(d_h2 * unit_two, axis=0, keepdims=True)
    d_middle = upstream + norm_back(d_h2, unit_two, inverse_two, gain_two)

    *parts, d_h1 = back(
        d_middle.astype(LOW), w_mine, mixed, projected, probs_low, tail, gain_all, frequency, h1,
        w_all, tokens, h2, columns([d_logits], length), d_gain_two, planes, owners, 4,
    )
    d_w_out, d_qkv_weight, d_router, d_gains, result, d_tokens = finish_grads(
        *parts, tokens, middle, mixture, d_middle, d_h1, gain_one[None], owners
    )
    return (
        result,
        d_tokens,
        d_gains[GAIN_ONE - experts_all],
        d_qkv_weight,
        lax.dynamic_slice_in_dim(d_gains[GAIN_QUERY - experts_all], plane * per, per, 0),
        lax.dynamic_slice_in_dim(d_gains[GAIN_KEY - experts_all], plane * per, per, 0),
        d_w_out,
        d_gains[0],
        d_router,
        d_gate,
        d_up,
        d_down,
    )


def per_device(*args):
    blocks = lax.axis_size("expert") * lax.axis_size("shard")
    row_bytes = 2 * (MODEL_WIDTH + TAIL)
    if blocks * args[0].shape[0] * row_bytes <= RESIDENT:
        return resident_layer(*args)
    return gathered_layer(*args)


def solution(mesh):
    placed = (
        P(("expert", "shard"), None),
        P(("expert", "shard"), None),
        P(("expert", "shard"), None),
        P("shard"),
        P("shard", None),
        P("shard"),
        P("shard"),
        P("shard", None),
        P("shard"),
        P("shard", None),
        P("expert", "shard", None),
        P("expert", "shard", None),
        P("expert", None, "shard"),
        P(("expert", "shard"), None),
    )
    return jax.shard_map(
        per_device,
        mesh=mesh,
        in_specs=placed,
        out_specs=(
            P(("expert", "shard"), None),
            P(("expert", "shard"), None),
            P("shard"),
            P("shard", None),
            P("shard"),
            P("shard"),
            P("shard", None),
            P("shard"),
            P("shard", None),
            P("expert", "shard", None),
            P("expert", "shard", None),
            P("expert", None, "shard"),
        ),
        check_vma=False,
    )
```
